32 devices in a mesh: dp: 16 (over z, y, x), mp: 2 (over core).
Axes of the slice: x: 2, y: 2, z: 4, core: 2. Of those that a mesh axis runs over, the one named last changes fastest.
Arguments:
- tokens: bfloat16 [16384, 768], P('dp'), may hold values from -6 to 6
- masked: int32 [16384], P('dp'), may hold values 0 or 1
- lengths: int32 [128], P('dp'), may hold values from 66 to 128, as said below
- mask_vector: bfloat16 [768], replicated, may hold values from -6 to 6
- w_query: bfloat16 [768, 768], P('dp', 'mp'), may hold values from -0.21875 to 0.21875
- b_query: bfloat16 [768], P('mp'), may hold values from -3 to 3
- w_key: bfloat16 [768, 768], P('dp', 'mp'), may hold values from -0.21875 to 0.21875
- w_value: bfloat16 [768, 768], P('dp', 'mp'), may hold values from -0.21875 to 0.21875
- b_value: bfloat16 [768], P('mp'), may hold values from -3 to 3
- w_out: bfloat16 [768, 768], P('mp', 'dp'), may hold values from -1.25 to 1.25
- b_out: bfloat16 [768], replicated, may hold values from -3 to 3
- gain_one: bfloat16 [768], replicated, may hold values from 0.099609375 to 1.8984375
- shift_one: bfloat16 [768], replicated, may hold values from -2 to 2
- w_up: bfloat16 [768, 3072], P('dp', 'mp'), may hold values from -0.21875 to 0.21875
- b_up: bfloat16 [3072], P('mp'), may hold values from -3 to 3
- w_down: bfloat16 [3072, 768], P('mp', 'dp'), may hold values from -0.109375 to 0.109375
- b_down: bfloat16 [768], replicated, may hold values from -3 to 3
- gain_two: bfloat16 [768], replicated, may hold values from 0.099609375 to 1.8984375
- shift_two: bfloat16 [768], replicated, may hold values from -2 to 2
- grad_out: bfloat16 [16384, 768], P('dp'), may hold values from -6 to 6
Outputs:
- out: bfloat16 [16384, 768], P('dp')
- d_tokens: float32 [16384, 768], P('dp')
- d_mask_vector: float32 [768], replicated
- d_w_query: float32 [768, 768], P('dp', 'mp')
- d_b_query: float32 [768], P('mp')
- d_w_key: float32 [768, 768], P('dp', 'mp')
- d_w_value: float32 [768, 768], P('dp', 'mp')
- d_b_value: float32 [768], P('mp')
- d_w_out: float32 [768, 768], P('mp', 'dp')
- d_b_out: float32 [768], replicated
- d_gain_one: float32 [768], replicated
- d_shift_one: float32 [768], replicated
- d_w_up: float32 [768, 3072], P('dp', 'mp')
- d_b_up: float32 [3072], P('mp')
- d_w_down: float32 [3072, 768], P('mp', 'dp')
- d_b_down: float32 [768], replicated
- d_gain_two: float32 [768], replicated
- d_shift_two: float32 [768], replicated
The draws below stay inside these ranges and needn't reach their ends.
Inputs may be any that keep to these rules, and one draw needn't show every extreme that they name: `lengths`: the first chain of each aligned block of 8 chains uses all 128 slots; the others lose up to 62 slots, small losses more often than large ones.
All inputs are finite; a program needn't handle non-finite values. No bound on the sum of `masked` on one device may be relied on, other than what follows from the above.
Results may differ from the reference program's by a relative error of at most 0.018.
Values may be sent and summed in bfloat16 or wider, within the bound.
No kernel may reach another device: no remote copies, remote signals or barrier semaphores. Data moves between devices by JAX's collectives and lax.ppermute only.
A program may use at most 128 MiB of HBM per device.

```python
import jax
import jax.numpy as jnp
from jax import lax

D = 768
HEADS = 12
HEAD = 64
FF = 3072
SLOTS = 128
CHAINS_DEV = 8
CHAINS = 128
TOKENS = 16384
N_MP = 2


def draw_lengths(key, part):
    key = jax.random.fold_in(key, 5)
    half_slots = SLOTS // 2
    picked = jax.random.randint(key, (CHAINS,), 0, half_slots)
    shorten = picked * picked // half_slots
    leading = jnp.arange(CHAINS) % CHAINS_DEV == 0
    return jnp.where(leading, SLOTS, SLOTS - shorten).astype(jnp.int32)


def with_ends(values, key, low, high):
    dims = values.shape
    index_at = [jax.random.randint(jax.random.fold_in(key, axis), (), 0, dims[axis]) for axis in range(len(dims))]
    values = values.at[tuple(index_at)].set(low)
    longest = dims.index(max(dims))
    index_at[longest] = (index_at[longest] + 1) % dims[longest]
    return values.at[tuple(index_at)].set(high)


def spiked(drawn, stream_key, source, target, blocks, factor):
    def block_of(axis_at):
        return (jnp.arange(drawn.shape[axis_at]) // (drawn.shape[axis_at] // blocks)).reshape((-1,) + (1,) * (drawn.ndim - 1 - axis_at))

    near = jax.random.permutation(stream_key, blocks)[block_of(target)]
    other_side = (block_of(target) + blocks // 2) % blocks
    return jnp.where((block_of(source) == near) | (block_of(source) == other_side), factor * drawn, drawn)


def block_scale(rng, dims, pieces, low, top_value):
    loudness = 1.0
    for dim, parts in pieces:
        heights = jax.random.uniform(jax.random.fold_in(jax.random.fold_in(rng, 6), dim), (parts,), jnp.float32, low / len(pieces), top_value / len(pieces))
        loudness = loudness * jnp.repeat(jnp.exp(heights), dims[dim] // parts).reshape((-1,) + (1,) * (len(dims) - 1 - dim))
    return loudness


def scatter_about(rng, extent, deviation, limit, cuts=(), held_as=jnp.bfloat16):
    drawn = jax.random.normal(rng, extent, jnp.float32) * deviation
    if len(cuts) > 0:
        drawn = block_scale(rng, extent, cuts, -0.22, 0.18) * drawn
    return jnp.clip(drawn, min=-limit, max=limit).astype(held_as)


def gaussian_with(key, shape, spread, most, cuts, heavy, dtype=jnp.bfloat16):
    entries = spread * jax.random.normal(key, shape, jnp.float32)
    if cuts:
        entries = entries * block_scale(key, shape, cuts, -0.22, 0.18)
    return jnp.clip(spiked(entries, jax.random.fold_in(key, 3), *heavy), -most, most).astype(dtype)


def setup_inputs(seed: int = 0) -> dict:
    seeds = jax.random.split(jax.random.key(seed), 21)
    return {
        "tokens": scatter_about(seeds[0], (TOKENS, D), 1.0, 6.0, ((0, 16),)),
        "masked": with_ends((jax.random.randint(seeds[1], (TOKENS,), 0, 20) < 3).astype(jnp.int32), jax.random.fold_in(seeds[1], 1), 0, 1),
        "lengths": draw_lengths(jax.random.fold_in(seeds[20], 71), 0),
        "mask_vector": scatter_about(seeds[3], (D,), 1.0, 6.0),
        "w_query": scatter_about(seeds[4], (D, D), D ** -0.5, 0.21875, ((0, 16), (1, 2))),
        "b_query": scatter_about(seeds[5], (D,), 0.5, 3.0, ((0, 2),)),
        "w_key": scatter_about(seeds[6], (D, D), D ** -0.5, 0.21875, ((0, 16), (1, 2))),
        "w_value": scatter_about(seeds[7], (D, D), D ** -0.5, 0.21875, ((0, 16), (1, 2))),
        "b_value": scatter_about(seeds[8], (D,), 0.5, 3.0, ((0, 2),)),
        "w_out": scatter_about(seeds[9], (D, D), (max(4 * D // SLOTS, 1)) ** -0.5, 1.25, ((0, 2), (1, 16))),
        "b_out": scatter_about(seeds[10], (D,), 0.5, 3.0),
        "gain_one": jnp.clip(1.0 + 0.18 * jax.random.normal(seeds[11], (D,), jnp.float32), 0.099609375, 1.8984375).astype(jnp.bfloat16),
        "shift_one": scatter_about(seeds[12], (D,), 0.3, 2.0),
        "w_up": scatter_about(seeds[13], (D, FF), D ** -0.5, 0.21875, ((0, 16), (1, 2))),
        "b_up": scatter_about(seeds[14], (FF,), 0.5, 3.0, ((0, 2),)),
        "w_down": scatter_about(seeds[15], (FF, D), FF ** -0.5, 0.109375, ((0, 2), (1, 16))),
        "b_down": scatter_about(seeds[16], (D,), 0.5, 3.0),
        "gain_two": jnp.clip(1.0 + 0.18 * jax.random.normal(seeds[17], (D,), jnp.float32), 0.099609375, 1.8984375).astype(jnp.bfloat16),
        "shift_two": scatter_about(seeds[18], (D,), 0.3, 2.0),
        "grad_out": gaussian_with(seeds[19], (TOKENS, D), 1.0, 6.0, ((0, 16),), (0, 1, 16, 2.0)),
    }


@jax.custom_vjp
def low(v):
    return lax.optimization_barrier(v.astype(jnp.bfloat16)).astype(jnp.float32)

@jax.custom_vjp
def low_back(v):
    return v

def low_keep(v):
    return (low(v), None)

def low_pass(kept, grad):
    return (grad,)

def back_keep(v):
    return (v, None)

def back_low(kept, grad):
    return (low(grad),)
low.defvjp(low_keep, low_pass)
low_back.defvjp(back_keep, back_low)
NORM_EPS = 1e-05
PRECISE = lax.Precision.HIGHEST

def product(left, right):
    return jnp.dot(left, right, precision=PRECISE, preferred_element_type=jnp.float32)

def layer_norm(values, norm_gain, norm_shift):
    row_mean = lax.optimization_barrier(jnp.mean(values, axis=-1, keepdims=True))
    centred = values - row_mean
    variance = lax.optimization_barrier(jnp.mean(centred * centred, axis=-1, keepdims=True))
    return centred * lax.rsqrt(variance + NORM_EPS) * norm_gain + norm_shift

def split_sum(left, right):
    part_cols = left.shape[1] // N_MP
    summed = jnp.zeros((left.shape[0], right.shape[1]), jnp.float32)
    for member in range(N_MP):
        partial_out = product(left[:, member * part_cols:(member + 1) * part_cols], right[member * part_cols:(member + 1) * part_cols])
        summed = summed + low_back(low(partial_out))
    return summed

def attend(queries, keys_in, values_in, key_valid):
    scores = jnp.einsum('cqhe,ckhe->chqk', queries, keys_in, precision=PRECISE)
    scores = low_back(scores * HEAD ** (-0.5))
    scores = jnp.where(key_valid[:, None, None, :], scores, -1e+30)
    row_max = lax.optimization_barrier(jnp.max(scores, axis=-1, keepdims=True))
    exp_terms = jnp.exp(scores - row_max)
    attn_prob = exp_terms / lax.optimization_barrier(jnp.sum(exp_terms, axis=-1, keepdims=True))
    return jnp.einsum('chqk,ckhe->cqhe', low(attn_prob), values_in, precision=PRECISE)

def layer_group(params, group_tokens, mask_flags, chain_lens):
    mask_vector, w_query, b_query, w_key, w_value, b_value, w_out, b_out, gain_one, shift_one, w_up, b_up, w_down, b_down, gain_two, shift_two = params
    chain_count = chain_lens.shape[0]
    layer_in = jnp.where((mask_flags == 1)[:, None], mask_vector[None, :], group_tokens)
    in_low = low(layer_in)
    head_shape = (chain_count, SLOTS, HEADS, HEAD)
    query_low = low_back(low(product(in_low, w_query) + b_query)).reshape(head_shape)
    key_low = low_back(low(product(in_low, w_key))).reshape(head_shape)
    value_low = low_back(low(product(in_low, w_value) + b_value)).reshape(head_shape)
    key_valid = jnp.arange(SLOTS)[None, :] < chain_lens[:, None]
    attended = attend(query_low, key_low, value_low, key_valid).reshape(chain_count * SLOTS, D)
    attended = low_back(low(attended))
    hidden = layer_norm(layer_in + split_sum(attended, w_out) + b_out, gain_one, shift_one)
    pre_act = low_back(product(low(hidden), w_up)) + b_up
    activated = low(jax.nn.gelu(pre_act, approximate=False))
    return layer_norm(hidden + split_sum(activated, w_down) + b_down, gain_two, shift_two)

def reference(tokens, masked, lengths, mask_vector, w_query, b_query, w_key, w_value, b_value, w_out, b_out, gain_one, shift_one, w_up, b_up, w_down, b_down, gain_two, shift_two, grad_out):
    params = tuple((weight.astype(jnp.float32) for weight in (mask_vector, w_query, b_query, w_key, w_value, b_value, w_out, b_out, gain_one, shift_one, w_up, b_up, w_down, b_down, gain_two, shift_two)))
    group_count = lengths.shape[0] // CHAINS_DEV
    flag_groups = masked.reshape(group_count, -1)
    length_groups = lengths.reshape(group_count, -1)

    def forward(weights, inputs):

        def run_group(group_item):
            return layer_group(weights, group_item[0], group_item[1], group_item[2])
        outputs = lax.map(jax.checkpoint(run_group), (inputs.reshape(group_count, -1, D), flag_groups, length_groups))
        return outputs.reshape(-1, D)
    result, pullback = jax.vjp(forward, params, tokens.astype(jnp.float32))
    weight_grads, token_grads = pullback(grad_out.astype(jnp.float32))
    d_mask_vector, d_w_query, d_b_query, d_w_key, d_w_value, d_b_value, d_w_out, d_b_out, d_gain_one, d_shift_one, d_w_up, d_b_up, d_w_down, d_b_down, d_gain_two, d_shift_two = weight_grads
    return (result.astype(jnp.bfloat16), token_grads, d_mask_vector, d_w_query, d_b_query, d_w_key, d_w_value, d_b_value, d_w_out, d_b_out, d_gain_one, d_shift_one, d_w_up, d_b_up, d_w_down, d_b_down, d_gain_two, d_shift_two)
```

```python
import functools

import jax
import jax.numpy as jnp
from jax import lax
from jax.experimental import pallas as pl
from jax.experimental.pallas import tpu as pltpu
from jax.sharding import PartitionSpec as P

HEAD = 64
NORM_EPS = 1e-05

F32 = jnp.float32
B16 = jnp.bfloat16


def norm_back(incoming, normed, inverse, norm_gain):
    scaled = incoming * norm_gain
    inner = (
        scaled
        - jnp.mean(scaled, axis=-1, keepdims=True)
        - normed * jnp.mean(scaled * normed, axis=-1, keepdims=True)
    )
    return (inverse * inner, jnp.sum(incoming * normed, axis=0), jnp.sum(incoming, axis=0))


def layer_norm(values, norm_gain, norm_shift):
    row_mean = jnp.mean(values, axis=-1, keepdims=True)
    centred = values - row_mean
    inverse = lax.rsqrt(jnp.mean(centred * centred, axis=-1, keepdims=True) + NORM_EPS)
    normed = centred * inverse
    return (normed * norm_gain + norm_shift, normed, inverse)


def swap(values, bit, size, axis="dp"):
    return lax.ppermute(values, axis, [(i, i ^ bit) for i in range(size)])


def arrange_body(me_ref, own_ref, x_ref, y_ref, d1_ref, d2_ref, out_ref):
    me = me_ref[0]
    planes = own_ref.shape[0]
    half = planes // 2
    for k in range(planes):
        out_ref[me ^ (4 * k)] = own_ref[k]
        out_ref[me ^ (4 * k + 1)] = x_ref[k]
        out_ref[me ^ (4 * k + 2)] = y_ref[k]
        out_ref[me ^ (4 * k + 3)] = d1_ref[k] if k < half else d2_ref[k - half]


def spread_body(me_ref, in_ref, own_ref, x_ref, y_ref, d1_ref, d2_ref):
    me = me_ref[0]
    planes = own_ref.shape[0]
    half = planes // 2
    for k in range(planes):
        own_ref[k] = in_ref[me ^ (4 * k)]
        x_ref[k] = in_ref[me ^ (4 * k + 1)]
        y_ref[k] = in_ref[me ^ (4 * k + 2)]
        if k < half:
            d1_ref[k] = in_ref[me ^ (4 * k + 3)]
        else:
            d2_ref[k - half] = in_ref[me ^ (4 * k + 3)]


VMEM_SPEC = pl.BlockSpec(memory_space=pltpu.VMEM)
SMEM_SPEC = pl.BlockSpec(memory_space=pltpu.SMEM)


def gather_rows(piece, me, size):
    rows, cols = piece.shape
    planes = size // 4
    half = planes // 2
    own = jnp.stack([piece] + [swap(piece, 4 * k, size) for k in range(1, planes)])
    by_x = swap(own, 1, size)
    by_y = swap(own, 2, size)
    diag_one = swap(by_x[:half], 2, size)
    diag_two = swap(by_y[half:], 1, size)
    full = pl.pallas_call(
        arrange_body,
        out_shape=jax.ShapeDtypeStruct((size, rows, cols), piece.dtype),
        in_specs=[SMEM_SPEC] + [VMEM_SPEC] * 5,
        out_specs=VMEM_SPEC,
    )(me, own, by_x, by_y, diag_one, diag_two)
    return full.reshape(size * rows, cols)


def scatter_rows(full, me, size):
    all_rows, cols = full.shape
    rows = all_rows // size
    planes = size // 4
    half = planes // 2
    shape = functools.partial(jax.ShapeDtypeStruct, dtype=full.dtype)
    own, for_x, for_y, diag_one, diag_two = pl.pallas_call(
        spread_body,
        out_shape=[
            shape((planes, rows, cols)),
            shape((planes, rows, cols)),
            shape((planes, rows, cols)),
            shape((half, rows, cols)),
            shape((planes - half, rows, cols)),
        ],
        in_specs=[SMEM_SPEC, VMEM_SPEC],
        out_specs=[VMEM_SPEC] * 5,
    )(me, full.reshape(size, rows, cols))
    from_x = swap(diag_one, 1, size)
    from_y = swap(diag_two, 2, size)
    for_y = jnp.concatenate(
        [(for_y[:half].astype(F32) + from_x.astype(F32)).astype(B16), for_y[half:]]
    )
    for_x = jnp.concatenate(
        [for_x[:half], (for_x[half:].astype(F32) + from_y.astype(F32)).astype(B16)]
    )
    from_x = swap(for_x, 1, size)
    from_y = swap(for_y, 2, size)
    total = own.astype(F32) + from_x.astype(F32) + from_y.astype(F32)
    result = total[0]
    for k in range(1, planes):
        result = result + swap(total[k].astype(B16), 4 * k, size).astype(F32)
    return result


def sum_small(values, size):
    values = values + swap(values, 1, size)
    values = values + swap(values, 2, size)
    bit = 4
    while bit < size:
        values = values + swap(values, bit, size)
        bit *= 2
    return values


def pair_sum(partial):
    low = partial.astype(B16)
    other = lax.ppermute(low, "mp", [(0, 1), (1, 0)])
    return low.astype(F32) + other.astype(F32)


def per_device(dp_size, tokens, masked, lengths, mask_vector, w_query, b_query, w_key, w_value,
               b_value, w_out, b_out, gain_one, shift_one, w_up, b_up, w_down, b_down, gain_two,
               shift_two, grad_out):
    rows_own = w_query.shape[0]
    head_cols = w_query.shape[1]
    units = w_up.shape[1]
    fast = rows_own % 16 == 0 and dp_size % 8 == 0 and dp_size & (dp_size - 1) == 0
    me = lax.axis_index("dp").astype(jnp.int32).reshape(1)

    def gather(piece):
        if fast:
            return gather_rows(piece, me, dp_size)
        return lax.all_gather(piece, "dp", axis=0, tiled=True)

    def scatter(full):
        if fast:
            return scatter_rows(full.astype(B16), me, dp_size)
        return lax.psum_scatter(full, "dp", scatter_dimension=0, tiled=True)

    def total(values):
        if fast:
            return sum_small(values, dp_size)
        return lax.psum(values, "dp")

    (mask_vector, b_query, b_value, b_out, gain_one, shift_one, b_up, b_down, gain_two, shift_two) = (
        member.astype(F32)
        for member in (mask_vector, b_query, b_value, b_out, gain_one, shift_one, b_up, b_down,
                       gain_two, shift_two)
    )
    wa = gather(jnp.concatenate([w_query, w_key, w_value, w_out.T], axis=1))
    w_up = gather(w_up)
    w_down_t = gather(w_down.T)
    w_qkv = wa[:, : 3 * head_cols]
    w_out_t = wa[:, 3 * head_cols :]

    chain_count = lengths.shape[0]
    row_count = tokens.shape[0]
    slot_count = row_count // chain_count
    local_heads = head_cols // HEAD
    score_scale = HEAD ** (-0.5)
    dot = functools.partial(jnp.dot, preferred_element_type=F32)
    ein = functools.partial(jnp.einsum, preferred_element_type=F32)

    is_masked = (masked == 1)[:, None]
    layer_in = jnp.where(is_masked, mask_vector[None, :], tokens.astype(F32))
    in_low = layer_in.astype(B16)
    head_shape = (chain_count, slot_count, local_heads, HEAD)
    qkv_bias = jnp.concatenate([b_query, jnp.zeros_like(b_query), b_value])
    qkv = (dot(in_low, w_qkv) + qkv_bias).astype(B16)
    query_low, key_low, value_low = (part.reshape(head_shape) for part in jnp.split(qkv, 3, axis=1))
    key_valid = (jnp.arange(slot_count)[None, :] < lengths[:, None])[:, None, None, :]
    scores = ein("cqhe,ckhe->chqk", query_low, key_low) * score_scale
    scores = jnp.where(key_valid, scores, -1e30)
    row_max = jnp.max(scores, axis=-1, keepdims=True)
    exp_terms = jnp.exp(scores - row_max)
    attn_prob = exp_terms / jnp.sum(exp_terms, axis=-1, keepdims=True)
    prob_low = attn_prob.astype(B16)
    attended = ein("chqk,ckhe->cqhe", prob_low, value_low)
    attended = attended.reshape(row_count, -1).astype(B16)
    attn_sum = pair_sum(ein("nh,dh->nd", attended, w_out_t)) + b_out
    hidden, normed_one, inverse_one = layer_norm(layer_in + attn_sum, gain_one, shift_one)
    hidden_low = hidden.astype(B16)
    pre_act = dot(hidden_low, w_up) + b_up
    cdf = 0.5 * (1.0 + lax.erf(pre_act * (2.0**-0.5)))
    slope = cdf + pre_act * jnp.exp(-0.5 * pre_act * pre_act) * (0.5 / jnp.pi) ** 0.5
    act_low = (pre_act * cdf).astype(B16)
    ffn_sum = pair_sum(ein("nf,df->nd", act_low, w_down_t)) + b_down
    result, normed_two, inverse_two = layer_norm(hidden + ffn_sum, gain_two, shift_two)
    out_grad = grad_out.astype(F32)
    dz_two, d_gain_two, d_shift_two = norm_back(out_grad, normed_two, inverse_two, gain_two)
    d_b_down = jnp.sum(dz_two, axis=0)
    dz_two_low = dz_two.astype(B16)
    d_w_down_t = scatter(ein("nd,nf->df", dz_two_low, act_low))
    d_act = dot(dz_two_low, w_down_t)
    d_pre = d_act * slope
    d_b_up = jnp.sum(d_pre, axis=0)
    d_pre_low = d_pre.astype(B16)
    d_w_up = scatter(ein("nd,nf->df", hidden_low, d_pre_low))
    d_hidden = dz_two + pair_sum(ein("nf,df->nd", d_pre_low, w_up))
    dz_one, d_gain_one, d_shift_one = norm_back(d_hidden, normed_one, inverse_one, gain_one)
    d_b_out = jnp.sum(dz_one, axis=0)
    dz_one_low = dz_one.astype(B16)
    d_w_out_t = ein("nd,nh->dh", dz_one_low, attended)
    d_attended = dot(dz_one_low, w_out_t).astype(B16).reshape(head_shape)
    d_prob = ein("cqhe,ckhe->chqk", d_attended, value_low)
    d_scores = attn_prob * (d_prob - jnp.sum(attn_prob * d_prob, axis=-1, keepdims=True))
    d_scores_low = d_scores.astype(B16)
    d_query = ein("chqk,ckhe->cqhe", d_scores_low, key_low) * score_scale
    d_key = ein("chqk,cqhe->ckhe", d_scores_low, query_low) * score_scale
    d_value = ein("chqk,cqhe->ckhe", prob_low, d_attended)
    d_qkv = jnp.concatenate(
        [part.astype(B16).reshape(row_count, -1) for part in (d_query, d_key, d_value)], axis=1
    )
    d_b_qkv = jnp.sum(d_qkv.astype(F32), axis=0)
    d_w_qkv = ein("nd,nh->dh", in_low, d_qkv)
    d_wa = scatter(jnp.concatenate([d_w_qkv, d_w_out_t], axis=1))
    d_layer_in = dz_one + pair_sum(ein("nh,dh->nd", d_qkv, w_qkv))
    d_tokens = jnp.where(is_masked, 0.0, d_layer_in)
    d_mask_vector = jnp.sum(jnp.where(is_masked, d_layer_in, 0.0), axis=0)
    parts = (
        d_mask_vector,
        d_b_qkv[:head_cols],
        d_b_qkv[2 * head_cols :],
        d_b_out,
        d_gain_one,
        d_shift_one,
        d_b_up,
        d_b_down,
        d_gain_two,
        d_shift_two,
    )
    joined = total(jnp.concatenate(parts).reshape(-1, 128)).reshape(-1)
    summed = []
    start = 0
    for part in parts:
        summed.append(joined[start : start + part.shape[0]])
        start += part.shape[0]
    return (
        result.astype(B16),
        d_tokens,
        summed[0],
        d_wa[:, :head_cols],
        summed[1],
        d_wa[:, head_cols : 2 * head_cols],
        d_wa[:, 2 * head_cols : 3 * head_cols],
        summed[2],
        d_wa[:, 3 * head_cols :].T,
        summed[3],
        summed[4],
        summed[5],
        d_w_up,
        summed[6],
        d_w_down_t.T,
        summed[7],
        summed[8],
        summed[9],
    )


def solution(mesh):
    rows, flat, both = P("dp", None), P(), P("dp", "mp")
    return jax.shard_map(
        functools.partial(per_device, mesh.shape["dp"]),
        mesh=mesh,
        in_specs=(rows, P("dp"), P("dp"), flat, both, P("mp"), both, both, P("mp"), P("mp", "dp"),
                  flat, flat, flat, both, P("mp"), P("mp", "dp"), flat, flat, flat, rows),
        out_specs=(rows, rows, flat, both, P("mp"), both, both, P("mp"), P("mp", "dp"), flat, flat,
                   flat, both, P("mp"), P("mp", "dp"), flat, flat, flat),
        check_vma=False,
    )
```

```python
import functools

import jax
import jax.numpy as jnp
from jax import lax
from jax.experimental import pallas as pl
from jax.experimental.pallas import tpu as pltpu
from jax.sharding import PartitionSpec as P

HEAD = 64
NORM_EPS = 1e-05

F32 = jnp.float32
B16 = jnp.bfloat16


def norm_back(incoming, normed, inverse, norm_gain):
    scaled = incoming * norm_gain
    inner = (
        scaled
        - jnp.mean(scaled, axis=-1, keepdims=True)
        - normed * jnp.mean(scaled * normed, axis=-1, keepdims=True)
    )
    return (inverse * inner, jnp.sum(incoming * normed, axis=0), jnp.sum(incoming, axis=0))


def layer_norm(values, norm_gain, norm_shift):
    row_mean = jnp.mean(values, axis=-1, keepdims=True)
    centred = values - row_mean
    inverse = lax.rsqrt(jnp.mean(centred * centred, axis=-1, keepdims=True) + NORM_EPS)
    normed = centred * inverse
    return (normed * norm_gain + norm_shift, normed, inverse)


def swap(values, bit, size, axis="dp"):
    return lax.ppermute(values, axis, [(i, i ^ bit) for i in range(size)])


def arrange_body(me_ref, own_ref, x_ref, y_ref, d1_ref, d2_ref, out_ref):
    me = me_ref[0]
    planes = own_ref.shape[0]
    half = planes // 2
    for k in range(planes):
        out_ref[me ^ (4 * k)] = own_ref[k]
        out_ref[me ^ (4 * k + 1)] = x_ref[k]
        out_ref[me ^ (4 * k + 2)] = y_ref[k]
        out_ref[me ^ (4 * k + 3)] = d1_ref[k] if k < half else d2_ref[k - half]


def spread_body(me_ref, in_ref, own_ref, x_ref, y_ref, d1_ref, d2_ref):
    me = me_ref[0]
    planes = own_ref.shape[0]
    half = planes // 2
    for k in range(planes):
        own_ref[k] = in_ref[me ^ (4 * k)]
        x_ref[k] = in_ref[me ^ (4 * k + 1)]
        y_ref[k] = in_ref[me ^ (4 * k + 2)]
        if k < half:
            d1_ref[k] = in_ref[me ^ (4 * k + 3)]
        else:
            d2_ref[k - half] = in_ref[me ^ (4 * k + 3)]


VMEM_SPEC = pl.BlockSpec(memory_space=pltpu.VMEM)
SMEM_SPEC = pl.BlockSpec(memory_space=pltpu.SMEM)


def arrange(me, own, by_x, by_y, diag_one, diag_two):
    planes, rows, cols = own.shape
    full = pl.pallas_call(
        arrange_body,
        out_shape=jax.ShapeDtypeStruct((4 * planes, rows, cols), own.dtype),
        in_specs=[SMEM_SPEC] + [VMEM_SPEC] * 5,
        out_specs=VMEM_SPEC,
    )(me, own, by_x, by_y, diag_one, diag_two)
    return full.reshape(4 * planes * rows, cols)


def spread(me, full, size):
    all_rows, cols = full.shape
    rows = all_rows // size
    planes = size // 4
    half = planes // 2
    shape = functools.partial(jax.ShapeDtypeStruct, dtype=full.dtype)
    return pl.pallas_call(
        spread_body,
        out_shape=[
            shape((planes, rows, cols)),
            shape((planes, rows, cols)),
            shape((planes, rows, cols)),
            shape((half, rows, cols)),
            shape((planes - half, rows, cols)),
        ],
        in_specs=[SMEM_SPEC, VMEM_SPEC],
        out_specs=[VMEM_SPEC] * 5,
    )(me, full.reshape(size, rows, cols))


def along_z(piece, size):
    return jnp.stack([piece] + [swap(piece, 4 * k, size) for k in range(1, size // 4)])


def plane_one(own, size):
    return swap(own, 1, size), swap(own, 2, size)


def plane_two(by_x, by_y, size):
    half = by_x.shape[0] // 2
    return swap(by_x[:half], 2, size), swap(by_y[half:], 1, size)


def fold_one(diag_one, diag_two, size):
    return swap(diag_one, 1, size), swap(diag_two, 2, size)


def fold_two(for_x, for_y, from_x, from_y, size):
    half = from_x.shape[0]
    for_y = jnp.concatenate(
        [(for_y[:half].astype(F32) + from_x.astype(F32)).astype(B16), for_y[half:]]
    )
    for_x = jnp.concatenate(
        [for_x[:half], (for_x[half:].astype(F32) + from_y.astype(F32)).astype(B16)]
    )
    return swap(for_x, 1, size), swap(for_y, 2, size)


def fold_total(own, from_x, from_y):
    return own.astype(F32) + from_x.astype(F32) + from_y.astype(F32)


def fold_z(total, size):
    return [swap(total[k].astype(B16), 4 * k, size) for k in range(1, total.shape[0])]


def fold_sum(total, received):
    result = total[0]
    for piece in received:
        result = result + piece.astype(F32)
    return result


def tie(*values):
    return lax.optimization_barrier(values)


def sum_small(values, size):
    values = values + swap(values, 1, size)
    values = values + swap(values, 2, size)
    bit = 4
    while bit < size:
        values = values + swap(values, bit, size)
        bit *= 2
    return values


def pair_sum(partial):
    low = partial.astype(B16)
    other = lax.ppermute(low, "mp", [(0, 1), (1, 0)])
    return low.astype(F32) + other.astype(F32)


def per_device(dp_size, tokens, masked, lengths, mask_vector, w_query, b_query, w_key, w_value,
               b_value, w_out, b_out, gain_one, shift_one, w_up, b_up, w_down, b_down, gain_two,
               shift_two, grad_out):
    rows_own = w_query.shape[0]
    head_cols = w_query.shape[1]
    units = w_up.shape[1]
    fast = rows_own % 16 == 0 and dp_size % 8 == 0 and dp_size & (dp_size - 1) == 0
    me = lax.axis_index("dp").astype(jnp.int32).reshape(1)

    def total(values):
        if fast:
            return sum_small(values, dp_size)
        return lax.psum(values, "dp")

    (mask_vector, b_query, b_value, b_out, gain_one, shift_one, b_up, b_down, gain_two, shift_two) = (
        member.astype(F32)
        for member in (mask_vector, b_query, b_value, b_out, gain_one, shift_one, b_up, b_down,
                       gain_two, shift_two)
    )
    piece_a = jnp.concatenate([w_query, w_key, w_value, w_out.T], axis=1)
    piece_c = w_up
    piece_d = w_down.T
    if fast:
        own_a = along_z(piece_a, dp_size)
        own_a, piece_c = tie(own_a, piece_c)
        near_a = plane_one(own_a, dp_size)
        own_c = along_z(piece_c, dp_size)
        own_a, near_a, own_c, piece_d = tie(own_a, near_a, own_c, piece_d)
        far_a = plane_two(*near_a, dp_size)
        near_c = plane_one(own_c, dp_size)
        own_d = along_z(piece_d, dp_size)
        own_a, near_a, far_a, own_c, near_c, own_d = tie(own_a, near_a, far_a, own_c, near_c, own_d)
        wa = arrange(me, own_a, *near_a, *far_a)
    else:
        wa, w_up, w_down_t = (
            lax.all_gather(piece, "dp", axis=0, tiled=True) for piece in (piece_a, piece_c, piece_d)
        )
    w_qkv = wa[:, : 3 * head_cols]
    w_out_t = wa[:, 3 * head_cols :]

    chain_count = lengths.shape[0]
    row_count = tokens.shape[0]
    slot_count = row_count // chain_count
    local_heads = head_cols // HEAD
    score_scale = HEAD ** (-0.5)
    dot = functools.partial(jnp.dot, preferred_element_type=F32)
    ein = functools.partial(jnp.einsum, preferred_element_type=F32)

    is_masked = (masked == 1)[:, None]
    layer_in = jnp.where(is_masked, mask_vector[None, :], tokens.astype(F32))
    in_low = layer_in.astype(B16)
    head_shape = (chain_count, slot_count, local_heads, HEAD)
    qkv_bias = jnp.concatenate([b_query, jnp.zeros_like(b_query), b_value])
    qkv = (dot(in_low, w_qkv) + qkv_bias).astype(B16)
    query_low, key_low, value_low = (part.reshape(head_shape) for part in jnp.split(qkv, 3, axis=1))
    key_valid = (jnp.arange(slot_count)[None, :] < lengths[:, None])[:, None, None, :]
    scores = ein("cqhe,ckhe->chqk", query_low, key_low) * score_scale
    scores = jnp.where(key_valid, scores, -1e30)
    row_max = jnp.max(scores, axis=-1, keepdims=True)
    exp_terms = jnp.exp(scores - row_max)
    attn_prob = exp_terms / jnp.sum(exp_terms, axis=-1, keepdims=True)
    prob_low = attn_prob.astype(B16)
    attended = ein("chqk,ckhe->cqhe", prob_low, value_low)
    attended = attended.reshape(row_count, -1).astype(B16)
    attn_part = ein("nh,dh->nd", attended, w_out_t).astype(B16)
    if fast:
        far_c = plane_two(*near_c, dp_size)
        near_d = plane_one(own_d, dp_size)
        attn_part, far_c, near_d, own_c, near_c, own_d = tie(
            attn_part, far_c, near_d, own_c, near_c, own_d
        )
        far_d = plane_two(*near_d, dp_size)
        w_up = arrange(me, own_c, *near_c, *far_c)
    attn_sum = pair_sum(attn_part) + b_out
    hidden, normed_one, inverse_one = layer_norm(layer_in + attn_sum, gain_one, shift_one)
    hidden_low = hidden.astype(B16)
    pre_act = dot(hidden_low, w_up) + b_up
    cdf = 0.5 * (1.0 + lax.erf(pre_act * (2.0**-0.5)))
    slope = cdf + pre_act * jnp.exp(-0.5 * pre_act * pre_act) * (0.5 / jnp.pi) ** 0.5
    act_low = (pre_act * cdf).astype(B16)
    if fast:
        act_low, far_d, near_d, own_d = tie(act_low, far_d, near_d, own_d)
        w_down_t = arrange(me, own_d, *near_d, *far_d)
    ffn_sum = pair_sum(ein("nf,df->nd", act_low, w_down_t)) + b_down
    result, normed_two, inverse_two = layer_norm(hidden + ffn_sum, gain_two, shift_two)
    out_grad = grad_out.astype(F32)
    dz_two, d_gain_two, d_shift_two = norm_back(out_grad, normed_two, inverse_two, gain_two)
    d_b_down = jnp.sum(dz_two, axis=0)
    dz_two_low = dz_two.astype(B16)
    d_w_down_t = ein("nd,nf->df", dz_two_low, act_low)
    if fast:
        own_d, for_x_d, for_y_d, *far_d = spread(me, d_w_down_t.astype(B16), dp_size)
        far_d, own_d, for_x_d, for_y_d, dz_two_low = tie(far_d, own_d, for_x_d, for_y_d, dz_two_low)
        far_d = fold_one(*far_d, dp_size)
    d_act = dot(dz_two_low, w_down_t)
    d_pre = d_act * slope
    d_b_up = jnp.sum(d_pre, axis=0)
    d_pre_low = d_pre.astype(B16)
    d_w_up = ein("nd,nf->df", hidden_low, d_pre_low)
    hidden_part = ein("nf,df->nd", d_pre_low, w_up).astype(B16)
    if fast:
        far_d, d_w_up, hidden_part = tie(far_d, d_w_up, hidden_part)
        near_d = fold_two(for_x_d, for_y_d, *far_d, dp_size)
        own_c, for_x_c, for_y_c, *far_c = spread(me, d_w_up.astype(B16), dp_size)
        far_c = fold_one(*far_c, dp_size)
    d_hidden = dz_two + pair_sum(hidden_part)
    dz_one, d_gain_one, d_shift_one = norm_back(d_hidden, normed_one, inverse_one, gain_one)
    d_b_out = jnp.sum(dz_one, axis=0)
    dz_one_low = dz_one.astype(B16)
    if fast:
        near_d, far_c, for_x_c, for_y_c, dz_one_low = tie(near_d, far_c, for_x_c, for_y_c, dz_one_low)
        total_d = fold_total(own_d, *near_d)
        z_d = fold_z(total_d, dp_size)
        near_c = fold_two(for_x_c, for_y_c, *far_c, dp_size)
    d_w_out_t = ein("nd,nh->dh", dz_one_low, attended)
    d_attended = dot(dz_one_low, w_out_t).astype(B16).reshape(head_shape)
    d_prob = ein("cqhe,ckhe->chqk", d_attended, value_low)
    d_scores = attn_prob * (d_prob - jnp.sum(attn_prob * d_prob, axis=-1, keepdims=True))
    d_scores_low = d_scores.astype(B16)
    d_query = ein("chqk,ckhe->cqhe", d_scores_low, key_low) * score_scale
    d_key = ein("chqk,cqhe->ckhe", d_scores_low, query_low) * score_scale
    d_value = ein("chqk,cqhe->ckhe", prob_low, d_attended)
    d_qkv = jnp.concatenate(
        [part.astype(B16).reshape(row_count, -1) for part in (d_query, d_key, d_value)], axis=1
    )
    d_b_qkv = jnp.sum(d_qkv.astype(F32), axis=0)
    d_w_qkv = ein("nd,nh->dh", in_low, d_qkv)
    d_wa = jnp.concatenate([d_w_qkv, d_w_out_t], axis=1)
    if fast:
        d_wa, z_d, near_c = tie(d_wa, z_d, near_c)
        own_a, for_x_a, for_y_a, *far_a = spread(me, d_wa.astype(B16), dp_size)
        total_c = fold_total(own_c, *near_c)
        far_a = fold_one(*far_a, dp_size)
        z_c = fold_z(total_c, dp_size)
        far_a, for_x_a, for_y_a, z_c = tie(far_a, for_x_a, for_y_a, z_c)
        near_a = fold_two(for_x_a, for_y_a, *far_a, dp_size)
        total_a = fold_total(own_a, *near_a)
        z_a = fold_z(total_a, dp_size)
        d_wa = fold_sum(total_a, z_a)
        d_w_up = fold_sum(total_c, z_c)
        d_w_down_t = fold_sum(total_d, z_d)
    else:
        d_wa, d_w_up, d_w_down_t = (
            lax.psum_scatter(full, "dp", scatter_dimension=0, tiled=True)
            for full in (d_wa, d_w_up, d_w_down_t)
        )
    d_layer_in = dz_one + pair_sum(ein("nh,dh->nd", d_qkv, w_qkv))
    d_tokens = jnp.where(is_masked, 0.0, d_layer_in)
    d_mask_vector = jnp.sum(jnp.where(is_masked, d_layer_in, 0.0), axis=0)
    parts = (
        d_mask_vector,
        d_b_qkv[:head_cols],
        d_b_qkv[2 * head_cols :],
        d_b_out,
        d_gain_one,
        d_shift_one,
        d_b_up,
        d_b_down,
        d_gain_two,
        d_shift_two,
    )
    joined = total(jnp.concatenate(parts).reshape(-1, 128)).reshape(-1)
    summed = []
    start = 0
    for part in parts:
        summed.append(joined[start : start + part.shape[0]])
        start += part.shape[0]
    return (
        result.astype(B16),
        d_tokens,
        summed[0],
        d_wa[:, :head_cols],
        summed[1],
        d_wa[:, head_cols : 2 * head_cols],
        d_wa[:, 2 * head_cols : 3 * head_cols],
        summed[2],
        d_wa[:, 3 * head_cols :].T,
        summed[3],
        summed[4],
        summed[5],
        d_w_up,
        summed[6],
        d_w_down_t.T,
        summed[7],
        summed[8],
        summed[9],
    )


def solution(mesh):
    rows, flat, both = P("dp", None), P(), P("dp", "mp")
    return jax.shard_map(
        functools.partial(per_device, mesh.shape["dp"]),
        mesh=mesh,
        in_specs=(rows, P("dp"), P("dp"), flat, both, P("mp"), both, both, P("mp"), P("mp", "dp"),
                  flat, flat, flat, both, P("mp"), P("mp", "dp"), flat, flat, flat, rows),
        out_specs=(rows, rows, flat, both, P("mp"), both, both, P("mp"), P("mp", "dp"), flat, flat,
                   flat, both, P("mp"), P("mp", "dp"), flat, flat, flat),
        check_vma=False,
    )
```

```python
import functools

import jax
import jax.numpy as jnp
from jax import lax
from jax.experimental import pallas as pl
from jax.experimental.pallas import tpu as pltpu
from jax.sharding import PartitionSpec as P

HEAD = 64
NORM_EPS = 1e-05
F32 = jnp.float32
B16 = jnp.bfloat16
MIB = 1 << 20

BLOCKS = 16
NEAR = (0, 12)
MID = (4, 8)


def swap(values, bit):
    return lax.ppermute(values, "dp", [(i, i ^ bit) for i in range(BLOCKS)])


def tie(*values):
    return lax.optimization_barrier(values)


def pair_swap(partial):
    return lax.ppermute(partial, "mp", [(0, 1), (1, 0)])


def as_pieces(full):
    rows = full.shape[0] // BLOCKS
    blocks = full.reshape(BLOCKS, rows, full.shape[1])
    return [
        jnp.stack([blocks[offset + bits[0]], blocks[offset + bits[1]]])
        for offset in range(4)
        for bits in (NEAR, MID)
    ]


SMEM_SPEC = pl.BlockSpec(memory_space=pltpu.SMEM)


def whole(shape):
    zeros = (0,) * len(shape)
    return pl.BlockSpec(tuple(shape), lambda i: zeros)


def rows_of(count, width):
    return pl.BlockSpec((count, width), lambda i: (i, 0))


def fill(me, pieces, full_ref):
    rows = pieces[0].shape[1]
    for index, piece in enumerate(pieces):
        bits = (NEAR, MID)[index % 2]
        for k in range(2):
            block = me ^ (index // 2 + bits[k])
            full_ref[pl.ds(pl.multiple_of(block * rows, rows), rows), :] = piece[k]


def dot(left, right):
    return jnp.dot(left, right, preferred_element_type=F32)


def dot_t(left, right):
    return lax.dot_general(left, right, (((1,), (1,)), ((), ())), preferred_element_type=F32)


def t_dot(left, right):
    return lax.dot_general(left, right, (((0,), (0,)), ((), ())), preferred_element_type=F32)


def row_mean(values):
    return jnp.mean(values, axis=-1, keepdims=True)


def normalize(values):
    centred = values - row_mean(values)
    inverse = lax.rsqrt(row_mean(centred * centred) + NORM_EPS)
    return centred * inverse, inverse


def col_sum(values):
    return jnp.sum(values, axis=0, keepdims=True)


def norm_back(scaled, normed, inverse):
    return inverse * (scaled - row_mean(scaled) - normed * row_mean(scaled * normed))


def two_heads(slots):
    row = lax.broadcasted_iota(jnp.int32, (2 * slots, 2 * HEAD), 0) // slots
    lane = lax.broadcasted_iota(jnp.int32, (2 * slots, 2 * HEAD), 1) // HEAD
    return (row == lane).astype(F32).astype(B16)


def doubled(values, mask):
    return jnp.concatenate([values, values], axis=0) * mask


def attend_body(chains, slots, me_ref, len_ref, in_ref, bias_ref, *rest):
    pieces, (w_ref, qkv_ref, prob_ref, att_ref, part_ref) = rest[:8], rest[8:]
    step = pl.program_id(0)
    width = att_ref.shape[1]

    @pl.when(step == 0)
    def _():
        fill(me_ref[0], pieces, w_ref)

    qkv_ref[...] = (dot(in_ref[...], w_ref[:, : 3 * width]) + bias_ref[...]).astype(B16)
    mask = two_heads(slots)
    key_slot = lax.broadcasted_iota(jnp.int32, (slots, slots), 1)
    for chain in range(chains):
        valid = key_slot < len_ref[step * chains + chain]
        rows = pl.ds(chain * slots, slots)
        for pair in range(width // (2 * HEAD)):
            lanes = 2 * HEAD * pair
            query = qkv_ref[rows, lanes : lanes + 2 * HEAD]
            key = qkv_ref[rows, width + lanes : width + lanes + 2 * HEAD]
            value = qkv_ref[rows, 2 * width + lanes : 2 * width + lanes + 2 * HEAD]
            scores = dot_t(query * (HEAD**-0.5), doubled(key, mask))
            probs = []
            for head in range(2):
                part = jnp.where(valid, scores[:, head * slots : (head + 1) * slots], -1e30)
                terms = jnp.exp(part - jnp.max(part, axis=-1, keepdims=True))
                probs.append((terms / jnp.sum(terms, axis=-1, keepdims=True)).astype(B16))
            prob = jnp.concatenate(probs, axis=1)
            prob_ref[rows, 2 * slots * pair : 2 * slots * (pair + 1)] = prob
            att_ref[rows, lanes : lanes + 2 * HEAD] = dot(prob, doubled(value, mask)).astype(B16)
    part_ref[...] = dot_t(att_ref[...], w_ref[:, 3 * width :]).astype(B16)


def attend(me, lengths, in_low, bias, pieces):
    count, width = in_low.shape
    heads = bias.shape[1] // 3
    chains = 2 if lengths.shape[0] % 2 == 0 else 1
    slots = count // lengths.shape[0]
    rows = chains * slots
    shape = jax.ShapeDtypeStruct
    return pl.pallas_call(
        functools.partial(attend_body, chains, slots),
        grid=(count // rows,),
        in_specs=[SMEM_SPEC, SMEM_SPEC, rows_of(rows, width), whole(bias.shape)]
        + [whole(piece.shape) for piece in pieces],
        out_specs=[
            whole((width, 4 * heads)),
            rows_of(rows, 3 * heads),
            rows_of(rows, heads // HEAD * slots),
            rows_of(rows, heads),
            rows_of(rows, width),
        ],
        out_shape=[
            shape((width, 4 * heads), B16),
            shape((count, 3 * heads), B16),
            shape((count, heads // HEAD * slots), B16),
            shape((count, heads), B16),
            shape((count, width), B16),
        ],
        compiler_params=pltpu.CompilerParams(vmem_limit_bytes=32 * MIB),
        cost_estimate=pl.CostEstimate(
            flops=2 * count * width * 4 * heads, bytes_accessed=12 * MIB, transcendentals=0
        ),
        name="attend",
    )(me, lengths, in_low, bias, *pieces)


def up_body(me_ref, in_ref, own_ref, other_ref, vec_ref, bias_ref, *rest):
    pieces, (w_ref, normed_ref, inverse_ref, low_ref, act_ref, slope_ref) = rest[:8], rest[8:]

    @pl.when(pl.program_id(0) == 0)
    def _():
        fill(me_ref[0], pieces, w_ref)

    vectors = vec_ref[...]
    attn = own_ref[...].astype(F32) + other_ref[...].astype(F32) + vectors[0:1]
    normed, inverse = normalize(in_ref[...].astype(F32) + attn)
    normed_ref[...] = normed
    inverse_ref[...] = jnp.broadcast_to(inverse, inverse_ref.shape)
    hidden = normed * vectors[1:2] + vectors[2:3]
    low_ref[...] = hidden.astype(B16)
    pre = dot(low_ref[...], w_ref[...]) + bias_ref[...]
    cdf = 0.5 + 0.5 * lax.erf(pre * (2.0**-0.5))
    act_ref[...] = (pre * cdf).astype(B16)
    density = jnp.exp(pre * pre * -0.5) * 0.3989422804014327
    slope_ref[...] = (cdf + pre * density).astype(B16)


def up(me, in_low, own, other, vectors, bias, pieces):
    count, width = in_low.shape
    units = bias.shape[1]
    rows = count // 4
    shape = jax.ShapeDtypeStruct
    return pl.pallas_call(
        up_body,
        grid=(4,),
        in_specs=[SMEM_SPEC]
        + [rows_of(rows, width)] * 3
        + [whole(vectors.shape), whole(bias.shape)]
        + [whole(piece.shape) for piece in pieces],
        out_specs=[
            whole((width, units)),
            rows_of(rows, width),
            rows_of(rows, 128),
            rows_of(rows, width),
            rows_of(rows, units),
            rows_of(rows, units),
        ],
        out_shape=[
            shape((width, units), B16),
            shape((count, width), F32),
            shape((count, 128), F32),
            shape((count, width), B16),
            shape((count, units), B16),
            shape((count, units), B16),
        ],
        compiler_params=pltpu.CompilerParams(vmem_limit_bytes=40 * MIB),
        cost_estimate=pl.CostEstimate(
            flops=2 * count * width * units, bytes_accessed=20 * MIB, transcendentals=0
        ),
        name="up",
    )(me, in_low, own, other, vectors, bias, *pieces)


def down_body(me_ref, act_ref, *rest):
    pieces, (w_ref, part_ref) = rest[:8], rest[8:]

    @pl.when(pl.program_id(0) == 0)
    def _():
        fill(me_ref[0], pieces, w_ref)

    part_ref[...] = dot_t(act_ref[...], w_ref[...]).astype(B16)


def down(me, act, pieces):
    count, units = act.shape
    width = BLOCKS * pieces[0].shape[1]
    rows = count // 4
    shape = jax.ShapeDtypeStruct
    return pl.pallas_call(
        down_body,
        grid=(4,),
        in_specs=[SMEM_SPEC, rows_of(rows, units)] + [whole(piece.shape) for piece in pieces],
        out_specs=[whole((width, units)), rows_of(rows, width)],
        out_shape=[shape((width, units), B16), shape((count, width), B16)],
        compiler_params=pltpu.CompilerParams(vmem_limit_bytes=24 * MIB),
        cost_estimate=pl.CostEstimate(
            flops=2 * count * width * units, bytes_accessed=8 * MIB, transcendentals=0
        ),
        name="down",
    )(me, act, *pieces)


def second_norm_body(normed_ref, own_ref, other_ref, grad_ref, vec_ref, out_ref, dz_ref, low_ref, sum_ref):
    vectors = vec_ref[...]
    hidden = normed_ref[...] * vectors[0:1] + vectors[1:2]
    ffn = own_ref[...].astype(F32) + other_ref[...].astype(F32) + vectors[2:3]
    normed, inverse = normalize(hidden + ffn)
    out_ref[...] = (normed * vectors[3:4] + vectors[4:5]).astype(B16)
    grad = grad_ref[...].astype(F32)
    dz = norm_back(grad * vectors[3:4], normed, inverse)
    dz_ref[...] = dz
    low_ref[...] = dz.astype(B16)

    @pl.when(pl.program_id(0) == 0)
    def _():
        sum_ref[...] = jnp.zeros_like(sum_ref)

    sum_ref[0:1] += col_sum(grad * normed)
    sum_ref[1:2] += col_sum(grad)
    sum_ref[2:3] += col_sum(dz)


def second_norm(normed, own, other, grad, vectors):
    count, width = own.shape
    rows = count // 4
    shape = jax.ShapeDtypeStruct
    return pl.pallas_call(
        second_norm_body,
        grid=(4,),
        in_specs=[rows_of(rows, width)] * 4 + [whole(vectors.shape)],
        out_specs=[rows_of(rows, width)] * 3 + [whole((8, width))],
        out_shape=[
            shape((count, width), B16),
            shape((count, width), F32),
            shape((count, width), B16),
            shape((8, width), F32),
        ],
        compiler_params=pltpu.CompilerParams(vmem_limit_bytes=24 * MIB),
        cost_estimate=pl.CostEstimate(flops=40 * count * width, bytes_accessed=14 * MIB, transcendentals=0),
        name="second_norm",
    )(normed, own, other, grad, vectors)


def weight_grad_body(me_ref, lefts, right_ref, outs, turned_ref, full_ref):
    x_ref, y_ref, x_late_ref, y_late_ref, own_ref = outs
    step = pl.program_id(0)
    rows = own_ref.shape[1]
    first = 0
    for left_ref, tiles in lefts:

        @pl.when(step == first)
        def _(left_ref=left_ref):
            turned_ref[...] = left_ref[...].T

        first += tiles
    full_ref[...] = dot(turned_ref[...], right_ref[...]).astype(B16)

    def block(offset):
        at = me_ref[0] ^ offset
        return full_ref[pl.ds(pl.multiple_of(at * rows, rows), rows), :]

    for k in range(2):
        x_ref[k] = block(3 + NEAR[k])
        x_ref[2 + k] = block(1 + NEAR[k])
        x_late_ref[k] = block(1 + MID[k])
        y_ref[k] = block(3 + MID[k])
        y_ref[2 + k] = block(2 + MID[k])
        y_late_ref[k] = block(2 + NEAR[k])
        own_ref[k] = block(NEAR[k])
        own_ref[2 + k] = block(MID[k])


def weight_grad(me, lefts, rights):
    count, width = lefts[0].shape
    tile = 384 if all(right.shape[1] % 384 == 0 for right in rights) else 128
    tiles = [right.shape[1] // tile for right in rights]
    total = sum(tiles)
    rows = width // BLOCKS
    firsts = [sum(tiles[:k]) for k in range(len(tiles))]
    shape = jax.ShapeDtypeStruct

    def body(me_ref, *refs):
        n = len(lefts)
        left_refs, right_refs, outs = refs[:n], refs[n : 2 * n], refs[2 * n : 2 * n + 5]
        turned_ref, full_ref = refs[2 * n + 5 :]
        if n == 1:
            weight_grad_body(me_ref, [(left_refs[0], total)], right_refs[0], outs, turned_ref, full_ref)
            return
        step = pl.program_id(0)
        for k in range(n):

            @pl.when(jnp.logical_and(step >= firsts[k], step < firsts[k] + tiles[k]))
            def _(k=k):
                @pl.when(step == firsts[k])
                def _():
                    turned_ref[...] = left_refs[k][...].T

                weight_grad_body(me_ref, [], right_refs[k], outs, turned_ref, full_ref)

    def tile_of(first, number):
        return lambda i: (0, jnp.clip(i - first, 0, number - 1))

    def out_spec(number):
        return pl.BlockSpec((number, rows, tile), lambda i: (0, 0, i))

    sizes = (4, 4, 2, 2, 4)
    return pl.pallas_call(
        body,
        grid=(total,),
        in_specs=[SMEM_SPEC]
        + [whole(left.shape) for left in lefts]
        + [pl.BlockSpec((count, tile), tile_of(firsts[k], tiles[k])) for k in range(len(rights))],
        out_specs=[out_spec(number) for number in sizes],
        out_shape=[shape((number, rows, total * tile), B16) for number in sizes],
        scratch_shapes=[pltpu.VMEM((width, count), B16), pltpu.VMEM((width, tile), B16)],
        compiler_params=pltpu.CompilerParams(vmem_limit_bytes=28 * MIB),
        cost_estimate=pl.CostEstimate(
            flops=2 * count * width * total * tile, bytes_accessed=9 * MIB, transcendentals=0
        ),
        name="weight_grad",
    )(me, *lefts, *rights)


def hidden_back_body(low_ref, slope_ref, down_ref, up_ref, pre_ref, part_ref, sum_ref):
    d_pre = dot(low_ref[...], down_ref[...]) * slope_ref[...].astype(F32)

    @pl.when(pl.program_id(0) == 0)
    def _():
        sum_ref[...] = jnp.zeros_like(sum_ref)

    sum_ref[0:1] += col_sum(d_pre)
    pre_ref[...] = d_pre.astype(B16)
    part_ref[...] = dot_t(pre_ref[...], up_ref[...]).astype(B16)


def hidden_back(dz_low, slope, w_down_t, w_up):
    count, width = dz_low.shape
    units = slope.shape[1]
    rows = count // 4
    shape = jax.ShapeDtypeStruct
    return pl.pallas_call(
        hidden_back_body,
        grid=(4,),
        in_specs=[
            rows_of(rows, width),
            rows_of(rows, units),
            whole((width, units)),
            whole((width, units)),
        ],
        out_specs=[rows_of(rows, units), rows_of(rows, width), whole((8, units))],
        out_shape=[
            shape((count, units), B16),
            shape((count, width), B16),
            shape((8, units), F32),
        ],
        compiler_params=pltpu.CompilerParams(vmem_limit_bytes=28 * MIB),
        cost_estimate=pl.CostEstimate(
            flops=4 * count * width * units, bytes_accessed=12 * MIB, transcendentals=0
        ),
        name="hidden_back",
    )(dz_low, slope, w_down_t, w_up)


def attend_back_body(chains, slots, dz_ref, own_ref, other_ref, normed_ref, inverse_ref, gain_ref,
                     qkv_ref, prob_ref, w_ref, dz_one_ref, low_ref, d_qkv_ref, part_ref, sum_ref,
                     sum_qkv_ref, d_att_ref):
    width = d_att_ref.shape[1]
    normed = normed_ref[...]
    d_hidden = dz_ref[...] + (own_ref[...].astype(F32) + other_ref[...].astype(F32))
    dz_one = norm_back(d_hidden * gain_ref[...], normed, inverse_ref[:, 0:1])
    dz_one_ref[...] = dz_one
    low_ref[...] = dz_one.astype(B16)

    @pl.when(pl.program_id(0) == 0)
    def _():
        sum_ref[...] = jnp.zeros_like(sum_ref)
        sum_qkv_ref[...] = jnp.zeros_like(sum_qkv_ref)

    sum_ref[0:1] += col_sum(d_hidden * normed)
    sum_ref[1:2] += col_sum(d_hidden)
    sum_ref[2:3] += col_sum(dz_one)
    d_att_ref[...] = dot(low_ref[...], w_ref[:, 3 * width :]).astype(B16)
    mask = two_heads(slots)
    for chain in range(chains):
        rows = pl.ds(chain * slots, slots)
        for pair in range(width // (2 * HEAD)):
            lanes = 2 * HEAD * pair
            query = qkv_ref[rows, lanes : lanes + 2 * HEAD]
            key = qkv_ref[rows, width + lanes : width + lanes + 2 * HEAD]
            value = qkv_ref[rows, 2 * width + lanes : 2 * width + lanes + 2 * HEAD]
            d_att = d_att_ref[rows, lanes : lanes + 2 * HEAD]
            prob = prob_ref[rows, 2 * slots * pair : 2 * slots * (pair + 1)]
            d_prob = dot_t(d_att, doubled(value, mask))
            weights = prob.astype(F32)
            products = weights * d_prob
            lows = []
            for head in range(2):
                half = slice(head * slots, (head + 1) * slots)
                total = jnp.sum(products[:, half], axis=-1, keepdims=True)
                lows.append((products[:, half] - weights[:, half] * total).astype(B16))
            low = jnp.concatenate(lows, axis=1)
            d_query = dot(low, doubled(key, mask)) * (HEAD**-0.5)
            tall = jnp.concatenate(lows, axis=0)
            d_key = t_dot(tall, doubled(query, mask)) * (HEAD**-0.5)
            tall = jnp.concatenate([prob[:, :slots], prob[:, slots:]], axis=0)
            d_value = t_dot(tall, doubled(d_att, mask))
            d_qkv_ref[rows, lanes : lanes + 2 * HEAD] = d_query.astype(B16)
            d_qkv_ref[rows, width + lanes : width + lanes + 2 * HEAD] = d_key.astype(B16)
            d_qkv_ref[rows, 2 * width + lanes : 2 * width + lanes + 2 * HEAD] = d_value.astype(B16)
    sum_qkv_ref[0:1] += col_sum(d_qkv_ref[...].astype(F32))
    part_ref[...] = dot_t(d_qkv_ref[...], w_ref[:, : 3 * width]).astype(B16)


def attend_back(chain_count, dz_two, own, other, normed, inverse, gain, qkv, prob, w_a):
    count, width = dz_two.shape
    heads = qkv.shape[1] // 3
    chains = 2 if chain_count % 2 == 0 else 1
    slots = count // chain_count
    rows = chains * slots
    shape = jax.ShapeDtypeStruct
    return pl.pallas_call(
        functools.partial(attend_back_body, chains, slots),
        grid=(count // rows,),
        in_specs=[
            rows_of(rows, width),
            rows_of(rows, width),
            rows_of(rows, width),
            rows_of(rows, width),
            rows_of(rows, 128),
            whole(gain.shape),
            rows_of(rows, 3 * heads),
            rows_of(rows, prob.shape[1]),
            whole(w_a.shape),
        ],
        out_specs=[
            rows_of(rows, width),
            rows_of(rows, width),
            rows_of(rows, 3 * heads),
            rows_of(rows, width),
            whole((8, width)),
            whole((8, 3 * heads)),
        ],
        out_shape=[
            shape((count, width), F32),
            shape((count, width), B16),
            shape((count, 3 * heads), B16),
            shape((count, width), B16),
            shape((8, width), F32),
            shape((8, 3 * heads), F32),
        ],
        scratch_shapes=[pltpu.VMEM((rows, heads), B16)],
        compiler_params=pltpu.CompilerParams(vmem_limit_bytes=32 * MIB),
        cost_estimate=pl.CostEstimate(
            flops=2 * count * width * 6 * heads, bytes_accessed=20 * MIB, transcendentals=0
        ),
        name="attend_back",
    )(dz_two, own, other, normed, inverse, gain, qkv, prob, w_a)


def last_body(dz_ref, own_ref, other_ref, flag_ref, out_ref, sum_ref):
    total = dz_ref[...] + (own_ref[...].astype(F32) + other_ref[...].astype(F32))
    flag = flag_ref[:, 0:1]
    masked = total * flag

    @pl.when(pl.program_id(0) == 0)
    def _():
        sum_ref[...] = jnp.zeros_like(sum_ref)

    sum_ref[0:1] += col_sum(masked)
    out_ref[...] = total - masked


def last(dz_one, own, other, flag):
    count, width = dz_one.shape
    rows = count // 4
    shape = jax.ShapeDtypeStruct
    return pl.pallas_call(
        last_body,
        grid=(4,),
        in_specs=[rows_of(rows, width)] * 3 + [rows_of(rows, 128)],
        out_specs=[rows_of(rows, width), whole((8, width))],
        out_shape=[shape((count, width), F32), shape((8, width), F32)],
        compiler_params=pltpu.CompilerParams(vmem_limit_bytes=20 * MIB),
        cost_estimate=pl.CostEstimate(flops=10 * count * width, bytes_accessed=10 * MIB, transcendentals=0),
        name="last",
    )(dz_one, own, other, flag)


def near_total(own, from_x, from_y):
    return own[:2].astype(F32) + from_x.astype(F32) + from_y.astype(F32)


def add_low(left, right):
    return (left.astype(F32) + right.astype(F32)).astype(B16)


def per_device(dp_size, tokens, masked, lengths, mask_vector, w_query, b_query, w_key, w_value,
               b_value, w_out, b_out, gain_one, shift_one, w_up, b_up, w_down, b_down, gain_two,
               shift_two, grad_out):
    head_cols = w_query.shape[1]
    width = tokens.shape[1]
    fast = dp_size == BLOCKS and w_query.shape[0] % 16 == 0
    me = lax.axis_index("dp").astype(jnp.int32).reshape(1)
    if not fast:
        me = jnp.zeros_like(me)

    (b_query, b_value, b_out, gain_one, shift_one, b_up, b_down, gain_two, shift_two) = (
        member.astype(F32)
        for member in (b_query, b_value, b_out, gain_one, shift_one, b_up, b_down, gain_two, shift_two)
    )
    is_masked = (masked == 1)[:, None]
    flag = jnp.broadcast_to(is_masked, (masked.shape[0], 128)).astype(F32)
    in_low = jnp.where(is_masked, mask_vector[None, :], tokens)
    bias_qkv = jnp.concatenate([b_query, jnp.zeros_like(b_query), b_value])[None, :]
    vectors_one = jnp.stack([b_out, gain_one, shift_one])
    vectors_two = jnp.stack([gain_one, shift_one, b_down, gain_two, shift_two])

    a = jnp.concatenate([w_query, w_key, w_value, w_out.T], axis=1)
    c = w_up
    d = w_down.T
    if fast:
        az = swap(a, 12)
        a, az, c = tie(a, az, c)
        an = jnp.stack([a, az])
        am, anx, any_ = swap(an, 4), swap(an, 1), swap(an, 2)
        cz = swap(c, 12)
        an, am, anx, any_, c, cz, d = tie(an, am, anx, any_, c, cz, d)
        cn = jnp.stack([c, cz])
        amx, amy = swap(am, 1), swap(am, 2)
        cm = swap(cn, 4)
        an, am, anx, any_, amx, amy, cn, cm, d = tie(an, am, anx, any_, amx, amy, cn, cm, d)
        and_, amd = swap(anx, 2), swap(amy, 1)
        cnx, cny = swap(cn, 1), swap(cn, 2)
        dz = swap(d, 12)
        an, am, anx, any_, amx, amy, and_, amd, cn, cm, cnx, cny, d, dz = tie(
            an, am, anx, any_, amx, amy, and_, amd, cn, cm, cnx, cny, d, dz
        )
        dn = jnp.stack([d, dz])
        cmx, cmy = swap(cm, 1), swap(cm, 2)
        dm = swap(dn, 4)
        pieces_a = [an, am, anx, amx, any_, amy, and_, amd]
    else:
        a, c, d = (lax.all_gather(piece, "dp", axis=0, tiled=True) for piece in (a, c, d))
        pieces_a, pieces_c, pieces_d = as_pieces(a), as_pieces(c), as_pieces(d)
    w_a, qkv, prob, attended, part = attend(me, lengths, in_low, bias_qkv, pieces_a)
    if fast:
        part, cn, cm, cnx, cny, cmx, cmy, dn, dm = tie(part, cn, cm, cnx, cny, cmx, cmy, dn, dm)
        other = pair_swap(part)
        cnd, cmd = swap(cnx, 2), swap(cmy, 1)
        dnx, dny = swap(dn, 1), swap(dn, 2)
        other, part, cnd, cmd, cn, cm, cnx, cny, cmx, cmy, dn, dm, dnx, dny = tie(
            other, part, cnd, cmd, cn, cm, cnx, cny, cmx, cmy, dn, dm, dnx, dny
        )
        dmx, dmy = swap(dm, 1), swap(dm, 2)
        dnd = swap(dnx, 2)
        pieces_c = [cn, cm, cnx, cmx, cny, cmy, cnd, cmd]
    else:
        other = pair_swap(part)
    w_u, normed_one, inverse_one, hidden_low, act_low, slope = up(
        me, in_low, part, other, vectors_one, b_up[None, :], pieces_c
    )
    if fast:
        act_low, dmx, dmy, dnd = tie(act_low, dmx, dmy, dnd)
        dmd = swap(dmy, 1)
        pieces_d = [dn, dm, dnx, dmx, dny, dmy, dnd, dmd]
    w_d, part = down(me, act_low, pieces_d)
    other = pair_swap(part)
    result, dz_two, dz_two_low, sums_two = second_norm(normed_one, part, other, grad_out, vectors_two)
    dx, dy, dxl, dyl, do = weight_grad(me, [dz_two_low], [act_low])
    if fast:
        dx, dy, dxl, dyl, dz_two_low = tie(dx, dy, dxl, dyl, dz_two_low)
        dxr, dyr = swap(dx, 1), swap(dy, 2)
    d_pre_low, part, sums_up = hidden_back(dz_two_low, slope, w_d, w_u)
    if fast:
        part, dxr, dyr, d_pre_low = tie(part, dxr, dyr, d_pre_low)
        other = pair_swap(part)
        dxlr, dylr = swap(add_low(dxl, dyr[:2]), 1), swap(add_low(dyl, dxr[:2]), 2)
        cx, cy, cxl, cyl, co = weight_grad(me, [hidden_low], [d_pre_low])
        other, dxlr, dylr, cx, cy = tie(other, dxlr, dylr, cx, cy)
        cxr, cyr = swap(cx, 1), swap(cy, 2)
        d_mid = (do[2:].astype(F32) + dxlr.astype(F32) + dyr[2:].astype(F32)).astype(B16)
        d_near = do[:2].astype(F32) + dxr[2:].astype(F32) + dylr.astype(F32)
        d_midr = swap(d_mid, 4)
    else:
        other = pair_swap(part)
        cx, cy, cxl, cyl, co = weight_grad(me, [hidden_low], [d_pre_low])
    dz_one, dz_one_low, d_qkv, part, sums_one, sums_qkv = attend_back(
        lengths.shape[0], dz_two, part, other, normed_one, inverse_one, gain_one[None, :], qkv, prob, w_a
    )
    if fast:
        part, d_qkv, cxr, cyr, d_midr, d_near = tie(part, d_qkv, cxr, cyr, d_midr, d_near)
        other = pair_swap(part)
        d_near = d_near + d_midr.astype(F32)
        d_far = swap(d_near[1].astype(B16), 12)
        cxlr, cylr = swap(add_low(cxl, cyr[:2]), 1), swap(add_low(cyl, cxr[:2]), 2)
        ax, ay, axl, ayl, ao = weight_grad(me, [in_low, dz_one_low], [d_qkv, attended])
        other, d_far, cxlr, cylr, ax, ay = tie(other, d_far, cxlr, cylr, ax, ay)
        axr, ayr = swap(ax, 1), swap(ay, 2)
        c_mid = (co[2:].astype(F32) + cxlr.astype(F32) + cyr[2:].astype(F32)).astype(B16)
        c_near = co[:2].astype(F32) + cxr[2:].astype(F32) + cylr.astype(F32)
        c_midr = swap(c_mid, 4)
    else:
        other = pair_swap(part)
        ax, ay, axl, ayl, ao = weight_grad(me, [in_low, dz_one_low], [d_qkv, attended])
    d_tokens, sums_mask = last(dz_one, part, other, flag)
    parts = (
        sums_mask[0],
        sums_qkv[0, :head_cols],
        sums_qkv[0, 2 * head_cols :],
        sums_one[2],
        sums_one[0],
        sums_one[1],
        sums_up[0],
        sums_two[2],
        sums_two[0],
        sums_two[1],
    )
    joined = jnp.concatenate(parts).reshape(-1, 128)
    if fast:
        joined, axr, ayr, c_midr, c_near = tie(joined, axr, ayr, c_midr, c_near)
        axlr, aylr = swap(add_low(axl, ayr[:2]), 1), swap(add_low(ayl, axr[:2]), 2)
        c_near = c_near + c_midr.astype(F32)
        c_far = swap(c_near[1].astype(B16), 12)
        joined = joined + swap(joined, 1)
        joined = joined + swap(joined, 2)
        axlr, aylr, c_far, joined = tie(axlr, aylr, c_far, joined)
        a_mid = (ao[2:].astype(F32) + axlr.astype(F32) + ayr[2:].astype(F32)).astype(B16)
        a_near = ao[:2].astype(F32) + axr[2:].astype(F32) + aylr.astype(F32)
        a_midr = swap(a_mid, 4)
        joined = joined + swap(joined, 4)
        a_midr, joined = tie(a_midr, joined)
        a_near = a_near + a_midr.astype(F32)
        a_far = swap(a_near[1].astype(B16), 12)
        joined = joined + swap(joined, 8)
        d_wa = a_near[0] + a_far.astype(F32)
        d_w_up = c_near[0] + c_far.astype(F32)
        d_w_down_t = d_near[0] + d_far.astype(F32)
    else:
        full = []
        for x, y, xl, yl, o in ((ax, ay, axl, ayl, ao), (cx, cy, cxl, cyl, co), (dx, dy, dxl, dyl, do)):
            blocks = [None] * BLOCKS
            for k in range(2):
                blocks[3 + NEAR[k]], blocks[1 + NEAR[k]], blocks[1 + MID[k]] = x[k], x[2 + k], xl[k]
                blocks[3 + MID[k]], blocks[2 + MID[k]], blocks[2 + NEAR[k]] = y[k], y[2 + k], yl[k]
                blocks[NEAR[k]], blocks[MID[k]] = o[k], o[2 + k]
            full.append(jnp.concatenate(blocks).astype(F32))
        joined = lax.psum(joined, "dp")
        d_wa, d_w_up, d_w_down_t = (
            lax.psum_scatter(member, "dp", scatter_dimension=0, tiled=True) for member in full
        )
    joined = joined.reshape(-1)
    summed = []
    start = 0
    for member in parts:
        summed.append(joined[start : start + member.shape[0]])
        start += member.shape[0]
    return (
        result,
        d_tokens,
        summed[0],
        d_wa[:, :head_cols],
        summed[1],
        d_wa[:, head_cols : 2 * head_cols],
        d_wa[:, 2 * head_cols : 3 * head_cols],
        summed[2],
        d_wa[:, 3 * head_cols :].T,
        summed[3],
        summed[4],
        summed[5],
        d_w_up,
        summed[6],
        d_w_down_t.T,
        summed[7],
        summed[8],
        summed[9],
    )


def solution(mesh):
    rows, flat, both = P("dp", None), P(), P("dp", "mp")
    return jax.shard_map(
        functools.partial(per_device, mesh.shape["dp"]),
        mesh=mesh,
        in_specs=(rows, P("dp"), P("dp"), flat, both, P("mp"), both, both, P("mp"), P("mp", "dp"),
                  flat, flat, flat, both, P("mp"), P("mp", "dp"), flat, flat, flat, rows),
        out_specs=(rows, rows, flat, both, P("mp"), both, both, P("mp"), P("mp", "dp"), flat, flat,
                   flat, both, P("mp"), P("mp", "dp"), flat, flat, flat),
        check_vma=False,
    )
```

```python
import functools

import jax
import jax.numpy as jnp
from jax import lax
from jax.experimental import pallas as pl
from jax.experimental.pallas import tpu as pltpu
from jax.sharding import PartitionSpec as P

HEAD = 64
NORM_EPS = 1e-05
F32 = jnp.float32
B16 = jnp.bfloat16
MIB = 1 << 20

BLOCKS = 16
NEAR = (0, 12)
MID = (4, 8)


def swap(values, bit):
    return lax.ppermute(values, "dp", [(i, i ^ bit) for i in range(BLOCKS)])


def tie(*values):
    return lax.optimization_barrier(values)


def after(value, *earlier):
    return tie(value, *earlier)[0]


def pair_swap(partial):
    return lax.ppermute(partial, "mp", [(0, 1), (1, 0)])


def as_pieces(full):
    rows = full.shape[0] // BLOCKS
    blocks = full.reshape(BLOCKS, rows, full.shape[1])
    return [
        jnp.stack([blocks[offset + bits[0]], blocks[offset + bits[1]]])
        for offset in range(4)
        for bits in (NEAR, MID)
    ]


SMEM_SPEC = pl.BlockSpec(memory_space=pltpu.SMEM)
BIG = 1 << 18
LIGHT = pl.CostEstimate(flops=1, bytes_accessed=1, transcendentals=0)


def call(body, *, out_shape, received=(), **options):
    def place(member):
        if member.size * member.dtype.itemsize < BIG:
            return member
        return pltpu.HBM(member.shape, member.dtype)

    def keep(member):
        if member.size * member.dtype.itemsize < BIG:
            return member
        return pltpu.with_memory_space_constraint(member, pltpu.HBM)

    kernel = pl.pallas_call(body, out_shape=[place(member) for member in out_shape], **options)
    return lambda *operands: kernel(
        *[
            member if member.ndim == 3 or index in received else keep(member)
            for index, member in enumerate(operands)
        ]
    )


def whole(shape):
    zeros = (0,) * len(shape)
    return pl.BlockSpec(tuple(shape), lambda i: zeros)


def rows_of(count, width):
    return pl.BlockSpec((count, width), lambda i: (i, 0))


def fill(me, pieces, full_ref):
    rows = pieces[0].shape[1]
    for index, piece in enumerate(pieces):
        bits = (NEAR, MID)[index % 2]
        for k in range(2):
            block = me ^ (index // 2 + bits[k])
            full_ref[pl.ds(pl.multiple_of(block * rows, rows), rows), :] = piece[k]


def dot(left, right):
    return jnp.dot(left, right, preferred_element_type=F32)


def dot_t(left, right):
    return lax.dot_general(left, right, (((1,), (1,)), ((), ())), preferred_element_type=F32)


def t_dot(left, right):
    return lax.dot_general(left, right, (((0,), (0,)), ((), ())), preferred_element_type=F32)


def row_mean(values):
    return jnp.mean(values, axis=-1, keepdims=True)


def normalize(values):
    centred = values - row_mean(values)
    inverse = lax.rsqrt(row_mean(centred * centred) + NORM_EPS)
    return centred * inverse, inverse


def col_sum(values):
    return jnp.sum(values, axis=0, keepdims=True)


def norm_back(scaled, normed, inverse):
    return inverse * (scaled - row_mean(scaled) - normed * row_mean(scaled * normed))


def two_heads(slots):
    row = lax.broadcasted_iota(jnp.int32, (2 * slots, 2 * HEAD), 0) // slots
    lane = lax.broadcasted_iota(jnp.int32, (2 * slots, 2 * HEAD), 1) // HEAD
    return (row == lane).astype(F32).astype(B16)


def doubled(values, mask):
    return jnp.concatenate([values, values], axis=0) * mask


def attend_body(chains, slots, me_ref, len_ref, in_ref, bias_ref, *rest):
    pieces, (w_ref, qkv_ref, prob_ref, att_ref, part_ref) = rest[:8], rest[8:]
    step = pl.program_id(0)
    width = att_ref.shape[1]

    @pl.when(step == 0)
    def _():
        fill(me_ref[0], pieces, w_ref)

    qkv_ref[...] = (dot(in_ref[...], w_ref[:, : 3 * width]) + bias_ref[...]).astype(B16)
    mask = two_heads(slots)
    key_slot = lax.broadcasted_iota(jnp.int32, (slots, slots), 1)
    for chain in range(chains):
        valid = key_slot < len_ref[step * chains + chain]
        rows = pl.ds(chain * slots, slots)
        for pair in range(width // (2 * HEAD)):
            lanes = 2 * HEAD * pair
            query = qkv_ref[rows, lanes : lanes + 2 * HEAD]
            key = qkv_ref[rows, width + lanes : width + lanes + 2 * HEAD]
            value = qkv_ref[rows, 2 * width + lanes : 2 * width + lanes + 2 * HEAD]
            scores = dot_t(query * (HEAD**-0.5), doubled(key, mask))
            probs = []
            for head in range(2):
                part = jnp.where(valid, scores[:, head * slots : (head + 1) * slots], -1e30)
                terms = jnp.exp(part - jnp.max(part, axis=-1, keepdims=True))
                probs.append((terms / jnp.sum(terms, axis=-1, keepdims=True)).astype(B16))
            prob = jnp.concatenate(probs, axis=1)
            prob_ref[rows, 2 * slots * pair : 2 * slots * (pair + 1)] = prob
            att_ref[rows, lanes : lanes + 2 * HEAD] = dot(prob, doubled(value, mask)).astype(B16)
    part_ref[...] = dot_t(att_ref[...], w_ref[:, 3 * width :]).astype(B16)


def attend(me, lengths, in_low, bias, pieces):
    count, width = in_low.shape
    heads = bias.shape[1] // 3
    chains = 2 if lengths.shape[0] % 2 == 0 else 1
    slots = count // lengths.shape[0]
    rows = chains * slots
    shape = jax.ShapeDtypeStruct
    return call(
        functools.partial(attend_body, chains, slots),
        grid=(count // rows,),
        in_specs=[SMEM_SPEC, SMEM_SPEC, rows_of(rows, width), whole(bias.shape)]
        + [whole(piece.shape) for piece in pieces],
        out_specs=[
            whole((width, 4 * heads)),
            rows_of(rows, 3 * heads),
            rows_of(rows, heads // HEAD * slots),
            rows_of(rows, heads),
            rows_of(rows, width),
        ],
        out_shape=[
            shape((width, 4 * heads), B16),
            shape((count, 3 * heads), B16),
            shape((count, heads // HEAD * slots), B16),
            shape((count, heads), B16),
            shape((count, width), B16),
        ],
        compiler_params=pltpu.CompilerParams(vmem_limit_bytes=32 * MIB),
        cost_estimate=LIGHT,
        name="attend",
    )(me, lengths, in_low, bias, *pieces)


def up_body(me_ref, in_ref, own_ref, other_ref, vec_ref, bias_ref, *rest):
    pieces, (w_ref, normed_ref, inverse_ref, low_ref, act_ref, slope_ref) = rest[:8], rest[8:]

    @pl.when(pl.program_id(0) == 0)
    def _():
        fill(me_ref[0], pieces, w_ref)

    vectors = vec_ref[...]
    attn = own_ref[...].astype(F32) + other_ref[...].astype(F32) + vectors[0:1]
    normed, inverse = normalize(in_ref[...].astype(F32) + attn)
    normed_ref[...] = normed
    inverse_ref[...] = jnp.broadcast_to(inverse, inverse_ref.shape)
    hidden = normed * vectors[1:2] + vectors[2:3]
    low_ref[...] = hidden.astype(B16)
    pre = dot(low_ref[...], w_ref[...]) + bias_ref[...]
    cdf = 0.5 + 0.5 * lax.erf(pre * (2.0**-0.5))
    act_ref[...] = (pre * cdf).astype(B16)
    density = jnp.exp(pre * pre * -0.5) * 0.3989422804014327
    slope_ref[...] = (cdf + pre * density).astype(B16)


def up(me, in_low, own, other, vectors, bias, pieces):
    count, width = in_low.shape
    units = bias.shape[1]
    rows = count // 4
    shape = jax.ShapeDtypeStruct
    return call(
        up_body,
        received=(3,),
        grid=(4,),
        in_specs=[SMEM_SPEC]
        + [rows_of(rows, width)] * 3
        + [whole(vectors.shape), whole(bias.shape)]
        + [whole(piece.shape) for piece in pieces],
        out_specs=[
            whole((width, units)),
            rows_of(rows, width),
            rows_of(rows, 128),
            rows_of(rows, width),
            rows_of(rows, units),
            rows_of(rows, units),
        ],
        out_shape=[
            shape((width, units), B16),
            shape((count, width), F32),
            shape((count, 128), F32),
            shape((count, width), B16),
            shape((count, units), B16),
            shape((count, units), B16),
        ],
        compiler_params=pltpu.CompilerParams(vmem_limit_bytes=40 * MIB),
        cost_estimate=LIGHT,
        name="up",
    )(me, in_low, own, other, vectors, bias, *pieces)


def down_body(me_ref, act_ref, *rest):
    pieces, (w_ref, part_ref) = rest[:8], rest[8:]

    @pl.when(pl.program_id(0) == 0)
    def _():
        fill(me_ref[0], pieces, w_ref)

    part_ref[...] = dot_t(act_ref[...], w_ref[...]).astype(B16)


def down(me, act, pieces):
    count, units = act.shape
    width = BLOCKS * pieces[0].shape[1]
    rows = count // 4
    shape = jax.ShapeDtypeStruct
    return call(
        down_body,
        grid=(4,),
        in_specs=[SMEM_SPEC, rows_of(rows, units)] + [whole(piece.shape) for piece in pieces],
        out_specs=[whole((width, units)), rows_of(rows, width)],
        out_shape=[shape((width, units), B16), shape((count, width), B16)],
        compiler_params=pltpu.CompilerParams(vmem_limit_bytes=24 * MIB),
        cost_estimate=LIGHT,
        name="down",
    )(me, act, *pieces)


def second_norm_body(normed_ref, own_ref, other_ref, grad_ref, vec_ref, out_ref, dz_ref, low_ref, sum_ref):
    vectors = vec_ref[...]
    hidden = normed_ref[...] * vectors[0:1] + vectors[1:2]
    ffn = own_ref[...].astype(F32) + other_ref[...].astype(F32) + vectors[2:3]
    normed, inverse = normalize(hidden + ffn)
    out_ref[...] = (normed * vectors[3:4] + vectors[4:5]).astype(B16)
    grad = grad_ref[...].astype(F32)
    dz = norm_back(grad * vectors[3:4], normed, inverse)
    dz_ref[...] = dz
    low_ref[...] = dz.astype(B16)

    @pl.when(pl.program_id(0) == 0)
    def _():
        sum_ref[...] = jnp.zeros_like(sum_ref)

    sum_ref[0:1] += col_sum(grad * normed)
    sum_ref[1:2] += col_sum(grad)
    sum_ref[2:3] += col_sum(dz)


def second_norm(normed, own, other, grad, vectors):
    count, width = own.shape
    rows = count // 4
    shape = jax.ShapeDtypeStruct
    return call(
        second_norm_body,
        received=(2,),
        grid=(4,),
        in_specs=[rows_of(rows, width)] * 4 + [whole(vectors.shape)],
        out_specs=[rows_of(rows, width)] * 3 + [whole((8, width))],
        out_shape=[
            shape((count, width), B16),
            shape((count, width), F32),
            shape((count, width), B16),
            shape((8, width), F32),
        ],
        compiler_params=pltpu.CompilerParams(vmem_limit_bytes=24 * MIB),
        cost_estimate=LIGHT,
        name="second_norm",
    )(normed, own, other, grad, vectors)


def weight_grad_body(me_ref, lefts, right_ref, outs, turned_ref, full_ref):
    x_ref, y_ref, x_late_ref, y_late_ref, own_ref = outs
    step = pl.program_id(0)
    rows = own_ref.shape[1]
    first = 0
    for left_ref, tiles in lefts:

        @pl.when(step == first)
        def _(left_ref=left_ref):
            turned_ref[...] = left_ref[...].T

        first += tiles
    full_ref[...] = dot(turned_ref[...], right_ref[...]).astype(B16)

    def block(offset):
        at = me_ref[0] ^ offset
        return full_ref[pl.ds(pl.multiple_of(at * rows, rows), rows), :]

    for k in range(2):
        x_ref[k] = block(3 + NEAR[k])
        x_ref[2 + k] = block(1 + NEAR[k])
        x_late_ref[k] = block(1 + MID[k])
        y_ref[k] = block(3 + MID[k])
        y_ref[2 + k] = block(2 + MID[k])
        y_late_ref[k] = block(2 + NEAR[k])
        own_ref[k] = block(NEAR[k])
        own_ref[2 + k] = block(MID[k])


def weight_grad(me, lefts, rights):
    count, width = lefts[0].shape
    tile = 384 if all(right.shape[1] % 384 == 0 for right in rights) else 128
    tiles = [right.shape[1] // tile for right in rights]
    total = sum(tiles)
    rows = width // BLOCKS
    firsts = [sum(tiles[:k]) for k in range(len(tiles))]
    shape = jax.ShapeDtypeStruct

    def body(me_ref, *refs):
        n = len(lefts)
        left_refs, right_refs, outs = refs[:n], refs[n : 2 * n], refs[2 * n : 2 * n + 5]
        turned_ref, full_ref = refs[2 * n + 5 :]
        if n == 1:
            weight_grad_body(me_ref, [(left_refs[0], total)], right_refs[0], outs, turned_ref, full_ref)
            return
        step = pl.program_id(0)
        for k in range(n):

            @pl.when(jnp.logical_and(step >= firsts[k], step < firsts[k] + tiles[k]))
            def _(k=k):
                @pl.when(step == firsts[k])
                def _():
                    turned_ref[...] = left_refs[k][...].T

                weight_grad_body(me_ref, [], right_refs[k], outs, turned_ref, full_ref)

    def tile_of(first, number):
        return lambda i: (0, jnp.clip(i - first, 0, number - 1))

    def out_spec(number):
        return pl.BlockSpec((number, rows, tile), lambda i: (0, 0, i))

    sizes = (4, 4, 2, 2, 4)
    return call(
        body,
        grid=(total,),
        in_specs=[SMEM_SPEC]
        + [whole(left.shape) for left in lefts]
        + [pl.BlockSpec((count, tile), tile_of(firsts[k], tiles[k])) for k in range(len(rights))],
        out_specs=[out_spec(number) for number in sizes],
        out_shape=[shape((number, rows, total * tile), B16) for number in sizes],
        scratch_shapes=[pltpu.VMEM((width, count), B16), pltpu.VMEM((width, tile), B16)],
        compiler_params=pltpu.CompilerParams(vmem_limit_bytes=28 * MIB),
        cost_estimate=LIGHT,
        name="weight_grad",
    )(me, *lefts, *rights)


def hidden_back_body(low_ref, slope_ref, down_ref, up_ref, pre_ref, part_ref, sum_ref):
    d_pre = dot(low_ref[...], down_ref[...]) * slope_ref[...].astype(F32)

    @pl.when(pl.program_id(0) == 0)
    def _():
        sum_ref[...] = jnp.zeros_like(sum_ref)

    sum_ref[0:1] += col_sum(d_pre)
    pre_ref[...] = d_pre.astype(B16)
    part_ref[...] = dot_t(pre_ref[...], up_ref[...]).astype(B16)


def hidden_back(dz_low, slope, w_down_t, w_up):
    count, width = dz_low.shape
    units = slope.shape[1]
    rows = count // 4
    shape = jax.ShapeDtypeStruct
    return call(
        hidden_back_body,
        grid=(4,),
        in_specs=[
            rows_of(rows, width),
            rows_of(rows, units),
            whole((width, units)),
            whole((width, units)),
        ],
        out_specs=[rows_of(rows, units), rows_of(rows, width), whole((8, units))],
        out_shape=[
            shape((count, units), B16),
            shape((count, width), B16),
            shape((8, units), F32),
        ],
        compiler_params=pltpu.CompilerParams(vmem_limit_bytes=28 * MIB),
        cost_estimate=LIGHT,
        name="hidden_back",
    )(dz_low, slope, w_down_t, w_up)


def attend_back_body(chains, slots, dz_ref, own_ref, other_ref, normed_ref, inverse_ref, gain_ref,
                     qkv_ref, prob_ref, w_ref, dz_one_ref, low_ref, d_qkv_ref, part_ref, sum_ref,
                     sum_qkv_ref, d_att_ref):
    width = d_att_ref.shape[1]
    normed = normed_ref[...]
    d_hidden = dz_ref[...] + (own_ref[...].astype(F32) + other_ref[...].astype(F32))
    dz_one = norm_back(d_hidden * gain_ref[...], normed, inverse_ref[:, 0:1])
    dz_one_ref[...] = dz_one
    low_ref[...] = dz_one.astype(B16)

    @pl.when(pl.program_id(0) == 0)
    def _():
        sum_ref[...] = jnp.zeros_like(sum_ref)
        sum_qkv_ref[...] = jnp.zeros_like(sum_qkv_ref)

    sum_ref[0:1] += col_sum(d_hidden * normed)
    sum_ref[1:2] += col_sum(d_hidden)
    sum_ref[2:3] += col_sum(dz_one)
    d_att_ref[...] = dot(low_ref[...], w_ref[:, 3 * width :]).astype(B16)
    mask = two_heads(slots)
    for chain in range(chains):
        rows = pl.ds(chain * slots, slots)
        for pair in range(width // (2 * HEAD)):
            lanes = 2 * HEAD * pair
            query = qkv_ref[rows, lanes : lanes + 2 * HEAD]
            key = qkv_ref[rows, width + lanes : width + lanes + 2 * HEAD]
            value = qkv_ref[rows, 2 * width + lanes : 2 * width + lanes + 2 * HEAD]
            d_att = d_att_ref[rows, lanes : lanes + 2 * HEAD]
            prob = prob_ref[rows, 2 * slots * pair : 2 * slots * (pair + 1)]
            d_prob = dot_t(d_att, doubled(value, mask))
            weights = prob.astype(F32)
            products = weights * d_prob
            lows = []
            for head in range(2):
                half = slice(head * slots, (head + 1) * slots)
                total = jnp.sum(products[:, half], axis=-1, keepdims=True)
                lows.append((products[:, half] - weights[:, half] * total).astype(B16))
            low = jnp.concatenate(lows, axis=1)
            d_query = dot(low, doubled(key, mask)) * (HEAD**-0.5)
            tall = jnp.concatenate(lows, axis=0)
            d_key = t_dot(tall, doubled(query, mask)) * (HEAD**-0.5)
            tall = jnp.concatenate([prob[:, :slots], prob[:, slots:]], axis=0)
            d_value = t_dot(tall, doubled(d_att, mask))
            d_qkv_ref[rows, lanes : lanes + 2 * HEAD] = d_query.astype(B16)
            d_qkv_ref[rows, width + lanes : width + lanes + 2 * HEAD] = d_key.astype(B16)
            d_qkv_ref[rows, 2 * width + lanes : 2 * width + lanes + 2 * HEAD] = d_value.astype(B16)
    sum_qkv_ref[0:1] += col_sum(d_qkv_ref[...].astype(F32))
    part_ref[...] = dot_t(d_qkv_ref[...], w_ref[:, : 3 * width]).astype(B16)


def attend_back(chain_count, dz_two, own, other, normed, inverse, gain, qkv, prob, w_a):
    count, width = dz_two.shape
    heads = qkv.shape[1] // 3
    chains = 2 if chain_count % 2 == 0 else 1
    slots = count // chain_count
    rows = chains * slots
    shape = jax.ShapeDtypeStruct
    return call(
        functools.partial(attend_back_body, chains, slots),
        received=(2,),
        grid=(count // rows,),
        in_specs=[
            rows_of(rows, width),
            rows_of(rows, width),
            rows_of(rows, width),
            rows_of(rows, width),
            rows_of(rows, 128),
            whole(gain.shape),
            rows_of(rows, 3 * heads),
            rows_of(rows, prob.shape[1]),
            whole(w_a.shape),
        ],
        out_specs=[
            rows_of(rows, width),
            rows_of(rows, width),
            rows_of(rows, 3 * heads),
            rows_of(rows, width),
            whole((8, width)),
            whole((8, 3 * heads)),
        ],
        out_shape=[
            shape((count, width), F32),
            shape((count, width), B16),
            shape((count, 3 * heads), B16),
            shape((count, width), B16),
            shape((8, width), F32),
            shape((8, 3 * heads), F32),
        ],
        scratch_shapes=[pltpu.VMEM((rows, heads), B16)],
        compiler_params=pltpu.CompilerParams(vmem_limit_bytes=32 * MIB),
        cost_estimate=LIGHT,
        name="attend_back",
    )(dz_two, own, other, normed, inverse, gain, qkv, prob, w_a)


def last_body(dz_ref, own_ref, other_ref, flag_ref, one_ref, two_ref, up_ref, qkv_ref, out_ref, sum_ref):
    total = dz_ref[...] + (own_ref[...].astype(F32) + other_ref[...].astype(F32))
    flag = flag_ref[:, 0:1]
    masked = total * flag
    width = total.shape[1]
    heads = qkv_ref.shape[1] // 3

    @pl.when(pl.program_id(0) == 0)
    def _():
        sum_ref[...] = jnp.zeros_like(sum_ref)
        sum_ref[1:4] = one_ref[0:3]
        sum_ref[4:7] = two_ref[0:3]
        sum_ref[7:8, :heads] = qkv_ref[0:1, :heads]
        sum_ref[7:8, heads : 2 * heads] = qkv_ref[0:1, 2 * heads :]
        for k in range(up_ref.shape[1] // width):
            sum_ref[8 + k : 9 + k] = up_ref[0:1, k * width : (k + 1) * width]

    sum_ref[0:1] += col_sum(masked)
    out_ref[...] = total - masked


def last(dz_one, own, other, flag, sums_one, sums_two, sums_up, sums_qkv):
    count, width = dz_one.shape
    rows = count // 4
    sums = [sums_one, sums_two, sums_up, sums_qkv]
    shape = jax.ShapeDtypeStruct
    joined = (8 + 8 * pl.cdiv(sums_up.shape[1], 8 * width), width)
    return call(
        last_body,
        received=(2,),
        grid=(4,),
        in_specs=[rows_of(rows, width)] * 3
        + [rows_of(rows, 128)]
        + [whole(member.shape) for member in sums],
        out_specs=[rows_of(rows, width), whole(joined)],
        out_shape=[shape((count, width), F32), shape(joined, F32)],
        compiler_params=pltpu.CompilerParams(vmem_limit_bytes=20 * MIB),
        cost_estimate=LIGHT,
        name="last",
    )(dz_one, own, other, flag, *sums)


def add_late_body(x_ref, y_ref, from_x_ref, from_y_ref, out_x_ref, out_y_ref):
    out_x_ref[...] = (x_ref[...].astype(F32) + from_y_ref[:2].astype(F32)).astype(B16)
    out_y_ref[...] = (y_ref[...].astype(F32) + from_x_ref[:2].astype(F32)).astype(B16)


def add_own_body(own_ref, from_x_ref, from_y_ref, late_x_ref, late_y_ref, near_ref, mid_ref):
    near_ref[...] = (
        own_ref[:2].astype(F32) + from_x_ref[2:].astype(F32) + late_y_ref[...].astype(F32)
    )
    mid_ref[...] = (
        own_ref[2:].astype(F32) + late_x_ref[...].astype(F32) + from_y_ref[2:].astype(F32)
    ).astype(B16)


def add_mid_body(near_ref, mid_ref, own_ref, far_ref):
    own_ref[...] = near_ref[0] + mid_ref[0].astype(F32)
    far_ref[...] = (near_ref[1] + mid_ref[1].astype(F32)).astype(B16)


def add_up(body, name, shapes, *operands):
    vmem = pl.BlockSpec(memory_space=pltpu.VMEM)
    return pl.pallas_call(
        body,
        in_specs=[vmem] * len(operands),
        out_specs=[vmem] * len(shapes),
        out_shape=[jax.ShapeDtypeStruct(shape, dtype) for shape, dtype in shapes],
        compiler_params=pltpu.CompilerParams(vmem_limit_bytes=8 * MIB),
        cost_estimate=LIGHT,
        name=name,
    )(*operands)


def add_late(late_x, late_y, from_x, from_y):
    shape = (late_x.shape, B16)
    return add_up(add_late_body, "add_late", [shape, shape], late_x, late_y, from_x, from_y)


def add_own(own, from_x, from_y, late_x, late_y):
    shapes = [(late_x.shape, F32), (late_x.shape, B16)]
    return add_up(add_own_body, "add_own", shapes, own, from_x, from_y, late_x, late_y)


def add_mid(near, mid):
    shapes = [(near.shape[1:], F32), (near.shape[1:], B16)]
    return add_up(add_mid_body, "add_mid", shapes, near, mid)


def per_device(dp_size, tokens, masked, lengths, mask_vector, w_query, b_query, w_key, w_value,
               b_value, w_out, b_out, gain_one, shift_one, w_up, b_up, w_down, b_down, gain_two,
               shift_two, grad_out):
    head_cols = w_query.shape[1]
    width = tokens.shape[1]
    fast = dp_size == BLOCKS and w_query.shape[0] % 16 == 0
    me = lax.axis_index("dp").astype(jnp.int32).reshape(1)
    if not fast:
        me = jnp.zeros_like(me)

    (b_query, b_value, b_out, gain_one, shift_one, b_up, b_down, gain_two, shift_two) = (
        member.astype(F32)
        for member in (b_query, b_value, b_out, gain_one, shift_one, b_up, b_down, gain_two, shift_two)
    )
    is_masked = (masked == 1)[:, None]
    flag = jnp.broadcast_to(is_masked, (masked.shape[0], 128)).astype(F32)
    in_low = jnp.where(is_masked, mask_vector[None, :], tokens)
    bias_qkv = jnp.concatenate([b_query, jnp.zeros_like(b_query), b_value])[None, :]
    vectors_one = jnp.stack([b_out, gain_one, shift_one])
    vectors_two = jnp.stack([gain_one, shift_one, b_down, gain_two, shift_two])

    a = jnp.concatenate([w_query, w_key, w_value, w_out.T], axis=1)
    c = w_up
    d = w_down.T
    if fast:
        az = swap(a, 12)
        an = jnp.stack([a, az])
        anx, any_, am = swap(an, 1), swap(an, 2), swap(an, 4)
        cz = swap(after(c, az), 12)
        amx, amy = swap(am, 1), swap(am, 2)
        cn = jnp.stack([c, cz])
        cm = swap(after(cn, am), 4)
        cnx, cny = swap(after(cn, anx), 1), swap(after(cn, any_), 2)
        dz = swap(after(d, cz), 12)
        dn = jnp.stack([d, dz])
        amd, and_ = swap(amy, 1), swap(after(anx, amy), 2)
        in_low, an, am, anx, amx, any_, amy, and_, amd, cn, cm, cnx, cny, dn = tie(
            in_low, an, am, anx, amx, any_, amy, and_, amd, cn, cm, cnx, cny, dn
        )
        pieces_a = [an, am, anx, amx, any_, amy, and_, amd]
        cmx, cmy, dm = swap(cm, 1), swap(cm, 2), swap(dn, 4)
        dnx, cnd = swap(dn, 1), swap(cnx, 2)
    else:
        a, c, d = (lax.all_gather(piece, "dp", axis=0, tiled=True) for piece in (a, c, d))
        pieces_a, pieces_c, pieces_d = as_pieces(a), as_pieces(c), as_pieces(d)
    w_a, qkv, prob, attended, part = attend(me, lengths, in_low, bias_qkv, pieces_a)
    if fast:
        part, cmx, cmy, cnd, dn, dm, dnx = tie(part, cmx, cmy, cnd, dn, dm, dnx)
        cmd, dny = swap(cmy, 1), swap(dn, 2)
    other = pair_swap(part)
    if fast:
        other, cmd, dny, dm = tie(other, cmd, dny, dm)
        pieces_c = [cn, cm, cnx, cmx, cny, cmy, cnd, cmd]
        dmx, dmy = swap(dm, 1), swap(dm, 2)
    w_u, normed_one, inverse_one, hidden_low, act_low, slope = up(
        me, in_low, part, other, vectors_one, b_up[None, :], pieces_c
    )
    if fast:
        act_low, dnx, dmx, dmy = tie(act_low, dnx, dmx, dmy)
        dmd, dnd = swap(dmy, 1), swap(dnx, 2)
        pieces_d = [dn, dm, dnx, dmx, dny, dmy, dnd, dmd]
    w_d, part = down(me, act_low, pieces_d)
    other = pair_swap(part)
    result, dz_two, dz_two_low, sums_two = second_norm(normed_one, part, other, grad_out, vectors_two)
    dx, dy, dxl, dyl, do = weight_grad(me, [dz_two_low], [act_low])
    if fast:
        dx, dy, dxl, dyl, dz_two_low = tie(dx, dy, dxl, dyl, dz_two_low)
        dxr, dyr = swap(dx, 1), swap(dy, 2)
    d_pre_low, part, sums_up = hidden_back(dz_two_low, slope, w_d, w_u)
    cx, cy, cxl, cyl, co = weight_grad(me, [hidden_low], [d_pre_low])
    if fast:
        part, dxr, dyr, cx, cy = tie(part, dxr, dyr, cx, cy)
        dxl, dyl = add_late(dxl, dyl, dxr, dyr)
        dxlr, dylr, cxr, cyr = swap(dxl, 1), swap(dyl, 2), swap(cx, 1), swap(cy, 2)
    other = pair_swap(part)
    dz_one, dz_one_low, d_qkv, part, sums_one, sums_qkv = attend_back(
        lengths.shape[0], dz_two, part, other, normed_one, inverse_one, gain_one[None, :], qkv, prob, w_a
    )
    if fast:
        part, d_qkv, dxlr, dylr, cxr, cyr = tie(part, d_qkv, dxlr, dylr, cxr, cyr)
        cxl, cyl = add_late(cxl, cyl, cxr, cyr)
        cxlr, cylr = swap(cxl, 1), swap(cyl, 2)
        d_near, d_mid = add_own(do, dxr, dyr, dxlr, dylr)
        d_midr = swap(d_mid, 4)
    other = pair_swap(part)
    ax, ay, axl, ayl, ao = weight_grad(me, [in_low, dz_one_low], [d_qkv, attended])
    if fast:
        other, ax, ay, cxlr, cylr, d_midr = tie(other, ax, ay, cxlr, cylr, d_midr)
        axr, ayr = swap(ax, 1), swap(ay, 2)
        c_near, c_mid = add_own(co, cxr, cyr, cxlr, cylr)
        c_midr = swap(c_mid, 4)
        d_near, d_far = add_mid(d_near, d_midr)
        d_farr = swap(d_far, 12)
        other, axr, ayr, c_midr, d_farr = tie(other, axr, ayr, c_midr, d_farr)
        axl, ayl = add_late(axl, ayl, axr, ayr)
        axlr, aylr = swap(axl, 1), swap(ayl, 2)
        c_near, c_far = add_mid(c_near, c_midr)
        c_farr = swap(c_far, 12)
        d_w_down_t = d_near + d_farr.astype(F32)
    d_tokens, joined = last(dz_one, part, other, flag, sums_one, sums_two, sums_up, sums_qkv)
    if fast:
        axlr, aylr, c_farr, joined = tie(axlr, aylr, c_farr, joined)
        a_near, a_mid = add_own(ao, axr, ayr, axlr, aylr)
        a_midr = swap(a_mid, 4)
        joined = joined + swap(joined, 1)
        joined = joined + swap(joined, 2)
        d_w_up = c_near + c_farr.astype(F32)
        a_midr, joined = tie(a_midr, joined)
        a_near, a_far = add_mid(a_near, a_midr)
        a_farr = swap(a_far, 12)
        joined = joined + swap(joined, 4)
        joined = joined + swap(joined, 8)
        d_wa = a_near + a_farr.astype(F32)
    else:
        full = []
        for x, y, xl, yl, o in ((ax, ay, axl, ayl, ao), (cx, cy, cxl, cyl, co), (dx, dy, dxl, dyl, do)):
            blocks = [None] * BLOCKS
            for k in range(2):
                blocks[3 + NEAR[k]], blocks[1 + NEAR[k]], blocks[1 + MID[k]] = x[k], x[2 + k], xl[k]
                blocks[3 + MID[k]], blocks[2 + MID[k]], blocks[2 + NEAR[k]] = y[k], y[2 + k], yl[k]
                blocks[NEAR[k]], blocks[MID[k]] = o[k], o[2 + k]
            full.append(jnp.concatenate(blocks).astype(F32))
        joined = lax.psum(joined, "dp")
        d_wa, d_w_up, d_w_down_t = (
            lax.psum_scatter(member, "dp", scatter_dimension=0, tiled=True) for member in full
        )
    units = w_up.shape[1]
    return (
        result,
        d_tokens,
        joined[0],
        d_wa[:, :head_cols],
        joined[7, :head_cols],
        d_wa[:, head_cols : 2 * head_cols],
        d_wa[:, 2 * head_cols : 3 * head_cols],
        joined[7, head_cols : 2 * head_cols],
        d_wa[:, 3 * head_cols :].T,
        joined[3],
        joined[1],
        joined[2],
        d_w_up,
        joined[8:].reshape(-1)[:units],
        d_w_down_t.T,
        joined[6],
        joined[4],
        joined[5],
    )


def solution(mesh):
    rows, flat, both = P("dp", None), P(), P("dp", "mp")
    return jax.shard_map(
        functools.partial(per_device, mesh.shape["dp"]),
        mesh=mesh,
        in_specs=(rows, P("dp"), P("dp"), flat, both, P("mp"), both, both, P("mp"), P("mp", "dp"),
                  flat, flat, flat, both, P("mp"), P("mp", "dp"), flat, flat, flat, rows),
        out_specs=(rows, rows, flat, both, P("mp"), both, both, P("mp"), P("mp", "dp"), flat, flat,
                   flat, both, P("mp"), P("mp", "dp"), flat, flat, flat),
        check_vma=False,
    )
```

```python
import functools

import jax
import jax.numpy as jnp
from jax import lax
from jax.experimental import pallas as pl
from jax.experimental.pallas import tpu as pltpu
from jax.sharding import PartitionSpec as P

HEAD = 64
NORM_EPS = 1e-05
F32 = jnp.float32
B16 = jnp.bfloat16
MIB = 1 << 20

BLOCKS = 16
NEAR = (0, 12)
MID = (4, 8)


def swap(values, bit):
    return lax.ppermute(values, "dp", [(i, i ^ bit) for i in range(BLOCKS)])


def tie(*values):
    return lax.optimization_barrier(values)


def after(value, *earlier):
    return tie(value, *earlier)[0]


def pair_swap(partial):
    return lax.ppermute(partial, "mp", [(0, 1), (1, 0)])


def as_pieces(full):
    rows = full.shape[0] // BLOCKS
    blocks = full.reshape(BLOCKS, rows, full.shape[1])
    return [
        jnp.stack([blocks[offset + bits[0]], blocks[offset + bits[1]]])
        for offset in range(4)
        for bits in (NEAR, MID)
    ]


SMEM_SPEC = pl.BlockSpec(memory_space=pltpu.SMEM)
VMEM_SPEC = pl.BlockSpec(memory_space=pltpu.VMEM)
CHUNK = 256
UNROLL = 2
LIGHT = pl.CostEstimate(flops=1, bytes_accessed=1, transcendentals=0)


def call(body, name, shapes, operands, scratch=(), limit=16):
    return pl.pallas_call(
        body,
        in_specs=[
            SMEM_SPEC if member.dtype == jnp.int32 and member.ndim == 1 else VMEM_SPEC
            for member in operands
        ],
        out_specs=[VMEM_SPEC] * len(shapes),
        out_shape=[jax.ShapeDtypeStruct(shape, dtype) for shape, dtype in shapes],
        scratch_shapes=[pltpu.VMEM(shape, dtype) for shape, dtype in scratch],
        compiler_params=pltpu.CompilerParams(vmem_limit_bytes=limit * MIB),
        cost_estimate=LIGHT,
        name=name,
    )(*operands)


def chunks(count):
    return [slice(start, start + CHUNK) for start in range(0, count, CHUNK)]


def fill(me, pieces, full_ref):
    rows = pieces[0].shape[1]
    for index, piece in enumerate(pieces):
        bits = (NEAR, MID)[index % 2]
        for k in range(2):
            block = me ^ (index // 2 + bits[k])
            full_ref[pl.ds(pl.multiple_of(block * rows, rows), rows), :] = piece[k]


def dot(left, right):
    return jnp.dot(left, right, preferred_element_type=F32)


def dot_t(left, right):
    return lax.dot_general(left, right, (((1,), (1,)), ((), ())), preferred_element_type=F32)


def t_dot(left, right):
    return lax.dot_general(left, right, (((0,), (0,)), ((), ())), preferred_element_type=F32)


def row_mean(values):
    return jnp.mean(values, axis=-1, keepdims=True)


def normalize(values):
    centred = values - row_mean(values)
    inverse = lax.rsqrt(row_mean(centred * centred) + NORM_EPS)
    return centred * inverse, inverse


def col_sum(values):
    return jnp.sum(values, axis=0, keepdims=True)


def norm_back(scaled, normed, inverse):
    return inverse * (scaled - row_mean(scaled) - normed * row_mean(scaled * normed))


def two_heads(slots):
    row = lax.broadcasted_iota(jnp.int32, (2 * slots, 2 * HEAD), 0) // slots
    lane = lax.broadcasted_iota(jnp.int32, (2 * slots, 2 * HEAD), 1) // HEAD
    return (row == lane).astype(F32).astype(B16)


def doubled(values, mask):
    return jnp.concatenate([values, values], axis=0) * mask


def attend_body(slots, me_ref, len_ref, in_ref, bias_ref, *rest):
    pieces, (w_ref, qkv_ref, prob_ref, att_ref, part_ref) = rest[:8], rest[8:]
    count, width = att_ref.shape
    fill(me_ref[0], pieces, w_ref)
    for rows in chunks(count):
        qkv_ref[rows] = (dot(in_ref[rows], w_ref[:, : 3 * width]) + bias_ref[...]).astype(B16)
    mask = two_heads(slots)
    key_slot = lax.broadcasted_iota(jnp.int32, (slots, slots), 1)

    def chain_step(chain, carry):
        valid = key_slot < len_ref[chain]
        rows = pl.ds(pl.multiple_of(chain * slots, slots), slots)
        for pair in range(width // (2 * HEAD)):
            lanes = 2 * HEAD * pair
            query = qkv_ref[rows, lanes : lanes + 2 * HEAD]
            key = qkv_ref[rows, width + lanes : width + lanes + 2 * HEAD]
            value = qkv_ref[rows, 2 * width + lanes : 2 * width + lanes + 2 * HEAD]
            scores = dot_t(query * (HEAD**-0.5), doubled(key, mask))
            probs = []
            for head in range(2):
                part = jnp.where(valid, scores[:, head * slots : (head + 1) * slots], -1e30)
                terms = jnp.exp(part - jnp.max(part, axis=-1, keepdims=True))
                probs.append((terms / jnp.sum(terms, axis=-1, keepdims=True)).astype(B16))
            prob = jnp.concatenate(probs, axis=1)
            prob_ref[rows, 2 * slots * pair : 2 * slots * (pair + 1)] = prob
            att_ref[rows, lanes : lanes + 2 * HEAD] = dot(prob, doubled(value, mask)).astype(B16)
        return carry

    lax.fori_loop(0, count // slots, chain_step, 0, unroll=UNROLL)
    for rows in chunks(count):
        part_ref[rows] = dot_t(att_ref[rows], w_ref[:, 3 * width :]).astype(B16)


def attend(me, lengths, in_low, bias, pieces):
    count, width = in_low.shape
    heads = bias.shape[1] // 3
    slots = count // lengths.shape[0]
    shapes = [
        ((width, 4 * heads), B16),
        ((count, 3 * heads), B16),
        ((count, heads // HEAD * slots), B16),
        ((count, heads), B16),
        ((count, width), B16),
    ]
    body = functools.partial(attend_body, slots)
    return call(body, "attend", shapes, [me, lengths, in_low, bias, *pieces])


def up_body(me_ref, in_ref, own_ref, other_ref, vec_ref, bias_ref, *rest):
    pieces, (w_ref, normed_ref, inverse_ref, low_ref, act_ref, slope_ref) = rest[:8], rest[8:]
    fill(me_ref[0], pieces, w_ref)
    vectors = vec_ref[...]
    for rows in chunks(in_ref.shape[0]):
        attn = own_ref[rows].astype(F32) + other_ref[rows].astype(F32) + vectors[0:1]
        normed, inverse = normalize(in_ref[rows].astype(F32) + attn)
        normed_ref[rows] = normed
        inverse_ref[rows] = jnp.broadcast_to(inverse, (CHUNK, inverse_ref.shape[1]))
        low_ref[rows] = (normed * vectors[1:2] + vectors[2:3]).astype(B16)
        pre = dot(low_ref[rows], w_ref[...]) + bias_ref[...]
        cdf = 0.5 + 0.5 * lax.erf(pre * (2.0**-0.5))
        act_ref[rows] = (pre * cdf).astype(B16)
        density = jnp.exp(pre * pre * -0.5) * 0.3989422804014327
        slope_ref[rows] = (cdf + pre * density).astype(B16)


def up(me, in_low, own, other, vectors, bias, pieces):
    count, width = in_low.shape
    units = bias.shape[1]
    shapes = [
        ((width, units), B16),
        ((count, width), F32),
        ((count, 128), F32),
        ((count, width), B16),
        ((count, units), B16),
        ((count, units), B16),
    ]
    return call(up_body, "up", shapes, [me, in_low, own, other, vectors, bias, *pieces])


def down_body(me_ref, act_ref, *rest):
    pieces, (w_ref, part_ref) = rest[:8], rest[8:]
    fill(me_ref[0], pieces, w_ref)
    for rows in chunks(act_ref.shape[0]):
        part_ref[rows] = dot_t(act_ref[rows], w_ref[...]).astype(B16)


def down(me, act, pieces):
    count, units = act.shape
    width = BLOCKS * pieces[0].shape[1]
    shapes = [((width, units), B16), ((count, width), B16)]
    return call(down_body, "down", shapes, [me, act, *pieces])


def second_norm_body(normed_ref, own_ref, other_ref, grad_ref, vec_ref, out_ref, dz_ref, low_ref, sum_ref):
    vectors = vec_ref[...]
    sum_ref[...] = jnp.zeros_like(sum_ref)
    for rows in chunks(own_ref.shape[0]):
        hidden = normed_ref[rows] * vectors[0:1] + vectors[1:2]
        ffn = own_ref[rows].astype(F32) + other_ref[rows].astype(F32) + vectors[2:3]
        normed, inverse = normalize(hidden + ffn)
        out_ref[rows] = (normed * vectors[3:4] + vectors[4:5]).astype(B16)
        grad = grad_ref[rows].astype(F32)
        dz = norm_back(grad * vectors[3:4], normed, inverse)
        dz_ref[rows] = dz
        low_ref[rows] = dz.astype(B16)
        sum_ref[0:1] += col_sum(grad * normed)
        sum_ref[1:2] += col_sum(grad)
        sum_ref[2:3] += col_sum(dz)


def second_norm(normed, own, other, grad, vectors):
    shape = own.shape
    shapes = [(shape, B16), (shape, F32), (shape, B16), ((8, shape[1]), F32)]
    return call(second_norm_body, "second_norm", shapes, [normed, own, other, grad, vectors])


def weight_grad(me, lefts, rights):
    count, width = lefts[0].shape
    tile = 384 if all(right.shape[1] % 384 == 0 for right in rights) else 128
    total = sum(right.shape[1] for right in rights)
    rows = width // BLOCKS
    n = len(lefts)

    def body(me_ref, *refs):
        x_ref, y_ref, x_late_ref, y_late_ref, own_ref, turned_ref, full_ref = refs[2 * n :]
        at = 0
        for left_ref, right_ref in zip(refs[:n], refs[n : 2 * n]):
            turned_ref[...] = left_ref[...].T
            for start in range(0, right_ref.shape[1], tile):
                full_ref[...] = dot(turned_ref[...], right_ref[:, start : start + tile]).astype(B16)
                cols = slice(at, at + tile)

                def block(offset):
                    place = (me_ref[0] ^ offset) * rows
                    return full_ref[pl.ds(pl.multiple_of(place, rows), rows), :]

                for k in range(2):
                    x_ref[k, :, cols] = block(3 + NEAR[k])
                    x_ref[2 + k, :, cols] = block(1 + NEAR[k])
                    x_late_ref[k, :, cols] = block(1 + MID[k])
                    y_ref[k, :, cols] = block(3 + MID[k])
                    y_ref[2 + k, :, cols] = block(2 + MID[k])
                    y_late_ref[k, :, cols] = block(2 + NEAR[k])
                    own_ref[k, :, cols] = block(NEAR[k])
                    own_ref[2 + k, :, cols] = block(MID[k])
                at += tile

    shapes = [((number, rows, total), B16) for number in (4, 4, 2, 2, 4)]
    scratch = [((width, count), B16), ((width, tile), B16)]
    return call(body, "weight_grad", shapes, [me, *lefts, *rights], scratch)


def hidden_back_body(low_ref, slope_ref, down_ref, up_ref, pre_ref, part_ref, sum_ref):
    sum_ref[...] = jnp.zeros_like(sum_ref)
    for rows in chunks(low_ref.shape[0]):
        d_pre = dot(low_ref[rows], down_ref[...]) * slope_ref[rows].astype(F32)
        sum_ref[0:1] += col_sum(d_pre)
        pre_ref[rows] = d_pre.astype(B16)
        part_ref[rows] = dot_t(pre_ref[rows], up_ref[...]).astype(B16)


def hidden_back(dz_low, slope, w_down_t, w_up):
    count, width = dz_low.shape
    units = slope.shape[1]
    shapes = [((count, units), B16), ((count, width), B16), ((8, units), F32)]
    return call(hidden_back_body, "hidden_back", shapes, [dz_low, slope, w_down_t, w_up])


def attend_back_body(slots, dz_ref, own_ref, other_ref, normed_ref, inverse_ref, gain_ref,
                     qkv_ref, prob_ref, w_ref, dz_one_ref, low_ref, d_qkv_ref, part_ref, sum_ref,
                     sum_qkv_ref, d_att_ref):
    count, width = d_att_ref.shape
    sum_ref[...] = jnp.zeros_like(sum_ref)
    sum_qkv_ref[...] = jnp.zeros_like(sum_qkv_ref)
    for rows in chunks(count):
        normed = normed_ref[rows]
        d_hidden = dz_ref[rows] + (own_ref[rows].astype(F32) + other_ref[rows].astype(F32))
        dz_one = norm_back(d_hidden * gain_ref[...], normed, inverse_ref[rows, 0:1])
        dz_one_ref[rows] = dz_one
        low_ref[rows] = dz_one.astype(B16)
        sum_ref[0:1] += col_sum(d_hidden * normed)
        sum_ref[1:2] += col_sum(d_hidden)
        sum_ref[2:3] += col_sum(dz_one)
        d_att_ref[rows] = dot(low_ref[rows], w_ref[:, 3 * width :]).astype(B16)
    mask = two_heads(slots)

    def chain_step(chain, carry):
        rows = pl.ds(pl.multiple_of(chain * slots, slots), slots)
        for pair in range(width // (2 * HEAD)):
            lanes = 2 * HEAD * pair
            query = qkv_ref[rows, lanes : lanes + 2 * HEAD]
            key = qkv_ref[rows, width + lanes : width + lanes + 2 * HEAD]
            value = qkv_ref[rows, 2 * width + lanes : 2 * width + lanes + 2 * HEAD]
            d_att = d_att_ref[rows, lanes : lanes + 2 * HEAD]
            prob = prob_ref[rows, 2 * slots * pair : 2 * slots * (pair + 1)]
            d_prob = dot_t(d_att, doubled(value, mask))
            weights = prob.astype(F32)
            products = weights * d_prob
            lows = []
            for head in range(2):
                half = slice(head * slots, (head + 1) * slots)
                total = jnp.sum(products[:, half], axis=-1, keepdims=True)
                lows.append((products[:, half] - weights[:, half] * total).astype(B16))
            low = jnp.concatenate(lows, axis=1)
            d_query = dot(low, doubled(key, mask)) * (HEAD**-0.5)
            tall = jnp.concatenate(lows, axis=0)
            d_key = t_dot(tall, doubled(query, mask)) * (HEAD**-0.5)
            tall = jnp.concatenate([prob[:, :slots], prob[:, slots:]], axis=0)
            d_value = t_dot(tall, doubled(d_att, mask))
            d_qkv_ref[rows, lanes : lanes + 2 * HEAD] = d_query.astype(B16)
            d_qkv_ref[rows, width + lanes : width + lanes + 2 * HEAD] = d_key.astype(B16)
            d_qkv_ref[rows, 2 * width + lanes : 2 * width + lanes + 2 * HEAD] = d_value.astype(B16)
        return carry

    lax.fori_loop(0, count // slots, chain_step, 0, unroll=UNROLL)
    for rows in chunks(count):
        sum_qkv_ref[0:1] += col_sum(d_qkv_ref[rows].astype(F32))
        part_ref[rows] = dot_t(d_qkv_ref[rows], w_ref[:, : 3 * width]).astype(B16)


def attend_back(chain_count, dz_two, own, other, normed, inverse, gain, qkv, prob, w_a):
    shape = dz_two.shape
    heads = qkv.shape[1] // 3
    shapes = [
        (shape, F32),
        (shape, B16),
        (qkv.shape, B16),
        (shape, B16),
        ((8, shape[1]), F32),
        ((8, 3 * heads), F32),
    ]
    operands = [dz_two, own, other, normed, inverse, gain, qkv, prob, w_a]
    body = functools.partial(attend_back_body, shape[0] // chain_count)
    return call(body, "attend_back", shapes, operands, [((shape[0], heads), B16)])


def last_body(dz_ref, own_ref, other_ref, flag_ref, one_ref, two_ref, up_ref, qkv_ref, out_ref, sum_ref):
    width = dz_ref.shape[1]
    heads = qkv_ref.shape[1] // 3
    sum_ref[...] = jnp.zeros_like(sum_ref)
    sum_ref[1:4] = one_ref[0:3]
    sum_ref[4:7] = two_ref[0:3]
    sum_ref[7:8, :heads] = qkv_ref[0:1, :heads]
    sum_ref[7:8, heads : 2 * heads] = qkv_ref[0:1, 2 * heads :]
    for k in range(up_ref.shape[1] // width):
        sum_ref[8 + k : 9 + k] = up_ref[0:1, k * width : (k + 1) * width]
    for rows in chunks(dz_ref.shape[0]):
        total = dz_ref[rows] + (own_ref[rows].astype(F32) + other_ref[rows].astype(F32))
        masked = total * flag_ref[rows, 0:1]
        sum_ref[0:1] += col_sum(masked)
        out_ref[rows] = total - masked


def last(dz_one, own, other, flag, sums_one, sums_two, sums_up, sums_qkv):
    width = dz_one.shape[1]
    joined = (8 + 8 * pl.cdiv(sums_up.shape[1], 8 * width), width)
    operands = [dz_one, own, other, flag, sums_one, sums_two, sums_up, sums_qkv]
    return call(last_body, "last", [(dz_one.shape, F32), (joined, F32)], operands)


def add_late_body(x_ref, y_ref, from_x_ref, from_y_ref, out_x_ref, out_y_ref):
    out_x_ref[...] = (x_ref[...].astype(F32) + from_y_ref[:2].astype(F32)).astype(B16)
    out_y_ref[...] = (y_ref[...].astype(F32) + from_x_ref[:2].astype(F32)).astype(B16)


def add_own_body(own_ref, from_x_ref, from_y_ref, late_x_ref, late_y_ref, near_ref, mid_ref):
    near_ref[...] = (
        own_ref[:2].astype(F32) + from_x_ref[2:].astype(F32) + late_y_ref[...].astype(F32)
    )
    mid_ref[...] = (
        own_ref[2:].astype(F32) + late_x_ref[...].astype(F32) + from_y_ref[2:].astype(F32)
    ).astype(B16)


def add_mid_body(near_ref, mid_ref, own_ref, far_ref):
    own_ref[...] = near_ref[0] + mid_ref[0].astype(F32)
    far_ref[...] = (near_ref[1] + mid_ref[1].astype(F32)).astype(B16)


def add_late(late_x, late_y, from_x, from_y):
    shape = (late_x.shape, B16)
    return call(add_late_body, "add_late", [shape, shape], [late_x, late_y, from_x, from_y], limit=8)


def add_own(own, from_x, from_y, late_x, late_y):
    shapes = [(late_x.shape, F32), (late_x.shape, B16)]
    return call(add_own_body, "add_own", shapes, [own, from_x, from_y, late_x, late_y], limit=8)


def add_mid(near, mid):
    shapes = [(near.shape[1:], F32), (near.shape[1:], B16)]
    return call(add_mid_body, "add_mid", shapes, [near, mid], limit=8)


def per_device(dp_size, tokens, masked, lengths, mask_vector, w_query, b_query, w_key, w_value,
               b_value, w_out, b_out, gain_one, shift_one, w_up, b_up, w_down, b_down, gain_two,
               shift_two, grad_out):
    head_cols = w_query.shape[1]
    width = tokens.shape[1]
    fast = dp_size == BLOCKS and w_query.shape[0] % 16 == 0
    me = lax.axis_index("dp").astype(jnp.int32).reshape(1)
    if not fast:
        me = jnp.zeros_like(me)

    (b_query, b_value, b_out, gain_one, shift_one, b_up, b_down, gain_two, shift_two) = (
        member.astype(F32)
        for member in (b_query, b_value, b_out, gain_one, shift_one, b_up, b_down, gain_two, shift_two)
    )
    is_masked = (masked == 1)[:, None]
    flag = jnp.broadcast_to(is_masked, (masked.shape[0], 128)).astype(F32)
    in_low = jnp.where(is_masked, mask_vector[None, :], tokens)
    bias_qkv = jnp.concatenate([b_query, jnp.zeros_like(b_query), b_value])[None, :]
    vectors_one = jnp.stack([b_out, gain_one, shift_one])
    vectors_two = jnp.stack([gain_one, shift_one, b_down, gain_two, shift_two])
    b_up, gain_one = b_up[None, :], gain_one[None, :]

    a = jnp.concatenate([w_query, w_key, w_value, w_out.T], axis=1)
    c = w_up
    d = w_down.T
    if fast:
        az = swap(a, 12)
        az, me, flag, in_low, bias_qkv, vectors_one, vectors_two, b_up, gain_one = tie(
            az, me, flag, in_low, bias_qkv, vectors_one, vectors_two, b_up, gain_one
        )
        an = jnp.stack([a, az])
        anx, any_, am = swap(an, 1), swap(an, 2), swap(an, 4)
        cz = swap(after(c, az), 12)
        amx, amy = swap(am, 1), swap(am, 2)
        cn = jnp.stack([c, cz])
        cm = swap(after(cn, am), 4)
        cnx, cny = swap(after(cn, anx), 1), swap(after(cn, any_), 2)
        dz = swap(after(d, cz), 12)
        dn = jnp.stack([d, dz])
        amd, and_ = swap(amy, 1), swap(after(anx, amy), 2)
        an, am, anx, amx, any_, amy, and_, amd, cn, cm, cnx, cny, dn = tie(
            an, am, anx, amx, any_, amy, and_, amd, cn, cm, cnx, cny, dn
        )
        pieces_a = [an, am, anx, amx, any_, amy, and_, amd]
        cmx, cmy, dm = swap(cm, 1), swap(cm, 2), swap(dn, 4)
        dnx, cnd = swap(dn, 1), swap(cnx, 2)
    else:
        a, c, d = (lax.all_gather(piece, "dp", axis=0, tiled=True) for piece in (a, c, d))
        pieces_a, pieces_c, pieces_d = as_pieces(a), as_pieces(c), as_pieces(d)
    w_a, qkv, prob, attended, part = attend(me, lengths, in_low, bias_qkv, pieces_a)
    if fast:
        part, cmx, cmy, cnd, dn, dm, dnx = tie(part, cmx, cmy, cnd, dn, dm, dnx)
        cmd, dny = swap(cmy, 1), swap(dn, 2)
    other = pair_swap(part)
    if fast:
        other, cmd, dny, dm = tie(other, cmd, dny, dm)
        pieces_c = [cn, cm, cnx, cmx, cny, cmy, cnd, cmd]
        dmx, dmy = swap(dm, 1), swap(dm, 2)
    w_u, normed_one, inverse_one, hidden_low, act_low, slope = up(
        me, in_low, part, other, vectors_one, b_up, pieces_c
    )
    if fast:
        act_low, dnx, dmx, dmy = tie(act_low, dnx, dmx, dmy)
        dmd, dnd = swap(dmy, 1), swap(dnx, 2)
        pieces_d = [dn, dm, dnx, dmx, dny, dmy, dnd, dmd]
    w_d, part = down(me, act_low, pieces_d)
    other = pair_swap(part)
    result, dz_two, dz_two_low, sums_two = second_norm(normed_one, part, other, grad_out, vectors_two)
    dx, dy, dxl, dyl, do = weight_grad(me, [dz_two_low], [act_low])
    if fast:
        dx, dy, dxl, dyl, dz_two_low = tie(dx, dy, dxl, dyl, dz_two_low)
        dxr, dyr = swap(dx, 1), swap(dy, 2)
    d_pre_low, part, sums_up = hidden_back(dz_two_low, slope, w_d, w_u)
    cx, cy, cxl, cyl, co = weight_grad(me, [hidden_low], [d_pre_low])
    if fast:
        part, dxr, dyr, cx, cy = tie(part, dxr, dyr, cx, cy)
        dxl, dyl = add_late(dxl, dyl, dxr, dyr)
        dxlr, dylr, cxr, cyr = swap(dxl, 1), swap(dyl, 2), swap(cx, 1), swap(cy, 2)
    other = pair_swap(part)
    dz_one, dz_one_low, d_qkv, part, sums_one, sums_qkv = attend_back(
        lengths.shape[0], dz_two, part, other, normed_one, inverse_one, gain_one, qkv, prob, w_a
    )
    if fast:
        part, d_qkv, dxlr, dylr, cxr, cyr = tie(part, d_qkv, dxlr, dylr, cxr, cyr)
        cxl, cyl = add_late(cxl, cyl, cxr, cyr)
        cxlr, cylr = swap(cxl, 1), swap(cyl, 2)
        d_near, d_mid = add_own(do, dxr, dyr, dxlr, dylr)
        d_midr = swap(d_mid, 4)
    other = pair_swap(part)
    ax, ay, axl, ayl, ao = weight_grad(me, [in_low, dz_one_low], [d_qkv, attended])
    if fast:
        other, ax, ay, cxlr, cylr, d_midr = tie(other, ax, ay, cxlr, cylr, d_midr)
        axr, ayr = swap(ax, 1), swap(ay, 2)
        c_near, c_mid = add_own(co, cxr, cyr, cxlr, cylr)
        c_midr = swap(c_mid, 4)
        d_near, d_far = add_mid(d_near, d_midr)
        d_farr = swap(d_far, 12)
        other, axr, ayr, c_midr, d_farr = tie(other, axr, ayr, c_midr, d_farr)
        axl, ayl = add_late(axl, ayl, axr, ayr)
        axlr, aylr = swap(axl, 1), swap(ayl, 2)
        c_near, c_far = add_mid(c_near, c_midr)
        c_farr = swap(c_far, 12)
        d_w_down_t = d_near + d_farr.astype(F32)
    d_tokens, joined = last(dz_one, part, other, flag, sums_one, sums_two, sums_up, sums_qkv)
    if fast:
        axlr, aylr, c_farr, joined = tie(axlr, aylr, c_farr, joined)
        a_near, a_mid = add_own(ao, axr, ayr, axlr, aylr)
        a_midr = swap(a_mid, 4)
        joined = joined + swap(joined, 1)
        joined = joined + swap(joined, 2)
        d_w_up = c_near + c_farr.astype(F32)
        a_midr, joined = tie(a_midr, joined)
        a_near, a_far = add_mid(a_near, a_midr)
        a_farr = swap(a_far, 12)
        joined = joined + swap(joined, 4)
        joined = joined + swap(joined, 8)
        d_wa = a_near + a_farr.astype(F32)
    else:
        full = []
        for x, y, xl, yl, o in ((ax, ay, axl, ayl, ao), (cx, cy, cxl, cyl, co), (dx, dy, dxl, dyl, do)):
            blocks = [None] * BLOCKS
            for k in range(2):
                blocks[3 + NEAR[k]], blocks[1 + NEAR[k]], blocks[1 + MID[k]] = x[k], x[2 + k], xl[k]
                blocks[3 + MID[k]], blocks[2 + MID[k]], blocks[2 + NEAR[k]] = y[k], y[2 + k], yl[k]
                blocks[NEAR[k]], blocks[MID[k]] = o[k], o[2 + k]
            full.append(jnp.concatenate(blocks).astype(F32))
        joined = lax.psum(joined, "dp")
        d_wa, d_w_up, d_w_down_t = (
            lax.psum_scatter(member, "dp", scatter_dimension=0, tiled=True) for member in full
        )
    units = w_up.shape[1]
    return (
        result,
        d_tokens,
        joined[0],
        d_wa[:, :head_cols],
        joined[7, :head_cols],
        d_wa[:, head_cols : 2 * head_cols],
        d_wa[:, 2 * head_cols : 3 * head_cols],
        joined[7, head_cols : 2 * head_cols],
        d_wa[:, 3 * head_cols :].T,
        joined[3],
        joined[1],
        joined[2],
        d_w_up,
        joined[8:].reshape(-1)[:units],
        d_w_down_t.T,
        joined[6],
        joined[4],
        joined[5],
    )


def solution(mesh):
    rows, flat, both = P("dp", None), P(), P("dp", "mp")
    return jax.shard_map(
        functools.partial(per_device, mesh.shape["dp"]),
        mesh=mesh,
        in_specs=(rows, P("dp"), P("dp"), flat, both, P("mp"), both, both, P("mp"), P("mp", "dp"),
                  flat, flat, flat, both, P("mp"), P("mp", "dp"), flat, flat, flat, rows),
        out_specs=(rows, rows, flat, both, P("mp"), both, both, P("mp"), P("mp", "dp"), flat, flat,
                   flat, both, P("mp"), P("mp", "dp"), flat, flat, flat),
        check_vma=False,
    )
```

```python
import functools

import jax
import jax.numpy as jnp
from jax import lax
from jax.experimental import pallas as pl
from jax.experimental.pallas import tpu as pltpu
from jax.sharding import PartitionSpec as P

HEAD = 64
NORM_EPS = 1e-05
F32 = jnp.float32
B16 = jnp.bfloat16
MIB = 1 << 20

BLOCKS = 16
NEAR = (0, 12)
MID = (4, 8)


def swap(values, bit):
    return lax.ppermute(values, "dp", [(i, i ^ bit) for i in range(BLOCKS)])


def tie(*values):
    return lax.optimization_barrier(values)


def after(value, *earlier):
    return tie(value, *earlier)[0]


def pair_swap(partial):
    return lax.ppermute(partial, "mp", [(0, 1), (1, 0)])


def as_pieces(full):
    rows = full.shape[0] // BLOCKS
    blocks = full.reshape(BLOCKS, rows, full.shape[1])
    return [
        jnp.stack([blocks[offset + bits[0]], blocks[offset + bits[1]]])
        for offset in range(4)
        for bits in (NEAR, MID)
    ]


SMEM_SPEC = pl.BlockSpec(memory_space=pltpu.SMEM)
VMEM_SPEC = pl.BlockSpec(memory_space=pltpu.VMEM)
CHUNK = 256
UNROLL = 2
LIGHT = pl.CostEstimate(flops=1, bytes_accessed=1, transcendentals=0)


def call(body, name, shapes, operands, scratch=(), limit=16):
    return pl.pallas_call(
        body,
        in_specs=[
            SMEM_SPEC if member.dtype == jnp.int32 and member.ndim == 1 else VMEM_SPEC
            for member in operands
        ],
        out_specs=[VMEM_SPEC] * len(shapes),
        out_shape=[jax.ShapeDtypeStruct(shape, dtype) for shape, dtype in shapes],
        scratch_shapes=[pltpu.VMEM(shape, dtype) for shape, dtype in scratch],
        compiler_params=pltpu.CompilerParams(vmem_limit_bytes=limit * MIB),
        cost_estimate=LIGHT,
        name=name,
    )(*operands)


def chunks(count):
    return [slice(start, start + CHUNK) for start in range(0, count, CHUNK)]


PAIRS = [(q + bits[k], 2 * q + m, k) for q in range(4) for m, bits in enumerate((NEAR, MID)) for k in range(2)]
QUADS = [(q + (NEAR + MID)[k], q, k) for q in range(3) for k in range(4)]
QUADS += [(3 + (NEAR + MID)[k], 3 + k // 2, k % 2) for k in range(4)]


def fill(me, plan, pieces, full_ref):
    rows = pieces[0].shape[1]
    for offset, piece, index in plan:
        block = me ^ offset
        full_ref[pl.ds(pl.multiple_of(block * rows, rows), rows), :] = pieces[piece][index]


def dot(left, right):
    return jnp.dot(left, right, preferred_element_type=F32)


def dot_t(left, right):
    return lax.dot_general(left, right, (((1,), (1,)), ((), ())), preferred_element_type=F32)


def t_dot(left, right):
    return lax.dot_general(left, right, (((0,), (0,)), ((), ())), preferred_element_type=F32)


def row_mean(values):
    return jnp.mean(values, axis=-1, keepdims=True)


def normalize(values):
    centred = values - row_mean(values)
    inverse = lax.rsqrt(row_mean(centred * centred) + NORM_EPS)
    return centred * inverse, inverse


def col_sum(values):
    return jnp.sum(values, axis=0, keepdims=True)


def norm_back(scaled, normed, inverse):
    return inverse * (scaled - row_mean(scaled) - normed * row_mean(scaled * normed))


def two_heads(slots):
    row = lax.broadcasted_iota(jnp.int32, (2 * slots, 2 * HEAD), 0) // slots
    lane = lax.broadcasted_iota(jnp.int32, (2 * slots, 2 * HEAD), 1) // HEAD
    return (row == lane).astype(F32).astype(B16)


def doubled(values, mask):
    return jnp.concatenate([values, values], axis=0) * mask


def attend_body(slots, plan, me_ref, len_ref, in_ref, bias_ref, *rest):
    pieces, (w_ref, qkv_ref, prob_ref, att_ref, part_ref) = rest[:-5], rest[-5:]
    count, width = att_ref.shape
    fill(me_ref[0], plan, pieces, w_ref)
    for rows in chunks(count):
        qkv_ref[rows] = (dot(in_ref[rows], w_ref[:, : 3 * width]) + bias_ref[...]).astype(B16)
    mask = two_heads(slots)
    key_slot = lax.broadcasted_iota(jnp.int32, (slots, slots), 1)

    def chain_step(chain, carry):
        valid = key_slot < len_ref[chain]
        rows = pl.ds(pl.multiple_of(chain * slots, slots), slots)
        for pair in range(width // (2 * HEAD)):
            lanes = 2 * HEAD * pair
            query = qkv_ref[rows, lanes : lanes + 2 * HEAD]
            key = qkv_ref[rows, width + lanes : width + lanes + 2 * HEAD]
            value = qkv_ref[rows, 2 * width + lanes : 2 * width + lanes + 2 * HEAD]
            scores = dot_t(query * (HEAD**-0.5), doubled(key, mask))
            probs = []
            for head in range(2):
                part = jnp.where(valid, scores[:, head * slots : (head + 1) * slots], -1e30)
                terms = jnp.exp(part - jnp.max(part, axis=-1, keepdims=True))
                probs.append((terms / jnp.sum(terms, axis=-1, keepdims=True)).astype(B16))
            prob = jnp.concatenate(probs, axis=1)
            prob_ref[rows, 2 * slots * pair : 2 * slots * (pair + 1)] = prob
            att_ref[rows, lanes : lanes + 2 * HEAD] = dot(prob, doubled(value, mask)).astype(B16)
        return carry

    lax.fori_loop(0, count // slots, chain_step, 0, unroll=UNROLL)
    for rows in chunks(count):
        part_ref[rows] = dot_t(att_ref[rows], w_ref[:, 3 * width :]).astype(B16)


def attend(me, lengths, in_low, bias, plan, pieces):
    count, width = in_low.shape
    heads = bias.shape[1] // 3
    slots = count // lengths.shape[0]
    shapes = [
        ((width, 4 * heads), B16),
        ((count, 3 * heads), B16),
        ((count, heads // HEAD * slots), B16),
        ((count, heads), B16),
        ((count, width), B16),
    ]
    body = functools.partial(attend_body, slots, plan)
    return call(body, "attend", shapes, [me, lengths, in_low, bias, *pieces])


def up_body(plan, me_ref, in_ref, own_ref, other_ref, vec_ref, bias_ref, *rest):
    pieces, (w_ref, normed_ref, inverse_ref, low_ref, act_ref, slope_ref) = rest[:-6], rest[-6:]
    fill(me_ref[0], plan, pieces, w_ref)
    vectors = vec_ref[...]
    for rows in chunks(in_ref.shape[0]):
        attn = own_ref[rows].astype(F32) + other_ref[rows].astype(F32) + vectors[0:1]
        normed, inverse = normalize(in_ref[rows].astype(F32) + attn)
        normed_ref[rows] = normed
        inverse_ref[rows] = jnp.broadcast_to(inverse, (CHUNK, inverse_ref.shape[1]))
        low_ref[rows] = (normed * vectors[1:2] + vectors[2:3]).astype(B16)
        pre = dot(low_ref[rows], w_ref[...]) + bias_ref[...]
        cdf = 0.5 + 0.5 * lax.erf(pre * (2.0**-0.5))
        act_ref[rows] = (pre * cdf).astype(B16)
        density = jnp.exp(pre * pre * -0.5) * 0.3989422804014327
        slope_ref[rows] = (cdf + pre * density).astype(B16)


def up(me, in_low, own, other, vectors, bias, plan, pieces):
    count, width = in_low.shape
    units = bias.shape[1]
    shapes = [
        ((width, units), B16),
        ((count, width), F32),
        ((count, 128), F32),
        ((count, width), B16),
        ((count, units), B16),
        ((count, units), B16),
    ]
    body = functools.partial(up_body, plan)
    return call(body, "up", shapes, [me, in_low, own, other, vectors, bias, *pieces])


def down_body(plan, me_ref, act_ref, *rest):
    pieces, (w_ref, part_ref) = rest[:-2], rest[-2:]
    fill(me_ref[0], plan, pieces, w_ref)
    for rows in chunks(act_ref.shape[0]):
        part_ref[rows] = dot_t(act_ref[rows], w_ref[...]).astype(B16)


def down(me, act, plan, pieces):
    count, units = act.shape
    width = BLOCKS * pieces[0].shape[1]
    shapes = [((width, units), B16), ((count, width), B16)]
    body = functools.partial(down_body, plan)
    return call(body, "down", shapes, [me, act, *pieces])


def second_norm_body(normed_ref, own_ref, other_ref, grad_ref, vec_ref, out_ref, dz_ref, low_ref, sum_ref):
    vectors = vec_ref[...]
    sum_ref[...] = jnp.zeros_like(sum_ref)
    for rows in chunks(own_ref.shape[0]):
        hidden = normed_ref[rows] * vectors[0:1] + vectors[1:2]
        ffn = own_ref[rows].astype(F32) + other_ref[rows].astype(F32) + vectors[2:3]
        normed, inverse = normalize(hidden + ffn)
        out_ref[rows] = (normed * vectors[3:4] + vectors[4:5]).astype(B16)
        grad = grad_ref[rows].astype(F32)
        dz = norm_back(grad * vectors[3:4], normed, inverse)
        dz_ref[rows] = dz
        low_ref[rows] = dz.astype(B16)
        sum_ref[0:1] += col_sum(grad * normed)
        sum_ref[1:2] += col_sum(grad)
        sum_ref[2:3] += col_sum(dz)


def second_norm(normed, own, other, grad, vectors):
    shape = own.shape
    shapes = [(shape, B16), (shape, F32), (shape, B16), ((8, shape[1]), F32)]
    return call(second_norm_body, "second_norm", shapes, [normed, own, other, grad, vectors])


def weight_grad(me, lefts, rights):
    count, width = lefts[0].shape
    tile = 384 if all(right.shape[1] % 384 == 0 for right in rights) else 128
    total = sum(right.shape[1] for right in rights)
    rows = width // BLOCKS
    n = len(lefts)

    def body(me_ref, *refs):
        x_ref, y_ref, x_late_ref, y_late_ref, own_ref, turned_ref, full_ref = refs[2 * n :]
        at = 0
        for left_ref, right_ref in zip(refs[:n], refs[n : 2 * n]):
            turned_ref[...] = left_ref[...].T
            for start in range(0, right_ref.shape[1], tile):
                full_ref[...] = dot(turned_ref[...], right_ref[:, start : start + tile]).astype(B16)
                cols = slice(at, at + tile)

                def block(offset):
                    place = (me_ref[0] ^ offset) * rows
                    return full_ref[pl.ds(pl.multiple_of(place, rows), rows), :]

                for k in range(2):
                    x_ref[k, :, cols] = block(3 + NEAR[k])
                    x_ref[2 + k, :, cols] = block(1 + NEAR[k])
                    x_late_ref[k, :, cols] = block(1 + MID[k])
                    y_ref[k, :, cols] = block(3 + MID[k])
                    y_ref[2 + k, :, cols] = block(2 + MID[k])
                    y_late_ref[k, :, cols] = block(2 + NEAR[k])
                    own_ref[k, :, cols] = block(NEAR[k])
                    own_ref[2 + k, :, cols] = block(MID[k])
                at += tile

    shapes = [((number, rows, total), B16) for number in (4, 4, 2, 2, 4)]
    scratch = [((width, count), B16), ((width, tile), B16)]
    return call(body, "weight_grad", shapes, [me, *lefts, *rights], scratch)


def hidden_back_body(low_ref, slope_ref, down_ref, up_ref, pre_ref, part_ref, sum_ref):
    sum_ref[...] = jnp.zeros_like(sum_ref)
    for rows in chunks(low_ref.shape[0]):
        d_pre = dot(low_ref[rows], down_ref[...]) * slope_ref[rows].astype(F32)
        sum_ref[0:1] += col_sum(d_pre)
        pre_ref[rows] = d_pre.astype(B16)
        part_ref[rows] = dot_t(pre_ref[rows], up_ref[...]).astype(B16)


def hidden_back(dz_low, slope, w_down_t, w_up):
    count, width = dz_low.shape
    units = slope.shape[1]
    shapes = [((count, units), B16), ((count, width), B16), ((8, units), F32)]
    return call(hidden_back_body, "hidden_back", shapes, [dz_low, slope, w_down_t, w_up])


def attend_back_body(slots, dz_ref, own_ref, other_ref, normed_ref, inverse_ref, gain_ref,
                     qkv_ref, prob_ref, w_ref, dz_one_ref, low_ref, d_qkv_ref, part_ref, sum_ref,
                     sum_qkv_ref, d_att_ref):
    count, width = d_att_ref.shape
    sum_ref[...] = jnp.zeros_like(sum_ref)
    sum_qkv_ref[...] = jnp.zeros_like(sum_qkv_ref)
    for rows in chunks(count):
        normed = normed_ref[rows]
        d_hidden = dz_ref[rows] + (own_ref[rows].astype(F32) + other_ref[rows].astype(F32))
        dz_one = norm_back(d_hidden * gain_ref[...], normed, inverse_ref[rows, 0:1])
        dz_one_ref[rows] = dz_one
        low_ref[rows] = dz_one.astype(B16)
        sum_ref[0:1] += col_sum(d_hidden * normed)
        sum_ref[1:2] += col_sum(d_hidden)
        sum_ref[2:3] += col_sum(dz_one)
        d_att_ref[rows] = dot(low_ref[rows], w_ref[:, 3 * width :]).astype(B16)
    mask = two_heads(slots)

    def chain_step(chain, carry):
        rows = pl.ds(pl.multiple_of(chain * slots, slots), slots)
        for pair in range(width // (2 * HEAD)):
            lanes = 2 * HEAD * pair
            query = qkv_ref[rows, lanes : lanes + 2 * HEAD]
            key = qkv_ref[rows, width + lanes : width + lanes + 2 * HEAD]
            value = qkv_ref[rows, 2 * width + lanes : 2 * width + lanes + 2 * HEAD]
            d_att = d_att_ref[rows, lanes : lanes + 2 * HEAD]
            prob = prob_ref[rows, 2 * slots * pair : 2 * slots * (pair + 1)]
            d_prob = dot_t(d_att, doubled(value, mask))
            weights = prob.astype(F32)
            products = weights * d_prob
            lows = []
            for head in range(2):
                half = slice(head * slots, (head + 1) * slots)
                total = jnp.sum(products[:, half], axis=-1, keepdims=True)
                lows.append((products[:, half] - weights[:, half] * total).astype(B16))
            low = jnp.concatenate(lows, axis=1)
            d_query = dot(low, doubled(key, mask)) * (HEAD**-0.5)
            tall = jnp.concatenate(lows, axis=0)
            d_key = t_dot(tall, doubled(query, mask)) * (HEAD**-0.5)
            tall = jnp.concatenate([prob[:, :slots], prob[:, slots:]], axis=0)
            d_value = t_dot(tall, doubled(d_att, mask))
            d_qkv_ref[rows, lanes : lanes + 2 * HEAD] = d_query.astype(B16)
            d_qkv_ref[rows, width + lanes : width + lanes + 2 * HEAD] = d_key.astype(B16)
            d_qkv_ref[rows, 2 * width + lanes : 2 * width + lanes + 2 * HEAD] = d_value.astype(B16)
        return carry

    lax.fori_loop(0, count // slots, chain_step, 0, unroll=UNROLL)
    for rows in chunks(count):
        sum_qkv_ref[0:1] += col_sum(d_qkv_ref[rows].astype(F32))
        part_ref[rows] = dot_t(d_qkv_ref[rows], w_ref[:, : 3 * width]).astype(B16)


def attend_back(chain_count, dz_two, own, other, normed, inverse, gain, qkv, prob, w_a):
    shape = dz_two.shape
    heads = qkv.shape[1] // 3
    shapes = [
        (shape, F32),
        (shape, B16),
        (qkv.shape, B16),
        (shape, B16),
        ((8, shape[1]), F32),
        ((8, 3 * heads), F32),
    ]
    operands = [dz_two, own, other, normed, inverse, gain, qkv, prob, w_a]
    body = functools.partial(attend_back_body, shape[0] // chain_count)
    return call(body, "attend_back", shapes, operands, [((shape[0], heads), B16)])


def last_body(dz_ref, own_ref, other_ref, flag_ref, one_ref, two_ref, up_ref, qkv_ref, out_ref, sum_ref):
    width = dz_ref.shape[1]
    heads = qkv_ref.shape[1] // 3
    sum_ref[...] = jnp.zeros_like(sum_ref)
    sum_ref[1:4] = one_ref[0:3]
    sum_ref[4:7] = two_ref[0:3]
    sum_ref[7:8, :heads] = qkv_ref[0:1, :heads]
    sum_ref[7:8, heads : 2 * heads] = qkv_ref[0:1, 2 * heads :]
    for k in range(up_ref.shape[1] // width):
        sum_ref[8 + k : 9 + k] = up_ref[0:1, k * width : (k + 1) * width]
    for rows in chunks(dz_ref.shape[0]):
        total = dz_ref[rows] + (own_ref[rows].astype(F32) + other_ref[rows].astype(F32))
        masked = total * flag_ref[rows, 0:1]
        sum_ref[0:1] += col_sum(masked)
        out_ref[rows] = total - masked


def last(dz_one, own, other, flag, sums_one, sums_two, sums_up, sums_qkv):
    width = dz_one.shape[1]
    joined = (8 + 8 * pl.cdiv(sums_up.shape[1], 8 * width), width)
    operands = [dz_one, own, other, flag, sums_one, sums_two, sums_up, sums_qkv]
    return call(last_body, "last", [(dz_one.shape, F32), (joined, F32)], operands)


def add_late_body(x_ref, y_ref, from_x_ref, from_y_ref, out_x_ref, out_y_ref):
    out_x_ref[...] = (x_ref[...].astype(F32) + from_y_ref[:2].astype(F32)).astype(B16)
    out_y_ref[...] = (y_ref[...].astype(F32) + from_x_ref[:2].astype(F32)).astype(B16)


def add_own_body(own_ref, from_x_ref, from_y_ref, late_x_ref, late_y_ref, near_ref, mid_ref):
    near_ref[...] = (
        own_ref[:2].astype(F32) + from_x_ref[2:].astype(F32) + late_y_ref[...].astype(F32)
    )
    mid_ref[...] = (
        own_ref[2:].astype(F32) + late_x_ref[...].astype(F32) + from_y_ref[2:].astype(F32)
    ).astype(B16)


def add_mid_body(near_ref, mid_ref, own_ref, far_ref):
    own_ref[...] = near_ref[0] + mid_ref[0].astype(F32)
    far_ref[...] = (near_ref[1] + mid_ref[1].astype(F32)).astype(B16)


def add_late(late_x, late_y, from_x, from_y):
    shape = (late_x.shape, B16)
    return call(add_late_body, "add_late", [shape, shape], [late_x, late_y, from_x, from_y], limit=8)


def add_own(own, from_x, from_y, late_x, late_y):
    shapes = [(late_x.shape, F32), (late_x.shape, B16)]
    return call(add_own_body, "add_own", shapes, [own, from_x, from_y, late_x, late_y], limit=8)


def add_mid(near, mid):
    shapes = [(near.shape[1:], F32), (near.shape[1:], B16)]
    return call(add_mid_body, "add_mid", shapes, [near, mid], limit=8)


def per_device(dp_size, tokens, masked, lengths, mask_vector, w_query, b_query, w_key, w_value,
               b_value, w_out, b_out, gain_one, shift_one, w_up, b_up, w_down, b_down, gain_two,
               shift_two, grad_out):
    head_cols = w_query.shape[1]
    width = tokens.shape[1]
    fast = dp_size == BLOCKS and w_query.shape[0] % 16 == 0
    me = lax.axis_index("dp").astype(jnp.int32).reshape(1)
    if not fast:
        me = jnp.zeros_like(me)

    (b_query, b_value, b_out, gain_one, shift_one, b_up, b_down, gain_two, shift_two) = (
        member.astype(F32)
        for member in (b_query, b_value, b_out, gain_one, shift_one, b_up, b_down, gain_two, shift_two)
    )
    is_masked = (masked == 1)[:, None]
    flag = jnp.broadcast_to(is_masked, (masked.shape[0], 128)).astype(F32)
    in_low = jnp.where(is_masked, mask_vector[None, :], tokens)
    bias_qkv = jnp.concatenate([b_query, jnp.zeros_like(b_query), b_value])[None, :]
    vectors_one = jnp.stack([b_out, gain_one, shift_one])
    vectors_two = jnp.stack([gain_one, shift_one, b_down, gain_two, shift_two])
    b_up, gain_one = b_up[None, :], gain_one[None, :]

    a = jnp.concatenate([w_query, w_key, w_value, w_out.T], axis=1)
    c = w_up
    d = w_down.T
    plan = QUADS if fast else PAIRS
    if fast:
        az = swap(a, 12)
        az, me, flag, in_low, bias_qkv, vectors_one, vectors_two, b_up, gain_one = tie(
            az, me, flag, in_low, bias_qkv, vectors_one, vectors_two, b_up, gain_one
        )
        an = jnp.stack([a, az])
        anx, any_, am = swap(an, 1), swap(an, 2), swap(an, 4)
        cz = swap(after(c, am), 12)
        amx, amy = swap(am, 1), swap(am, 2)
        cn = jnp.stack([c, cz])
        cm = swap(after(cn, am), 4)
        and_, amd = swap(after(anx, any_), 2), swap(amy, 1)
        dz = swap(after(d, cz), 12)
        dn = jnp.stack([d, dz])
        c4 = jnp.concatenate([cn, cm])
        an, am, anx, amx, any_, amy, and_, amd, c4, dn = tie(
            an, am, anx, amx, any_, amy, and_, amd, c4, dn
        )
        pieces_a = [an, am, anx, amx, any_, amy, and_, amd]
        c4x, c4y, dm = swap(c4, 1), swap(c4, 2), swap(dn, 4)
    else:
        a, c, d = (lax.all_gather(piece, "dp", axis=0, tiled=True) for piece in (a, c, d))
        pieces_a, pieces_c, pieces_d = as_pieces(a), as_pieces(c), as_pieces(d)
    w_a, qkv, prob, attended, part = attend(me, lengths, in_low, bias_qkv, PAIRS, pieces_a)
    if fast:
        c4x, c4y, dm, part = tie(c4x, c4y, dm, part)
        cmd, cnd = swap(c4y[2:], 1), swap(c4x[:2], 2)
        d4 = jnp.concatenate([dn, dm])
        d4x, d4y = swap(d4, 1), swap(d4, 2)
    other = pair_swap(part)
    if fast:
        d4x, d4y, cmd, cnd, other, part = tie(d4x, d4y, cmd, cnd, other, part)
        pieces_c = [c4, c4x, c4y, cnd, cmd]
        dmd, dnd = swap(d4y[2:], 1), swap(d4x[:2], 2)
    w_u, normed_one, inverse_one, hidden_low, act_low, slope = up(
        me, in_low, part, other, vectors_one, b_up, plan, pieces_c
    )
    if fast:
        dmd, dnd, act_low = tie(dmd, dnd, act_low)
        pieces_d = [d4, d4x, d4y, dnd, dmd]
    w_d, part = down(me, act_low, plan, pieces_d)
    other = pair_swap(part)
    result, dz_two, dz_two_low, sums_two = second_norm(normed_one, part, other, grad_out, vectors_two)
    dx, dy, dxl, dyl, do = weight_grad(me, [dz_two_low], [act_low])
    if fast:
        dx, dy, dxl, dyl, dz_two_low = tie(dx, dy, dxl, dyl, dz_two_low)
        dxr, dyr = swap(dx, 1), swap(dy, 2)
    d_pre_low, part, sums_up = hidden_back(dz_two_low, slope, w_d, w_u)
    cx, cy, cxl, cyl, co = weight_grad(me, [hidden_low], [d_pre_low])
    if fast:
        dxr, dyr, part, cx, cy = tie(dxr, dyr, part, cx, cy)
        cxr, cyr = swap(cx, 1), swap(cy, 2)
        dxl, dyl = add_late(dxl, dyl, dxr, dyr)
        dxlr, dylr = swap(dxl, 1), swap(dyl, 2)
    other = pair_swap(part)
    dz_one, dz_one_low, d_qkv, part, sums_one, sums_qkv = attend_back(
        lengths.shape[0], dz_two, part, other, normed_one, inverse_one, gain_one, qkv, prob, w_a
    )
    ax, ay, axl, ayl, ao = weight_grad(me, [in_low, dz_one_low], [d_qkv, attended])
    if fast:
        cxr, cyr, dxlr, dylr, part, ax, ay = tie(cxr, cyr, dxlr, dylr, part, ax, ay)
        axr, ayr = swap(ax, 1), swap(ay, 2)
        cxl, cyl = add_late(cxl, cyl, cxr, cyr)
        cxlr, cylr = swap(cxl, 1), swap(cyl, 2)
        d_near, d_mid = add_own(do, dxr, dyr, dxlr, dylr)
        d_midr = swap(d_mid, 4)
    other = pair_swap(part)
    d_tokens, joined = last(dz_one, part, other, flag, sums_one, sums_two, sums_up, sums_qkv)
    if fast:
        axr, ayr, cxlr, cylr, d_midr, joined = tie(axr, ayr, cxlr, cylr, d_midr, joined)
        axl, ayl = add_late(axl, ayl, axr, ayr)
        axlr, aylr = swap(axl, 1), swap(ayl, 2)
        c_near, c_mid = add_own(co, cxr, cyr, cxlr, cylr)
        c_midr = swap(c_mid, 4)
        d_near, d_far = add_mid(d_near, d_midr)
        d_farr = swap(d_far, 12)
        joined = joined + swap(joined, 1)
        axlr, aylr, c_midr, d_farr, joined = tie(axlr, aylr, c_midr, d_farr, joined)
        a_near, a_mid = add_own(ao, axr, ayr, axlr, aylr)
        a_midr = swap(a_mid, 4)
        c_near, c_far = add_mid(c_near, c_midr)
        c_farr = swap(c_far, 12)
        joined = joined + swap(joined, 2)
        d_w_down_t = d_near + d_farr.astype(F32)
        a_midr, c_farr, joined = tie(a_midr, c_farr, joined)
        a_near, a_far = add_mid(a_near, a_midr)
        a_farr = swap(a_far, 12)
        joined = joined + swap(joined, 4)
        joined = joined + swap(joined, 8)
        d_w_up = c_near + c_farr.astype(F32)
        d_wa = a_near + a_farr.astype(F32)
    else:
        full = []
        for x, y, xl, yl, o in ((ax, ay, axl, ayl, ao), (cx, cy, cxl, cyl, co), (dx, dy, dxl, dyl, do)):
            blocks = [None] * BLOCKS
            for k in range(2):
                blocks[3 + NEAR[k]], blocks[1 + NEAR[k]], blocks[1 + MID[k]] = x[k], x[2 + k], xl[k]
                blocks[3 + MID[k]], blocks[2 + MID[k]], blocks[2 + NEAR[k]] = y[k], y[2 + k], yl[k]
                blocks[NEAR[k]], blocks[MID[k]] = o[k], o[2 + k]
            full.append(jnp.concatenate(blocks).astype(F32))
        joined = lax.psum(joined, "dp")
        d_wa, d_w_up, d_w_down_t = (
            lax.psum_scatter(member, "dp", scatter_dimension=0, tiled=True) for member in full
        )
    units = w_up.shape[1]
    return (
        result,
        d_tokens,
        joined[0],
        d_wa[:, :head_cols],
        joined[7, :head_cols],
        d_wa[:, head_cols : 2 * head_cols],
        d_wa[:, 2 * head_cols : 3 * head_cols],
        joined[7, head_cols : 2 * head_cols],
        d_wa[:, 3 * head_cols :].T,
        joined[3],
        joined[1],
        joined[2],
        d_w_up,
        joined[8:].reshape(-1)[:units],
        d_w_down_t.T,
        joined[6],
        joined[4],
        joined[5],
    )


def solution(mesh):
    rows, flat, both = P("dp", None), P(), P("dp", "mp")
    return jax.shard_map(
        functools.partial(per_device, mesh.shape["dp"]),
        mesh=mesh,
        in_specs=(rows, P("dp"), P("dp"), flat, both, P("mp"), both, both, P("mp"), P("mp", "dp"),
                  flat, flat, flat, both, P("mp"), P("mp", "dp"), flat, flat, flat, rows),
        out_specs=(rows, rows, flat, both, P("mp"), both, both, P("mp"), P("mp", "dp"), flat, flat,
                   flat, both, P("mp"), P("mp", "dp"), flat, flat, flat),
        check_vma=False,
    )
```

```python
import functools

import jax
import jax.numpy as jnp
from jax import lax
from jax.experimental import pallas as pl
from jax.experimental.pallas import tpu as pltpu
from jax.sharding import PartitionSpec as P

HEAD = 64
NORM_EPS = 1e-05
F32 = jnp.float32
B16 = jnp.bfloat16
MIB = 1 << 20

BLOCKS = 16
NEAR = (0, 12)
MID = (4, 8)


def swap(values, bit):
    return lax.ppermute(values, "dp", [(i, i ^ bit) for i in range(BLOCKS)])


def tie(*values):
    return lax.optimization_barrier(values)


def after(value, *earlier):
    return tie(value, *earlier)[0]


def pair_swap(partial):
    return lax.ppermute(partial, "mp", [(0, 1), (1, 0)])


def as_pieces(full):
    rows = full.shape[0] // BLOCKS
    blocks = full.reshape(BLOCKS, rows, full.shape[1])
    return [
        jnp.stack([blocks[offset + bits[0]], blocks[offset + bits[1]]])
        for offset in range(4)
        for bits in (NEAR, MID)
    ]


SMEM_SPEC = pl.BlockSpec(memory_space=pltpu.SMEM)
VMEM_SPEC = pl.BlockSpec(memory_space=pltpu.VMEM)
CHUNK = 256
UNROLL = 2
LIGHT = pl.CostEstimate(flops=1, bytes_accessed=1, transcendentals=0)


def call(body, name, shapes, operands, scratch=(), limit=16):
    return pl.pallas_call(
        body,
        in_specs=[
            SMEM_SPEC if member.dtype == jnp.int32 and member.ndim == 1 else VMEM_SPEC
            for member in operands
        ],
        out_specs=[VMEM_SPEC] * len(shapes),
        out_shape=[jax.ShapeDtypeStruct(shape, dtype) for shape, dtype in shapes],
        scratch_shapes=[pltpu.VMEM(shape, dtype) for shape, dtype in scratch],
        compiler_params=pltpu.CompilerParams(vmem_limit_bytes=limit * MIB),
        cost_estimate=LIGHT,
        name=name,
    )(*operands)


def chunks(count):
    return [slice(start, start + CHUNK) for start in range(0, count, CHUNK)]


PAIRS = [(q + bits[k], 2 * q + m, k) for q in range(4) for m, bits in enumerate((NEAR, MID)) for k in range(2)]


def fill(me, pieces, full_ref):
    rows = pieces[0].shape[1]
    for offset, piece, index in PAIRS:
        block = me ^ offset
        full_ref[pl.ds(pl.multiple_of(block * rows, rows), rows), :] = pieces[piece][index]


def dot(left, right):
    return jnp.dot(left, right, preferred_element_type=F32)


def dot_t(left, right):
    return lax.dot_general(left, right, (((1,), (1,)), ((), ())), preferred_element_type=F32)


def t_dot(left, right):
    return lax.dot_general(left, right, (((0,), (0,)), ((), ())), preferred_element_type=F32)


def row_mean(values):
    return jnp.mean(values, axis=-1, keepdims=True)


def normalize(values):
    centred = values - row_mean(values)
    inverse = lax.rsqrt(row_mean(centred * centred) + NORM_EPS)
    return centred * inverse, inverse


def col_sum(values):
    return jnp.sum(values, axis=0, keepdims=True)


def norm_back(scaled, normed, inverse):
    return inverse * (scaled - row_mean(scaled) - normed * row_mean(scaled * normed))


def two_heads(slots):
    row = lax.broadcasted_iota(jnp.int32, (2 * slots, 2 * HEAD), 0) // slots
    lane = lax.broadcasted_iota(jnp.int32, (2 * slots, 2 * HEAD), 1) // HEAD
    return (row == lane).astype(F32).astype(B16)


def doubled(values, mask):
    return jnp.concatenate([values, values], axis=0) * mask


def attend_body(slots, me_ref, len_ref, in_ref, bias_ref, *rest):
    pieces, (w_ref, qkv_ref, prob_ref, att_ref, part_ref) = rest[:-5], rest[-5:]
    count, width = att_ref.shape
    fill(me_ref[0], pieces, w_ref)
    for rows in chunks(count):
        qkv_ref[rows] = (dot(in_ref[rows], w_ref[:, : 3 * width]) + bias_ref[...]).astype(B16)
    mask = two_heads(slots)
    key_slot = lax.broadcasted_iota(jnp.int32, (slots, slots), 1)

    def chain_step(chain, carry):
        valid = key_slot < len_ref[chain]
        rows = pl.ds(pl.multiple_of(chain * slots, slots), slots)
        for pair in range(width // (2 * HEAD)):
            lanes = 2 * HEAD * pair
            query = qkv_ref[rows, lanes : lanes + 2 * HEAD]
            key = qkv_ref[rows, width + lanes : width + lanes + 2 * HEAD]
            value = qkv_ref[rows, 2 * width + lanes : 2 * width + lanes + 2 * HEAD]
            scores = dot_t(query * (HEAD**-0.5), doubled(key, mask))
            probs = []
            for head in range(2):
                part = jnp.where(valid, scores[:, head * slots : (head + 1) * slots], -1e30)
                terms = jnp.exp(part - jnp.max(part, axis=-1, keepdims=True))
                probs.append((terms / jnp.sum(terms, axis=-1, keepdims=True)).astype(B16))
            prob = jnp.concatenate(probs, axis=1)
            prob_ref[rows, 2 * slots * pair : 2 * slots * (pair + 1)] = prob
            att_ref[rows, lanes : lanes + 2 * HEAD] = dot(prob, doubled(value, mask)).astype(B16)
        return carry

    lax.fori_loop(0, count // slots, chain_step, 0, unroll=UNROLL)
    for rows in chunks(count):
        part_ref[rows] = dot_t(att_ref[rows], w_ref[:, 3 * width :]).astype(B16)


def attend(me, lengths, in_low, bias, pieces):
    count, width = in_low.shape
    heads = bias.shape[1] // 3
    slots = count // lengths.shape[0]
    shapes = [
        ((width, 4 * heads), B16),
        ((count, 3 * heads), B16),
        ((count, heads // HEAD * slots), B16),
        ((count, heads), B16),
        ((count, width), B16),
    ]
    body = functools.partial(attend_body, slots)
    return call(body, "attend", shapes, [me, lengths, in_low, bias, *pieces])


def up_body(me_ref, in_ref, own_ref, other_ref, vec_ref, bias_ref, *rest):
    pieces, (w_ref, normed_ref, inverse_ref, low_ref, act_ref, slope_ref) = rest[:-6], rest[-6:]
    fill(me_ref[0], pieces, w_ref)
    vectors = vec_ref[...]
    for rows in chunks(in_ref.shape[0]):
        attn = own_ref[rows].astype(F32) + other_ref[rows].astype(F32) + vectors[0:1]
        normed, inverse = normalize(in_ref[rows].astype(F32) + attn)
        normed_ref[rows] = normed
        inverse_ref[rows] = jnp.broadcast_to(inverse, (CHUNK, inverse_ref.shape[1]))
        low_ref[rows] = (normed * vectors[1:2] + vectors[2:3]).astype(B16)
        pre = dot(low_ref[rows], w_ref[...]) + bias_ref[...]
        cdf = 0.5 + 0.5 * lax.erf(pre * (2.0**-0.5))
        act_ref[rows] = (pre * cdf).astype(B16)
        density = jnp.exp(pre * pre * -0.5) * 0.3989422804014327
        slope_ref[rows] = (cdf + pre * density).astype(B16)


def up(me, in_low, own, other, vectors, bias, pieces):
    count, width = in_low.shape
    units = bias.shape[1]
    shapes = [
        ((width, units), B16),
        ((count, width), F32),
        ((count, 128), F32),
        ((count, width), B16),
        ((count, units), B16),
        ((count, units), B16),
    ]
    return call(up_body, "up", shapes, [me, in_low, own, other, vectors, bias, *pieces])


def down_body(me_ref, act_ref, *rest):
    pieces, (w_ref, part_ref) = rest[:-2], rest[-2:]
    fill(me_ref[0], pieces, w_ref)
    for rows in chunks(act_ref.shape[0]):
        part_ref[rows] = dot_t(act_ref[rows], w_ref[...]).astype(B16)


def down(me, act, pieces):
    count, units = act.shape
    width = BLOCKS * pieces[0].shape[1]
    shapes = [((width, units), B16), ((count, width), B16)]
    return call(down_body, "down", shapes, [me, act, *pieces])


def second_norm_body(normed_ref, own_ref, other_ref, grad_ref, vec_ref, out_ref, dz_ref, low_ref, sum_ref):
    vectors = vec_ref[...]
    sum_ref[...] = jnp.zeros_like(sum_ref)
    for rows in chunks(own_ref.shape[0]):
        hidden = normed_ref[rows] * vectors[0:1] + vectors[1:2]
        ffn = own_ref[rows].astype(F32) + other_ref[rows].astype(F32) + vectors[2:3]
        normed, inverse = normalize(hidden + ffn)
        out_ref[rows] = (normed * vectors[3:4] + vectors[4:5]).astype(B16)
        grad = grad_ref[rows].astype(F32)
        dz = norm_back(grad * vectors[3:4], normed, inverse)
        dz_ref[rows] = dz
        low_ref[rows] = dz.astype(B16)
        sum_ref[0:1] += col_sum(grad * normed)
        sum_ref[1:2] += col_sum(grad)
        sum_ref[2:3] += col_sum(dz)


def second_norm(normed, own, other, grad, vectors):
    shape = own.shape
    shapes = [(shape, B16), (shape, F32), (shape, B16), ((8, shape[1]), F32)]
    return call(second_norm_body, "second_norm", shapes, [normed, own, other, grad, vectors])


ORDER = (
    (3, 15, 1, 13),
    (7, 11, 6, 10),
    (5, 9),
    (2, 14),
    (0, 12, 4, 8),
)


def weight_grad(me, lefts, rights):
    count, width = lefts[0].shape
    tile = 384 if all(right.shape[1] % 384 == 0 for right in rights) else 128
    total = sum(right.shape[1] for right in rights)
    rows = width // BLOCKS
    n = len(lefts)

    def body(me_ref, *refs):
        outs, (turned_ref, full_ref) = refs[2 * n : -2], refs[-2:]
        at = 0
        for left_ref, right_ref in zip(refs[:n], refs[n : 2 * n]):
            turned_ref[...] = left_ref[...].T
            for start in range(0, right_ref.shape[1], tile):
                full_ref[...] = dot(turned_ref[...], right_ref[:, start : start + tile]).astype(B16)
                for out_ref, offsets in zip(outs, ORDER):
                    for k, offset in enumerate(offsets):
                        place = pl.multiple_of((me_ref[0] ^ offset) * rows, rows)
                        out_ref[k, :, at : at + tile] = full_ref[pl.ds(place, rows), :]
                at += tile

    shapes = [((len(offsets), rows, total), B16) for offsets in ORDER]
    scratch = [((width, count), B16), ((width, tile), B16)]
    return call(body, "weight_grad", shapes, [me, *lefts, *rights], scratch)


def hidden_back_body(low_ref, slope_ref, down_ref, up_ref, pre_ref, part_ref, sum_ref):
    sum_ref[...] = jnp.zeros_like(sum_ref)
    for rows in chunks(low_ref.shape[0]):
        d_pre = dot(low_ref[rows], down_ref[...]) * slope_ref[rows].astype(F32)
        sum_ref[0:1] += col_sum(d_pre)
        pre_ref[rows] = d_pre.astype(B16)
        part_ref[rows] = dot_t(pre_ref[rows], up_ref[...]).astype(B16)


def hidden_back(dz_low, slope, w_down_t, w_up):
    count, width = dz_low.shape
    units = slope.shape[1]
    shapes = [((count, units), B16), ((count, width), B16), ((8, units), F32)]
    return call(hidden_back_body, "hidden_back", shapes, [dz_low, slope, w_down_t, w_up])


def attend_back_body(slots, dz_ref, own_ref, other_ref, normed_ref, inverse_ref, gain_ref,
                     qkv_ref, prob_ref, w_ref, dz_one_ref, low_ref, d_qkv_ref, part_ref, sum_ref,
                     sum_qkv_ref, d_att_ref):
    count, width = d_att_ref.shape
    sum_ref[...] = jnp.zeros_like(sum_ref)
    sum_qkv_ref[...] = jnp.zeros_like(sum_qkv_ref)
    for rows in chunks(count):
        normed = normed_ref[rows]
        d_hidden = dz_ref[rows] + (own_ref[rows].astype(F32) + other_ref[rows].astype(F32))
        dz_one = norm_back(d_hidden * gain_ref[...], normed, inverse_ref[rows, 0:1])
        dz_one_ref[rows] = dz_one
        low_ref[rows] = dz_one.astype(B16)
        sum_ref[0:1] += col_sum(d_hidden * normed)
        sum_ref[1:2] += col_sum(d_hidden)
        sum_ref[2:3] += col_sum(dz_one)
        d_att_ref[rows] = dot(low_ref[rows], w_ref[:, 3 * width :]).astype(B16)
    mask = two_heads(slots)

    def chain_step(chain, carry):
        rows = pl.ds(pl.multiple_of(chain * slots, slots), slots)
        for pair in range(width // (2 * HEAD)):
            lanes = 2 * HEAD * pair
            query = qkv_ref[rows, lanes : lanes + 2 * HEAD]
            key = qkv_ref[rows, width + lanes : width + lanes + 2 * HEAD]
            value = qkv_ref[rows, 2 * width + lanes : 2 * width + lanes + 2 * HEAD]
            d_att = d_att_ref[rows, lanes : lanes + 2 * HEAD]
            prob = prob_ref[rows, 2 * slots * pair : 2 * slots * (pair + 1)]
            d_prob = dot_t(d_att, doubled(value, mask))
            weights = prob.astype(F32)
            products = weights * d_prob
            lows = []
            for head in range(2):
                half = slice(head * slots, (head + 1) * slots)
                total = jnp.sum(products[:, half], axis=-1, keepdims=True)
                lows.append((products[:, half] - weights[:, half] * total).astype(B16))
            low = jnp.concatenate(lows, axis=1)
            d_query = dot(low, doubled(key, mask)) * (HEAD**-0.5)
            tall = jnp.concatenate(lows, axis=0)
            d_key = t_dot(tall, doubled(query, mask)) * (HEAD**-0.5)
            tall = jnp.concatenate([prob[:, :slots], prob[:, slots:]], axis=0)
            d_value = t_dot(tall, doubled(d_att, mask))
            d_qkv_ref[rows, lanes : lanes + 2 * HEAD] = d_query.astype(B16)
            d_qkv_ref[rows, width + lanes : width + lanes + 2 * HEAD] = d_key.astype(B16)
            d_qkv_ref[rows, 2 * width + lanes : 2 * width + lanes + 2 * HEAD] = d_value.astype(B16)
        return carry

    lax.fori_loop(0, count // slots, chain_step, 0, unroll=UNROLL)
    for rows in chunks(count):
        sum_qkv_ref[0:1] += col_sum(d_qkv_ref[rows].astype(F32))
        part_ref[rows] = dot_t(d_qkv_ref[rows], w_ref[:, : 3 * width]).astype(B16)


def attend_back(chain_count, dz_two, own, other, normed, inverse, gain, qkv, prob, w_a):
    shape = dz_two.shape
    heads = qkv.shape[1] // 3
    shapes = [
        (shape, F32),
        (shape, B16),
        (qkv.shape, B16),
        (shape, B16),
        ((8, shape[1]), F32),
        ((8, 3 * heads), F32),
    ]
    operands = [dz_two, own, other, normed, inverse, gain, qkv, prob, w_a]
    body = functools.partial(attend_back_body, shape[0] // chain_count)
    return call(body, "attend_back", shapes, operands, [((shape[0], heads), B16)])


def last_body(dz_ref, own_ref, other_ref, flag_ref, one_ref, two_ref, up_ref, qkv_ref, out_ref, sum_ref):
    width = dz_ref.shape[1]
    heads = qkv_ref.shape[1] // 3
    sum_ref[...] = jnp.zeros_like(sum_ref)
    sum_ref[1:4] = one_ref[0:3]
    sum_ref[4:7] = two_ref[0:3]
    sum_ref[7:8, :heads] = qkv_ref[0:1, :heads]
    sum_ref[7:8, heads : 2 * heads] = qkv_ref[0:1, 2 * heads :]
    for k in range(up_ref.shape[1] // width):
        sum_ref[8 + k : 9 + k] = up_ref[0:1, k * width : (k + 1) * width]
    for rows in chunks(dz_ref.shape[0]):
        total = dz_ref[rows] + (own_ref[rows].astype(F32) + other_ref[rows].astype(F32))
        masked = total * flag_ref[rows, 0:1]
        sum_ref[0:1] += col_sum(masked)
        out_ref[rows] = total - masked


def last(dz_one, own, other, flag, sums_one, sums_two, sums_up, sums_qkv):
    width = dz_one.shape[1]
    joined = (8 + 8 * pl.cdiv(sums_up.shape[1], 8 * width), width)
    operands = [dz_one, own, other, flag, sums_one, sums_two, sums_up, sums_qkv]
    return call(last_body, "last", [(dz_one.shape, F32), (joined, F32)], operands)


def add_late_body(x_ref, y_ref, from_x_ref, from_y_ref, out_x_ref, out_y_ref):
    out_x_ref[...] = (x_ref[...].astype(F32) + from_y_ref[:2].astype(F32)).astype(B16)
    out_y_ref[...] = (y_ref[...].astype(F32) + from_x_ref[:2].astype(F32)).astype(B16)


def add_own_body(own_ref, from_x_ref, from_y_ref, late_x_ref, late_y_ref, near_ref, mid_ref):
    near_ref[...] = (
        own_ref[:2].astype(F32) + from_x_ref[2:].astype(F32) + late_y_ref[...].astype(F32)
    )
    mid_ref[...] = (
        own_ref[2:].astype(F32) + late_x_ref[...].astype(F32) + from_y_ref[2:].astype(F32)
    ).astype(B16)


def add_mid_body(near_ref, mid_ref, own_ref, far_ref):
    own_ref[...] = near_ref[0] + mid_ref[0].astype(F32)
    far_ref[...] = (near_ref[1] + mid_ref[1].astype(F32)).astype(B16)


def add_late(late_x, late_y, from_x, from_y):
    shape = (late_x.shape, B16)
    return call(add_late_body, "add_late", [shape, shape], [late_x, late_y, from_x, from_y], limit=8)


def add_own(own, from_x, from_y, late_x, late_y):
    shapes = [(late_x.shape, F32), (late_x.shape, B16)]
    return call(add_own_body, "add_own", shapes, [own, from_x, from_y, late_x, late_y], limit=8)


def add_mid(near, mid):
    shapes = [(near.shape[1:], F32), (near.shape[1:], B16)]
    return call(add_mid_body, "add_mid", shapes, [near, mid], limit=8)


def per_device(dp_size, tokens, masked, lengths, mask_vector, w_query, b_query, w_key, w_value,
               b_value, w_out, b_out, gain_one, shift_one, w_up, b_up, w_down, b_down, gain_two,
               shift_two, grad_out):
    head_cols = w_query.shape[1]
    width = tokens.shape[1]
    fast = dp_size == BLOCKS and w_query.shape[0] % 16 == 0
    me = lax.axis_index("dp").astype(jnp.int32).reshape(1)
    if not fast:
        me = jnp.zeros_like(me)

    (b_query, b_value, b_out, gain_one, shift_one, b_up, b_down, gain_two, shift_two) = (
        member.astype(F32)
        for member in (b_query, b_value, b_out, gain_one, shift_one, b_up, b_down, gain_two, shift_two)
    )
    is_masked = (masked == 1)[:, None]
    flag = jnp.broadcast_to(is_masked, (masked.shape[0], 128)).astype(F32)
    in_low = jnp.where(is_masked, mask_vector[None, :], tokens)
    bias_qkv = jnp.concatenate([b_query, jnp.zeros_like(b_query), b_value])[None, :]
    vectors_one = jnp.stack([b_out, gain_one, shift_one])
    vectors_two = jnp.stack([gain_one, shift_one, b_down, gain_two, shift_two])
    b_up, gain_one = b_up[None, :], gain_one[None, :]

    a = jnp.concatenate([w_query, w_key, w_value, w_out.T], axis=1)
    c = w_up
    d = w_down.T
    if fast:
        az = swap(a, 12)
        az, me, flag, in_low, bias_qkv, vectors_one, vectors_two, b_up, gain_one = tie(
            az, me, flag, in_low, bias_qkv, vectors_one, vectors_two, b_up, gain_one
        )
        an = jnp.stack([a, az])
        anx, any_, am = swap(an, 1), swap(an, 2), swap(an, 4)
        anx, any_, am, an, c = tie(anx, any_, am, an, c)
        amx, amy, cz = swap(am, 1), swap(am, 2), swap(c, 12)
        amx, amy, cz, anx, c, d = tie(amx, amy, cz, anx, c, d)
        cn = jnp.stack([c, cz])
        amd, and_, cm = swap(amy, 1), swap(anx, 2), swap(cn, 4)
        cnx, cny, dz = swap(cn, 1), swap(cn, 2), swap(d, 12)
        amd, and_, cm, cnx, cny, dz, d = tie(amd, and_, cm, cnx, cny, dz, d)
        dn = jnp.stack([d, dz])
        pieces_a = [an, am, anx, amx, any_, amy, and_, amd]
        cmx, cnd, dm = swap(cm, 1), swap(cnx, 2), swap(dn, 4)
        dnx, dny = swap(dn, 1), swap(dn, 2)
    else:
        a, c, d = (lax.all_gather(piece, "dp", axis=0, tiled=True) for piece in (a, c, d))
        pieces_a, pieces_c, pieces_d = as_pieces(a), as_pieces(c), as_pieces(d)
    w_a, qkv, prob, attended, part = attend(me, lengths, in_low, bias_qkv, pieces_a)
    if fast:
        cmx, cnd, dm, dnx, dny, cm, part = tie(cmx, cnd, dm, dnx, dny, cm, part)
        cmy, dnd, cmd = swap(cm, 2), swap(dny, 1), swap(cnd, 4)
    other = pair_swap(part)
    if fast:
        cmy, dnd, cmd, dm, other, part = tie(cmy, dnd, cmd, dm, other, part)
        pieces_c = [cn, cm, cnx, cmx, cny, cmy, cnd, cmd]
        dmx, dmy, dmd = swap(dm, 1), swap(dm, 2), swap(dnd, 4)
    w_u, normed_one, inverse_one, hidden_low, act_low, slope = up(
        me, in_low, part, other, vectors_one, b_up, pieces_c
    )
    if fast:
        dmx, dmy, dmd, act_low = tie(dmx, dmy, dmd, act_low)
        pieces_d = [dn, dm, dnx, dmx, dny, dmy, dnd, dmd]
    w_d, part = down(me, act_low, pieces_d)
    other = pair_swap(part)
    result, dz_two, dz_two_low, sums_two = second_norm(normed_one, part, other, grad_out, vectors_two)
    dx, dy, dxl, dyl, do = weight_grad(me, [dz_two_low], [act_low])
    if fast:
        dx, dy, dxl, dyl, dz_two_low = tie(dx, dy, dxl, dyl, dz_two_low)
        dxr, dyr = swap(dx, 1), swap(dy, 2)
    d_pre_low, part, sums_up = hidden_back(dz_two_low, slope, w_d, w_u)
    cx, cy, cxl, cyl, co = weight_grad(me, [hidden_low], [d_pre_low])
    if fast:
        dxr, dyr, part, cx, cy = tie(dxr, dyr, part, cx, cy)
        cxr, cyr = swap(cx, 1), swap(cy, 2)
        dxl, dyl = add_late(dxl, dyl, dxr, dyr)
        dxlr, dylr = swap(dxl, 1), swap(dyl, 2)
    other = pair_swap(part)
    dz_one, dz_one_low, d_qkv, part, sums_one, sums_qkv = attend_back(
        lengths.shape[0], dz_two, part, other, normed_one, inverse_one, gain_one, qkv, prob, w_a
    )
    if fast:
        cxr, cyr, dxlr, dylr, part, d_qkv, dz_one_low = tie(cxr, cyr, dxlr, dylr, part, d_qkv, dz_one_low)
        cxl, cyl = add_late(cxl, cyl, cxr, cyr)
        cxlr, cylr = swap(cxl, 1), swap(cyl, 2)
        d_near, d_mid = add_own(do, dxr, dyr, dxlr, dylr)
        d_midr = swap(d_mid, 4)
    ax, ay, axl, ayl, ao = weight_grad(me, [in_low, dz_one_low], [d_qkv, attended])
    if fast:
        cxlr, cylr, d_midr, ax, ay, part = tie(cxlr, cylr, d_midr, ax, ay, part)
        axr, ayr = swap(ax, 1), swap(ay, 2)
        c_near, c_mid = add_own(co, cxr, cyr, cxlr, cylr)
        d_near, d_far = add_mid(d_near, d_midr)
        c_midr, d_farr = swap(c_mid, 4), swap(d_far, 12)
    other = pair_swap(part)
    d_tokens, joined = last(dz_one, part, other, flag, sums_one, sums_two, sums_up, sums_qkv)
    if fast:
        from_x = swap(joined, 1)
        axr, ayr, c_midr, d_farr, from_x = tie(axr, ayr, c_midr, d_farr, from_x)
        axl, ayl = add_late(axl, ayl, axr, ayr)
        axlr, aylr = swap(axl, 1), swap(ayl, 2)
        c_near, c_far = add_mid(c_near, c_midr)
        c_farr = swap(c_far, 12)
        joined = joined + from_x
        from_y = swap(joined, 2)
        axlr, aylr, c_farr, from_y = tie(axlr, aylr, c_farr, from_y)
        a_near, a_mid = add_own(ao, axr, ayr, axlr, aylr)
        a_midr = swap(a_mid, 4)
        joined = joined + from_y
        from_z = swap(joined, 4)
        a_midr, from_z = tie(a_midr, from_z)
        a_near, a_far = add_mid(a_near, a_midr)
        a_farr = swap(a_far, 12)
        joined = joined + from_z
        joined = joined + swap(joined, 8)
        d_w_down_t = d_near + d_farr.astype(F32)
        d_w_up = c_near + c_farr.astype(F32)
        d_wa = a_near + a_farr.astype(F32)
    else:
        full = []
        for parts in ((ax, ay, axl, ayl, ao), (cx, cy, cxl, cyl, co), (dx, dy, dxl, dyl, do)):
            blocks = [None] * BLOCKS
            for member, offsets in zip(parts, ORDER):
                for k, offset in enumerate(offsets):
                    blocks[offset] = member[k]
            full.append(jnp.concatenate(blocks).astype(F32))
        joined = lax.psum(joined, "dp")
        d_wa, d_w_up, d_w_down_t = (
            lax.psum_scatter(member, "dp", scatter_dimension=0, tiled=True) for member in full
        )
    units = w_up.shape[1]
    return (
        result,
        d_tokens,
        joined[0],
        d_wa[:, :head_cols],
        joined[7, :head_cols],
        d_wa[:, head_cols : 2 * head_cols],
        d_wa[:, 2 * head_cols : 3 * head_cols],
        joined[7, head_cols : 2 * head_cols],
        d_wa[:, 3 * head_cols :].T,
        joined[3],
        joined[1],
        joined[2],
        d_w_up,
        joined[8:].reshape(-1)[:units],
        d_w_down_t.T,
        joined[6],
        joined[4],
        joined[5],
    )


def solution(mesh):
    rows, flat, both = P("dp", None), P(), P("dp", "mp")
    return jax.shard_map(
        functools.partial(per_device, mesh.shape["dp"]),
        mesh=mesh,
        in_specs=(rows, P("dp"), P("dp"), flat, both, P("mp"), both, both, P("mp"), P("mp", "dp"),
                  flat, flat, flat, both, P("mp"), P("mp", "dp"), flat, flat, flat, rows),
        out_specs=(rows, rows, flat, both, P("mp"), both, both, P("mp"), P("mp", "dp"), flat, flat,
                   flat, both, P("mp"), P("mp", "dp"), flat, flat, flat),
        check_vma=False,
    )
```

```python
import functools

import jax
import jax.numpy as jnp
from jax import lax
from jax.experimental import pallas as pl
from jax.experimental.pallas import tpu as pltpu
from jax.sharding import PartitionSpec as P

HEAD = 64
NORM_EPS = 1e-05
F32 = jnp.float32
B16 = jnp.bfloat16
MIB = 1 << 20

BLOCKS = 16
NEAR = (0, 12)
MID = (4, 8)


def swap(values, bit):
    return lax.ppermute(values, "dp", [(i, i ^ bit) for i in range(BLOCKS)])


def tie(*values):
    return lax.optimization_barrier(values)


def after(value, *earlier):
    return tie(value, *earlier)[0]


def pair_swap(partial):
    return lax.ppermute(partial, "mp", [(0, 1), (1, 0)])


def as_pieces(full):
    rows = full.shape[0] // BLOCKS
    blocks = full.reshape(BLOCKS, rows, full.shape[1])
    return [
        jnp.stack([blocks[offset + bits[0]], blocks[offset + bits[1]]])
        for offset in range(4)
        for bits in (NEAR, MID)
    ]


SMEM_SPEC = pl.BlockSpec(memory_space=pltpu.SMEM)
VMEM_SPEC = pl.BlockSpec(memory_space=pltpu.VMEM)
CHUNK = 256
UNROLL = 2
LIGHT = pl.CostEstimate(flops=1, bytes_accessed=1, transcendentals=0)


def call(body, name, shapes, operands, scratch=(), limit=16):
    return pl.pallas_call(
        body,
        in_specs=[
            SMEM_SPEC if member.dtype == jnp.int32 and member.ndim == 1 else VMEM_SPEC
            for member in operands
        ],
        out_specs=[VMEM_SPEC] * len(shapes),
        out_shape=[jax.ShapeDtypeStruct(shape, dtype) for shape, dtype in shapes],
        scratch_shapes=[pltpu.VMEM(shape, dtype) for shape, dtype in scratch],
        compiler_params=pltpu.CompilerParams(vmem_limit_bytes=limit * MIB),
        cost_estimate=LIGHT,
        name=name,
    )(*operands)


def chunks(count):
    return [slice(start, start + CHUNK) for start in range(0, count, CHUNK)]


PAIRS = [(q + bits[k], 2 * q + m, k) for q in range(4) for m, bits in enumerate((NEAR, MID)) for k in range(2)]


def fill(me, pieces, full_ref):
    rows = pieces[0].shape[1]
    for offset, piece, index in PAIRS:
        block = me ^ offset
        full_ref[pl.ds(pl.multiple_of(block * rows, rows), rows), :] = pieces[piece][index]


def dot(left, right):
    return jnp.dot(left, right, preferred_element_type=F32)


def dot_t(left, right):
    return lax.dot_general(left, right, (((1,), (1,)), ((), ())), preferred_element_type=F32)


def t_dot(left, right):
    return lax.dot_general(left, right, (((0,), (0,)), ((), ())), preferred_element_type=F32)


def row_mean(values):
    return jnp.mean(values, axis=-1, keepdims=True)


def normalize(values):
    centred = values - row_mean(values)
    inverse = lax.rsqrt(row_mean(centred * centred) + NORM_EPS)
    return centred * inverse, inverse


def col_sum(values):
    return jnp.sum(values, axis=0, keepdims=True)


def norm_back(scaled, normed, inverse):
    return inverse * (scaled - row_mean(scaled) - normed * row_mean(scaled * normed))


def two_heads(slots):
    row = lax.broadcasted_iota(jnp.int32, (2 * slots, 2 * HEAD), 0) // slots
    lane = lax.broadcasted_iota(jnp.int32, (2 * slots, 2 * HEAD), 1) // HEAD
    return (row == lane).astype(F32).astype(B16)


def doubled(values, mask):
    return jnp.concatenate([values, values], axis=0) * mask


def attend_body(slots, me_ref, len_ref, in_ref, bias_ref, *rest):
    pieces, (w_ref, qkv_ref, prob_ref, att_ref, part_ref) = rest[:-5], rest[-5:]
    count, width = att_ref.shape
    fill(me_ref[0], pieces, w_ref)
    for rows in chunks(count):
        qkv_ref[rows] = (dot(in_ref[rows], w_ref[:, : 3 * width]) + bias_ref[...]).astype(B16)
    mask = two_heads(slots)
    key_slot = lax.broadcasted_iota(jnp.int32, (slots, slots), 1)

    def chain_step(chain, carry):
        valid = key_slot < len_ref[chain]
        rows = pl.ds(pl.multiple_of(chain * slots, slots), slots)
        for pair in range(width // (2 * HEAD)):
            lanes = 2 * HEAD * pair
            query = qkv_ref[rows, lanes : lanes + 2 * HEAD]
            key = qkv_ref[rows, width + lanes : width + lanes + 2 * HEAD]
            value = qkv_ref[rows, 2 * width + lanes : 2 * width + lanes + 2 * HEAD]
            scores = dot_t(query * (HEAD**-0.5), doubled(key, mask))
            probs = []
            for head in range(2):
                part = jnp.where(valid, scores[:, head * slots : (head + 1) * slots], -1e30)
                terms = jnp.exp(part - jnp.max(part, axis=-1, keepdims=True))
                probs.append((terms / jnp.sum(terms, axis=-1, keepdims=True)).astype(B16))
            prob = jnp.concatenate(probs, axis=1)
            prob_ref[rows, 2 * slots * pair : 2 * slots * (pair + 1)] = prob
            att_ref[rows, lanes : lanes + 2 * HEAD] = dot(prob, doubled(value, mask)).astype(B16)
        return carry

    lax.fori_loop(0, count // slots, chain_step, 0, unroll=UNROLL)
    for rows in chunks(count):
        part_ref[rows] = dot_t(att_ref[rows], w_ref[:, 3 * width :]).astype(B16)


def attend(me, lengths, in_low, bias, pieces):
    count, width = in_low.shape
    heads = bias.shape[1] // 3
    slots = count // lengths.shape[0]
    shapes = [
        ((width, 4 * heads), B16),
        ((count, 3 * heads), B16),
        ((count, heads // HEAD * slots), B16),
        ((count, heads), B16),
        ((count, width), B16),
    ]
    body = functools.partial(attend_body, slots)
    return call(body, "attend", shapes, [me, lengths, in_low, bias, *pieces])


def up_body(me_ref, in_ref, own_ref, other_ref, vec_ref, bias_ref, *rest):
    pieces, (w_ref, normed_ref, inverse_ref, low_ref, act_ref, slope_ref) = rest[:-6], rest[-6:]
    fill(me_ref[0], pieces, w_ref)
    vectors = vec_ref[...]
    for rows in chunks(in_ref.shape[0]):
        attn = own_ref[rows].astype(F32) + other_ref[rows].astype(F32) + vectors[0:1]
        normed, inverse = normalize(in_ref[rows].astype(F32) + attn)
        normed_ref[rows] = normed
        inverse_ref[rows] = jnp.broadcast_to(inverse, (CHUNK, inverse_ref.shape[1]))
        low_ref[rows] = (normed * vectors[1:2] + vectors[2:3]).astype(B16)
        pre = dot(low_ref[rows], w_ref[...]) + bias_ref[...]
        cdf = 0.5 + 0.5 * lax.erf(pre * (2.0**-0.5))
        act_ref[rows] = (pre * cdf).astype(B16)
        density = jnp.exp(pre * pre * -0.5) * 0.3989422804014327
        slope_ref[rows] = (cdf + pre * density).astype(B16)


def up(me, in_low, own, other, vectors, bias, pieces):
    count, width = in_low.shape
    units = bias.shape[1]
    shapes = [
        ((width, units), B16),
        ((count, width), F32),
        ((count, 128), F32),
        ((count, width), B16),
        ((count, units), B16),
        ((count, units), B16),
    ]
    return call(up_body, "up", shapes, [me, in_low, own, other, vectors, bias, *pieces])


def down_body(me_ref, act_ref, *rest):
    pieces, (w_ref, part_ref) = rest[:-2], rest[-2:]
    fill(me_ref[0], pieces, w_ref)
    for rows in chunks(act_ref.shape[0]):
        part_ref[rows] = dot_t(act_ref[rows], w_ref[...]).astype(B16)


def down(me, act, pieces):
    count, units = act.shape
    width = BLOCKS * pieces[0].shape[1]
    shapes = [((width, units), B16), ((count, width), B16)]
    return call(down_body, "down", shapes, [me, act, *pieces])


def second_norm_body(normed_ref, own_ref, other_ref, grad_ref, vec_ref, out_ref, dz_ref, low_ref, sum_ref):
    vectors = vec_ref[...]
    sum_ref[...] = jnp.zeros_like(sum_ref)
    for rows in chunks(own_ref.shape[0]):
        hidden = normed_ref[rows] * vectors[0:1] + vectors[1:2]
        ffn = own_ref[rows].astype(F32) + other_ref[rows].astype(F32) + vectors[2:3]
        normed, inverse = normalize(hidden + ffn)
        out_ref[rows] = (normed * vectors[3:4] + vectors[4:5]).astype(B16)
        grad = grad_ref[rows].astype(F32)
        dz = norm_back(grad * vectors[3:4], normed, inverse)
        dz_ref[rows] = dz
        low_ref[rows] = dz.astype(B16)
        sum_ref[0:1] += col_sum(grad * normed)
        sum_ref[1:2] += col_sum(grad)
        sum_ref[2:3] += col_sum(dz)


def second_norm(normed, own, other, grad, vectors):
    shape = own.shape
    shapes = [(shape, B16), (shape, F32), (shape, B16), ((8, shape[1]), F32)]
    return call(second_norm_body, "second_norm", shapes, [normed, own, other, grad, vectors])


ORDER = (
    (3, 15, 1, 13),
    (7, 11, 6, 10),
    (5, 9),
    (2, 14),
    (0, 12, 4, 8),
)


def weight_grad(me, lefts, rights):
    count, width = lefts[0].shape
    tile = 384 if all(right.shape[1] % 384 == 0 for right in rights) else 128
    total = sum(right.shape[1] for right in rights)
    rows = width // BLOCKS
    n = len(lefts)

    def body(me_ref, *refs):
        outs, (turned_ref, full_ref) = refs[2 * n : -2], refs[-2:]
        at = 0
        for left_ref, right_ref in zip(refs[:n], refs[n : 2 * n]):
            turned_ref[...] = left_ref[...].T
            for start in range(0, right_ref.shape[1], tile):
                full_ref[...] = dot(turned_ref[...], right_ref[:, start : start + tile]).astype(B16)
                for out_ref, offsets in zip(outs, ORDER):
                    for k, offset in enumerate(offsets):
                        place = pl.multiple_of((me_ref[0] ^ offset) * rows, rows)
                        out_ref[k, :, at : at + tile] = full_ref[pl.ds(place, rows), :]
                at += tile

    shapes = [((len(offsets), rows, total), B16) for offsets in ORDER]
    scratch = [((width, count), B16), ((width, tile), B16)]
    return call(body, "weight_grad", shapes, [me, *lefts, *rights], scratch)


def hidden_back_body(low_ref, slope_ref, down_ref, up_ref, pre_ref, part_ref, sum_ref):
    sum_ref[...] = jnp.zeros_like(sum_ref)
    for rows in chunks(low_ref.shape[0]):
        d_pre = dot(low_ref[rows], down_ref[...]) * slope_ref[rows].astype(F32)
        sum_ref[0:1] += col_sum(d_pre)
        pre_ref[rows] = d_pre.astype(B16)
        part_ref[rows] = dot_t(pre_ref[rows], up_ref[...]).astype(B16)


def hidden_back(dz_low, slope, w_down_t, w_up):
    count, width = dz_low.shape
    units = slope.shape[1]
    shapes = [((count, units), B16), ((count, width), B16), ((8, units), F32)]
    return call(hidden_back_body, "hidden_back", shapes, [dz_low, slope, w_down_t, w_up])


def attend_back_body(slots, dz_ref, own_ref, other_ref, normed_ref, inverse_ref, gain_ref,
                     flag_ref, qkv_ref, prob_ref, w_ref, dz_one_ref, low_ref, d_qkv_ref, part_ref, sum_ref,
                     sum_qkv_ref, d_att_ref):
    count, width = d_att_ref.shape
    sum_ref[...] = jnp.zeros_like(sum_ref)
    sum_qkv_ref[...] = jnp.zeros_like(sum_qkv_ref)
    for rows in chunks(count):
        normed = normed_ref[rows]
        d_hidden = dz_ref[rows] + (own_ref[rows].astype(F32) + other_ref[rows].astype(F32))
        dz_one = norm_back(d_hidden * gain_ref[...], normed, inverse_ref[rows, 0:1])
        dz_one_ref[rows] = dz_one
        low_ref[rows] = dz_one.astype(B16)
        sum_ref[0:1] += col_sum(d_hidden * normed)
        sum_ref[1:2] += col_sum(d_hidden)
        sum_ref[2:3] += col_sum(dz_one)
        sum_ref[3:4] += col_sum(dz_one * flag_ref[rows, 0:1])
        d_att_ref[rows] = dot(low_ref[rows], w_ref[:, 3 * width :]).astype(B16)
    mask = two_heads(slots)

    def chain_step(chain, carry):
        rows = pl.ds(pl.multiple_of(chain * slots, slots), slots)
        for pair in range(width // (2 * HEAD)):
            lanes = 2 * HEAD * pair
            query = qkv_ref[rows, lanes : lanes + 2 * HEAD]
            key = qkv_ref[rows, width + lanes : width + lanes + 2 * HEAD]
            value = qkv_ref[rows, 2 * width + lanes : 2 * width + lanes + 2 * HEAD]
            d_att = d_att_ref[rows, lanes : lanes + 2 * HEAD]
            prob = prob_ref[rows, 2 * slots * pair : 2 * slots * (pair + 1)]
            d_prob = dot_t(d_att, doubled(value, mask))
            weights = prob.astype(F32)
            products = weights * d_prob
            lows = []
            for head in range(2):
                half = slice(head * slots, (head + 1) * slots)
                total = jnp.sum(products[:, half], axis=-1, keepdims=True)
                lows.append((products[:, half] - weights[:, half] * total).astype(B16))
            low = jnp.concatenate(lows, axis=1)
            d_query = dot(low, doubled(key, mask)) * (HEAD**-0.5)
            tall = jnp.concatenate(lows, axis=0)
            d_key = t_dot(tall, doubled(query, mask)) * (HEAD**-0.5)
            tall = jnp.concatenate([prob[:, :slots], prob[:, slots:]], axis=0)
            d_value = t_dot(tall, doubled(d_att, mask))
            d_qkv_ref[rows, lanes : lanes + 2 * HEAD] = d_query.astype(B16)
            d_qkv_ref[rows, width + lanes : width + lanes + 2 * HEAD] = d_key.astype(B16)
            d_qkv_ref[rows, 2 * width + lanes : 2 * width + lanes + 2 * HEAD] = d_value.astype(B16)
        return carry

    lax.fori_loop(0, count // slots, chain_step, 0, unroll=UNROLL)
    for rows in chunks(count):
        sum_qkv_ref[0:1] += col_sum(d_qkv_ref[rows].astype(F32))
        part = dot_t(d_qkv_ref[rows], w_ref[:, : 3 * width]).astype(B16)
        part_ref[rows] = part
        sum_ref[4:5] += col_sum(part.astype(F32) * flag_ref[rows, 0:1])


def attend_back(chain_count, dz_two, own, other, normed, inverse, gain, flag, qkv, prob, w_a):
    shape = dz_two.shape
    heads = qkv.shape[1] // 3
    shapes = [
        (shape, F32),
        (shape, B16),
        (qkv.shape, B16),
        (shape, B16),
        ((8, shape[1]), F32),
        ((8, 3 * heads), F32),
    ]
    operands = [dz_two, own, other, normed, inverse, gain, flag, qkv, prob, w_a]
    body = functools.partial(attend_back_body, shape[0] // chain_count)
    return call(body, "attend_back", shapes, operands, [((shape[0], heads), B16)])


def join_body(one_ref, other_ref, two_ref, up_ref, qkv_ref, out_ref):
    width = one_ref.shape[1]
    heads = qkv_ref.shape[1] // 3
    rows = out_ref.shape[1]
    out_ref[...] = jnp.zeros_like(out_ref)

    def put(start, values):
        for k in range(values.shape[1] // 128):
            place = (start + 128 * k) // 128
            out_ref[place // rows, place % rows : place % rows + 1] = values[:, 128 * k : 128 * (k + 1)]

    put(0, one_ref[3:4] + (one_ref[4:5] + other_ref[4:5]))
    for k in range(3):
        put((1 + k) * width, one_ref[k : k + 1])
        put((4 + k) * width, two_ref[k : k + 1])
    put(7 * width, qkv_ref[0:1, :heads])
    put(7 * width + heads, qkv_ref[0:1, 2 * heads :])
    put(7 * width + 2 * heads, up_ref[0:1])


def join(rows, sums_one, sums_other, sums_two, sums_up, sums_qkv):
    width = sums_one.shape[1]
    length = 7 * width + 2 * sums_qkv.shape[1] // 3 + sums_up.shape[1]
    assert length <= 2 * rows * 128
    operands = [sums_one, sums_other, sums_two, sums_up, sums_qkv]
    return call(join_body, "join", [((2, rows, 128), F32)], operands, limit=4)[0]


def last_body(dz_ref, own_ref, other_ref, flag_ref, out_ref):
    for rows in chunks(dz_ref.shape[0]):
        total = dz_ref[rows] + (own_ref[rows].astype(F32) + other_ref[rows].astype(F32))
        out_ref[rows] = jnp.where(flag_ref[rows, 0:1] > 0.0, 0.0, total)


def last(dz_one, own, other, flag):
    return call(last_body, "last", [(dz_one.shape, F32)], [dz_one, own, other, flag])[0]


def add_late_body(x_ref, y_ref, from_x_ref, from_y_ref, out_x_ref, out_y_ref):
    out_x_ref[...] = (x_ref[...].astype(F32) + from_y_ref[:2].astype(F32)).astype(B16)
    out_y_ref[...] = (y_ref[...].astype(F32) + from_x_ref[:2].astype(F32)).astype(B16)


def add_own_body(own_ref, from_x_ref, from_y_ref, late_x_ref, late_y_ref, near_ref, mid_ref):
    near_ref[...] = (
        own_ref[:2].astype(F32) + from_x_ref[2:].astype(F32) + late_y_ref[...].astype(F32)
    )
    mid_ref[...] = (
        own_ref[2:].astype(F32) + late_x_ref[...].astype(F32) + from_y_ref[2:].astype(F32)
    ).astype(B16)


def add_mid_body(near_ref, mid_ref, own_ref, far_ref):
    own_ref[...] = near_ref[0] + mid_ref[0].astype(F32)
    far_ref[...] = (near_ref[1] + mid_ref[1].astype(F32)).astype(B16)


def last_own_body(own_ref, from_x_ref, from_y_ref, late_x_ref, late_y_ref, v_ref, vx_ref, vy_ref, vd_ref,
                  near_ref, mid_ref, vector_ref):
    cols = own_ref.shape[2]
    near_ref[...] = (
        own_ref[:2].astype(F32) + from_x_ref[2:].astype(F32) + late_y_ref[...].astype(F32)
    )
    mid_ref[:, :, :cols] = (
        own_ref[2:].astype(F32) + late_x_ref[...].astype(F32) + from_y_ref[2:].astype(F32)
    ).astype(B16)
    vector = ((v_ref[...] + vx_ref[...]) + (vy_ref[...] + vd_ref[...])).astype(B16)
    mid_ref[:, :, cols:] = vector
    vector_ref[...] = vector


def last_mid_body(near_ref, mid_ref, v_ref, own_ref, far_ref, vector_ref):
    cols = own_ref.shape[1]
    own_ref[...] = near_ref[0] + mid_ref[0, :, :cols].astype(F32)
    far_ref[:, :cols] = (near_ref[1] + mid_ref[1, :, :cols].astype(F32)).astype(B16)
    vector = (v_ref[...].astype(F32) + mid_ref[:, :, cols:].astype(F32)).astype(B16)
    for k in range(2):
        far_ref[:, cols + 128 * k : cols + 128 * (k + 1)] = vector[k]
    vector_ref[...] = vector


def last_far_body(own_ref, far_ref, v_ref, *outs):
    cols = own_ref.shape[1]
    part = cols // 4
    for k in range(4):
        lanes = slice(k * part, (k + 1) * part)
        outs[k][...] = own_ref[:, lanes] + far_ref[:, lanes].astype(F32)
    for k in range(2):
        other = far_ref[:, cols + 128 * k : cols + 128 * (k + 1)]
        outs[4][k] = v_ref[k].astype(F32) + other.astype(F32)


def last_own(own, from_x, from_y, late_x, late_y, *vectors):
    rows, cols = own.shape[1:]
    shapes = [(late_x.shape, F32), ((2, rows, cols + 128), B16), (vectors[0].shape, B16)]
    operands = [own, from_x, from_y, late_x, late_y, *vectors]
    return call(last_own_body, "last_own", shapes, operands, limit=8)


def last_mid(near, mid, vector):
    rows, cols = near.shape[1:]
    shapes = [((rows, cols), F32), ((rows, cols + 256), B16), (vector.shape, B16)]
    return call(last_mid_body, "last_mid", shapes, [near, mid, vector], limit=8)


def last_far(own, far, vector):
    rows, cols = own.shape
    shapes = [((rows, cols // 4), F32)] * 4 + [(vector.shape, F32)]
    return call(last_far_body, "last_far", shapes, [own, far, vector], limit=8)


def add_late(late_x, late_y, from_x, from_y):
    shape = (late_x.shape, B16)
    return call(add_late_body, "add_late", [shape, shape], [late_x, late_y, from_x, from_y], limit=8)


def add_own(own, from_x, from_y, late_x, late_y):
    shapes = [(late_x.shape, F32), (late_x.shape, B16)]
    return call(add_own_body, "add_own", shapes, [own, from_x, from_y, late_x, late_y], limit=8)


def add_mid(near, mid):
    shapes = [(near.shape[1:], F32), (near.shape[1:], B16)]
    return call(add_mid_body, "add_mid", shapes, [near, mid], limit=8)


def per_device(dp_size, tokens, masked, lengths, mask_vector, w_query, b_query, w_key, w_value,
               b_value, w_out, b_out, gain_one, shift_one, w_up, b_up, w_down, b_down, gain_two,
               shift_two, grad_out):
    head_cols = w_query.shape[1]
    width = tokens.shape[1]
    fast = dp_size == BLOCKS and w_query.shape[0] % 16 == 0
    me = lax.axis_index("dp").astype(jnp.int32).reshape(1)
    if not fast:
        me = jnp.zeros_like(me)

    (b_query, b_value, b_out, gain_one, shift_one, b_up, b_down, gain_two, shift_two) = (
        member.astype(F32)
        for member in (b_query, b_value, b_out, gain_one, shift_one, b_up, b_down, gain_two, shift_two)
    )
    is_masked = (masked == 1)[:, None]
    flag = jnp.broadcast_to(is_masked, (masked.shape[0], 128)).astype(F32)
    in_low = jnp.where(is_masked, mask_vector[None, :], tokens)
    bias_qkv = jnp.concatenate([b_query, jnp.zeros_like(b_query), b_value])[None, :]
    vectors_one = jnp.stack([b_out, gain_one, shift_one])
    vectors_two = jnp.stack([gain_one, shift_one, b_down, gain_two, shift_two])
    b_up, gain_one = b_up[None, :], gain_one[None, :]

    a = jnp.concatenate([w_query, w_key, w_value, w_out.T], axis=1)
    c = w_up
    d = w_down.T
    if fast:
        az = swap(a, 12)
        az, me, flag, in_low, bias_qkv, vectors_one, vectors_two, b_up, gain_one = tie(
            az, me, flag, in_low, bias_qkv, vectors_one, vectors_two, b_up, gain_one
        )
        an = jnp.stack([a, az])
        anx, any_, am = swap(an, 1), swap(an, 2), swap(an, 4)
        anx, any_, am, an, c = tie(anx, any_, am, an, c)
        amx, amy, cz = swap(am, 1), swap(am, 2), swap(c, 12)
        amx, amy, cz, anx, c, d = tie(amx, amy, cz, anx, c, d)
        cn = jnp.stack([c, cz])
        amd, and_, cm = swap(amy, 1), swap(anx, 2), swap(cn, 4)
        cnx, cny, dz = swap(cn, 1), swap(cn, 2), swap(d, 12)
        amd, and_, cm, cnx, cny, dz, d = tie(amd, and_, cm, cnx, cny, dz, d)
        dn = jnp.stack([d, dz])
        pieces_a = [an, am, anx, amx, any_, amy, and_, amd]
        cmx, cnd, dm = swap(cm, 1), swap(cnx, 2), swap(dn, 4)
        dnx, dny = swap(dn, 1), swap(dn, 2)
    else:
        a, c, d = (lax.all_gather(piece, "dp", axis=0, tiled=True) for piece in (a, c, d))
        pieces_a, pieces_c, pieces_d = as_pieces(a), as_pieces(c), as_pieces(d)
    w_a, qkv, prob, attended, part = attend(me, lengths, in_low, bias_qkv, pieces_a)
    if fast:
        cmx, cnd, dm, dnx, dny, cm, part = tie(cmx, cnd, dm, dnx, dny, cm, part)
        cmy, dnd, cmd = swap(cm, 2), swap(dny, 1), swap(cnd, 4)
    other = pair_swap(part)
    if fast:
        cmy, dnd, cmd, dm, other, part = tie(cmy, dnd, cmd, dm, other, part)
        pieces_c = [cn, cm, cnx, cmx, cny, cmy, cnd, cmd]
        dmx, dmy, dmd = swap(dm, 1), swap(dm, 2), swap(dnd, 4)
    w_u, normed_one, inverse_one, hidden_low, act_low, slope = up(
        me, in_low, part, other, vectors_one, b_up, pieces_c
    )
    if fast:
        dmx, dmy, dmd, act_low = tie(dmx, dmy, dmd, act_low)
        pieces_d = [dn, dm, dnx, dmx, dny, dmy, dnd, dmd]
    w_d, part = down(me, act_low, pieces_d)
    other = pair_swap(part)
    result, dz_two, dz_two_low, sums_two = second_norm(normed_one, part, other, grad_out, vectors_two)
    dx, dy, dxl, dyl, do = weight_grad(me, [dz_two_low], [act_low])
    if fast:
        dx, dy, dxl, dyl, dz_two_low = tie(dx, dy, dxl, dyl, dz_two_low)
        dxr, dyr = swap(dx, 1), swap(dy, 2)
    d_pre_low, part, sums_up = hidden_back(dz_two_low, slope, w_d, w_u)
    cx, cy, cxl, cyl, co = weight_grad(me, [hidden_low], [d_pre_low])
    if fast:
        dxr, dyr, part, cx, cy = tie(dxr, dyr, part, cx, cy)
        cxr, cyr = swap(cx, 1), swap(cy, 2)
        dxl, dyl = add_late(dxl, dyl, dxr, dyr)
        dxlr, dylr = swap(dxl, 1), swap(dyl, 2)
    other = pair_swap(part)
    dz_one, dz_one_low, d_qkv, part, sums_one, sums_qkv = attend_back(
        lengths.shape[0], dz_two, part, other, normed_one, inverse_one, gain_one, flag, qkv, prob, w_a
    )
    if fast:
        cxr, cyr, dxlr, dylr, part, d_qkv, dz_one_low = tie(cxr, cyr, dxlr, dylr, part, d_qkv, dz_one_low)
        cxl, cyl = add_late(cxl, cyl, cxr, cyr)
        cxlr, cylr = swap(cxl, 1), swap(cyl, 2)
        d_near, d_mid = add_own(do, dxr, dyr, dxlr, dylr)
        d_midr = swap(d_mid, 4)
    sums_other = pair_swap(sums_one)
    ax, ay, axl, ayl, ao = weight_grad(me, [in_low, dz_one_low], [d_qkv, attended])
    if fast:
        cxlr, cylr, d_midr, ax, ay, part, sums_other = tie(cxlr, cylr, d_midr, ax, ay, part, sums_other)
        axr, ayr = swap(ax, 1), swap(ay, 2)
        c_near, c_mid = add_own(co, cxr, cyr, cxlr, cylr)
        d_near, d_far = add_mid(d_near, d_midr)
        c_midr, d_farr = swap(c_mid, 4), swap(d_far, 12)
    other = pair_swap(part)
    d_tokens = last(dz_one, part, other, flag)
    joined = join(width // BLOCKS, sums_one, sums_other, sums_two, sums_up, sums_qkv)
    if fast:
        axr, ayr, c_midr, d_farr, joined, d_tokens = tie(axr, ayr, c_midr, d_farr, joined, d_tokens)
        jx, jy, jd = swap(joined, 1), swap(joined, 2), swap(joined, 3)
        axl, ayl = add_late(axl, ayl, axr, ayr)
        axlr, aylr = swap(axl, 1), swap(ayl, 2)
        c_near, c_far = add_mid(c_near, c_midr)
        c_farr = swap(c_far, 12)
        axlr, aylr, c_farr, jx, jy, jd = tie(axlr, aylr, c_farr, jx, jy, jd)
        a_near, a_mid, vector = last_own(ao, axr, ayr, axlr, aylr, joined, jx, jy, jd)
        a_midr = swap(a_mid, 4)
        d_w_down_t = d_near + d_farr.astype(F32)
        a_midr, d_w_down_t = tie(a_midr, d_w_down_t)
        a_near, a_far, vector = last_mid(a_near, a_midr, vector)
        a_farr = swap(a_far, 12)
        d_w_up = c_near + c_farr.astype(F32)
        *d_wa, joined = last_far(a_near, a_farr, vector)
    else:
        full = []
        for parts in ((ax, ay, axl, ayl, ao), (cx, cy, cxl, cyl, co), (dx, dy, dxl, dyl, do)):
            blocks = [None] * BLOCKS
            for member, offsets in zip(parts, ORDER):
                for k, offset in enumerate(offsets):
                    blocks[offset] = member[k]
            full.append(jnp.concatenate(blocks).astype(F32))
        joined = lax.psum(joined, "dp")
        d_wa, d_w_up, d_w_down_t = (
            lax.psum_scatter(member, "dp", scatter_dimension=0, tiled=True) for member in full
        )
        d_wa = [d_wa[:, k * head_cols : (k + 1) * head_cols] for k in range(4)]
    joined = joined.reshape(-1)
    summed = []
    start = 0
    for size in [width] * 7 + [head_cols] * 2 + [w_up.shape[1]]:
        summed.append(joined[start : start + size])
        start += size
    return (
        result,
        d_tokens,
        summed[0],
        d_wa[0],
        summed[7],
        d_wa[1],
        d_wa[2],
        summed[8],
        d_wa[3].T,
        summed[3],
        summed[1],
        summed[2],
        d_w_up,
        summed[9],
        d_w_down_t.T,
        summed[6],
        summed[4],
        summed[5],
    )


def solution(mesh):
    rows, flat, both = P("dp", None), P(), P("dp", "mp")
    return jax.shard_map(
        functools.partial(per_device, mesh.shape["dp"]),
        mesh=mesh,
        in_specs=(rows, P("dp"), P("dp"), flat, both, P("mp"), both, both, P("mp"), P("mp", "dp"),
                  flat, flat, flat, both, P("mp"), P("mp", "dp"), flat, flat, flat, rows),
        out_specs=(rows, rows, flat, both, P("mp"), both, both, P("mp"), P("mp", "dp"), flat, flat,
                   flat, both, P("mp"), P("mp", "dp"), flat, flat, flat),
        check_vma=False,
    )
```

```python
import functools

import jax
import jax.numpy as jnp
from jax import lax
from jax.experimental import pallas as pl
from jax.experimental.pallas import tpu as pltpu
from jax.sharding import PartitionSpec as P

HEAD = 64
NORM_EPS = 1e-05
F32 = jnp.float32
B16 = jnp.bfloat16
MIB = 1 << 20

BLOCKS = 16
NEAR = (0, 12)
MID = (4, 8)


def swap(values, bit):
    return lax.ppermute(values, "dp", [(i, i ^ bit) for i in range(BLOCKS)])


def tie(*values):
    return lax.optimization_barrier(values)


def after(value, *earlier):
    return tie(value, *earlier)[0]


def pair_swap(partial):
    return lax.ppermute(partial, "mp", [(0, 1), (1, 0)])


def as_pieces(full):
    rows = full.shape[0] // BLOCKS
    blocks = full.reshape(BLOCKS, rows, full.shape[1])
    return [
        jnp.stack([blocks[offset + bits[0]], blocks[offset + bits[1]]])
        for offset in range(4)
        for bits in (NEAR, MID)
    ]


SMEM_SPEC = pl.BlockSpec(memory_space=pltpu.SMEM)
VMEM_SPEC = pl.BlockSpec(memory_space=pltpu.VMEM)
CHUNK = 256
UNROLL = 2
LIGHT = pl.CostEstimate(flops=1, bytes_accessed=1, transcendentals=0)


def call(body, name, shapes, operands, scratch=(), limit=16):
    return pl.pallas_call(
        body,
        in_specs=[
            SMEM_SPEC if member.dtype == jnp.int32 and member.ndim == 1 else VMEM_SPEC
            for member in operands
        ],
        out_specs=[VMEM_SPEC] * len(shapes),
        out_shape=[jax.ShapeDtypeStruct(shape, dtype) for shape, dtype in shapes],
        scratch_shapes=[pltpu.VMEM(shape, dtype) for shape, dtype in scratch],
        compiler_params=pltpu.CompilerParams(vmem_limit_bytes=limit * MIB),
        cost_estimate=LIGHT,
        name=name,
    )(*operands)


def chunks(count):
    return [slice(start, start + CHUNK) for start in range(0, count, CHUNK)]


PAIRS = [(q + bits[k], 2 * q + m, k) for q in range(4) for m, bits in enumerate((NEAR, MID)) for k in range(2)]


def fill(me, pieces, full_ref):
    rows = pieces[0].shape[1]
    for offset, piece, index in PAIRS:
        block = me ^ offset
        full_ref[pl.ds(pl.multiple_of(block * rows, rows), rows), :] = pieces[piece][index]


def dot(left, right):
    return jnp.dot(left, right, preferred_element_type=F32)


def dot_t(left, right):
    return lax.dot_general(left, right, (((1,), (1,)), ((), ())), preferred_element_type=F32)


def t_dot(left, right):
    return lax.dot_general(left, right, (((0,), (0,)), ((), ())), preferred_element_type=F32)


def row_mean(values):
    return jnp.mean(values, axis=-1, keepdims=True)


def normalize(values):
    centred = values - row_mean(values)
    inverse = lax.rsqrt(row_mean(centred * centred) + NORM_EPS)
    return centred * inverse, inverse


def col_sum(values):
    return jnp.sum(values, axis=0, keepdims=True)


def norm_back(scaled, normed, inverse):
    return inverse * (scaled - row_mean(scaled) - normed * row_mean(scaled * normed))


def two_heads(slots):
    row = lax.broadcasted_iota(jnp.int32, (2 * slots, 2 * HEAD), 0) // slots
    lane = lax.broadcasted_iota(jnp.int32, (2 * slots, 2 * HEAD), 1) // HEAD
    return (row == lane).astype(F32).astype(B16)


def doubled(values, mask):
    return jnp.concatenate([values, values], axis=0) * mask


def attend_body(slots, me_ref, len_ref, in_ref, bias_ref, *rest):
    pieces, (w_ref, qkv_ref, prob_ref, att_ref, part_ref) = rest[:-5], rest[-5:]
    count, width = att_ref.shape
    fill(me_ref[0], pieces, w_ref)
    for rows in chunks(count):
        qkv_ref[rows] = (dot(in_ref[rows], w_ref[:, : 3 * width]) + bias_ref[...]).astype(B16)
    mask = two_heads(slots)
    key_slot = lax.broadcasted_iota(jnp.int32, (slots, slots), 1)

    def chain_step(chain, carry):
        valid = key_slot < len_ref[chain]
        rows = pl.ds(pl.multiple_of(chain * slots, slots), slots)
        for pair in range(width // (2 * HEAD)):
            lanes = 2 * HEAD * pair
            query = qkv_ref[rows, lanes : lanes + 2 * HEAD]
            key = qkv_ref[rows, width + lanes : width + lanes + 2 * HEAD]
            value = qkv_ref[rows, 2 * width + lanes : 2 * width + lanes + 2 * HEAD]
            scores = dot_t(query * (HEAD**-0.5), doubled(key, mask))
            probs = []
            for head in range(2):
                part = jnp.where(valid, scores[:, head * slots : (head + 1) * slots], -1e30)
                terms = jnp.exp(part - jnp.max(part, axis=-1, keepdims=True))
                probs.append((terms / jnp.sum(terms, axis=-1, keepdims=True)).astype(B16))
            prob = jnp.concatenate(probs, axis=1)
            prob_ref[rows, 2 * slots * pair : 2 * slots * (pair + 1)] = prob
            att_ref[rows, lanes : lanes + 2 * HEAD] = dot(prob, doubled(value, mask)).astype(B16)
        return carry

    lax.fori_loop(0, count // slots, chain_step, 0, unroll=UNROLL)
    for rows in chunks(count):
        part_ref[rows] = dot_t(att_ref[rows], w_ref[:, 3 * width :]).astype(B16)


def attend(me, lengths, in_low, bias, pieces):
    count, width = in_low.shape
    heads = bias.shape[1] // 3
    slots = count // lengths.shape[0]
    shapes = [
        ((width, 4 * heads), B16),
        ((count, 3 * heads), B16),
        ((count, heads // HEAD * slots), B16),
        ((count, heads), B16),
        ((count, width), B16),
    ]
    body = functools.partial(attend_body, slots)
    return call(body, "attend", shapes, [me, lengths, in_low, bias, *pieces])


def up_body(me_ref, in_ref, own_ref, other_ref, vec_ref, bias_ref, *rest):
    pieces, (w_ref, normed_ref, inverse_ref, low_ref, act_ref, slope_ref) = rest[:-6], rest[-6:]
    fill(me_ref[0], pieces, w_ref)
    vectors = vec_ref[...]
    for rows in chunks(in_ref.shape[0]):
        attn = own_ref[rows].astype(F32) + other_ref[rows].astype(F32) + vectors[0:1]
        normed, inverse = normalize(in_ref[rows].astype(F32) + attn)
        normed_ref[rows] = normed
        inverse_ref[rows] = jnp.broadcast_to(inverse, (CHUNK, inverse_ref.shape[1]))
        low_ref[rows] = (normed * vectors[1:2] + vectors[2:3]).astype(B16)
        pre = dot(low_ref[rows], w_ref[...]) + bias_ref[...]
        cdf = 0.5 + 0.5 * lax.erf(pre * (2.0**-0.5))
        act_ref[rows] = (pre * cdf).astype(B16)
        density = jnp.exp(pre * pre * -0.5) * 0.3989422804014327
        slope_ref[rows] = (cdf + pre * density).astype(B16)


def up(me, in_low, own, other, vectors, bias, pieces):
    count, width = in_low.shape
    units = bias.shape[1]
    shapes = [
        ((width, units), B16),
        ((count, width), F32),
        ((count, 128), F32),
        ((count, width), B16),
        ((count, units), B16),
        ((count, units), B16),
    ]
    return call(up_body, "up", shapes, [me, in_low, own, other, vectors, bias, *pieces])


def down_body(me_ref, act_ref, *rest):
    pieces, (w_ref, part_ref) = rest[:-2], rest[-2:]
    fill(me_ref[0], pieces, w_ref)
    for rows in chunks(part_ref.shape[0]):
        part_ref[rows] = dot_t(act_ref[rows], w_ref[...]).astype(B16)


def down_rest_body(act_ref, w_ref, part_ref):
    half = part_ref.shape[0]
    for rows in chunks(half):
        part_ref[rows] = dot_t(act_ref[half + rows.start : half + rows.stop], w_ref[...]).astype(B16)


def down(me, act, pieces):
    count, units = act.shape
    width = BLOCKS * pieces[0].shape[1]
    half = ((count // 2, width), B16)
    w_down_t, first = call(down_body, "down", [((width, units), B16), half], [me, act, *pieces])
    (second,) = call(down_rest_body, "down_rest", [half], [act, w_down_t])
    return w_down_t, first, second


def second_norm_body(start, normed_ref, own_ref, other_ref, grad_ref, vec_ref, *rest):
    earlier, (out_ref, dz_ref, low_ref, sum_ref) = rest[:-4], rest[-4:]
    vectors = vec_ref[...]
    if start == 0:
        sum_ref[...] = jnp.zeros_like(sum_ref)
    else:
        for done_ref, now_ref in zip(earlier, (out_ref, dz_ref, low_ref)):
            now_ref[:start] = done_ref[...]
        sum_ref[...] = earlier[3][...]
    for half_rows in chunks(own_ref.shape[0]):
        rows = slice(start + half_rows.start, start + half_rows.stop)
        hidden = normed_ref[rows] * vectors[0:1] + vectors[1:2]
        ffn = own_ref[half_rows].astype(F32) + other_ref[half_rows].astype(F32) + vectors[2:3]
        normed, inverse = normalize(hidden + ffn)
        out_ref[rows] = (normed * vectors[3:4] + vectors[4:5]).astype(B16)
        grad = grad_ref[rows].astype(F32)
        dz = norm_back(grad * vectors[3:4], normed, inverse)
        dz_ref[rows] = dz
        low_ref[rows] = dz.astype(B16)
        sum_ref[0:1] += col_sum(grad * normed)
        sum_ref[1:2] += col_sum(grad)
        sum_ref[2:3] += col_sum(dz)


def second_norm(normed, halves, grad, vectors):
    width = normed.shape[1]
    results = []
    for index, (own, other) in enumerate(halves):
        start = index * own.shape[0]
        shape = (start + own.shape[0], width)
        shapes = [(shape, B16), (shape, F32), (shape, B16), ((8, width), F32)]
        operands = [normed, own, other, grad, vectors, *results]
        results = call(functools.partial(second_norm_body, start), "second_norm", shapes, operands)
    return results


ORDER = (
    (3, 15, 1, 13),
    (7, 11, 6, 10),
    (5, 9),
    (2, 14),
    (0, 12, 4, 8),
)


def weight_grad(me, lefts, rights):
    count, width = lefts[0].shape
    tile = 384 if all(right.shape[1] % 384 == 0 for right in rights) else 128
    total = sum(right.shape[1] for right in rights)
    rows = width // BLOCKS
    n = len(lefts)

    def body(me_ref, *refs):
        outs, (turned_ref, full_ref) = refs[2 * n : -2], refs[-2:]
        at = 0
        for left_ref, right_ref in zip(refs[:n], refs[n : 2 * n]):
            turned_ref[...] = left_ref[...].T
            for start in range(0, right_ref.shape[1], tile):
                full_ref[...] = dot(turned_ref[...], right_ref[:, start : start + tile]).astype(B16)
                for out_ref, offsets in zip(outs, ORDER):
                    for k, offset in enumerate(offsets):
                        place = pl.multiple_of((me_ref[0] ^ offset) * rows, rows)
                        out_ref[k, :, at : at + tile] = full_ref[pl.ds(place, rows), :]
                at += tile

    shapes = [((len(offsets), rows, total), B16) for offsets in ORDER]
    scratch = [((width, count), B16), ((width, tile), B16)]
    return call(body, "weight_grad", shapes, [me, *lefts, *rights], scratch)


def hidden_back_body(low_ref, slope_ref, down_ref, up_ref, pre_ref, part_ref, sum_ref):
    sum_ref[...] = jnp.zeros_like(sum_ref)
    for rows in chunks(low_ref.shape[0]):
        d_pre = dot(low_ref[rows], down_ref[...]) * slope_ref[rows].astype(F32)
        sum_ref[0:1] += col_sum(d_pre)
        pre_ref[rows] = d_pre.astype(B16)
        part_ref[rows] = dot_t(pre_ref[rows], up_ref[...]).astype(B16)


def hidden_back(dz_low, slope, w_down_t, w_up):
    count, width = dz_low.shape
    units = slope.shape[1]
    shapes = [((count, units), B16), ((count, width), B16), ((8, units), F32)]
    return call(hidden_back_body, "hidden_back", shapes, [dz_low, slope, w_down_t, w_up])


def attend_back_body(slots, dz_ref, own_ref, other_ref, normed_ref, inverse_ref, gain_ref,
                     flag_ref, qkv_ref, prob_ref, w_ref, dz_one_ref, low_ref, d_qkv_ref, part_ref, sum_ref,
                     sum_qkv_ref, d_att_ref):
    count, width = d_att_ref.shape
    sum_ref[...] = jnp.zeros_like(sum_ref)
    sum_qkv_ref[...] = jnp.zeros_like(sum_qkv_ref)
    for rows in chunks(count):
        normed = normed_ref[rows]
        d_hidden = dz_ref[rows] + (own_ref[rows].astype(F32) + other_ref[rows].astype(F32))
        dz_one = norm_back(d_hidden * gain_ref[...], normed, inverse_ref[rows, 0:1])
        dz_one_ref[rows] = dz_one
        low_ref[rows] = dz_one.astype(B16)
        sum_ref[0:1] += col_sum(d_hidden * normed)
        sum_ref[1:2] += col_sum(d_hidden)
        sum_ref[2:3] += col_sum(dz_one)
        sum_ref[3:4] += col_sum(dz_one * flag_ref[rows, 0:1])
        d_att_ref[rows] = dot(low_ref[rows], w_ref[:, 3 * width :]).astype(B16)
    mask = two_heads(slots)

    def chain_step(chain, carry):
        rows = pl.ds(pl.multiple_of(chain * slots, slots), slots)
        for pair in range(width // (2 * HEAD)):
            lanes = 2 * HEAD * pair
            query = qkv_ref[rows, lanes : lanes + 2 * HEAD]
            key = qkv_ref[rows, width + lanes : width + lanes + 2 * HEAD]
            value = qkv_ref[rows, 2 * width + lanes : 2 * width + lanes + 2 * HEAD]
            d_att = d_att_ref[rows, lanes : lanes + 2 * HEAD]
            prob = prob_ref[rows, 2 * slots * pair : 2 * slots * (pair + 1)]
            d_prob = dot_t(d_att, doubled(value, mask))
            weights = prob.astype(F32)
            products = weights * d_prob
            lows = []
            for head in range(2):
                half = slice(head * slots, (head + 1) * slots)
                total = jnp.sum(products[:, half], axis=-1, keepdims=True)
                lows.append((products[:, half] - weights[:, half] * total).astype(B16))
            low = jnp.concatenate(lows, axis=1)
            d_query = dot(low, doubled(key, mask)) * (HEAD**-0.5)
            tall = jnp.concatenate(lows, axis=0)
            d_key = t_dot(tall, doubled(query, mask)) * (HEAD**-0.5)
            tall = jnp.concatenate([prob[:, :slots], prob[:, slots:]], axis=0)
            d_value = t_dot(tall, doubled(d_att, mask))
            d_qkv_ref[rows, lanes : lanes + 2 * HEAD] = d_query.astype(B16)
            d_qkv_ref[rows, width + lanes : width + lanes + 2 * HEAD] = d_key.astype(B16)
            d_qkv_ref[rows, 2 * width + lanes : 2 * width + lanes + 2 * HEAD] = d_value.astype(B16)
        return carry

    lax.fori_loop(0, count // slots, chain_step, 0, unroll=UNROLL)
    for rows in chunks(count):
        sum_qkv_ref[0:1] += col_sum(d_qkv_ref[rows].astype(F32))
        part = dot_t(d_qkv_ref[rows], w_ref[:, : 3 * width]).astype(B16)
        part_ref[rows] = part
        sum_ref[4:5] += col_sum(part.astype(F32) * flag_ref[rows, 0:1])


def attend_back(chain_count, dz_two, own, other, normed, inverse, gain, flag, qkv, prob, w_a):
    shape = dz_two.shape
    heads = qkv.shape[1] // 3
    shapes = [
        (shape, F32),
        (shape, B16),
        (qkv.shape, B16),
        (shape, B16),
        ((8, shape[1]), F32),
        ((8, 3 * heads), F32),
    ]
    operands = [dz_two, own, other, normed, inverse, gain, flag, qkv, prob, w_a]
    body = functools.partial(attend_back_body, shape[0] // chain_count)
    return call(body, "attend_back", shapes, operands, [((shape[0], heads), B16)])


def join_body(one_ref, other_ref, two_ref, up_ref, qkv_ref, out_ref):
    width = one_ref.shape[1]
    heads = qkv_ref.shape[1] // 3
    rows = out_ref.shape[1]
    out_ref[...] = jnp.zeros_like(out_ref)

    def put(start, values):
        for k in range(values.shape[1] // 128):
            place = (start + 128 * k) // 128
            out_ref[place // rows, place % rows : place % rows + 1] = values[:, 128 * k : 128 * (k + 1)]

    put(0, one_ref[3:4] + (one_ref[4:5] + other_ref[4:5]))
    for k in range(3):
        put((1 + k) * width, one_ref[k : k + 1])
        put((4 + k) * width, two_ref[k : k + 1])
    put(7 * width, qkv_ref[0:1, :heads])
    put(7 * width + heads, qkv_ref[0:1, 2 * heads :])
    put(7 * width + 2 * heads, up_ref[0:1])


def join(rows, sums_one, sums_other, sums_two, sums_up, sums_qkv):
    width = sums_one.shape[1]
    length = 7 * width + 2 * sums_qkv.shape[1] // 3 + sums_up.shape[1]
    assert length <= 2 * rows * 128
    operands = [sums_one, sums_other, sums_two, sums_up, sums_qkv]
    return call(join_body, "join", [((2, rows, 128), F32)], operands, limit=4)[0]


def last_body(dz_ref, own_ref, other_ref, flag_ref, out_ref):
    for rows in chunks(dz_ref.shape[0]):
        total = dz_ref[rows] + (own_ref[rows].astype(F32) + other_ref[rows].astype(F32))
        out_ref[rows] = jnp.where(flag_ref[rows, 0:1] > 0.0, 0.0, total)


def last(dz_one, own, other, flag):
    return call(last_body, "last", [(dz_one.shape, F32)], [dz_one, own, other, flag])[0]


def add_late_body(x_ref, y_ref, from_x_ref, from_y_ref, out_x_ref, out_y_ref):
    out_x_ref[...] = (x_ref[...].astype(F32) + from_y_ref[:2].astype(F32)).astype(B16)
    out_y_ref[...] = (y_ref[...].astype(F32) + from_x_ref[:2].astype(F32)).astype(B16)


def add_own_body(own_ref, from_x_ref, from_y_ref, late_x_ref, late_y_ref, near_ref, mid_ref):
    near_ref[...] = (
        own_ref[:2].astype(F32) + from_x_ref[2:].astype(F32) + late_y_ref[...].astype(F32)
    )
    mid_ref[...] = (
        own_ref[2:].astype(F32) + late_x_ref[...].astype(F32) + from_y_ref[2:].astype(F32)
    ).astype(B16)


def add_mid_body(near_ref, mid_ref, own_ref, far_ref):
    own_ref[...] = near_ref[0] + mid_ref[0].astype(F32)
    far_ref[...] = (near_ref[1] + mid_ref[1].astype(F32)).astype(B16)


def far_vector_body(near_ref, mid_ref, v_ref, vx_ref, vy_ref, vd_ref, own_ref, far_ref, vector_ref):
    cols = own_ref.shape[1]
    own_ref[...] = near_ref[0] + mid_ref[0].astype(F32)
    far_ref[:, :cols] = (near_ref[1] + mid_ref[1].astype(F32)).astype(B16)
    vector = ((v_ref[...] + vx_ref[...]) + (vy_ref[...] + vd_ref[...])).astype(B16)
    for k in range(2):
        far_ref[:, cols + 128 * k : cols + 128 * (k + 1)] = vector[k]
    vector_ref[...] = vector


def own_vector_body(own_ref, from_x_ref, from_y_ref, late_x_ref, late_y_ref, v_ref, far_ref,
                    near_ref, mid_ref, vector_ref):
    cols = own_ref.shape[2]
    near_ref[...] = (
        own_ref[:2].astype(F32) + from_x_ref[2:].astype(F32) + late_y_ref[...].astype(F32)
    )
    mid_ref[:, :, :cols] = (
        own_ref[2:].astype(F32) + late_x_ref[...].astype(F32) + from_y_ref[2:].astype(F32)
    ).astype(B16)
    for k in range(2):
        other = far_ref[:, cols + 128 * k : cols + 128 * (k + 1)]
        vector = (v_ref[k].astype(F32) + other.astype(F32)).astype(B16)
        mid_ref[k, :, cols:] = vector
        vector_ref[k] = vector


def mid_vector_body(near_ref, mid_ref, v_ref, own_ref, far_ref, vector_ref):
    cols = own_ref.shape[1]
    own_ref[...] = near_ref[0] + mid_ref[0, :, :cols].astype(F32)
    far_ref[...] = (near_ref[1] + mid_ref[1, :, :cols].astype(F32)).astype(B16)
    vector_ref[...] = v_ref[...].astype(F32) + mid_ref[:, :, cols:].astype(F32)


def split_far_body(own_ref, far_ref, *outs):
    part = own_ref.shape[1] // 4
    for k in range(4):
        lanes = slice(k * part, (k + 1) * part)
        outs[k][...] = own_ref[:, lanes] + far_ref[:, lanes].astype(F32)


def far_vector(near, mid, *vectors):
    rows, cols = near.shape[1:]
    shapes = [((rows, cols), F32), ((rows, cols + 256), B16), (vectors[0].shape, B16)]
    return call(far_vector_body, "far_vector", shapes, [near, mid, *vectors], limit=8)


def own_vector(own, from_x, from_y, late_x, late_y, vector, far):
    rows, cols = own.shape[1:]
    shapes = [(late_x.shape, F32), ((2, rows, cols + 128), B16), (vector.shape, B16)]
    operands = [own, from_x, from_y, late_x, late_y, vector, far]
    return call(own_vector_body, "own_vector", shapes, operands, limit=8)


def mid_vector(near, mid, vector):
    rows, cols = near.shape[1:]
    shapes = [((rows, cols), F32), ((rows, cols), B16), (vector.shape, F32)]
    return call(mid_vector_body, "mid_vector", shapes, [near, mid, vector], limit=8)


def split_far(own, far):
    rows, cols = own.shape
    return call(split_far_body, "split_far", [((rows, cols // 4), F32)] * 4, [own, far], limit=8)


def add_late(late_x, late_y, from_x, from_y):
    shape = (late_x.shape, B16)
    return call(add_late_body, "add_late", [shape, shape], [late_x, late_y, from_x, from_y], limit=8)


def add_own(own, from_x, from_y, late_x, late_y):
    shapes = [(late_x.shape, F32), (late_x.shape, B16)]
    return call(add_own_body, "add_own", shapes, [own, from_x, from_y, late_x, late_y], limit=8)


def add_mid(near, mid):
    shapes = [(near.shape[1:], F32), (near.shape[1:], B16)]
    return call(add_mid_body, "add_mid", shapes, [near, mid], limit=8)


def per_device(dp_size, tokens, masked, lengths, mask_vector, w_query, b_query, w_key, w_value,
               b_value, w_out, b_out, gain_one, shift_one, w_up, b_up, w_down, b_down, gain_two,
               shift_two, grad_out):
    head_cols = w_query.shape[1]
    width = tokens.shape[1]
    fast = dp_size == BLOCKS and w_query.shape[0] % 16 == 0
    me = lax.axis_index("dp").astype(jnp.int32).reshape(1)
    if not fast:
        me = jnp.zeros_like(me)

    (b_query, b_value, b_out, gain_one, shift_one, b_up, b_down, gain_two, shift_two) = (
        member.astype(F32)
        for member in (b_query, b_value, b_out, gain_one, shift_one, b_up, b_down, gain_two, shift_two)
    )
    is_masked = (masked == 1)[:, None]
    flag = jnp.broadcast_to(is_masked, (masked.shape[0], 128)).astype(F32)
    in_low = jnp.where(is_masked, mask_vector[None, :], tokens)
    bias_qkv = jnp.concatenate([b_query, jnp.zeros_like(b_query), b_value])[None, :]
    vectors_one = jnp.stack([b_out, gain_one, shift_one])
    vectors_two = jnp.stack([gain_one, shift_one, b_down, gain_two, shift_two])
    b_up, gain_one = b_up[None, :], gain_one[None, :]

    a = jnp.concatenate([w_query, w_key, w_value, w_out.T], axis=1)
    c = w_up
    d = w_down.T
    if fast:
        az = swap(a, 12)
        az, me, flag, in_low, bias_qkv, vectors_one, vectors_two, b_up, gain_one = tie(
            az, me, flag, in_low, bias_qkv, vectors_one, vectors_two, b_up, gain_one
        )
        an = jnp.stack([a, az])
        anx, any_, am = swap(an, 1), swap(an, 2), swap(an, 4)
        anx, any_, am, an, c = tie(anx, any_, am, an, c)
        amx, amy, cz = swap(am, 1), swap(am, 2), swap(c, 12)
        amx, amy, cz, anx, c, d = tie(amx, amy, cz, anx, c, d)
        cn = jnp.stack([c, cz])
        amd, and_, cm = swap(amy, 1), swap(anx, 2), swap(cn, 4)
        cnx, cny, dz = swap(cn, 1), swap(cn, 2), swap(after(d, cm), 12)
        amd, and_, cm, cnx, cny, dz, d = tie(amd, and_, cm, cnx, cny, dz, d)
        dn = jnp.stack([d, dz])
        pieces_a = [an, am, anx, amx, any_, amy, and_, amd]
        cmx, cnd, dm = swap(cm, 1), swap(cnx, 2), swap(dn, 4)
        dnx, dny = swap(dn, 1), swap(dn, 2)
    else:
        a, c, d = (lax.all_gather(piece, "dp", axis=0, tiled=True) for piece in (a, c, d))
        pieces_a, pieces_c, pieces_d = as_pieces(a), as_pieces(c), as_pieces(d)
    w_a, qkv, prob, attended, part = attend(me, lengths, in_low, bias_qkv, pieces_a)
    if fast:
        cmx, cnd, dm, dnx, dny, cm, part = tie(cmx, cnd, dm, dnx, dny, cm, part)
        cmy, dnd, cmd = swap(cm, 2), swap(dny, 1), swap(cnd, 4)
    other = pair_swap(part)
    if fast:
        cmy, dnd, cmd, dm, other, part = tie(cmy, dnd, cmd, dm, other, part)
        pieces_c = [cn, cm, cnx, cmx, cny, cmy, cnd, cmd]
        dmx, dmy, dmd = swap(dm, 1), swap(dm, 2), swap(dnd, 4)
    w_u, normed_one, inverse_one, hidden_low, act_low, slope = up(
        me, in_low, part, other, vectors_one, b_up, pieces_c
    )
    if fast:
        dmx, dmy, dmd, act_low = tie(dmx, dmy, dmd, act_low)
        pieces_d = [dn, dm, dnx, dmx, dny, dmy, dnd, dmd]
    w_d, *parts = down(me, act_low, pieces_d)
    halves = [(part, pair_swap(part)) for part in parts]
    result, dz_two, dz_two_low, sums_two = second_norm(normed_one, halves, grad_out, vectors_two)
    dx, dy, dxl, dyl, do = weight_grad(me, [dz_two_low], [act_low])
    if fast:
        dx, dy, dxl, dyl, dz_two_low = tie(dx, dy, dxl, dyl, dz_two_low)
        dxr, dyr = swap(dx, 1), swap(dy, 2)
    d_pre_low, part, sums_up = hidden_back(dz_two_low, slope, w_d, w_u)
    cx, cy, cxl, cyl, co = weight_grad(me, [hidden_low], [d_pre_low])
    if fast:
        dxr, dyr, part, cx, cy = tie(dxr, dyr, part, cx, cy)
        cxr, cyr = swap(cx, 1), swap(cy, 2)
        dxl, dyl = add_late(dxl, dyl, dxr, dyr)
        dxlr, dylr = swap(dxl, 1), swap(dyl, 2)
    other = pair_swap(part)
    dz_one, dz_one_low, d_qkv, part, sums_one, sums_qkv = attend_back(
        lengths.shape[0], dz_two, part, other, normed_one, inverse_one, gain_one, flag, qkv, prob, w_a
    )
    if fast:
        cxr, cyr, dxlr, dylr, part, d_qkv, dz_one_low = tie(cxr, cyr, dxlr, dylr, part, d_qkv, dz_one_low)
        cxl, cyl = add_late(cxl, cyl, cxr, cyr)
        cxlr, cylr = swap(cxl, 1), swap(cyl, 2)
        d_near, d_mid = add_own(do, dxr, dyr, dxlr, dylr)
        d_midr = swap(d_mid, 4)
    sums_other = pair_swap(sums_one)
    ax, ay, axl, ayl, ao = weight_grad(me, [in_low, dz_one_low], [d_qkv, attended])
    if fast:
        cxlr, cylr, d_midr, ax, ay, part, sums_other = tie(cxlr, cylr, d_midr, ax, ay, part, sums_other)
        axr, ayr = swap(ax, 1), swap(ay, 2)
        c_near, c_mid = add_own(co, cxr, cyr, cxlr, cylr)
        d_near, d_far = add_mid(d_near, d_midr)
        c_midr, d_farr = swap(c_mid, 4), swap(d_far, 12)
    other = pair_swap(part)
    d_tokens = last(dz_one, part, other, flag)
    d_tokens, sums_one = tie(d_tokens, sums_one)
    joined = join(width // BLOCKS, sums_one, sums_other, sums_two, sums_up, sums_qkv)
    if fast:
        jx, jy, jd = swap(joined, 1), swap(joined, 2), swap(joined, 3)
        axr, ayr, c_midr, d_farr, jx, jy, jd = tie(axr, ayr, c_midr, d_farr, jx, jy, jd)
        axl, ayl = add_late(axl, ayl, axr, ayr)
        axlr, aylr = swap(axl, 1), swap(ayl, 2)
        c_near, c_far, vector = far_vector(c_near, c_midr, joined, jx, jy, jd)
        c_farr = swap(c_far, 12)
        axlr, aylr, c_farr = tie(axlr, aylr, c_farr)
        a_near, a_mid, vector = own_vector(ao, axr, ayr, axlr, aylr, vector, c_farr)
        a_midr = swap(a_mid, 4)
        d_w_down_t = d_near + d_farr.astype(F32)
        d_w_up = c_near + c_farr[:, : c_near.shape[1]].astype(F32)
        a_midr, d_w_down_t, d_w_up = tie(a_midr, d_w_down_t, d_w_up)
        a_near, a_far, joined = mid_vector(a_near, a_midr, vector)
        d_wa = split_far(a_near, swap(a_far, 12))
    else:
        full = []
        for parts in ((ax, ay, axl, ayl, ao), (cx, cy, cxl, cyl, co), (dx, dy, dxl, dyl, do)):
            blocks = [None] * BLOCKS
            for member, offsets in zip(parts, ORDER):
                for k, offset in enumerate(offsets):
                    blocks[offset] = member[k]
            full.append(jnp.concatenate(blocks).astype(F32))
        joined = lax.psum(joined, "dp")
        d_wa, d_w_up, d_w_down_t = (
            lax.psum_scatter(member, "dp", scatter_dimension=0, tiled=True) for member in full
        )
        d_wa = [d_wa[:, k * head_cols : (k + 1) * head_cols] for k in range(4)]
    joined = joined.reshape(-1)
    summed = []
    start = 0
    for size in [width] * 7 + [head_cols] * 2 + [w_up.shape[1]]:
        summed.append(joined[start : start + size])
        start += size
    return (
        result,
        d_tokens,
        summed[0],
        d_wa[0],
        summed[7],
        d_wa[1],
        d_wa[2],
        summed[8],
        d_wa[3].T,
        summed[3],
        summed[1],
        summed[2],
        d_w_up,
        summed[9],
        d_w_down_t.T,
        summed[6],
        summed[4],
        summed[5],
    )


def solution(mesh):
    rows, flat, both = P("dp", None), P(), P("dp", "mp")
    return jax.shard_map(
        functools.partial(per_device, mesh.shape["dp"]),
        mesh=mesh,
        in_specs=(rows, P("dp"), P("dp"), flat, both, P("mp"), both, both, P("mp"), P("mp", "dp"),
                  flat, flat, flat, both, P("mp"), P("mp", "dp"), flat, flat, flat, rows),
        out_specs=(rows, rows, flat, both, P("mp"), both, both, P("mp"), P("mp", "dp"), flat, flat,
                   flat, both, P("mp"), P("mp", "dp"), flat, flat, flat),
        check_vma=False,
    )
```

```python
import functools

import jax
import jax.numpy as jnp
from jax import lax
from jax.experimental import pallas as pl
from jax.experimental.pallas import tpu as pltpu
from jax.sharding import PartitionSpec as P

HEAD = 64
NORM_EPS = 1e-05
F32 = jnp.float32
B16 = jnp.bfloat16
MIB = 1 << 20

BLOCKS = 16
NEAR = (0, 12)
MID = (4, 8)


def swap(values, bit):
    return lax.ppermute(values, "dp", [(i, i ^ bit) for i in range(BLOCKS)])


def tie(*values):
    return lax.optimization_barrier(values)


def after(value, *earlier):
    return tie(value, *earlier)[0]


def pair_swap(partial):
    return lax.ppermute(partial, "mp", [(0, 1), (1, 0)])


def as_pieces(full):
    rows = full.shape[0] // BLOCKS
    blocks = full.reshape(BLOCKS, rows, full.shape[1])
    return [
        jnp.stack([blocks[offset + bits[0]], blocks[offset + bits[1]]])
        for offset in range(4)
        for bits in (NEAR, MID)
    ]


SMEM_SPEC = pl.BlockSpec(memory_space=pltpu.SMEM)
VMEM_SPEC = pl.BlockSpec(memory_space=pltpu.VMEM)
CHUNK = 256
UNROLL = 2
LIGHT = pl.CostEstimate(flops=1, bytes_accessed=1, transcendentals=0)


def call(body, name, shapes, operands, scratch=(), limit=16):
    return pl.pallas_call(
        body,
        in_specs=[
            SMEM_SPEC if member.dtype == jnp.int32 and member.ndim == 1 else VMEM_SPEC
            for member in operands
        ],
        out_specs=[VMEM_SPEC] * len(shapes),
        out_shape=[jax.ShapeDtypeStruct(shape, dtype) for shape, dtype in shapes],
        scratch_shapes=[pltpu.VMEM(shape, dtype) for shape, dtype in scratch],
        compiler_params=pltpu.CompilerParams(vmem_limit_bytes=limit * MIB),
        cost_estimate=LIGHT,
        name=name,
    )(*operands)


def chunks(count):
    return [slice(start, start + CHUNK) for start in range(0, count, CHUNK)]


PAIRS = [(q + bits[k], 2 * q + m, k) for q in range(4) for m, bits in enumerate((NEAR, MID)) for k in range(2)]


def fill(me, pieces, full_ref):
    rows = pieces[0].shape[1]
    for offset, piece, index in PAIRS:
        block = me ^ offset
        full_ref[pl.ds(pl.multiple_of(block * rows, rows), rows), :] = pieces[piece][index]


def dot(left, right):
    return jnp.dot(left, right, preferred_element_type=F32)


def dot_t(left, right):
    return lax.dot_general(left, right, (((1,), (1,)), ((), ())), preferred_element_type=F32)


def t_dot(left, right):
    return lax.dot_general(left, right, (((0,), (0,)), ((), ())), preferred_element_type=F32)


def row_mean(values):
    return jnp.mean(values, axis=-1, keepdims=True)


def normalize(values):
    centred = values - row_mean(values)
    inverse = lax.rsqrt(row_mean(centred * centred) + NORM_EPS)
    return centred * inverse, inverse


def col_sum(values):
    return jnp.sum(values, axis=0, keepdims=True)


def norm_back(scaled, normed, inverse):
    return inverse * (scaled - row_mean(scaled) - normed * row_mean(scaled * normed))


def two_heads(slots):
    row = lax.broadcasted_iota(jnp.int32, (2 * slots, 2 * HEAD), 0) // slots
    lane = lax.broadcasted_iota(jnp.int32, (2 * slots, 2 * HEAD), 1) // HEAD
    return (row == lane).astype(F32).astype(B16)


def doubled(values, mask):
    return jnp.concatenate([values, values], axis=0) * mask


def attend_body(slots, me_ref, len_ref, in_ref, bias_ref, *rest):
    pieces, (w_ref, qkv_ref, prob_ref, att_ref, part_ref) = rest[:-5], rest[-5:]
    count, width = att_ref.shape
    fill(me_ref[0], pieces, w_ref)
    for rows in chunks(count):
        qkv_ref[rows] = (dot(in_ref[rows], w_ref[:, : 3 * width]) + bias_ref[...]).astype(B16)
    mask = two_heads(slots)
    key_slot = lax.broadcasted_iota(jnp.int32, (slots, slots), 1)

    def chain_step(chain, carry):
        valid = key_slot < len_ref[chain]
        rows = pl.ds(pl.multiple_of(chain * slots, slots), slots)
        for pair in range(width // (2 * HEAD)):
            lanes = 2 * HEAD * pair
            query = qkv_ref[rows, lanes : lanes + 2 * HEAD]
            key = qkv_ref[rows, width + lanes : width + lanes + 2 * HEAD]
            value = qkv_ref[rows, 2 * width + lanes : 2 * width + lanes + 2 * HEAD]
            scores = dot_t(query * (HEAD**-0.5), doubled(key, mask))
            probs = []
            for head in range(2):
                part = jnp.where(valid, scores[:, head * slots : (head + 1) * slots], -1e30)
                terms = jnp.exp(part - jnp.max(part, axis=-1, keepdims=True))
                probs.append((terms / jnp.sum(terms, axis=-1, keepdims=True)).astype(B16))
            prob = jnp.concatenate(probs, axis=1)
            prob_ref[rows, 2 * slots * pair : 2 * slots * (pair + 1)] = prob
            att_ref[rows, lanes : lanes + 2 * HEAD] = dot(prob, doubled(value, mask)).astype(B16)
        return carry

    lax.fori_loop(0, count // slots, chain_step, 0, unroll=UNROLL)
    for rows in chunks(count):
        part_ref[rows] = dot_t(att_ref[rows], w_ref[:, 3 * width :]).astype(B16)


def attend(me, lengths, in_low, bias, pieces):
    count, width = in_low.shape
    heads = bias.shape[1] // 3
    slots = count // lengths.shape[0]
    shapes = [
        ((width, 4 * heads), B16),
        ((count, 3 * heads), B16),
        ((count, heads // HEAD * slots), B16),
        ((count, heads), B16),
        ((count, width), B16),
    ]
    body = functools.partial(attend_body, slots)
    return call(body, "attend", shapes, [me, lengths, in_low, bias, *pieces])


def up_body(me_ref, in_ref, own_ref, other_ref, vec_ref, bias_ref, *rest):
    pieces, (w_ref, normed_ref, inverse_ref, low_ref, act_ref, slope_ref) = rest[:-6], rest[-6:]
    fill(me_ref[0], pieces, w_ref)
    vectors = vec_ref[...]
    for rows in chunks(in_ref.shape[0]):
        attn = own_ref[rows].astype(F32) + other_ref[rows].astype(F32) + vectors[0:1]
        normed, inverse = normalize(in_ref[rows].astype(F32) + attn)
        normed_ref[rows] = normed
        inverse_ref[rows] = jnp.broadcast_to(inverse, (CHUNK, inverse_ref.shape[1]))
        low_ref[rows] = (normed * vectors[1:2] + vectors[2:3]).astype(B16)
        pre = dot(low_ref[rows], w_ref[...]) + bias_ref[...]
        cdf = 0.5 + 0.5 * lax.erf(pre * (2.0**-0.5))
        act_ref[rows] = (pre * cdf).astype(B16)
        density = jnp.exp(pre * pre * -0.5) * 0.3989422804014327
        slope_ref[rows] = (cdf + pre * density).astype(B16)


def up(me, in_low, own, other, vectors, bias, pieces):
    count, width = in_low.shape
    units = bias.shape[1]
    shapes = [
        ((width, units), B16),
        ((count, width), F32),
        ((count, 128), F32),
        ((count, width), B16),
        ((count, units), B16),
        ((count, units), B16),
    ]
    return call(up_body, "up", shapes, [me, in_low, own, other, vectors, bias, *pieces])


def down_body(me_ref, act_ref, *rest):
    pieces, (w_ref, part_ref) = rest[:-2], rest[-2:]
    fill(me_ref[0], pieces, w_ref)
    for rows in chunks(part_ref.shape[0]):
        part_ref[rows] = dot_t(act_ref[rows], w_ref[...]).astype(B16)


def down_rest_body(act_ref, w_ref, part_ref):
    half = part_ref.shape[0]
    for rows in chunks(half):
        part_ref[rows] = dot_t(act_ref[half + rows.start : half + rows.stop], w_ref[...]).astype(B16)


def down(me, act, pieces):
    count, units = act.shape
    width = BLOCKS * pieces[0].shape[1]
    half = ((count // 2, width), B16)
    w_down_t, first = call(down_body, "down", [((width, units), B16), half], [me, act, *pieces])
    (second,) = call(down_rest_body, "down_rest", [half], [act, w_down_t])
    return w_down_t, first, second


def second_norm_body(start, normed_ref, own_ref, other_ref, grad_ref, vec_ref, out_ref, dz_ref, low_ref, sum_ref):
    vectors = vec_ref[...]
    sum_ref[...] = jnp.zeros_like(sum_ref)
    for rows in chunks(own_ref.shape[0]):
        there = slice(start + rows.start, start + rows.stop)
        hidden = normed_ref[there] * vectors[0:1] + vectors[1:2]
        ffn = own_ref[rows].astype(F32) + other_ref[rows].astype(F32) + vectors[2:3]
        normed, inverse = normalize(hidden + ffn)
        out_ref[rows] = (normed * vectors[3:4] + vectors[4:5]).astype(B16)
        grad = grad_ref[there].astype(F32)
        dz = norm_back(grad * vectors[3:4], normed, inverse)
        dz_ref[rows] = dz
        low_ref[rows] = dz.astype(B16)
        sum_ref[0:1] += col_sum(grad * normed)
        sum_ref[1:2] += col_sum(grad)
        sum_ref[2:3] += col_sum(dz)


def second_norm(start, normed, own, other, grad, vectors):
    shape = own.shape
    shapes = [(shape, B16), (shape, F32), (shape, B16), ((8, shape[1]), F32)]
    body = functools.partial(second_norm_body, start)
    return call(body, "second_norm", shapes, [normed, own, other, grad, vectors])


def rows_in(halves, rows):
    size = halves[0].shape[0]
    half = halves[rows.start // size]
    return half[rows.start % size : rows.start % size + rows.stop - rows.start]


ORDER = (
    (3, 15, 1, 13),
    (7, 11, 6, 10),
    (5, 9),
    (2, 14),
    (0, 12, 4, 8),
)


def weight_grad(me, lefts, rights, vector=None):
    count, width = rights[0].shape[0], lefts[-1][0].shape[1]
    tile = 384 if all(right.shape[1] % 384 == 0 for right in rights) else 128
    total = sum(right.shape[1] for right in rights)
    rows = width // BLOCKS
    n = len(rights)
    flat = [half for left in lefts for half in left]
    wide = [] if vector is None else [vector]

    def body(me_ref, *refs):
        outs, (turned_ref, full_ref) = refs[-7:-2], refs[-2:]
        left_refs, right_refs = list(refs[: len(flat)]), refs[len(flat) : len(flat) + n]
        if wide:
            outs[0][0:2, :, total:] = refs[len(flat) + n][...]
            outs[0][2:4, :, total:] = jnp.zeros((2, rows, 128), B16)
        at = 0
        for left, right_ref in zip(lefts, right_refs):
            start = 0
            for _ in left:
                half_ref = left_refs.pop(0)
                turned_ref[:, start : start + half_ref.shape[0]] = half_ref[...].T
                start += half_ref.shape[0]
            for start in range(0, right_ref.shape[1], tile):
                full_ref[...] = dot(turned_ref[...], right_ref[:, start : start + tile]).astype(B16)
                for out_ref, offsets in zip(outs, ORDER):
                    for k, offset in enumerate(offsets):
                        place = pl.multiple_of((me_ref[0] ^ offset) * rows, rows)
                        out_ref[k, :, at : at + tile] = full_ref[pl.ds(place, rows), :]
                at += tile

    shapes = [((len(offsets), rows, total), B16) for offsets in ORDER]
    shapes[0] = ((4, rows, total + 128 * len(wide)), B16)
    scratch = [((width, count), B16), ((width, tile), B16)]
    return call(body, "weight_grad", shapes, [me, *flat, *rights, *wide], scratch)


def hidden_back_body(low_a_ref, low_b_ref, slope_ref, down_ref, up_ref, pre_ref, part_ref, sum_ref):
    sum_ref[...] = jnp.zeros_like(sum_ref)
    for rows in chunks(slope_ref.shape[0]):
        low = rows_in((low_a_ref, low_b_ref), rows)
        d_pre = dot(low, down_ref[...]) * slope_ref[rows].astype(F32)
        sum_ref[0:1] += col_sum(d_pre)
        pre_ref[rows] = d_pre.astype(B16)
        part_ref[rows] = dot_t(pre_ref[rows], up_ref[...]).astype(B16)


def hidden_back(lows, slope, w_down_t, w_up):
    count, units = slope.shape
    shapes = [((count, units), B16), ((count, w_up.shape[0]), B16), ((8, units), F32)]
    return call(hidden_back_body, "hidden_back", shapes, [*lows, slope, w_down_t, w_up])


def attend_back_body(slots, dz_a_ref, dz_b_ref, own_ref, other_ref, normed_ref, inverse_ref, gain_ref,
                     flag_ref, qkv_ref, prob_ref, w_ref, dz_one_ref, low_ref, d_qkv_ref, part_ref, sum_ref,
                     sum_qkv_ref, d_att_ref):
    count, width = d_att_ref.shape
    sum_ref[...] = jnp.zeros_like(sum_ref)
    sum_qkv_ref[...] = jnp.zeros_like(sum_qkv_ref)
    for rows in chunks(count):
        normed = normed_ref[rows]
        both = own_ref[rows].astype(F32) + other_ref[rows].astype(F32)
        d_hidden = rows_in((dz_a_ref, dz_b_ref), rows) + both
        dz_one = norm_back(d_hidden * gain_ref[...], normed, inverse_ref[rows, 0:1])
        dz_one_ref[rows] = dz_one
        low_ref[rows] = dz_one.astype(B16)
        sum_ref[0:1] += col_sum(d_hidden * normed)
        sum_ref[1:2] += col_sum(d_hidden)
        sum_ref[2:3] += col_sum(dz_one)
        sum_ref[3:4] += col_sum(dz_one * flag_ref[rows, 0:1])
        d_att_ref[rows] = dot(low_ref[rows], w_ref[:, 3 * width :]).astype(B16)
    mask = two_heads(slots)

    def chain_step(chain, carry):
        rows = pl.ds(pl.multiple_of(chain * slots, slots), slots)
        for pair in range(width // (2 * HEAD)):
            lanes = 2 * HEAD * pair
            query = qkv_ref[rows, lanes : lanes + 2 * HEAD]
            key = qkv_ref[rows, width + lanes : width + lanes + 2 * HEAD]
            value = qkv_ref[rows, 2 * width + lanes : 2 * width + lanes + 2 * HEAD]
            d_att = d_att_ref[rows, lanes : lanes + 2 * HEAD]
            prob = prob_ref[rows, 2 * slots * pair : 2 * slots * (pair + 1)]
            d_prob = dot_t(d_att, doubled(value, mask))
            weights = prob.astype(F32)
            products = weights * d_prob
            lows = []
            for head in range(2):
                half = slice(head * slots, (head + 1) * slots)
                total = jnp.sum(products[:, half], axis=-1, keepdims=True)
                lows.append((products[:, half] - weights[:, half] * total).astype(B16))
            low = jnp.concatenate(lows, axis=1)
            d_query = dot(low, doubled(key, mask)) * (HEAD**-0.5)
            tall = jnp.concatenate(lows, axis=0)
            d_key = t_dot(tall, doubled(query, mask)) * (HEAD**-0.5)
            tall = jnp.concatenate([prob[:, :slots], prob[:, slots:]], axis=0)
            d_value = t_dot(tall, doubled(d_att, mask))
            d_qkv_ref[rows, lanes : lanes + 2 * HEAD] = d_query.astype(B16)
            d_qkv_ref[rows, width + lanes : width + lanes + 2 * HEAD] = d_key.astype(B16)
            d_qkv_ref[rows, 2 * width + lanes : 2 * width + lanes + 2 * HEAD] = d_value.astype(B16)
        return carry

    lax.fori_loop(0, count // slots, chain_step, 0, unroll=UNROLL)
    for rows in chunks(count):
        sum_qkv_ref[0:1] += col_sum(d_qkv_ref[rows].astype(F32))
        part = dot_t(d_qkv_ref[rows], w_ref[:, : 3 * width]).astype(B16)
        part_ref[rows] = part
        sum_ref[4:5] += col_sum(part.astype(F32) * flag_ref[rows, 0:1])


def attend_back(chain_count, dz_two, own, other, normed, inverse, gain, flag, qkv, prob, w_a):
    shape = normed.shape
    heads = qkv.shape[1] // 3
    shapes = [
        (shape, F32),
        (shape, B16),
        (qkv.shape, B16),
        (shape, B16),
        ((8, shape[1]), F32),
        ((8, 3 * heads), F32),
    ]
    operands = [*dz_two, own, other, normed, inverse, gain, flag, qkv, prob, w_a]
    body = functools.partial(attend_back_body, shape[0] // chain_count)
    return call(body, "attend_back", shapes, operands, [((shape[0], heads), B16)])


def join_body(one_ref, other_ref, two_a_ref, two_b_ref, up_ref, qkv_ref, out_ref):
    width = one_ref.shape[1]
    heads = qkv_ref.shape[1] // 3
    rows = out_ref.shape[1]
    out_ref[...] = jnp.zeros_like(out_ref)

    def put(start, values):
        for k in range(values.shape[1] // 128):
            place = (start + 128 * k) // 128
            chunk = values[:, 128 * k : 128 * (k + 1)]
            out_ref[place // rows, place % rows : place % rows + 1] = chunk

    put(0, one_ref[3:4] + (one_ref[4:5] + other_ref[4:5]))
    for k in range(3):
        put((1 + k) * width, one_ref[k : k + 1])
        put((4 + k) * width, two_a_ref[k : k + 1] + two_b_ref[k : k + 1])
    put(7 * width, qkv_ref[0:1, :heads])
    put(7 * width + heads, qkv_ref[0:1, 2 * heads :])
    put(7 * width + 2 * heads, up_ref[0:1])


def join(rows, sums_one, sums_other, sums_two, sums_up, sums_qkv):
    width = sums_one.shape[1]
    length = 7 * width + 2 * sums_qkv.shape[1] // 3 + sums_up.shape[1]
    assert length <= 2 * rows * 128
    operands = [sums_one, sums_other, *sums_two, sums_up, sums_qkv]
    return call(join_body, "join", [((2, rows, 128), F32)], operands, limit=4)[0]


def last_body(dz_ref, own_ref, other_ref, flag_ref, out_a_ref, out_b_ref, tokens_ref, out_ref):
    for rows in chunks(dz_ref.shape[0]):
        total = dz_ref[rows] + (own_ref[rows].astype(F32) + other_ref[rows].astype(F32))
        tokens_ref[rows] = jnp.where(flag_ref[rows, 0:1] > 0.0, 0.0, total)
        out_ref[rows] = rows_in((out_a_ref, out_b_ref), rows)


def last(dz_one, own, other, flag, results):
    shapes = [(dz_one.shape, F32), (dz_one.shape, B16)]
    return call(last_body, "last", shapes, [dz_one, own, other, flag, *results])


def add_late_body(x_ref, y_ref, from_x_ref, from_y_ref, out_x_ref, out_y_ref):
    out_x_ref[...] = (x_ref[...].astype(F32) + from_y_ref[:2].astype(F32)).astype(B16)
    out_y_ref[...] = (y_ref[...].astype(F32) + from_x_ref[:2].astype(F32)).astype(B16)


def add_own_body(own_ref, from_x_ref, from_y_ref, late_x_ref, late_y_ref, near_ref, mid_ref):
    near_ref[...] = (
        own_ref[:2].astype(F32) + from_x_ref[2:].astype(F32) + late_y_ref[...].astype(F32)
    )
    mid_ref[...] = (
        own_ref[2:].astype(F32) + late_x_ref[...].astype(F32) + from_y_ref[2:].astype(F32)
    ).astype(B16)


def add_mid_body(near_ref, mid_ref, own_ref, far_ref):
    own_ref[...] = near_ref[0] + mid_ref[0].astype(F32)
    far_ref[...] = (near_ref[1] + mid_ref[1].astype(F32)).astype(B16)


def late_vector_body(x_ref, y_ref, from_x_ref, from_y_ref, v_ref, out_x_ref, out_y_ref, vector_ref):
    cols = x_ref.shape[2]
    out_x_ref[...] = (x_ref[...].astype(F32) + from_y_ref[:2].astype(F32)).astype(B16)
    out_y_ref[:, :, :cols] = (y_ref[...].astype(F32) + from_x_ref[:2, :, :cols].astype(F32)).astype(B16)
    vector = (v_ref[...].astype(F32) + from_x_ref[:2, :, cols:].astype(F32)).astype(B16)
    out_y_ref[:, :, cols:] = vector
    vector_ref[...] = vector


def own_vector_body(own_ref, from_x_ref, from_y_ref, late_x_ref, late_y_ref, v_ref, near_ref, mid_ref, vector_ref):
    cols = own_ref.shape[2]
    near_ref[...] = (
        own_ref[:2].astype(F32)
        + from_x_ref[2:, :, :cols].astype(F32)
        + late_y_ref[:, :, :cols].astype(F32)
    )
    mid_ref[:, :, :cols] = (
        own_ref[2:].astype(F32) + late_x_ref[...].astype(F32) + from_y_ref[2:].astype(F32)
    ).astype(B16)
    vector = (v_ref[...].astype(F32) + late_y_ref[:, :, cols:].astype(F32)).astype(B16)
    mid_ref[:, :, cols:] = vector
    vector_ref[...] = vector


def mid_vector_body(near_ref, mid_ref, v_ref, own_ref, far_ref, vector_ref):
    cols = own_ref.shape[1]
    own_ref[...] = near_ref[0] + mid_ref[0, :, :cols].astype(F32)
    far_ref[:, :cols] = (near_ref[1] + mid_ref[1, :, :cols].astype(F32)).astype(B16)
    vector = (v_ref[...].astype(F32) + mid_ref[:, :, cols:].astype(F32)).astype(B16)
    for k in range(2):
        far_ref[:, cols + 128 * k : cols + 128 * (k + 1)] = vector[k]
    vector_ref[...] = vector


def far_vector_body(own_ref, far_ref, v_ref, *outs):
    rows, cols = own_ref.shape
    part = cols // 4
    for k in range(4):
        lanes = slice(k * part, (k + 1) * part)
        outs[k][...] = own_ref[:, lanes] + far_ref[:, lanes].astype(F32)
    place = 0
    joined = [
        v_ref[k].astype(F32) + far_ref[:, cols + 128 * k : cols + 128 * (k + 1)].astype(F32) for k in range(2)
    ]
    for out_ref in outs[4:]:
        for k in range(out_ref.shape[0]):
            out_ref[k : k + 1] = joined[place // rows][place % rows : place % rows + 1]
            place += 1


def late_vector(late_x, late_y, from_x, from_y, vector):
    rows, cols = late_x.shape[1:]
    shapes = [(late_x.shape, B16), ((2, rows, cols + 128), B16), (vector.shape, B16)]
    operands = [late_x, late_y, from_x, from_y, vector]
    return call(late_vector_body, "late_vector", shapes, operands, limit=8)


def own_vector(own, from_x, from_y, late_x, late_y, vector):
    rows, cols = own.shape[1:]
    shapes = [((2, rows, cols), F32), ((2, rows, cols + 128), B16), (vector.shape, B16)]
    operands = [own, from_x, from_y, late_x, late_y, vector]
    return call(own_vector_body, "own_vector", shapes, operands, limit=8)


def mid_vector(near, mid, vector):
    rows, cols = near.shape[1:]
    shapes = [((rows, cols), F32), ((rows, cols + 256), B16), (vector.shape, B16)]
    return call(mid_vector_body, "mid_vector", shapes, [near, mid, vector], limit=8)


def far_vector(own, far, vector, sizes):
    rows, cols = own.shape
    shapes = [((rows, cols // 4), F32)] * 4 + [((size // 128, 128), F32) for size in sizes]
    outs = call(far_vector_body, "far_vector", shapes, [own, far, vector], limit=8)
    return outs[:4], [member.reshape(-1) for member in outs[4:]]


def add_late(late_x, late_y, from_x, from_y):
    shape = (late_x.shape, B16)
    return call(add_late_body, "add_late", [shape, shape], [late_x, late_y, from_x, from_y], limit=8)


def add_own(own, from_x, from_y, late_x, late_y):
    shapes = [(late_x.shape, F32), (late_x.shape, B16)]
    return call(add_own_body, "add_own", shapes, [own, from_x, from_y, late_x, late_y], limit=8)


def add_mid(near, mid):
    shapes = [(near.shape[1:], F32), (near.shape[1:], B16)]
    return call(add_mid_body, "add_mid", shapes, [near, mid], limit=8)


def per_device(dp_size, tokens, masked, lengths, mask_vector, w_query, b_query, w_key, w_value,
               b_value, w_out, b_out, gain_one, shift_one, w_up, b_up, w_down, b_down, gain_two,
               shift_two, grad_out):
    head_cols = w_query.shape[1]
    width = tokens.shape[1]
    fast = dp_size == BLOCKS and w_query.shape[0] % 16 == 0
    me = lax.axis_index("dp").astype(jnp.int32).reshape(1)
    if not fast:
        me = jnp.zeros_like(me)

    (b_query, b_value, b_out, gain_one, shift_one, b_up, b_down, gain_two, shift_two) = (
        member.astype(F32)
        for member in (b_query, b_value, b_out, gain_one, shift_one, b_up, b_down, gain_two, shift_two)
    )
    is_masked = (masked == 1)[:, None]
    flag = jnp.broadcast_to(is_masked, (masked.shape[0], 128)).astype(F32)
    in_low = jnp.where(is_masked, mask_vector[None, :], tokens)
    bias_qkv = jnp.concatenate([b_query, jnp.zeros_like(b_query), b_value])[None, :]
    vectors_one = jnp.stack([b_out, gain_one, shift_one])
    vectors_two = jnp.stack([gain_one, shift_one, b_down, gain_two, shift_two])
    b_up, gain_one = b_up[None, :], gain_one[None, :]

    a = jnp.concatenate([w_query, w_key, w_value, w_out.T], axis=1)
    c = w_up
    d = w_down.T
    if fast:
        az = swap(a, 12)
        az, me, flag, in_low, bias_qkv, vectors_one, vectors_two, b_up, gain_one = tie(
            az, me, flag, in_low, bias_qkv, vectors_one, vectors_two, b_up, gain_one
        )
        an = jnp.stack([a, az])
        anx, any_, am = swap(an, 1), swap(an, 2), swap(an, 4)
        anx, any_, am, an, c = tie(anx, any_, am, an, c)
        amx, amy, cz = swap(am, 1), swap(am, 2), swap(c, 12)
        amx, amy, cz, anx, c, d = tie(amx, amy, cz, anx, c, d)
        cn = jnp.stack([c, cz])
        amd, and_, cm = swap(amy, 1), swap(anx, 2), swap(cn, 4)
        cnx, cny, dz = swap(cn, 1), swap(cn, 2), swap(after(d, cm), 12)
        amd, and_, cm, cnx, cny = tie(amd, and_, cm, cnx, cny)
        dn = jnp.stack([d, dz])
        pieces_a = [an, am, anx, amx, any_, amy, and_, amd]
        cmx, cnd, dm = swap(cm, 1), swap(cnx, 2), swap(dn, 4)
        dnx, dny = swap(dn, 1), swap(dn, 2)
    else:
        a, c, d = (lax.all_gather(piece, "dp", axis=0, tiled=True) for piece in (a, c, d))
        pieces_a, pieces_c, pieces_d = as_pieces(a), as_pieces(c), as_pieces(d)
    w_a, qkv, prob, attended, part = attend(me, lengths, in_low, bias_qkv, pieces_a)
    if fast:
        cmx, cnd, dm, dnx, dny, cm, part = tie(cmx, cnd, dm, dnx, dny, cm, part)
        cmy, dnd, cmd = swap(cm, 2), swap(dny, 1), swap(cnd, 4)
    other = pair_swap(part)
    if fast:
        cmy, dnd, cmd, dm, other, part = tie(cmy, dnd, cmd, dm, other, part)
        pieces_c = [cn, cm, cnx, cmx, cny, cmy, cnd, cmd]
        dmx, dmy, dmd = swap(dm, 1), swap(dm, 2), swap(dnd, 4)
    w_u, normed_one, inverse_one, hidden_low, act_low, slope = up(
        me, in_low, part, other, vectors_one, b_up, pieces_c
    )
    if fast:
        dmx, dmy, dmd, act_low = tie(dmx, dmy, dmd, act_low)
        pieces_d = [dn, dm, dnx, dmx, dny, dmy, dnd, dmd]
    w_d, *parts = down(me, act_low, pieces_d)
    halves = [
        second_norm(index * part.shape[0], normed_one, part, pair_swap(part), grad_out, vectors_two)
        for index, part in enumerate(parts)
    ]
    results, dz_two, dz_two_low, sums_two = zip(*halves)
    dx, dy, dxl, dyl, do = weight_grad(me, [dz_two_low], [act_low])
    if fast:
        dx, dy, dxl, dyl, dz_two_low = tie(dx, dy, dxl, dyl, dz_two_low)
        dxr, dyr = swap(dx, 1), swap(dy, 2)
    d_pre_low, part, sums_up = hidden_back(dz_two_low, slope, w_d, w_u)
    cx, cy, cxl, cyl, co = weight_grad(me, [[hidden_low]], [d_pre_low])
    if fast:
        dxr, dyr, part, cx, cy = tie(dxr, dyr, part, cx, cy)
        cxr, cyr = swap(cx, 1), swap(cy, 2)
        dxl, dyl = add_late(dxl, dyl, dxr, dyr)
        dxlr, dylr = swap(dxl, 1), swap(dyl, 2)
    other = pair_swap(part)
    dz_one, dz_one_low, d_qkv, part, sums_one, sums_qkv = attend_back(
        lengths.shape[0], dz_two, part, other, normed_one, inverse_one, gain_one, flag, qkv, prob, w_a
    )
    if fast:
        cxr, cyr, dxlr, dylr, part, d_qkv, dz_one_low = tie(cxr, cyr, dxlr, dylr, part, d_qkv, dz_one_low)
        cxl, cyl = add_late(cxl, cyl, cxr, cyr)
        cxlr, cylr = swap(cxl, 1), swap(cyl, 2)
        d_near, d_mid = add_own(do, dxr, dyr, dxlr, dylr)
        d_midr = swap(d_mid, 4)
    sums_other = pair_swap(sums_one)
    joined = join(width // BLOCKS, sums_one, sums_other, sums_two, sums_up, sums_qkv)
    vector = joined.astype(B16) if fast else None
    ax, ay, axl, ayl, ao = weight_grad(me, [[in_low], [dz_one_low]], [d_qkv, attended], vector)
    if fast:
        cxlr, cylr, d_midr, ax, ay, part = tie(cxlr, cylr, d_midr, ax, ay, part)
        axr, ayr = swap(ax, 1), swap(ay, 2)
        c_near, c_mid = add_own(co, cxr, cyr, cxlr, cylr)
        d_near, d_far = add_mid(d_near, d_midr)
        c_midr, d_farr = swap(c_mid, 4), swap(d_far, 12)
    other = pair_swap(part)
    d_tokens, result = last(dz_one, part, other, flag, results)
    sizes = [width] * 7 + [head_cols] * 2 + [w_up.shape[1]]
    if fast:
        axr, ayr, c_midr, d_farr, d_tokens, result = tie(axr, ayr, c_midr, d_farr, d_tokens, result)
        axl, ayl, vector = late_vector(axl, ayl, axr, ayr, vector)
        axlr, aylr = swap(axl, 1), swap(ayl, 2)
        c_near, c_far = add_mid(c_near, c_midr)
        c_farr = swap(c_far, 12)
        axlr, aylr, c_farr = tie(axlr, aylr, c_farr)
        a_near, a_mid, vector = own_vector(ao, axr, ayr, axlr, aylr, vector)
        a_midr = swap(a_mid, 4)
        d_w_down_t = d_near + d_farr.astype(F32)
        a_midr, d_w_down_t = tie(a_midr, d_w_down_t)
        a_near, a_far, vector = mid_vector(a_near, a_midr, vector)
        a_farr = swap(a_far, 12)
        d_w_up = c_near + c_farr.astype(F32)
        d_wa, summed = far_vector(a_near, a_farr, vector, sizes)
    else:
        full = []
        for parts in ((ax, ay, axl, ayl, ao), (cx, cy, cxl, cyl, co), (dx, dy, dxl, dyl, do)):
            blocks = [None] * BLOCKS
            for member, offsets in zip(parts, ORDER):
                for k, offset in enumerate(offsets):
                    blocks[offset] = member[k]
            full.append(jnp.concatenate(blocks).astype(F32))
        joined = lax.psum(joined, "dp")
        d_wa, d_w_up, d_w_down_t = (
            lax.psum_scatter(member, "dp", scatter_dimension=0, tiled=True) for member in full
        )
        d_wa = [d_wa[:, k * head_cols : (k + 1) * head_cols] for k in range(4)]
        joined = joined.reshape(-1)
        summed = []
        start = 0
        for size in sizes:
            summed.append(joined[start : start + size])
            start += size
    return (
        result,
        d_tokens,
        summed[0],
        d_wa[0],
        summed[7],
        d_wa[1],
        d_wa[2],
        summed[8],
        d_wa[3].T,
        summed[3],
        summed[1],
        summed[2],
        d_w_up,
        summed[9],
        d_w_down_t.T,
        summed[6],
        summed[4],
        summed[5],
    )


def solution(mesh):
    rows, flat, both = P("dp", None), P(), P("dp", "mp")
    return jax.shard_map(
        functools.partial(per_device, mesh.shape["dp"]),
        mesh=mesh,
        in_specs=(rows, P("dp"), P("dp"), flat, both, P("mp"), both, both, P("mp"), P("mp", "dp"),
                  flat, flat, flat, both, P("mp"), P("mp", "dp"), flat, flat, flat, rows),
        out_specs=(rows, rows, flat, both, P("mp"), both, both, P("mp"), P("mp", "dp"), flat, flat,
                   flat, both, P("mp"), P("mp", "dp"), flat, flat, flat),
        check_vma=False,
    )
```

```python
import functools

import jax
import jax.numpy as jnp
from jax import lax
from jax.experimental import pallas as pl
from jax.experimental.pallas import tpu as pltpu
from jax.sharding import PartitionSpec as P

HEAD = 64
NORM_EPS = 1e-05
F32 = jnp.float32
B16 = jnp.bfloat16
MIB = 1 << 20

BLOCKS = 16
NEAR = (0, 12)
MID = (4, 8)


def swap(values, bit):
    return lax.ppermute(values, "dp", [(i, i ^ bit) for i in range(BLOCKS)])


def tie(*values):
    return lax.optimization_barrier(values)


def after(value, *earlier):
    return tie(value, *earlier)[0]


def pair_swap(partial):
    return lax.ppermute(partial, "mp", [(0, 1), (1, 0)])


def as_pieces(full):
    rows = full.shape[0] // BLOCKS
    blocks = full.reshape(BLOCKS, rows, full.shape[1])
    return [
        jnp.stack([blocks[offset + bits[0]], blocks[offset + bits[1]]])
        for offset in range(4)
        for bits in (NEAR, MID)
    ]


SMEM_SPEC = pl.BlockSpec(memory_space=pltpu.SMEM)
VMEM_SPEC = pl.BlockSpec(memory_space=pltpu.VMEM)
CHUNK = 256
UNROLL = 8
LIGHT = pl.CostEstimate(flops=1, bytes_accessed=1, transcendentals=0)


def call(body, name, shapes, operands, scratch=(), limit=16):
    return pl.pallas_call(
        body,
        in_specs=[
            SMEM_SPEC if member.dtype == jnp.int32 and member.ndim == 1 else VMEM_SPEC
            for member in operands
        ],
        out_specs=[VMEM_SPEC] * len(shapes),
        out_shape=[jax.ShapeDtypeStruct(shape, dtype) for shape, dtype in shapes],
        scratch_shapes=[pltpu.VMEM(shape, dtype) for shape, dtype in scratch],
        compiler_params=pltpu.CompilerParams(vmem_limit_bytes=limit * MIB),
        cost_estimate=LIGHT,
        name=name,
    )(*operands)


def chunks(count):
    return [slice(start, start + CHUNK) for start in range(0, count, CHUNK)]


PAIRS = [(q + bits[k], 2 * q + m, k) for q in range(4) for m, bits in enumerate((NEAR, MID)) for k in range(2)]


def fill(me, pieces, full_ref):
    rows = pieces[0].shape[1]
    for offset, piece, index in PAIRS:
        block = me ^ offset
        full_ref[pl.ds(pl.multiple_of(block * rows, rows), rows), :] = pieces[piece][index]


def dot(left, right):
    return jnp.dot(left, right, preferred_element_type=F32)


def dot_t(left, right):
    return lax.dot_general(left, right, (((1,), (1,)), ((), ())), preferred_element_type=F32)


def t_dot(left, right):
    return lax.dot_general(left, right, (((0,), (0,)), ((), ())), preferred_element_type=F32)


def row_mean(values):
    return jnp.mean(values, axis=-1, keepdims=True)


def normalize(values):
    centred = values - row_mean(values)
    inverse = lax.rsqrt(row_mean(centred * centred) + NORM_EPS)
    return centred * inverse, inverse


def col_sum(values):
    return jnp.sum(values, axis=0, keepdims=True)


def norm_back(scaled, normed, inverse):
    return inverse * (scaled - row_mean(scaled) - normed * row_mean(scaled * normed))


def two_heads(slots):
    row = lax.broadcasted_iota(jnp.int32, (2 * slots, 2 * HEAD), 0) // slots
    lane = lax.broadcasted_iota(jnp.int32, (2 * slots, 2 * HEAD), 1) // HEAD
    return (row == lane).astype(F32).astype(B16)


def doubled(values, mask):
    return jnp.concatenate([values, values], axis=0) * mask


def attend_body(slots, me_ref, len_ref, in_ref, bias_ref, *rest):
    pieces, (w_ref, qkv_ref, prob_ref, att_ref, part_ref) = rest[:-5], rest[-5:]
    count, width = att_ref.shape
    fill(me_ref[0], pieces, w_ref)
    for rows in chunks(count):
        qkv_ref[rows] = (dot(in_ref[rows], w_ref[:, : 3 * width]) + bias_ref[...]).astype(B16)
    mask = two_heads(slots)
    key_slot = lax.broadcasted_iota(jnp.int32, (slots, slots), 1)

    def chain_step(chain, carry):
        valid = key_slot < len_ref[chain]
        rows = pl.ds(pl.multiple_of(chain * slots, slots), slots)
        for pair in range(width // (2 * HEAD)):
            lanes = 2 * HEAD * pair
            query = qkv_ref[rows, lanes : lanes + 2 * HEAD]
            key = qkv_ref[rows, width + lanes : width + lanes + 2 * HEAD]
            value = qkv_ref[rows, 2 * width + lanes : 2 * width + lanes + 2 * HEAD]
            scores = dot_t(query * (HEAD**-0.5), doubled(key, mask))
            probs = []
            for head in range(2):
                part = jnp.where(valid, scores[:, head * slots : (head + 1) * slots], -1e30)
                terms = jnp.exp(part - jnp.max(part, axis=-1, keepdims=True))
                probs.append((terms / jnp.sum(terms, axis=-1, keepdims=True)).astype(B16))
            prob = jnp.concatenate(probs, axis=1)
            prob_ref[rows, 2 * slots * pair : 2 * slots * (pair + 1)] = prob
            att_ref[rows, lanes : lanes + 2 * HEAD] = dot(prob, doubled(value, mask)).astype(B16)
        return carry

    lax.fori_loop(0, count // slots, chain_step, 0, unroll=UNROLL)
    for rows in chunks(count):
        part_ref[rows] = dot_t(att_ref[rows], w_ref[:, 3 * width :]).astype(B16)


def attend(me, lengths, in_low, bias, pieces):
    count, width = in_low.shape
    heads = bias.shape[1] // 3
    slots = count // lengths.shape[0]
    shapes = [
        ((width, 4 * heads), B16),
        ((count, 3 * heads), B16),
        ((count, heads // HEAD * slots), B16),
        ((count, heads), B16),
        ((count, width), B16),
    ]
    body = functools.partial(attend_body, slots)
    return call(body, "attend", shapes, [me, lengths, in_low, bias, *pieces])


def up_body(me_ref, in_ref, own_ref, other_ref, vec_ref, bias_ref, *rest):
    pieces, (w_ref, normed_ref, inverse_ref, low_ref, act_ref, slope_ref) = rest[:-6], rest[-6:]
    fill(me_ref[0], pieces, w_ref)
    vectors = vec_ref[...]
    for rows in chunks(in_ref.shape[0]):
        attn = own_ref[rows].astype(F32) + other_ref[rows].astype(F32) + vectors[0:1]
        normed, inverse = normalize(in_ref[rows].astype(F32) + attn)
        normed_ref[rows] = normed
        inverse_ref[rows] = jnp.broadcast_to(inverse, (CHUNK, inverse_ref.shape[1]))
        low_ref[rows] = (normed * vectors[1:2] + vectors[2:3]).astype(B16)
        pre = dot(low_ref[rows], w_ref[...]) + bias_ref[...]
        cdf = 0.5 + 0.5 * lax.erf(pre * (2.0**-0.5))
        act_ref[rows] = (pre * cdf).astype(B16)
        density = jnp.exp(pre * pre * -0.5) * 0.3989422804014327
        slope_ref[rows] = (cdf + pre * density).astype(B16)


def up(me, in_low, own, other, vectors, bias, pieces):
    count, width = in_low.shape
    units = bias.shape[1]
    shapes = [
        ((width, units), B16),
        ((count, width), F32),
        ((count, 128), F32),
        ((count, width), B16),
        ((count, units), B16),
        ((count, units), B16),
    ]
    return call(up_body, "up", shapes, [me, in_low, own, other, vectors, bias, *pieces])


def down_body(me_ref, act_ref, *rest):
    pieces, (w_ref, part_ref) = rest[:-2], rest[-2:]
    fill(me_ref[0], pieces, w_ref)
    for rows in chunks(part_ref.shape[0]):
        part_ref[rows] = dot_t(act_ref[rows], w_ref[...]).astype(B16)


def down_rest_body(act_ref, w_ref, part_ref):
    half = part_ref.shape[0]
    for rows in chunks(half):
        part_ref[rows] = dot_t(act_ref[half + rows.start : half + rows.stop], w_ref[...]).astype(B16)


def down(me, act, pieces):
    count, units = act.shape
    width = BLOCKS * pieces[0].shape[1]
    half = ((count // 2, width), B16)
    w_down_t, first = call(down_body, "down", [((width, units), B16), half], [me, act, *pieces])
    (second,) = call(down_rest_body, "down_rest", [half], [act, w_down_t])
    return w_down_t, first, second


def second_norm_body(start, normed_ref, own_ref, other_ref, grad_ref, vec_ref, out_ref, dz_ref, low_ref, sum_ref):
    vectors = vec_ref[...]
    sum_ref[...] = jnp.zeros_like(sum_ref)
    for rows in chunks(own_ref.shape[0]):
        there = slice(start + rows.start, start + rows.stop)
        hidden = normed_ref[there] * vectors[0:1] + vectors[1:2]
        ffn = own_ref[rows].astype(F32) + other_ref[rows].astype(F32) + vectors[2:3]
        normed, inverse = normalize(hidden + ffn)
        out_ref[rows] = (normed * vectors[3:4] + vectors[4:5]).astype(B16)
        grad = grad_ref[there].astype(F32)
        dz = norm_back(grad * vectors[3:4], normed, inverse)
        dz_ref[rows] = dz
        low_ref[rows] = dz.astype(B16)
        sum_ref[0:1] += col_sum(grad * normed)
        sum_ref[1:2] += col_sum(grad)
        sum_ref[2:3] += col_sum(dz)


def second_norm(start, normed, own, other, grad, vectors):
    shape = own.shape
    shapes = [(shape, B16), (shape, F32), (shape, B16), ((8, shape[1]), F32)]
    body = functools.partial(second_norm_body, start)
    return call(body, "second_norm", shapes, [normed, own, other, grad, vectors])


def rows_in(halves, rows):
    size = halves[0].shape[0]
    half = halves[rows.start // size]
    return half[rows.start % size : rows.start % size + rows.stop - rows.start]


ORDER = (
    (3, 15, 1, 13),
    (7, 11, 6, 10),
    (5, 9),
    (2, 14),
    (0, 12, 4, 8),
)


def weight_grad(me, lefts, rights, groups=ORDER, vector=None, turned=None):
    count = rights[0].shape[0]
    width = lefts[-1][0].shape[1] if turned is None else turned.shape[0]
    tile = 384 if all(right.shape[1] % 384 == 0 for right in rights) else 128
    total = sum(right.shape[1] for right in rights)
    rows = width // BLOCKS
    n = len(rights)
    flat = [half for left in lefts for half in left] if turned is None else [turned]
    wide = [] if vector is None else [vector]
    keep = turned is None and len(groups) < len(ORDER)
    wanted = [offset for offsets in groups for offset in offsets]

    def body(me_ref, *refs):
        left_refs, right_refs = list(refs[: len(flat)]), refs[len(flat) : len(flat) + n]
        outs = refs[len(flat) + n + len(wide) :]
        placed_ref = outs[-1]
        if wide:
            outs[0][0:2, :, total:] = refs[len(flat) + n][...]
            outs[0][2:4, :, total:] = jnp.zeros((2, rows, 128), B16)
        at = 0
        for index, right_ref in enumerate(right_refs):
            turned_ref = left_refs[0] if turned is not None else outs[-2]
            if turned is None:
                start = 0
                for _ in lefts[index]:
                    half_ref = left_refs.pop(0)
                    turned_ref[:, start : start + half_ref.shape[0]] = half_ref[...].T
                    start += half_ref.shape[0]
            for k, offset in enumerate(wanted):
                place = pl.multiple_of((me_ref[0] ^ offset) * rows, rows)
                placed_ref[k * rows : (k + 1) * rows] = turned_ref[pl.ds(place, rows), :]
            for start in range(0, right_ref.shape[1], tile):
                product = dot(placed_ref[...], right_ref[:, start : start + tile]).astype(B16)
                first = 0
                for out_ref, offsets in zip(outs, groups):
                    for k in range(len(offsets)):
                        out_ref[k, :, at : at + tile] = product[first : first + rows]
                        first += rows
                at += tile

    shapes = [((len(offsets), rows, total), B16) for offsets in groups]
    shapes[0] = ((len(groups[0]), rows, total + 128 * len(wide)), B16)
    held = ((width, count), B16)
    shapes += [held] * keep
    scratch = [held] * (turned is None and not keep) + [((len(wanted) * rows, count), B16)]
    return call(body, "weight_grad", shapes, [me, *flat, *rights, *wide], scratch)


def hidden_back_body(low_a_ref, low_b_ref, slope_ref, down_ref, up_ref, pre_ref, part_ref, sum_ref):
    sum_ref[...] = jnp.zeros_like(sum_ref)
    for rows in chunks(slope_ref.shape[0]):
        low = rows_in((low_a_ref, low_b_ref), rows)
        d_pre = dot(low, down_ref[...]) * slope_ref[rows].astype(F32)
        sum_ref[0:1] += col_sum(d_pre)
        pre_ref[rows] = d_pre.astype(B16)
        part_ref[rows] = dot_t(pre_ref[rows], up_ref[...]).astype(B16)


def hidden_back(lows, slope, w_down_t, w_up):
    count, units = slope.shape
    shapes = [((count, units), B16), ((count, w_up.shape[0]), B16), ((8, units), F32)]
    return call(hidden_back_body, "hidden_back", shapes, [*lows, slope, w_down_t, w_up])


def attend_back_body(slots, dz_a_ref, dz_b_ref, own_ref, other_ref, normed_ref, inverse_ref, gain_ref,
                     flag_ref, qkv_ref, prob_ref, w_ref, dz_one_ref, low_ref, d_qkv_ref, part_ref, sum_ref,
                     sum_qkv_ref, d_att_ref):
    count, width = d_att_ref.shape
    sum_ref[...] = jnp.zeros_like(sum_ref)
    sum_qkv_ref[...] = jnp.zeros_like(sum_qkv_ref)
    for rows in chunks(count):
        normed = normed_ref[rows]
        both = own_ref[rows].astype(F32) + other_ref[rows].astype(F32)
        d_hidden = rows_in((dz_a_ref, dz_b_ref), rows) + both
        dz_one = norm_back(d_hidden * gain_ref[...], normed, inverse_ref[rows, 0:1])
        dz_one_ref[rows] = dz_one
        low_ref[rows] = dz_one.astype(B16)
        sum_ref[0:1] += col_sum(d_hidden * normed)
        sum_ref[1:2] += col_sum(d_hidden)
        sum_ref[2:3] += col_sum(dz_one)
        sum_ref[3:4] += col_sum(dz_one * flag_ref[rows, 0:1])
        d_att_ref[rows] = dot(low_ref[rows], w_ref[:, 3 * width :]).astype(B16)
    mask = two_heads(slots)

    def chain_step(chain, carry):
        rows = pl.ds(pl.multiple_of(chain * slots, slots), slots)
        for pair in range(width // (2 * HEAD)):
            lanes = 2 * HEAD * pair
            query = qkv_ref[rows, lanes : lanes + 2 * HEAD]
            key = qkv_ref[rows, width + lanes : width + lanes + 2 * HEAD]
            value = qkv_ref[rows, 2 * width + lanes : 2 * width + lanes + 2 * HEAD]
            d_att = d_att_ref[rows, lanes : lanes + 2 * HEAD]
            prob = prob_ref[rows, 2 * slots * pair : 2 * slots * (pair + 1)]
            d_prob = dot_t(d_att, doubled(value, mask))
            weights = prob.astype(F32)
            products = weights * d_prob
            lows = []
            for head in range(2):
                half = slice(head * slots, (head + 1) * slots)
                total = jnp.sum(products[:, half], axis=-1, keepdims=True)
                lows.append((products[:, half] - weights[:, half] * total).astype(B16))
            low = jnp.concatenate(lows, axis=1)
            d_query = dot(low, doubled(key, mask)) * (HEAD**-0.5)
            tall = jnp.concatenate(lows, axis=0)
            d_key = t_dot(tall, doubled(query, mask)) * (HEAD**-0.5)
            tall = jnp.concatenate([prob[:, :slots], prob[:, slots:]], axis=0)
            d_value = t_dot(tall, doubled(d_att, mask))
            d_qkv_ref[rows, lanes : lanes + 2 * HEAD] = d_query.astype(B16)
            d_qkv_ref[rows, width + lanes : width + lanes + 2 * HEAD] = d_key.astype(B16)
            d_qkv_ref[rows, 2 * width + lanes : 2 * width + lanes + 2 * HEAD] = d_value.astype(B16)
        return carry

    lax.fori_loop(0, count // slots, chain_step, 0, unroll=UNROLL)
    for rows in chunks(count):
        sum_qkv_ref[0:1] += col_sum(d_qkv_ref[rows].astype(F32))
        part = dot_t(d_qkv_ref[rows], w_ref[:, : 3 * width]).astype(B16)
        part_ref[rows] = part
        sum_ref[4:5] += col_sum(part.astype(F32) * flag_ref[rows, 0:1])


def attend_back(chain_count, dz_two, own, other, normed, inverse, gain, flag, qkv, prob, w_a):
    shape = normed.shape
    heads = qkv.shape[1] // 3
    shapes = [
        (shape, F32),
        (shape, B16),
        (qkv.shape, B16),
        (shape, B16),
        ((8, shape[1]), F32),
        ((8, 3 * heads), F32),
    ]
    operands = [*dz_two, own, other, normed, inverse, gain, flag, qkv, prob, w_a]
    body = functools.partial(attend_back_body, shape[0] // chain_count)
    return call(body, "attend_back", shapes, operands, [((shape[0], heads), B16)])


def join_body(one_ref, other_ref, two_a_ref, two_b_ref, up_ref, qkv_ref, out_ref):
    width = one_ref.shape[1]
    heads = qkv_ref.shape[1] // 3
    rows = out_ref.shape[1]
    out_ref[...] = jnp.zeros_like(out_ref)

    def put(start, values):
        for k in range(values.shape[1] // 128):
            place = (start + 128 * k) // 128
            chunk = values[:, 128 * k : 128 * (k + 1)]
            out_ref[place // rows, place % rows : place % rows + 1] = chunk

    put(0, one_ref[3:4] + (one_ref[4:5] + other_ref[4:5]))
    for k in range(3):
        put((1 + k) * width, one_ref[k : k + 1])
        put((4 + k) * width, two_a_ref[k : k + 1] + two_b_ref[k : k + 1])
    put(7 * width, qkv_ref[0:1, :heads])
    put(7 * width + heads, qkv_ref[0:1, 2 * heads :])
    put(7 * width + 2 * heads, up_ref[0:1])


def join(rows, sums_one, sums_other, sums_two, sums_up, sums_qkv):
    width = sums_one.shape[1]
    length = 7 * width + 2 * sums_qkv.shape[1] // 3 + sums_up.shape[1]
    assert length <= 2 * rows * 128
    operands = [sums_one, sums_other, *sums_two, sums_up, sums_qkv]
    return call(join_body, "join", [((2, rows, 128), F32)], operands, limit=4)[0]


def last_body(dz_ref, own_ref, other_ref, flag_ref, out_a_ref, out_b_ref, tokens_ref, out_ref):
    for rows in chunks(dz_ref.shape[0]):
        total = dz_ref[rows] + (own_ref[rows].astype(F32) + other_ref[rows].astype(F32))
        tokens_ref[rows] = jnp.where(flag_ref[rows, 0:1] > 0.0, 0.0, total)
        out_ref[rows] = rows_in((out_a_ref, out_b_ref), rows)


def last(dz_one, own, other, flag, results):
    shapes = [(dz_one.shape, F32), (dz_one.shape, B16)]
    return call(last_body, "last", shapes, [dz_one, own, other, flag, *results])


def add_late_body(x_ref, y_ref, from_x_ref, from_y_ref, out_x_ref, out_y_ref):
    out_x_ref[...] = (x_ref[...].astype(F32) + from_y_ref[:2].astype(F32)).astype(B16)
    out_y_ref[...] = (y_ref[...].astype(F32) + from_x_ref[:2].astype(F32)).astype(B16)


def add_own_body(own_ref, from_x_ref, from_y_ref, late_x_ref, late_y_ref, near_ref, mid_ref):
    near_ref[...] = (
        own_ref[:2].astype(F32) + from_x_ref[2:].astype(F32) + late_y_ref[...].astype(F32)
    )
    mid_ref[...] = (
        own_ref[2:].astype(F32) + late_x_ref[...].astype(F32) + from_y_ref[2:].astype(F32)
    ).astype(B16)


def add_mid_body(near_ref, mid_ref, own_ref, far_ref):
    own_ref[...] = near_ref[0] + mid_ref[0].astype(F32)
    far_ref[...] = (near_ref[1] + mid_ref[1].astype(F32)).astype(B16)


def late_vector_body(x_ref, y_ref, from_x_ref, from_y_ref, v_ref, out_x_ref, out_y_ref, vector_ref):
    cols = x_ref.shape[2]
    out_x_ref[...] = (x_ref[...].astype(F32) + from_y_ref[:2].astype(F32)).astype(B16)
    out_y_ref[:, :, :cols] = (y_ref[...].astype(F32) + from_x_ref[:2, :, :cols].astype(F32)).astype(B16)
    vector = (v_ref[...].astype(F32) + from_x_ref[:2, :, cols:].astype(F32)).astype(B16)
    out_y_ref[:, :, cols:] = vector
    vector_ref[...] = vector


def own_vector_body(own_ref, from_x_ref, from_y_ref, late_x_ref, late_y_ref, v_ref, near_ref, mid_ref, vector_ref):
    cols = own_ref.shape[2]
    near_ref[...] = (
        own_ref[:2].astype(F32)
        + from_x_ref[2:, :, :cols].astype(F32)
        + late_y_ref[:, :, :cols].astype(F32)
    )
    mid_ref[:, :, :cols] = (
        own_ref[2:].astype(F32) + late_x_ref[...].astype(F32) + from_y_ref[2:].astype(F32)
    ).astype(B16)
    vector = (v_ref[...].astype(F32) + late_y_ref[:, :, cols:].astype(F32)).astype(B16)
    mid_ref[:, :, cols:] = vector
    vector_ref[...] = vector


def mid_vector_body(near_ref, mid_ref, v_ref, own_ref, far_ref, vector_ref):
    cols = own_ref.shape[1]
    own_ref[...] = near_ref[0] + mid_ref[0, :, :cols].astype(F32)
    far_ref[:, :cols] = (near_ref[1] + mid_ref[1, :, :cols].astype(F32)).astype(B16)
    vector = (v_ref[...].astype(F32) + mid_ref[:, :, cols:].astype(F32)).astype(B16)
    for k in range(2):
        far_ref[:, cols + 128 * k : cols + 128 * (k + 1)] = vector[k]
    vector_ref[...] = vector


def far_vector_body(own_ref, far_ref, v_ref, *outs):
    rows, cols = own_ref.shape
    part = cols // 4
    for k in range(4):
        lanes = slice(k * part, (k + 1) * part)
        outs[k][...] = own_ref[:, lanes] + far_ref[:, lanes].astype(F32)
    place = 0
    joined = [
        v_ref[k].astype(F32) + far_ref[:, cols + 128 * k : cols + 128 * (k + 1)].astype(F32) for k in range(2)
    ]
    for out_ref in outs[4:]:
        for k in range(out_ref.shape[0]):
            out_ref[k : k + 1] = joined[place // rows][place % rows : place % rows + 1]
            place += 1


def late_vector(late_x, late_y, from_x, from_y, vector):
    rows, cols = late_x.shape[1:]
    shapes = [(late_x.shape, B16), ((2, rows, cols + 128), B16), (vector.shape, B16)]
    operands = [late_x, late_y, from_x, from_y, vector]
    return call(late_vector_body, "late_vector", shapes, operands, limit=8)


def own_vector(own, from_x, from_y, late_x, late_y, vector):
    rows, cols = own.shape[1:]
    shapes = [((2, rows, cols), F32), ((2, rows, cols + 128), B16), (vector.shape, B16)]
    operands = [own, from_x, from_y, late_x, late_y, vector]
    return call(own_vector_body, "own_vector", shapes, operands, limit=8)


def mid_vector(near, mid, vector):
    rows, cols = near.shape[1:]
    shapes = [((rows, cols), F32), ((rows, cols + 256), B16), (vector.shape, B16)]
    return call(mid_vector_body, "mid_vector", shapes, [near, mid, vector], limit=8)


def far_vector(own, far, vector, sizes):
    rows, cols = own.shape
    shapes = [((rows, cols // 4), F32)] * 4 + [((size // 128, 128), F32) for size in sizes]
    outs = call(far_vector_body, "far_vector", shapes, [own, far, vector], limit=8)
    return outs[:4], [member.reshape(-1) for member in outs[4:]]


def add_late(late_x, late_y, from_x, from_y):
    shape = (late_x.shape, B16)
    return call(add_late_body, "add_late", [shape, shape], [late_x, late_y, from_x, from_y], limit=8)


def add_own(own, from_x, from_y, late_x, late_y):
    shapes = [(late_x.shape, F32), (late_x.shape, B16)]
    return call(add_own_body, "add_own", shapes, [own, from_x, from_y, late_x, late_y], limit=8)


def add_mid(near, mid):
    shapes = [(near.shape[1:], F32), (near.shape[1:], B16)]
    return call(add_mid_body, "add_mid", shapes, [near, mid], limit=8)


def per_device(dp_size, tokens, masked, lengths, mask_vector, w_query, b_query, w_key, w_value,
               b_value, w_out, b_out, gain_one, shift_one, w_up, b_up, w_down, b_down, gain_two,
               shift_two, grad_out):
    head_cols = w_query.shape[1]
    width = tokens.shape[1]
    fast = dp_size == BLOCKS and w_query.shape[0] % 16 == 0
    me = lax.axis_index("dp").astype(jnp.int32).reshape(1)
    if not fast:
        me = jnp.zeros_like(me)

    (b_query, b_value, b_out, gain_one, shift_one, b_up, b_down, gain_two, shift_two) = (
        member.astype(F32)
        for member in (b_query, b_value, b_out, gain_one, shift_one, b_up, b_down, gain_two, shift_two)
    )
    is_masked = (masked == 1)[:, None]
    flag = jnp.broadcast_to(is_masked, (masked.shape[0], 128)).astype(F32)
    in_low = jnp.where(is_masked, mask_vector[None, :], tokens)
    bias_qkv = jnp.concatenate([b_query, jnp.zeros_like(b_query), b_value])[None, :]
    vectors_one = jnp.stack([b_out, gain_one, shift_one])
    vectors_two = jnp.stack([gain_one, shift_one, b_down, gain_two, shift_two])
    b_up, gain_one = b_up[None, :], gain_one[None, :]

    a = jnp.concatenate([w_query, w_key, w_value, w_out.T], axis=1)
    c = w_up
    d = w_down.T
    if fast:
        az = swap(a, 12)
        az, me, flag, in_low, bias_qkv, vectors_one, vectors_two, b_up, gain_one = tie(
            az, me, flag, in_low, bias_qkv, vectors_one, vectors_two, b_up, gain_one
        )
        an = jnp.stack([a, az])
        anx, any_, am = swap(an, 1), swap(an, 2), swap(an, 4)
        anx, any_, am, an, c = tie(anx, any_, am, an, c)
        amx, amy, cz = swap(am, 1), swap(am, 2), swap(c, 12)
        amx, amy, cz, anx, c, d = tie(amx, amy, cz, anx, c, d)
        cn = jnp.stack([c, cz])
        amd, and_, cm = swap(amy, 1), swap(anx, 2), swap(cn, 4)
        cnx, cny, dz = swap(cn, 1), swap(cn, 2), swap(after(d, cm), 12)
        amd, and_, cm, cnx, cny = tie(amd, and_, cm, cnx, cny)
        dn = jnp.stack([d, dz])
        pieces_a = [an, am, anx, amx, any_, amy, and_, amd]
        cmx, cnd, dm = swap(cm, 1), swap(cnx, 2), swap(dn, 4)
        dnx, dny = swap(dn, 1), swap(dn, 2)
    else:
        a, c, d = (lax.all_gather(piece, "dp", axis=0, tiled=True) for piece in (a, c, d))
        pieces_a, pieces_c, pieces_d = as_pieces(a), as_pieces(c), as_pieces(d)
    w_a, qkv, prob, attended, part = attend(me, lengths, in_low, bias_qkv, pieces_a)
    if fast:
        cmx, cnd, dm, dnx, dny, cm, part = tie(cmx, cnd, dm, dnx, dny, cm, part)
        cmy, dnd, cmd = swap(cm, 2), swap(dny, 1), swap(cnd, 4)
    other = pair_swap(part)
    if fast:
        cmy, dnd, cmd, dm, other, part = tie(cmy, dnd, cmd, dm, other, part)
        pieces_c = [cn, cm, cnx, cmx, cny, cmy, cnd, cmd]
        dmx, dmy, dmd = swap(dm, 1), swap(dm, 2), swap(dnd, 4)
    w_u, normed_one, inverse_one, hidden_low, act_low, slope = up(
        me, in_low, part, other, vectors_one, b_up, pieces_c
    )
    if fast:
        dmx, dmy, dmd, act_low = tie(dmx, dmy, dmd, act_low)
        pieces_d = [dn, dm, dnx, dmx, dny, dmy, dnd, dmd]
    w_d, *parts = down(me, act_low, pieces_d)
    halves = [
        second_norm(index * part.shape[0], normed_one, part, pair_swap(part), grad_out, vectors_two)
        for index, part in enumerate(parts)
    ]
    results, dz_two, dz_two_low, sums_two = zip(*halves)
    dx, dy, turned = weight_grad(me, [dz_two_low], [act_low], ORDER[:2])
    if fast:
        dx, dy, turned, dz_two_low = tie(dx, dy, turned, dz_two_low)
        dxr, dyr = swap(dx, 1), swap(dy, 2)
    dxl, dyl, do = weight_grad(me, None, [act_low], ORDER[2:], turned=turned)
    d_pre_low, part, sums_up = hidden_back(dz_two_low, slope, w_d, w_u)
    cx, cy, cxl, cyl, co = weight_grad(me, [[hidden_low]], [d_pre_low])
    if fast:
        dxr, dyr, part, cx, cy, dxl, dyl, do = tie(dxr, dyr, part, cx, cy, dxl, dyl, do)
        cxr, cyr = swap(cx, 1), swap(cy, 2)
        dxl, dyl = add_late(dxl, dyl, dxr, dyr)
        dxlr, dylr = swap(dxl, 1), swap(dyl, 2)
    other = pair_swap(part)
    dz_one, dz_one_low, d_qkv, part, sums_one, sums_qkv = attend_back(
        lengths.shape[0], dz_two, part, other, normed_one, inverse_one, gain_one, flag, qkv, prob, w_a
    )
    if fast:
        cxr, cyr, dxlr, dylr, part, d_qkv, dz_one_low = tie(cxr, cyr, dxlr, dylr, part, d_qkv, dz_one_low)
        cxl, cyl = add_late(cxl, cyl, cxr, cyr)
        cxlr, cylr = swap(cxl, 1), swap(cyl, 2)
        d_near, d_mid = add_own(do, dxr, dyr, dxlr, dylr)
        d_midr = swap(d_mid, 4)
    sums_other = pair_swap(sums_one)
    joined = join(width // BLOCKS, sums_one, sums_other, sums_two, sums_up, sums_qkv)
    vector = joined.astype(B16) if fast else None
    ax, ay, axl, ayl, ao = weight_grad(me, [[in_low], [dz_one_low]], [d_qkv, attended], vector=vector)
    if fast:
        cxlr, cylr, d_midr, ax, ay, part = tie(cxlr, cylr, d_midr, ax, ay, part)
        axr, ayr = swap(ax, 1), swap(ay, 2)
        c_near, c_mid = add_own(co, cxr, cyr, cxlr, cylr)
        d_near, d_far = add_mid(d_near, d_midr)
        c_midr, d_farr = swap(c_mid, 4), swap(d_far, 12)
    other = pair_swap(part)
    d_tokens, result = last(dz_one, part, other, flag, results)
    sizes = [width] * 7 + [head_cols] * 2 + [w_up.shape[1]]
    if fast:
        axr, ayr, c_midr, d_farr, d_tokens, result = tie(axr, ayr, c_midr, d_farr, d_tokens, result)
        axl, ayl, vector = late_vector(axl, ayl, axr, ayr, vector)
        axlr, aylr = swap(axl, 1), swap(ayl, 2)
        c_near, c_far = add_mid(c_near, c_midr)
        c_farr = swap(c_far, 12)
        axlr, aylr, c_farr = tie(axlr, aylr, c_farr)
        a_near, a_mid, vector = own_vector(ao, axr, ayr, axlr, aylr, vector)
        a_midr = swap(a_mid, 4)
        d_w_down_t = d_near + d_farr.astype(F32)
        a_midr, d_w_down_t = tie(a_midr, d_w_down_t)
        a_near, a_far, vector = mid_vector(a_near, a_midr, vector)
        a_farr = swap(a_far, 12)
        d_w_up = c_near + c_farr.astype(F32)
        d_wa, summed = far_vector(a_near, a_farr, vector, sizes)
    else:
        full = []
        for parts in ((ax, ay, axl, ayl, ao), (cx, cy, cxl, cyl, co), (dx, dy, dxl, dyl, do)):
            blocks = [None] * BLOCKS
            for member, offsets in zip(parts, ORDER):
                for k, offset in enumerate(offsets):
                    blocks[offset] = member[k]
            full.append(jnp.concatenate(blocks).astype(F32))
        joined = lax.psum(joined, "dp")
        d_wa, d_w_up, d_w_down_t = (
            lax.psum_scatter(member, "dp", scatter_dimension=0, tiled=True) for member in full
        )
        d_wa = [d_wa[:, k * head_cols : (k + 1) * head_cols] for k in range(4)]
        joined = joined.reshape(-1)
        summed = []
        start = 0
        for size in sizes:
            summed.append(joined[start : start + size])
            start += size
    return (
        result,
        d_tokens,
        summed[0],
        d_wa[0],
        summed[7],
        d_wa[1],
        d_wa[2],
        summed[8],
        d_wa[3].T,
        summed[3],
        summed[1],
        summed[2],
        d_w_up,
        summed[9],
        d_w_down_t.T,
        summed[6],
        summed[4],
        summed[5],
    )


def solution(mesh):
    rows, flat, both = P("dp", None), P(), P("dp", "mp")
    return jax.shard_map(
        functools.partial(per_device, mesh.shape["dp"]),
        mesh=mesh,
        in_specs=(rows, P("dp"), P("dp"), flat, both, P("mp"), both, both, P("mp"), P("mp", "dp"),
                  flat, flat, flat, both, P("mp"), P("mp", "dp"), flat, flat, flat, rows),
        out_specs=(rows, rows, flat, both, P("mp"), both, both, P("mp"), P("mp", "dp"), flat, flat,
                   flat, both, P("mp"), P("mp", "dp"), flat, flat, flat),
        check_vma=False,
    )
```

```python
import functools

import jax
import jax.numpy as jnp
from jax import lax
from jax.experimental import pallas as pl
from jax.experimental.pallas import tpu as pltpu
from jax.sharding import PartitionSpec as P

HEAD = 64
NORM_EPS = 1e-05
F32 = jnp.float32
B16 = jnp.bfloat16
MIB = 1 << 20

BLOCKS = 16
NEAR = (0, 12)
MID = (4, 8)


def swap(values, bit):
    return lax.ppermute(values, "dp", [(i, i ^ bit) for i in range(BLOCKS)])


def tie(*values):
    return lax.optimization_barrier(values)


def after(value, *earlier):
    return tie(value, *earlier)[0]


def pair_swap(partial):
    return lax.ppermute(partial, "mp", [(0, 1), (1, 0)])


def as_pieces(full):
    rows = full.shape[0] // BLOCKS
    blocks = full.reshape(BLOCKS, rows, full.shape[1])
    return [
        jnp.stack([blocks[offset + bits[0]], blocks[offset + bits[1]]])
        for offset in range(4)
        for bits in (NEAR, MID)
    ]


SMEM_SPEC = pl.BlockSpec(memory_space=pltpu.SMEM)
VMEM_SPEC = pl.BlockSpec(memory_space=pltpu.VMEM)
CHUNK = 256
UNROLL = 8
LIGHT = pl.CostEstimate(flops=1, bytes_accessed=1, transcendentals=0)


def call(body, name, shapes, operands, scratch=(), limit=16):
    return pl.pallas_call(
        body,
        in_specs=[
            SMEM_SPEC if member.dtype == jnp.int32 and member.ndim == 1 else VMEM_SPEC
            for member in operands
        ],
        out_specs=[VMEM_SPEC] * len(shapes),
        out_shape=[jax.ShapeDtypeStruct(shape, dtype) for shape, dtype in shapes],
        scratch_shapes=[pltpu.VMEM(shape, dtype) for shape, dtype in scratch],
        compiler_params=pltpu.CompilerParams(vmem_limit_bytes=limit * MIB),
        cost_estimate=LIGHT,
        name=name,
    )(*operands)


def chunks(count):
    return [slice(start, start + CHUNK) for start in range(0, count, CHUNK)]


def loop(count, step, size=CHUNK):
    def body(index, carry):
        step(pl.ds(pl.multiple_of(index * size, size), size))
        return carry

    lax.fori_loop(0, count // size, body, 0)


PAIRS = [(q + bits[k], 2 * q + m, k) for q in range(4) for m, bits in enumerate((NEAR, MID)) for k in range(2)]


def fill(me, pieces, full_ref):
    rows = pieces[0].shape[1]
    for offset, piece, index in PAIRS:
        block = me ^ offset
        full_ref[pl.ds(pl.multiple_of(block * rows, rows), rows), :] = pieces[piece][index]


def dot(left, right):
    return jnp.dot(left, right, preferred_element_type=F32)


def dot_t(left, right):
    return lax.dot_general(left, right, (((1,), (1,)), ((), ())), preferred_element_type=F32)


def t_dot(left, right):
    return lax.dot_general(left, right, (((0,), (0,)), ((), ())), preferred_element_type=F32)


def row_mean(values):
    return jnp.mean(values, axis=-1, keepdims=True)


def normalize(values):
    centred = values - row_mean(values)
    inverse = lax.rsqrt(row_mean(centred * centred) + NORM_EPS)
    return centred * inverse, inverse


def col_sum(values):
    return jnp.sum(values, axis=0, keepdims=True)


def norm_back(scaled, normed, inverse):
    return inverse * (scaled - row_mean(scaled) - normed * row_mean(scaled * normed))


def two_heads(slots):
    row = lax.broadcasted_iota(jnp.int32, (2 * slots, 2 * HEAD), 0) // slots
    lane = lax.broadcasted_iota(jnp.int32, (2 * slots, 2 * HEAD), 1) // HEAD
    return (row == lane).astype(F32).astype(B16)


def doubled(values, mask):
    return jnp.concatenate([values, values], axis=0) * mask


def attend_body(slots, me_ref, len_ref, in_ref, bias_ref, *rest):
    pieces, (w_ref, qkv_ref, prob_ref, att_ref, part_ref) = rest[:-5], rest[-5:]
    count, width = att_ref.shape
    fill(me_ref[0], pieces, w_ref)

    def project(rows):
        qkv_ref[rows] = (dot(in_ref[rows], w_ref[:, : 3 * width]) + bias_ref[...]).astype(B16)

    loop(count, project)
    mask = two_heads(slots)
    key_slot = lax.broadcasted_iota(jnp.int32, (slots, slots), 1)

    def chain_step(chain, carry):
        valid = key_slot < len_ref[chain]
        rows = pl.ds(pl.multiple_of(chain * slots, slots), slots)
        for pair in range(width // (2 * HEAD)):
            lanes = 2 * HEAD * pair
            query = qkv_ref[rows, lanes : lanes + 2 * HEAD]
            key = qkv_ref[rows, width + lanes : width + lanes + 2 * HEAD]
            value = qkv_ref[rows, 2 * width + lanes : 2 * width + lanes + 2 * HEAD]
            scores = dot_t(query * (HEAD**-0.5), doubled(key, mask))
            probs = []
            for head in range(2):
                part = jnp.where(valid, scores[:, head * slots : (head + 1) * slots], -1e30)
                terms = jnp.exp(part - jnp.max(part, axis=-1, keepdims=True))
                probs.append((terms / jnp.sum(terms, axis=-1, keepdims=True)).astype(B16))
            prob = jnp.concatenate(probs, axis=1)
            prob_ref[rows, 2 * slots * pair : 2 * slots * (pair + 1)] = prob
            att_ref[rows, lanes : lanes + 2 * HEAD] = dot(prob, doubled(value, mask)).astype(B16)
        return carry

    lax.fori_loop(0, count // slots, chain_step, 0, unroll=UNROLL)

    def bring_out(rows):
        part_ref[rows] = dot_t(att_ref[rows], w_ref[:, 3 * width :]).astype(B16)

    loop(count, bring_out)


def attend(me, lengths, in_low, bias, pieces):
    count, width = in_low.shape
    heads = bias.shape[1] // 3
    slots = count // lengths.shape[0]
    shapes = [
        ((width, 4 * heads), B16),
        ((count, 3 * heads), B16),
        ((count, heads // HEAD * slots), B16),
        ((count, heads), B16),
        ((count, width), B16),
    ]
    body = functools.partial(attend_body, slots)
    return call(body, "attend", shapes, [me, lengths, in_low, bias, *pieces])


def up_body(me_ref, in_ref, own_ref, other_ref, vec_ref, bias_ref, *rest):
    pieces, (w_ref, normed_ref, inverse_ref, low_ref, act_ref, slope_ref) = rest[:-6], rest[-6:]
    fill(me_ref[0], pieces, w_ref)
    vectors = vec_ref[...]

    def step(rows):
        attn = own_ref[rows].astype(F32) + other_ref[rows].astype(F32) + vectors[0:1]
        normed, inverse = normalize(in_ref[rows].astype(F32) + attn)
        normed_ref[rows] = normed
        inverse_ref[rows] = jnp.broadcast_to(inverse, (CHUNK, inverse_ref.shape[1]))
        low_ref[rows] = (normed * vectors[1:2] + vectors[2:3]).astype(B16)
        pre = dot(low_ref[rows], w_ref[...]) + bias_ref[...]
        cdf = 0.5 + 0.5 * lax.erf(pre * (2.0**-0.5))
        act_ref[rows] = (pre * cdf).astype(B16)
        density = jnp.exp(pre * pre * -0.5) * 0.3989422804014327
        slope_ref[rows] = (cdf + pre * density).astype(B16)

    loop(in_ref.shape[0], step)


def up(me, in_low, own, other, vectors, bias, pieces):
    count, width = in_low.shape
    units = bias.shape[1]
    shapes = [
        ((width, units), B16),
        ((count, width), F32),
        ((count, 128), F32),
        ((count, width), B16),
        ((count, units), B16),
        ((count, units), B16),
    ]
    return call(up_body, "up", shapes, [me, in_low, own, other, vectors, bias, *pieces])


def down_body(me_ref, act_ref, *rest):
    pieces, (w_ref, part_ref) = rest[:-2], rest[-2:]
    fill(me_ref[0], pieces, w_ref)
    for rows in chunks(part_ref.shape[0]):
        part_ref[rows] = dot_t(act_ref[rows], w_ref[...]).astype(B16)


def down_rest_body(act_ref, w_ref, part_ref):
    half = part_ref.shape[0]
    for rows in chunks(half):
        part_ref[rows] = dot_t(act_ref[half + rows.start : half + rows.stop], w_ref[...]).astype(B16)


def down(me, act, pieces):
    count, units = act.shape
    width = BLOCKS * pieces[0].shape[1]
    half = ((count // 2, width), B16)
    w_down_t, first = call(down_body, "down", [((width, units), B16), half], [me, act, *pieces])
    (second,) = call(down_rest_body, "down_rest", [half], [act, w_down_t])
    return w_down_t, first, second


def second_norm_body(start, normed_ref, own_ref, other_ref, grad_ref, vec_ref, out_ref, dz_ref, low_ref, sum_ref):
    vectors = vec_ref[...]
    sum_ref[...] = jnp.zeros_like(sum_ref)
    for rows in chunks(own_ref.shape[0]):
        there = slice(start + rows.start, start + rows.stop)
        hidden = normed_ref[there] * vectors[0:1] + vectors[1:2]
        ffn = own_ref[rows].astype(F32) + other_ref[rows].astype(F32) + vectors[2:3]
        normed, inverse = normalize(hidden + ffn)
        out_ref[rows] = (normed * vectors[3:4] + vectors[4:5]).astype(B16)
        grad = grad_ref[there].astype(F32)
        dz = norm_back(grad * vectors[3:4], normed, inverse)
        dz_ref[rows] = dz
        low_ref[rows] = dz.astype(B16)
        sum_ref[0:1] += col_sum(grad * normed)
        sum_ref[1:2] += col_sum(grad)
        sum_ref[2:3] += col_sum(dz)


def second_norm(start, normed, own, other, grad, vectors):
    shape = own.shape
    shapes = [(shape, B16), (shape, F32), (shape, B16), ((8, shape[1]), F32)]
    body = functools.partial(second_norm_body, start)
    return call(body, "second_norm", shapes, [normed, own, other, grad, vectors])


def rows_in(halves, rows):
    size = halves[0].shape[0]
    half = halves[rows.start // size]
    return half[rows.start % size : rows.start % size + rows.stop - rows.start]


ORDER = (
    (3, 15, 1, 13),
    (7, 11, 6, 10),
    (5, 9),
    (2, 14),
    (0, 12, 4, 8),
)


def weight_grad(me, lefts, rights, groups=ORDER, vector=None, turned=None):
    count = rights[0].shape[0]
    width = lefts[-1][0].shape[1] if turned is None else turned.shape[0]
    tile = 384 if all(right.shape[1] % 384 == 0 for right in rights) else 128
    total = sum(right.shape[1] for right in rights)
    rows = width // BLOCKS
    n = len(rights)
    flat = [half for left in lefts for half in left] if turned is None else [turned]
    wide = [] if vector is None else [vector]
    keep = turned is None and len(groups) < len(ORDER)
    wanted = [offset for offsets in groups for offset in offsets]

    def body(me_ref, *refs):
        left_refs, right_refs = list(refs[: len(flat)]), refs[len(flat) : len(flat) + n]
        outs = refs[len(flat) + n + len(wide) :]
        placed_ref = outs[-1]
        if wide:
            outs[0][0:2, :, total:] = refs[len(flat) + n][...]
            outs[0][2:4, :, total:] = jnp.zeros((2, rows, 128), B16)
        at = 0
        for index, right_ref in enumerate(right_refs):
            turned_ref = left_refs[0] if turned is not None else outs[-2]
            if turned is None:
                start = 0
                for _ in lefts[index]:
                    half_ref = left_refs.pop(0)
                    turned_ref[:, start : start + half_ref.shape[0]] = half_ref[...].T
                    start += half_ref.shape[0]
            for k, offset in enumerate(wanted):
                place = pl.multiple_of((me_ref[0] ^ offset) * rows, rows)
                placed_ref[k * rows : (k + 1) * rows] = turned_ref[pl.ds(place, rows), :]

            def step(cols, right_ref=right_ref, at=at):
                product = dot(placed_ref[...], right_ref[:, cols]).astype(B16)
                there = pl.ds(pl.multiple_of(at + cols.start, 128), tile)
                first = 0
                for out_ref, offsets in zip(outs, groups):
                    for k in range(len(offsets)):
                        out_ref[k, :, there] = product[first : first + rows]
                        first += rows

            loop(right_ref.shape[1], step, tile)
            at += right_ref.shape[1]

    shapes = [((len(offsets), rows, total), B16) for offsets in groups]
    shapes[0] = ((len(groups[0]), rows, total + 128 * len(wide)), B16)
    held = ((width, count), B16)
    shapes += [held] * keep
    scratch = [held] * (turned is None and not keep) + [((len(wanted) * rows, count), B16)]
    return call(body, "weight_grad", shapes, [me, *flat, *rights, *wide], scratch)


def hidden_back_body(low_a_ref, low_b_ref, slope_ref, down_ref, up_ref, pre_ref, part_ref, sum_ref):
    sum_ref[...] = jnp.zeros_like(sum_ref)
    half = low_a_ref.shape[0]
    for start, low_ref in ((0, low_a_ref), (half, low_b_ref)):

        def step(here, start=start, low_ref=low_ref):
            rows = pl.ds(pl.multiple_of(start + here.start, CHUNK), CHUNK)
            d_pre = dot(low_ref[here], down_ref[...]) * slope_ref[rows].astype(F32)
            sum_ref[0:1] += col_sum(d_pre)
            pre_ref[rows] = d_pre.astype(B16)
            part_ref[rows] = dot_t(pre_ref[rows], up_ref[...]).astype(B16)

        loop(half, step)


def hidden_back(lows, slope, w_down_t, w_up):
    count, units = slope.shape
    shapes = [((count, units), B16), ((count, w_up.shape[0]), B16), ((8, units), F32)]
    return call(hidden_back_body, "hidden_back", shapes, [*lows, slope, w_down_t, w_up])


def attend_back_body(slots, dz_a_ref, dz_b_ref, own_ref, other_ref, normed_ref, inverse_ref, gain_ref,
                     flag_ref, qkv_ref, prob_ref, w_ref, dz_one_ref, low_ref, d_qkv_ref, part_ref, sum_ref,
                     sum_qkv_ref, d_att_ref):
    count, width = d_att_ref.shape
    sum_ref[...] = jnp.zeros_like(sum_ref)
    sum_qkv_ref[...] = jnp.zeros_like(sum_qkv_ref)
    half = dz_a_ref.shape[0]
    for start, dz_ref in ((0, dz_a_ref), (half, dz_b_ref)):

        def step(here, start=start, dz_ref=dz_ref):
            rows = pl.ds(pl.multiple_of(start + here.start, CHUNK), CHUNK)
            normed = normed_ref[rows]
            d_hidden = dz_ref[here] + (own_ref[rows].astype(F32) + other_ref[rows].astype(F32))
            dz_one = norm_back(d_hidden * gain_ref[...], normed, inverse_ref[rows, 0:1])
            dz_one_ref[rows] = dz_one
            low_ref[rows] = dz_one.astype(B16)
            sum_ref[0:1] += col_sum(d_hidden * normed)
            sum_ref[1:2] += col_sum(d_hidden)
            sum_ref[2:3] += col_sum(dz_one)
            sum_ref[3:4] += col_sum(dz_one * flag_ref[rows, 0:1])
            d_att_ref[rows] = dot(low_ref[rows], w_ref[:, 3 * width :]).astype(B16)

        loop(half, step)
    mask = two_heads(slots)

    def chain_step(chain, carry):
        rows = pl.ds(pl.multiple_of(chain * slots, slots), slots)
        for pair in range(width // (2 * HEAD)):
            lanes = 2 * HEAD * pair
            query = qkv_ref[rows, lanes : lanes + 2 * HEAD]
            key = qkv_ref[rows, width + lanes : width + lanes + 2 * HEAD]
            value = qkv_ref[rows, 2 * width + lanes : 2 * width + lanes + 2 * HEAD]
            d_att = d_att_ref[rows, lanes : lanes + 2 * HEAD]
            prob = prob_ref[rows, 2 * slots * pair : 2 * slots * (pair + 1)]
            d_prob = dot_t(d_att, doubled(value, mask))
            weights = prob.astype(F32)
            products = weights * d_prob
            lows = []
            for head in range(2):
                half = slice(head * slots, (head + 1) * slots)
                total = jnp.sum(products[:, half], axis=-1, keepdims=True)
                lows.append((products[:, half] - weights[:, half] * total).astype(B16))
            low = jnp.concatenate(lows, axis=1)
            d_query = dot(low, doubled(key, mask)) * (HEAD**-0.5)
            tall = jnp.concatenate(lows, axis=0)
            d_key = t_dot(tall, doubled(query, mask)) * (HEAD**-0.5)
            tall = jnp.concatenate([prob[:, :slots], prob[:, slots:]], axis=0)
            d_value = t_dot(tall, doubled(d_att, mask))
            d_qkv_ref[rows, lanes : lanes + 2 * HEAD] = d_query.astype(B16)
            d_qkv_ref[rows, width + lanes : width + lanes + 2 * HEAD] = d_key.astype(B16)
            d_qkv_ref[rows, 2 * width + lanes : 2 * width + lanes + 2 * HEAD] = d_value.astype(B16)
        return carry

    lax.fori_loop(0, count // slots, chain_step, 0)

    def bring_back(rows):
        sum_qkv_ref[0:1] += col_sum(d_qkv_ref[rows].astype(F32))
        part = dot_t(d_qkv_ref[rows], w_ref[:, : 3 * width]).astype(B16)
        part_ref[rows] = part
        sum_ref[4:5] += col_sum(part.astype(F32) * flag_ref[rows, 0:1])

    loop(count, bring_back)


def attend_back(chain_count, dz_two, own, other, normed, inverse, gain, flag, qkv, prob, w_a):
    shape = normed.shape
    heads = qkv.shape[1] // 3
    shapes = [
        (shape, F32),
        (shape, B16),
        (qkv.shape, B16),
        (shape, B16),
        ((8, shape[1]), F32),
        ((8, 3 * heads), F32),
    ]
    operands = [*dz_two, own, other, normed, inverse, gain, flag, qkv, prob, w_a]
    body = functools.partial(attend_back_body, shape[0] // chain_count)
    return call(body, "attend_back", shapes, operands, [((shape[0], heads), B16)])


def join_body(one_ref, other_ref, two_a_ref, two_b_ref, up_ref, qkv_ref, out_ref):
    width = one_ref.shape[1]
    heads = qkv_ref.shape[1] // 3
    rows = out_ref.shape[1]
    out_ref[...] = jnp.zeros_like(out_ref)

    def put(start, values):
        for k in range(values.shape[1] // 128):
            place = (start + 128 * k) // 128
            chunk = values[:, 128 * k : 128 * (k + 1)]
            out_ref[place // rows, place % rows : place % rows + 1] = chunk

    put(0, one_ref[3:4] + (one_ref[4:5] + other_ref[4:5]))
    for k in range(3):
        put((1 + k) * width, one_ref[k : k + 1])
        put((4 + k) * width, two_a_ref[k : k + 1] + two_b_ref[k : k + 1])
    put(7 * width, qkv_ref[0:1, :heads])
    put(7 * width + heads, qkv_ref[0:1, 2 * heads :])
    put(7 * width + 2 * heads, up_ref[0:1])


def join(rows, sums_one, sums_other, sums_two, sums_up, sums_qkv):
    width = sums_one.shape[1]
    length = 7 * width + 2 * sums_qkv.shape[1] // 3 + sums_up.shape[1]
    assert length <= 2 * rows * 128
    operands = [sums_one, sums_other, *sums_two, sums_up, sums_qkv]
    return call(join_body, "join", [((2, rows, 128), F32)], operands, limit=4)[0]


def last_body(dz_ref, own_ref, other_ref, flag_ref, out_a_ref, out_b_ref, tokens_ref, out_ref):
    for rows in chunks(dz_ref.shape[0]):
        total = dz_ref[rows] + (own_ref[rows].astype(F32) + other_ref[rows].astype(F32))
        tokens_ref[rows] = jnp.where(flag_ref[rows, 0:1] > 0.0, 0.0, total)
        out_ref[rows] = rows_in((out_a_ref, out_b_ref), rows)


def last(dz_one, own, other, flag, results):
    shapes = [(dz_one.shape, F32), (dz_one.shape, B16)]
    return call(last_body, "last", shapes, [dz_one, own, other, flag, *results])


def add_late_body(x_ref, y_ref, from_x_ref, from_y_ref, out_x_ref, out_y_ref):
    out_x_ref[...] = (x_ref[...].astype(F32) + from_y_ref[:2].astype(F32)).astype(B16)
    out_y_ref[...] = (y_ref[...].astype(F32) + from_x_ref[:2].astype(F32)).astype(B16)


def add_own_body(own_ref, from_x_ref, from_y_ref, late_x_ref, late_y_ref, near_ref, mid_ref):
    near_ref[...] = (
        own_ref[:2].astype(F32) + from_x_ref[2:].astype(F32) + late_y_ref[...].astype(F32)
    )
    mid_ref[...] = (
        own_ref[2:].astype(F32) + late_x_ref[...].astype(F32) + from_y_ref[2:].astype(F32)
    ).astype(B16)


def add_mid_body(near_ref, mid_ref, own_ref, far_ref):
    own_ref[...] = near_ref[0] + mid_ref[0].astype(F32)
    far_ref[...] = (near_ref[1] + mid_ref[1].astype(F32)).astype(B16)


def late_vector_body(x_ref, y_ref, from_x_ref, from_y_ref, v_ref, out_x_ref, out_y_ref, vector_ref):
    cols = x_ref.shape[2]
    out_x_ref[...] = (x_ref[...].astype(F32) + from_y_ref[:2].astype(F32)).astype(B16)
    out_y_ref[:, :, :cols] = (y_ref[...].astype(F32) + from_x_ref[:2, :, :cols].astype(F32)).astype(B16)
    vector = (v_ref[...].astype(F32) + from_x_ref[:2, :, cols:].astype(F32)).astype(B16)
    out_y_ref[:, :, cols:] = vector
    vector_ref[...] = vector


def own_vector_body(own_ref, from_x_ref, from_y_ref, late_x_ref, late_y_ref, v_ref, near_ref, mid_ref, vector_ref):
    cols = own_ref.shape[2]
    near_ref[...] = (
        own_ref[:2].astype(F32)
        + from_x_ref[2:, :, :cols].astype(F32)
        + late_y_ref[:, :, :cols].astype(F32)
    )
    mid_ref[:, :, :cols] = (
        own_ref[2:].astype(F32) + late_x_ref[...].astype(F32) + from_y_ref[2:].astype(F32)
    ).astype(B16)
    vector = (v_ref[...].astype(F32) + late_y_ref[:, :, cols:].astype(F32)).astype(B16)
    mid_ref[:, :, cols:] = vector
    vector_ref[...] = vector


def mid_vector_body(near_ref, mid_ref, v_ref, own_ref, far_ref, vector_ref):
    cols = own_ref.shape[1]
    own_ref[...] = near_ref[0] + mid_ref[0, :, :cols].astype(F32)
    far_ref[:, :cols] = (near_ref[1] + mid_ref[1, :, :cols].astype(F32)).astype(B16)
    vector = (v_ref[...].astype(F32) + mid_ref[:, :, cols:].astype(F32)).astype(B16)
    for k in range(2):
        far_ref[:, cols + 128 * k : cols + 128 * (k + 1)] = vector[k]
    vector_ref[...] = vector


def far_vector_body(own_ref, far_ref, v_ref, *outs):
    rows, cols = own_ref.shape
    part = cols // 4
    for k in range(4):
        lanes = slice(k * part, (k + 1) * part)
        outs[k][...] = own_ref[:, lanes] + far_ref[:, lanes].astype(F32)
    place = 0
    joined = [
        v_ref[k].astype(F32) + far_ref[:, cols + 128 * k : cols + 128 * (k + 1)].astype(F32) for k in range(2)
    ]
    for out_ref in outs[4:]:
        for k in range(out_ref.shape[0]):
            out_ref[k : k + 1] = joined[place // rows][place % rows : place % rows + 1]
            place += 1


def late_vector(late_x, late_y, from_x, from_y, vector):
    rows, cols = late_x.shape[1:]
    shapes = [(late_x.shape, B16), ((2, rows, cols + 128), B16), (vector.shape, B16)]
    operands = [late_x, late_y, from_x, from_y, vector]
    return call(late_vector_body, "late_vector", shapes, operands, limit=8)


def own_vector(own, from_x, from_y, late_x, late_y, vector):
    rows, cols = own.shape[1:]
    shapes = [((2, rows, cols), F32), ((2, rows, cols + 128), B16), (vector.shape, B16)]
    operands = [own, from_x, from_y, late_x, late_y, vector]
    return call(own_vector_body, "own_vector", shapes, operands, limit=8)


def mid_vector(near, mid, vector):
    rows, cols = near.shape[1:]
    shapes = [((rows, cols), F32), ((rows, cols + 256), B16), (vector.shape, B16)]
    return call(mid_vector_body, "mid_vector", shapes, [near, mid, vector], limit=8)


def far_vector(own, far, vector, sizes):
    rows, cols = own.shape
    shapes = [((rows, cols // 4), F32)] * 4 + [((size // 128, 128), F32) for size in sizes]
    outs = call(far_vector_body, "far_vector", shapes, [own, far, vector], limit=8)
    return outs[:4], [member.reshape(-1) for member in outs[4:]]


def add_late(late_x, late_y, from_x, from_y):
    shape = (late_x.shape, B16)
    return call(add_late_body, "add_late", [shape, shape], [late_x, late_y, from_x, from_y], limit=8)


def add_own(own, from_x, from_y, late_x, late_y):
    shapes = [(late_x.shape, F32), (late_x.shape, B16)]
    return call(add_own_body, "add_own", shapes, [own, from_x, from_y, late_x, late_y], limit=8)


def add_mid(near, mid):
    shapes = [(near.shape[1:], F32), (near.shape[1:], B16)]
    return call(add_mid_body, "add_mid", shapes, [near, mid], limit=8)


def per_device(dp_size, tokens, masked, lengths, mask_vector, w_query, b_query, w_key, w_value,
               b_value, w_out, b_out, gain_one, shift_one, w_up, b_up, w_down, b_down, gain_two,
               shift_two, grad_out):
    head_cols = w_query.shape[1]
    width = tokens.shape[1]
    fast = dp_size == BLOCKS and w_query.shape[0] % 16 == 0
    me = lax.axis_index("dp").astype(jnp.int32).reshape(1)
    if not fast:
        me = jnp.zeros_like(me)

    (b_query, b_value, b_out, gain_one, shift_one, b_up, b_down, gain_two, shift_two) = (
        member.astype(F32)
        for member in (b_query, b_value, b_out, gain_one, shift_one, b_up, b_down, gain_two, shift_two)
    )
    is_masked = (masked == 1)[:, None]
    flag = jnp.broadcast_to(is_masked, (masked.shape[0], 128)).astype(F32)
    in_low = jnp.where(is_masked, mask_vector[None, :], tokens)
    bias_qkv = jnp.concatenate([b_query, jnp.zeros_like(b_query), b_value])[None, :]
    vectors_one = jnp.stack([b_out, gain_one, shift_one])
    vectors_two = jnp.stack([gain_one, shift_one, b_down, gain_two, shift_two])
    b_up, gain_one = b_up[None, :], gain_one[None, :]

    a = jnp.concatenate([w_query, w_key, w_value, w_out.T], axis=1)
    c = w_up
    d = w_down.T
    if fast:
        az = swap(a, 12)
        az, me, flag, in_low, bias_qkv, vectors_one, vectors_two, b_up, gain_one = tie(
            az, me, flag, in_low, bias_qkv, vectors_one, vectors_two, b_up, gain_one
        )
        an = jnp.stack([a, az])
        anx, any_, am = swap(an, 1), swap(an, 2), swap(an, 4)
        anx, any_, am, an, c = tie(anx, any_, am, an, c)
        amx, amy, cz = swap(am, 1), swap(am, 2), swap(c, 12)
        amx, amy, cz, anx, c, d = tie(amx, amy, cz, anx, c, d)
        cn = jnp.stack([c, cz])
        amd, and_, cm = swap(amy, 1), swap(anx, 2), swap(cn, 4)
        cnx, cny, dz = swap(cn, 1), swap(cn, 2), swap(after(d, cm), 12)
        amd, and_, cm, cnx, cny = tie(amd, and_, cm, cnx, cny)
        dn = jnp.stack([d, dz])
        pieces_a = [an, am, anx, amx, any_, amy, and_, amd]
        cmx, cnd, dm = swap(cm, 1), swap(cnx, 2), swap(dn, 4)
        dnx, dny = swap(dn, 1), swap(dn, 2)
    else:
        a, c, d = (lax.all_gather(piece, "dp", axis=0, tiled=True) for piece in (a, c, d))
        pieces_a, pieces_c, pieces_d = as_pieces(a), as_pieces(c), as_pieces(d)
    w_a, qkv, prob, attended, part = attend(me, lengths, in_low, bias_qkv, pieces_a)
    if fast:
        cmx, cnd, dm, dnx, dny, cm, part = tie(cmx, cnd, dm, dnx, dny, cm, part)
        cmy, dnd, cmd = swap(cm, 2), swap(dny, 1), swap(cnd, 4)
    other = pair_swap(part)
    if fast:
        cmy, dnd, cmd, dm, other, part = tie(cmy, dnd, cmd, dm, other, part)
        pieces_c = [cn, cm, cnx, cmx, cny, cmy, cnd, cmd]
        dmx, dmy, dmd = swap(dm, 1), swap(dm, 2), swap(dnd, 4)
    w_u, normed_one, inverse_one, hidden_low, act_low, slope = up(
        me, in_low, part, other, vectors_one, b_up, pieces_c
    )
    if fast:
        dmx, dmy, dmd, act_low = tie(dmx, dmy, dmd, act_low)
        pieces_d = [dn, dm, dnx, dmx, dny, dmy, dnd, dmd]
    w_d, *parts = down(me, act_low, pieces_d)
    halves = [
        second_norm(index * part.shape[0], normed_one, part, pair_swap(part), grad_out, vectors_two)
        for index, part in enumerate(parts)
    ]
    results, dz_two, dz_two_low, sums_two = zip(*halves)
    dx, dy, turned = weight_grad(me, [dz_two_low], [act_low], ORDER[:2])
    if fast:
        dx, dy, turned, dz_two_low = tie(dx, dy, turned, dz_two_low)
        dxr, dyr = swap(dx, 1), swap(dy, 2)
    dxl, dyl, do = weight_grad(me, None, [act_low], ORDER[2:], turned=turned)
    d_pre_low, part, sums_up = hidden_back(dz_two_low, slope, w_d, w_u)
    cx, cy, cxl, cyl, co = weight_grad(me, [[hidden_low]], [d_pre_low])
    if fast:
        dxr, dyr, part, cx, cy, dxl, dyl, do = tie(dxr, dyr, part, cx, cy, dxl, dyl, do)
        cxr, cyr = swap(cx, 1), swap(cy, 2)
        dxl, dyl = add_late(dxl, dyl, dxr, dyr)
        dxlr, dylr = swap(dxl, 1), swap(dyl, 2)
    other = pair_swap(part)
    dz_one, dz_one_low, d_qkv, part, sums_one, sums_qkv = attend_back(
        lengths.shape[0], dz_two, part, other, normed_one, inverse_one, gain_one, flag, qkv, prob, w_a
    )
    if fast:
        cxr, cyr, dxlr, dylr, part, d_qkv, dz_one_low = tie(cxr, cyr, dxlr, dylr, part, d_qkv, dz_one_low)
        cxl, cyl = add_late(cxl, cyl, cxr, cyr)
        cxlr, cylr = swap(cxl, 1), swap(cyl, 2)
        d_near, d_mid = add_own(do, dxr, dyr, dxlr, dylr)
        d_midr = swap(d_mid, 4)
    sums_other = pair_swap(sums_one)
    joined = join(width // BLOCKS, sums_one, sums_other, sums_two, sums_up, sums_qkv)
    vector = joined.astype(B16) if fast else None
    ax, ay, axl, ayl, ao = weight_grad(me, [[in_low], [dz_one_low]], [d_qkv, attended], vector=vector)
    if fast:
        cxlr, cylr, d_midr, ax, ay, part = tie(cxlr, cylr, d_midr, ax, ay, part)
        axr, ayr = swap(ax, 1), swap(ay, 2)
        c_near, c_mid = add_own(co, cxr, cyr, cxlr, cylr)
        d_near, d_far = add_mid(d_near, d_midr)
        c_midr, d_farr = swap(c_mid, 4), swap(d_far, 12)
    other = pair_swap(part)
    d_tokens, result = last(dz_one, part, other, flag, results)
    sizes = [width] * 7 + [head_cols] * 2 + [w_up.shape[1]]
    if fast:
        axr, ayr, c_midr, d_farr, d_tokens, result = tie(axr, ayr, c_midr, d_farr, d_tokens, result)
        axl, ayl, vector = late_vector(axl, ayl, axr, ayr, vector)
        axlr, aylr = swap(axl, 1), swap(ayl, 2)
        c_near, c_far = add_mid(c_near, c_midr)
        c_farr = swap(c_far, 12)
        axlr, aylr, c_farr = tie(axlr, aylr, c_farr)
        a_near, a_mid, vector = own_vector(ao, axr, ayr, axlr, aylr, vector)
        a_midr = swap(a_mid, 4)
        d_w_down_t = d_near + d_farr.astype(F32)
        a_midr, d_w_down_t = tie(a_midr, d_w_down_t)
        a_near, a_far, vector = mid_vector(a_near, a_midr, vector)
        a_farr = swap(a_far, 12)
        d_w_up = c_near + c_farr.astype(F32)
        d_wa, summed = far_vector(a_near, a_farr, vector, sizes)
    else:
        full = []
        for parts in ((ax, ay, axl, ayl, ao), (cx, cy, cxl, cyl, co), (dx, dy, dxl, dyl, do)):
            blocks = [None] * BLOCKS
            for member, offsets in zip(parts, ORDER):
                for k, offset in enumerate(offsets):
                    blocks[offset] = member[k]
            full.append(jnp.concatenate(blocks).astype(F32))
        joined = lax.psum(joined, "dp")
        d_wa, d_w_up, d_w_down_t = (
            lax.psum_scatter(member, "dp", scatter_dimension=0, tiled=True) for member in full
        )
        d_wa = [d_wa[:, k * head_cols : (k + 1) * head_cols] for k in range(4)]
        joined = joined.reshape(-1)
        summed = []
        start = 0
        for size in sizes:
            summed.append(joined[start : start + size])
            start += size
    return (
        result,
        d_tokens,
        summed[0],
        d_wa[0],
        summed[7],
        d_wa[1],
        d_wa[2],
        summed[8],
        d_wa[3].T,
        summed[3],
        summed[1],
        summed[2],
        d_w_up,
        summed[9],
        d_w_down_t.T,
        summed[6],
        summed[4],
        summed[5],
    )


def solution(mesh):
    rows, flat, both = P("dp", None), P(), P("dp", "mp")
    return jax.shard_map(
        functools.partial(per_device, mesh.shape["dp"]),
        mesh=mesh,
        in_specs=(rows, P("dp"), P("dp"), flat, both, P("mp"), both, both, P("mp"), P("mp", "dp"),
                  flat, flat, flat, both, P("mp"), P("mp", "dp"), flat, flat, flat, rows),
        out_specs=(rows, rows, flat, both, P("mp"), both, both, P("mp"), P("mp", "dp"), flat, flat,
                   flat, both, P("mp"), P("mp", "dp"), flat, flat, flat),
        check_vma=False,
    )
```

```python
import functools

import jax
import jax.numpy as jnp
from jax import lax
from jax.experimental import pallas as pl
from jax.experimental.pallas import tpu as pltpu
from jax.sharding import PartitionSpec as P

HEAD = 64
NORM_EPS = 1e-05
F32 = jnp.float32
B16 = jnp.bfloat16
MIB = 1 << 20

BLOCKS = 16
NEAR = (0, 12)
MID = (4, 8)


def swap(values, bit):
    return lax.ppermute(values, "dp", [(i, i ^ bit) for i in range(BLOCKS)])


def tie(*values):
    return lax.optimization_barrier(values)


def after(value, *earlier):
    return tie(value, *earlier)[0]


def pair_swap(partial):
    return lax.ppermute(partial, "mp", [(0, 1), (1, 0)])


def as_pieces(full):
    rows = full.shape[0] // BLOCKS
    blocks = full.reshape(BLOCKS, rows, full.shape[1])
    return [
        jnp.stack([blocks[offset + bits[0]], blocks[offset + bits[1]]])
        for offset in range(4)
        for bits in (NEAR, MID)
    ]


SMEM_SPEC = pl.BlockSpec(memory_space=pltpu.SMEM)
VMEM_SPEC = pl.BlockSpec(memory_space=pltpu.VMEM)
CHUNK = 256
UNROLL = 8
LIGHT = pl.CostEstimate(flops=1, bytes_accessed=1, transcendentals=0)


def call(body, name, shapes, operands, scratch=(), limit=16):
    return pl.pallas_call(
        body,
        in_specs=[
            SMEM_SPEC if member.dtype == jnp.int32 and member.ndim == 1 else VMEM_SPEC
            for member in operands
        ],
        out_specs=[VMEM_SPEC] * len(shapes),
        out_shape=[jax.ShapeDtypeStruct(shape, dtype) for shape, dtype in shapes],
        scratch_shapes=[pltpu.VMEM(shape, dtype) for shape, dtype in scratch],
        compiler_params=pltpu.CompilerParams(vmem_limit_bytes=limit * MIB),
        cost_estimate=LIGHT,
        name=name,
    )(*operands)


def chunks(count):
    return [slice(start, start + CHUNK) for start in range(0, count, CHUNK)]


def loop(count, step, size=CHUNK, unroll=1):
    def body(index, carry):
        step(pl.ds(pl.multiple_of(index * size, size), size))
        return carry

    lax.fori_loop(0, count // size, body, 0, unroll=unroll)


PAIRS = [(q + bits[k], 2 * q + m, k) for q in range(4) for m, bits in enumerate((NEAR, MID)) for k in range(2)]


def fill(me, pieces, full_ref):
    rows = pieces[0].shape[1]
    for offset, piece, index in PAIRS:
        block = me ^ offset
        full_ref[pl.ds(pl.multiple_of(block * rows, rows), rows), :] = pieces[piece][index]


def dot(left, right):
    return jnp.dot(left, right, preferred_element_type=F32)


def dot_t(left, right):
    return lax.dot_general(left, right, (((1,), (1,)), ((), ())), preferred_element_type=F32)


def t_dot(left, right):
    return lax.dot_general(left, right, (((0,), (0,)), ((), ())), preferred_element_type=F32)


def row_mean(values):
    return jnp.mean(values, axis=-1, keepdims=True)


def normalize(values):
    centred = values - row_mean(values)
    inverse = lax.rsqrt(row_mean(centred * centred) + NORM_EPS)
    return centred * inverse, inverse


def col_sum(values):
    return jnp.sum(values, axis=0, keepdims=True)


def norm_back(scaled, normed, inverse):
    return inverse * (scaled - row_mean(scaled) - normed * row_mean(scaled * normed))


def two_heads(slots):
    row = lax.broadcasted_iota(jnp.int32, (2 * slots, 2 * HEAD), 0) // slots
    lane = lax.broadcasted_iota(jnp.int32, (2 * slots, 2 * HEAD), 1) // HEAD
    return (row == lane).astype(F32).astype(B16)


def doubled(values, mask):
    return jnp.concatenate([values, values], axis=0) * mask


def attend_body(slots, me_ref, len_ref, in_ref, bias_ref, *rest):
    pieces, (w_ref, qkv_ref, prob_ref, att_ref, part_ref) = rest[:-5], rest[-5:]
    count, width = att_ref.shape
    fill(me_ref[0], pieces, w_ref)

    def project(rows):
        qkv_ref[rows] = (dot(in_ref[rows], w_ref[:, : 3 * width]) + bias_ref[...]).astype(B16)

    loop(count, project, unroll=4)
    mask = two_heads(slots)
    key_slot = lax.broadcasted_iota(jnp.int32, (slots, slots), 1)

    def chain_step(chain, carry):
        valid = key_slot < len_ref[chain]
        rows = pl.ds(pl.multiple_of(chain * slots, slots), slots)
        for pair in range(width // (2 * HEAD)):
            lanes = 2 * HEAD * pair
            query = qkv_ref[rows, lanes : lanes + 2 * HEAD]
            key = qkv_ref[rows, width + lanes : width + lanes + 2 * HEAD]
            value = qkv_ref[rows, 2 * width + lanes : 2 * width + lanes + 2 * HEAD]
            scores = dot_t(query * (HEAD**-0.5), doubled(key, mask))
            probs = []
            for head in range(2):
                part = jnp.where(valid, scores[:, head * slots : (head + 1) * slots], -1e30)
                terms = jnp.exp(part - jnp.max(part, axis=-1, keepdims=True))
                probs.append((terms / jnp.sum(terms, axis=-1, keepdims=True)).astype(B16))
            prob = jnp.concatenate(probs, axis=1)
            prob_ref[rows, 2 * slots * pair : 2 * slots * (pair + 1)] = prob
            att_ref[rows, lanes : lanes + 2 * HEAD] = dot(prob, doubled(value, mask)).astype(B16)
        return carry

    lax.fori_loop(0, count // slots, chain_step, 0, unroll=UNROLL)

    def bring_out(rows):
        part_ref[rows] = dot_t(att_ref[rows], w_ref[:, 3 * width :]).astype(B16)

    loop(count, bring_out, unroll=4)


def attend(me, lengths, in_low, bias, pieces):
    count, width = in_low.shape
    heads = bias.shape[1] // 3
    slots = count // lengths.shape[0]
    shapes = [
        ((width, 4 * heads), B16),
        ((count, 3 * heads), B16),
        ((count, heads // HEAD * slots), B16),
        ((count, heads), B16),
        ((count, width), B16),
    ]
    body = functools.partial(attend_body, slots)
    return call(body, "attend", shapes, [me, lengths, in_low, bias, *pieces])


def up_body(me_ref, in_ref, own_ref, other_ref, vec_ref, bias_ref, *rest):
    pieces, (w_ref, normed_ref, inverse_ref, low_ref, act_ref, slope_ref) = rest[:-6], rest[-6:]
    fill(me_ref[0], pieces, w_ref)
    vectors = vec_ref[...]

    def step(rows):
        attn = own_ref[rows].astype(F32) + other_ref[rows].astype(F32) + vectors[0:1]
        normed, inverse = normalize(in_ref[rows].astype(F32) + attn)
        normed_ref[rows] = normed
        inverse_ref[rows] = jnp.broadcast_to(inverse, (CHUNK, inverse_ref.shape[1]))
        low_ref[rows] = (normed * vectors[1:2] + vectors[2:3]).astype(B16)
        pre = dot(low_ref[rows], w_ref[...]) + bias_ref[...]
        cdf = 0.5 + 0.5 * lax.erf(pre * (2.0**-0.5))
        act_ref[rows] = (pre * cdf).astype(B16)
        density = jnp.exp(pre * pre * -0.5) * 0.3989422804014327
        slope_ref[rows] = (cdf + pre * density).astype(B16)

    loop(in_ref.shape[0], step)


def up(me, in_low, own, other, vectors, bias, pieces):
    count, width = in_low.shape
    units = bias.shape[1]
    shapes = [
        ((width, units), B16),
        ((count, width), F32),
        ((count, 128), F32),
        ((count, width), B16),
        ((count, units), B16),
        ((count, units), B16),
    ]
    return call(up_body, "up", shapes, [me, in_low, own, other, vectors, bias, *pieces])


def down_body(me_ref, act_ref, *rest):
    pieces, (w_ref, part_ref) = rest[:-2], rest[-2:]
    fill(me_ref[0], pieces, w_ref)
    for rows in chunks(part_ref.shape[0]):
        part_ref[rows] = dot_t(act_ref[rows], w_ref[...]).astype(B16)


def down_rest_body(act_ref, w_ref, part_ref):
    half = part_ref.shape[0]
    for rows in chunks(half):
        part_ref[rows] = dot_t(act_ref[half + rows.start : half + rows.stop], w_ref[...]).astype(B16)


def down(me, act, pieces):
    count, units = act.shape
    width = BLOCKS * pieces[0].shape[1]
    half = ((count // 2, width), B16)
    w_down_t, first = call(down_body, "down", [((width, units), B16), half], [me, act, *pieces])
    (second,) = call(down_rest_body, "down_rest", [half], [act, w_down_t])
    return w_down_t, first, second


def second_norm_body(start, normed_ref, own_ref, other_ref, grad_ref, vec_ref, out_ref, dz_ref, low_ref, sum_ref):
    vectors = vec_ref[...]
    sum_ref[...] = jnp.zeros_like(sum_ref)
    for rows in chunks(own_ref.shape[0]):
        there = slice(start + rows.start, start + rows.stop)
        hidden = normed_ref[there] * vectors[0:1] + vectors[1:2]
        ffn = own_ref[rows].astype(F32) + other_ref[rows].astype(F32) + vectors[2:3]
        normed, inverse = normalize(hidden + ffn)
        out_ref[rows] = (normed * vectors[3:4] + vectors[4:5]).astype(B16)
        grad = grad_ref[there].astype(F32)
        dz = norm_back(grad * vectors[3:4], normed, inverse)
        dz_ref[rows] = dz
        low_ref[rows] = dz.astype(B16)
        sum_ref[0:1] += col_sum(grad * normed)
        sum_ref[1:2] += col_sum(grad)
        sum_ref[2:3] += col_sum(dz)


def second_norm(start, normed, own, other, grad, vectors):
    shape = own.shape
    shapes = [(shape, B16), (shape, F32), (shape, B16), ((8, shape[1]), F32)]
    body = functools.partial(second_norm_body, start)
    return call(body, "second_norm", shapes, [normed, own, other, grad, vectors])


def rows_in(halves, rows):
    size = halves[0].shape[0]
    half = halves[rows.start // size]
    return half[rows.start % size : rows.start % size + rows.stop - rows.start]


ORDER = (
    (3, 15, 1, 13),
    (7, 11, 6, 10),
    (5, 9),
    (2, 14),
    (0, 12, 4, 8),
)


def weight_grad(me, lefts, rights, groups=ORDER, vector=None, turned=None):
    count = rights[0].shape[0]
    width = lefts[-1][0].shape[1] if turned is None else turned.shape[0]
    tile = 384 if all(right.shape[1] % 384 == 0 for right in rights) else 128
    total = sum(right.shape[1] for right in rights)
    rows = width // BLOCKS
    n = len(rights)
    flat = [half for left in lefts for half in left] if turned is None else [turned]
    wide = [] if vector is None else [vector]
    keep = turned is None and len(groups) < len(ORDER)
    wanted = [offset for offsets in groups for offset in offsets]

    def body(me_ref, *refs):
        left_refs, right_refs = list(refs[: len(flat)]), refs[len(flat) : len(flat) + n]
        outs = refs[len(flat) + n + len(wide) :]
        placed_ref = outs[-1]
        if wide:
            outs[0][0:2, :, total:] = refs[len(flat) + n][...]
            outs[0][2:4, :, total:] = jnp.zeros((2, rows, 128), B16)
        at = 0
        for index, right_ref in enumerate(right_refs):
            turned_ref = left_refs[0] if turned is not None else outs[-2]
            if turned is None:
                start = 0
                for _ in lefts[index]:
                    half_ref = left_refs.pop(0)
                    turned_ref[:, start : start + half_ref.shape[0]] = half_ref[...].T
                    start += half_ref.shape[0]
            for k, offset in enumerate(wanted):
                place = pl.multiple_of((me_ref[0] ^ offset) * rows, rows)
                placed_ref[k * rows : (k + 1) * rows] = turned_ref[pl.ds(place, rows), :]

            def step(cols, right_ref=right_ref, at=at):
                product = dot(placed_ref[...], right_ref[:, cols]).astype(B16)
                there = pl.ds(pl.multiple_of(at + cols.start, 128), tile)
                first = 0
                for out_ref, offsets in zip(outs, groups):
                    for k in range(len(offsets)):
                        out_ref[k, :, there] = product[first : first + rows]
                        first += rows

            loop(right_ref.shape[1], step, tile, unroll=4 if wide or keep else 1)
            at += right_ref.shape[1]

    shapes = [((len(offsets), rows, total), B16) for offsets in groups]
    shapes[0] = ((len(groups[0]), rows, total + 128 * len(wide)), B16)
    held = ((width, count), B16)
    shapes += [held] * keep
    scratch = [held] * (turned is None and not keep) + [((len(wanted) * rows, count), B16)]
    return call(body, "weight_grad", shapes, [me, *flat, *rights, *wide], scratch)


def hidden_back_body(low_a_ref, low_b_ref, slope_ref, down_ref, up_ref, pre_ref, part_ref, sum_ref):
    sum_ref[...] = jnp.zeros_like(sum_ref)
    half = low_a_ref.shape[0]
    for start, low_ref in ((0, low_a_ref), (half, low_b_ref)):

        def step(here, start=start, low_ref=low_ref):
            rows = pl.ds(pl.multiple_of(start + here.start, CHUNK), CHUNK)
            d_pre = dot(low_ref[here], down_ref[...]) * slope_ref[rows].astype(F32)
            sum_ref[0:1] += col_sum(d_pre)
            pre_ref[rows] = d_pre.astype(B16)
            part_ref[rows] = dot_t(pre_ref[rows], up_ref[...]).astype(B16)

        loop(half, step)


def hidden_back(lows, slope, w_down_t, w_up):
    count, units = slope.shape
    shapes = [((count, units), B16), ((count, w_up.shape[0]), B16), ((8, units), F32)]
    return call(hidden_back_body, "hidden_back", shapes, [*lows, slope, w_down_t, w_up])


def attend_back_body(slots, dz_a_ref, dz_b_ref, own_ref, other_ref, normed_ref, inverse_ref, gain_ref,
                     flag_ref, qkv_ref, prob_ref, w_ref, dz_one_ref, low_ref, d_qkv_ref, part_ref, sum_ref,
                     sum_qkv_ref, d_att_ref):
    count, width = d_att_ref.shape
    sum_ref[...] = jnp.zeros_like(sum_ref)
    sum_qkv_ref[...] = jnp.zeros_like(sum_qkv_ref)
    half = dz_a_ref.shape[0]
    for start, dz_ref in ((0, dz_a_ref), (half, dz_b_ref)):

        def step(here, start=start, dz_ref=dz_ref):
            rows = pl.ds(pl.multiple_of(start + here.start, CHUNK), CHUNK)
            normed = normed_ref[rows]
            d_hidden = dz_ref[here] + (own_ref[rows].astype(F32) + other_ref[rows].astype(F32))
            dz_one = norm_back(d_hidden * gain_ref[...], normed, inverse_ref[rows, 0:1])
            dz_one_ref[rows] = dz_one
            low_ref[rows] = dz_one.astype(B16)
            sum_ref[0:1] += col_sum(d_hidden * normed)
            sum_ref[1:2] += col_sum(d_hidden)
            sum_ref[2:3] += col_sum(dz_one)
            sum_ref[3:4] += col_sum(dz_one * flag_ref[rows, 0:1])
            d_att_ref[rows] = dot(low_ref[rows], w_ref[:, 3 * width :]).astype(B16)

        loop(half, step)
    mask = two_heads(slots)

    def chain_step(chain, carry):
        rows = pl.ds(pl.multiple_of(chain * slots, slots), slots)
        for pair in range(width // (2 * HEAD)):
            lanes = 2 * HEAD * pair
            query = qkv_ref[rows, lanes : lanes + 2 * HEAD]
            key = qkv_ref[rows, width + lanes : width + lanes + 2 * HEAD]
            value = qkv_ref[rows, 2 * width + lanes : 2 * width + lanes + 2 * HEAD]
            d_att = d_att_ref[rows, lanes : lanes + 2 * HEAD]
            prob = prob_ref[rows, 2 * slots * pair : 2 * slots * (pair + 1)]
            d_prob = dot_t(d_att, doubled(value, mask))
            weights = prob.astype(F32)
            products = weights * d_prob
            lows = []
            for head in range(2):
                half = slice(head * slots, (head + 1) * slots)
                total = jnp.sum(products[:, half], axis=-1, keepdims=True)
                lows.append((products[:, half] - weights[:, half] * total).astype(B16))
            low = jnp.concatenate(lows, axis=1)
            d_query = dot(low, doubled(key, mask)) * (HEAD**-0.5)
            tall = jnp.concatenate(lows, axis=0)
            d_key = t_dot(tall, doubled(query, mask)) * (HEAD**-0.5)
            tall = jnp.concatenate([prob[:, :slots], prob[:, slots:]], axis=0)
            d_value = t_dot(tall, doubled(d_att, mask))
            d_qkv_ref[rows, lanes : lanes + 2 * HEAD] = d_query.astype(B16)
            d_qkv_ref[rows, width + lanes : width + lanes + 2 * HEAD] = d_key.astype(B16)
            d_qkv_ref[rows, 2 * width + lanes : 2 * width + lanes + 2 * HEAD] = d_value.astype(B16)
        return carry

    lax.fori_loop(0, count // slots, chain_step, 0)

    def bring_back(rows):
        sum_qkv_ref[0:1] += col_sum(d_qkv_ref[rows].astype(F32))
        part = dot_t(d_qkv_ref[rows], w_ref[:, : 3 * width]).astype(B16)
        part_ref[rows] = part
        sum_ref[4:5] += col_sum(part.astype(F32) * flag_ref[rows, 0:1])

    loop(count, bring_back)


def attend_back(chain_count, dz_two, own, other, normed, inverse, gain, flag, qkv, prob, w_a):
    shape = normed.shape
    heads = qkv.shape[1] // 3
    shapes = [
        (shape, F32),
        (shape, B16),
        (qkv.shape, B16),
        (shape, B16),
        ((8, shape[1]), F32),
        ((8, 3 * heads), F32),
    ]
    operands = [*dz_two, own, other, normed, inverse, gain, flag, qkv, prob, w_a]
    body = functools.partial(attend_back_body, shape[0] // chain_count)
    return call(body, "attend_back", shapes, operands, [((shape[0], heads), B16)])


def join_body(one_ref, other_ref, two_a_ref, two_b_ref, up_ref, qkv_ref, out_ref):
    width = one_ref.shape[1]
    heads = qkv_ref.shape[1] // 3
    rows = out_ref.shape[1]
    out_ref[...] = jnp.zeros_like(out_ref)

    def put(start, values):
        for k in range(values.shape[1] // 128):
            place = (start + 128 * k) // 128
            chunk = values[:, 128 * k : 128 * (k + 1)]
            out_ref[place // rows, place % rows : place % rows + 1] = chunk

    put(0, one_ref[3:4] + (one_ref[4:5] + other_ref[4:5]))
    for k in range(3):
        put((1 + k) * width, one_ref[k : k + 1])
        put((4 + k) * width, two_a_ref[k : k + 1] + two_b_ref[k : k + 1])
    put(7 * width, qkv_ref[0:1, :heads])
    put(7 * width + heads, qkv_ref[0:1, 2 * heads :])
    put(7 * width + 2 * heads, up_ref[0:1])


def join(rows, sums_one, sums_other, sums_two, sums_up, sums_qkv):
    width = sums_one.shape[1]
    length = 7 * width + 2 * sums_qkv.shape[1] // 3 + sums_up.shape[1]
    assert length <= 2 * rows * 128
    operands = [sums_one, sums_other, *sums_two, sums_up, sums_qkv]
    return call(join_body, "join", [((2, rows, 128), F32)], operands, limit=4)[0]


def last_body(dz_ref, own_ref, other_ref, flag_ref, out_a_ref, out_b_ref, tokens_ref, out_ref):
    for rows in chunks(dz_ref.shape[0]):
        total = dz_ref[rows] + (own_ref[rows].astype(F32) + other_ref[rows].astype(F32))
        tokens_ref[rows] = jnp.where(flag_ref[rows, 0:1] > 0.0, 0.0, total)
        out_ref[rows] = rows_in((out_a_ref, out_b_ref), rows)


def last(dz_one, own, other, flag, results):
    shapes = [(dz_one.shape, F32), (dz_one.shape, B16)]
    return call(last_body, "last", shapes, [dz_one, own, other, flag, *results])


def add_late_body(x_ref, y_ref, from_x_ref, from_y_ref, out_x_ref, out_y_ref):
    out_x_ref[...] = (x_ref[...].astype(F32) + from_y_ref[:2].astype(F32)).astype(B16)
    out_y_ref[...] = (y_ref[...].astype(F32) + from_x_ref[:2].astype(F32)).astype(B16)


def add_own_body(own_ref, from_x_ref, from_y_ref, late_x_ref, late_y_ref, near_ref, mid_ref):
    near_ref[...] = (
        own_ref[:2].astype(F32) + from_x_ref[2:].astype(F32) + late_y_ref[...].astype(F32)
    )
    mid_ref[...] = (
        own_ref[2:].astype(F32) + late_x_ref[...].astype(F32) + from_y_ref[2:].astype(F32)
    ).astype(B16)


def add_mid_body(near_ref, mid_ref, own_ref, far_ref):
    own_ref[...] = near_ref[0] + mid_ref[0].astype(F32)
    far_ref[...] = (near_ref[1] + mid_ref[1].astype(F32)).astype(B16)


def late_vector_body(x_ref, y_ref, from_x_ref, from_y_ref, v_ref, out_x_ref, out_y_ref, vector_ref):
    cols = x_ref.shape[2]
    out_x_ref[...] = (x_ref[...].astype(F32) + from_y_ref[:2].astype(F32)).astype(B16)
    out_y_ref[:, :, :cols] = (y_ref[...].astype(F32) + from_x_ref[:2, :, :cols].astype(F32)).astype(B16)
    vector = (v_ref[...].astype(F32) + from_x_ref[:2, :, cols:].astype(F32)).astype(B16)
    out_y_ref[:, :, cols:] = vector
    vector_ref[...] = vector


def own_vector_body(own_ref, from_x_ref, from_y_ref, late_x_ref, late_y_ref, v_ref, near_ref, mid_ref, vector_ref):
    cols = own_ref.shape[2]
    near_ref[...] = (
        own_ref[:2].astype(F32)
        + from_x_ref[2:, :, :cols].astype(F32)
        + late_y_ref[:, :, :cols].astype(F32)
    )
    mid_ref[:, :, :cols] = (
        own_ref[2:].astype(F32) + late_x_ref[...].astype(F32) + from_y_ref[2:].astype(F32)
    ).astype(B16)
    vector = (v_ref[...].astype(F32) + late_y_ref[:, :, cols:].astype(F32)).astype(B16)
    mid_ref[:, :, cols:] = vector
    vector_ref[...] = vector


def mid_vector_body(near_ref, mid_ref, v_ref, own_ref, far_ref, vector_ref):
    cols = own_ref.shape[1]
    own_ref[...] = near_ref[0] + mid_ref[0, :, :cols].astype(F32)
    far_ref[:, :cols] = (near_ref[1] + mid_ref[1, :, :cols].astype(F32)).astype(B16)
    vector = (v_ref[...].astype(F32) + mid_ref[:, :, cols:].astype(F32)).astype(B16)
    for k in range(2):
        far_ref[:, cols + 128 * k : cols + 128 * (k + 1)] = vector[k]
    vector_ref[...] = vector


def far_vector_body(own_ref, far_ref, v_ref, *outs):
    rows, cols = own_ref.shape
    part = cols // 4
    for k in range(4):
        lanes = slice(k * part, (k + 1) * part)
        outs[k][...] = own_ref[:, lanes] + far_ref[:, lanes].astype(F32)
    place = 0
    joined = [
        v_ref[k].astype(F32) + far_ref[:, cols + 128 * k : cols + 128 * (k + 1)].astype(F32) for k in range(2)
    ]
    for out_ref in outs[4:]:
        for k in range(out_ref.shape[0]):
            out_ref[k : k + 1] = joined[place // rows][place % rows : place % rows + 1]
            place += 1


def late_vector(late_x, late_y, from_x, from_y, vector):
    rows, cols = late_x.shape[1:]
    shapes = [(late_x.shape, B16), ((2, rows, cols + 128), B16), (vector.shape, B16)]
    operands = [late_x, late_y, from_x, from_y, vector]
    return call(late_vector_body, "late_vector", shapes, operands, limit=8)


def own_vector(own, from_x, from_y, late_x, late_y, vector):
    rows, cols = own.shape[1:]
    shapes = [((2, rows, cols), F32), ((2, rows, cols + 128), B16), (vector.shape, B16)]
    operands = [own, from_x, from_y, late_x, late_y, vector]
    return call(own_vector_body, "own_vector", shapes, operands, limit=8)


def mid_vector(near, mid, vector):
    rows, cols = near.shape[1:]
    shapes = [((rows, cols), F32), ((rows, cols + 256), B16), (vector.shape, B16)]
    return call(mid_vector_body, "mid_vector", shapes, [near, mid, vector], limit=8)


def far_vector(own, far, vector, sizes):
    rows, cols = own.shape
    shapes = [((rows, cols // 4), F32)] * 4 + [((size // 128, 128), F32) for size in sizes]
    outs = call(far_vector_body, "far_vector", shapes, [own, far, vector], limit=8)
    return outs[:4], [member.reshape(-1) for member in outs[4:]]


def add_late(late_x, late_y, from_x, from_y):
    shape = (late_x.shape, B16)
    return call(add_late_body, "add_late", [shape, shape], [late_x, late_y, from_x, from_y], limit=8)


def add_own(own, from_x, from_y, late_x, late_y):
    shapes = [(late_x.shape, F32), (late_x.shape, B16)]
    return call(add_own_body, "add_own", shapes, [own, from_x, from_y, late_x, late_y], limit=8)


def add_mid(near, mid):
    shapes = [(near.shape[1:], F32), (near.shape[1:], B16)]
    return call(add_mid_body, "add_mid", shapes, [near, mid], limit=8)


def per_device(dp_size, tokens, masked, lengths, mask_vector, w_query, b_query, w_key, w_value,
               b_value, w_out, b_out, gain_one, shift_one, w_up, b_up, w_down, b_down, gain_two,
               shift_two, grad_out):
    head_cols = w_query.shape[1]
    width = tokens.shape[1]
    fast = dp_size == BLOCKS and w_query.shape[0] % 16 == 0
    me = lax.axis_index("dp").astype(jnp.int32).reshape(1)
    if not fast:
        me = jnp.zeros_like(me)

    (b_query, b_value, b_out, gain_one, shift_one, b_up, b_down, gain_two, shift_two) = (
        member.astype(F32)
        for member in (b_query, b_value, b_out, gain_one, shift_one, b_up, b_down, gain_two, shift_two)
    )
    is_masked = (masked == 1)[:, None]
    flag = jnp.broadcast_to(is_masked, (masked.shape[0], 128)).astype(F32)
    in_low = jnp.where(is_masked, mask_vector[None, :], tokens)
    bias_qkv = jnp.concatenate([b_query, jnp.zeros_like(b_query), b_value])[None, :]
    vectors_one = jnp.stack([b_out, gain_one, shift_one])
    vectors_two = jnp.stack([gain_one, shift_one, b_down, gain_two, shift_two])
    b_up, gain_one = b_up[None, :], gain_one[None, :]

    a = jnp.concatenate([w_query, w_key, w_value, w_out.T], axis=1)
    c = w_up
    d = w_down.T
    if fast:
        az = swap(a, 12)
        az, me, flag, in_low, bias_qkv, vectors_one, vectors_two, b_up, gain_one = tie(
            az, me, flag, in_low, bias_qkv, vectors_one, vectors_two, b_up, gain_one
        )
        an = jnp.stack([a, az])
        anx, any_, am = swap(an, 1), swap(an, 2), swap(an, 4)
        anx, any_, am, an, c = tie(anx, any_, am, an, c)
        amx, amy, cz = swap(am, 1), swap(am, 2), swap(c, 12)
        amx, amy, cz, anx, c, d = tie(amx, amy, cz, anx, c, d)
        cn = jnp.stack([c, cz])
        amd, and_, cm = swap(amy, 1), swap(anx, 2), swap(cn, 4)
        cnx, cny, dz = swap(cn, 1), swap(cn, 2), swap(after(d, cm), 12)
        amd, and_, cm, cnx, cny = tie(amd, and_, cm, cnx, cny)
        dn = jnp.stack([d, dz])
        pieces_a = [an, am, anx, amx, any_, amy, and_, amd]
        cmx, cnd, dm = swap(cm, 1), swap(cnx, 2), swap(dn, 4)
        dnx, dny = swap(dn, 1), swap(dn, 2)
    else:
        a, c, d = (lax.all_gather(piece, "dp", axis=0, tiled=True) for piece in (a, c, d))
        pieces_a, pieces_c, pieces_d = as_pieces(a), as_pieces(c), as_pieces(d)
    w_a, qkv, prob, attended, part = attend(me, lengths, in_low, bias_qkv, pieces_a)
    if fast:
        cmx, cnd, dm, dnx, dny, cm, part = tie(cmx, cnd, dm, dnx, dny, cm, part)
        cmy, dnd, cmd = swap(cm, 2), swap(dny, 1), swap(cnd, 4)
    other = pair_swap(part)
    if fast:
        cmy, dnd, cmd, dm, other, part = tie(cmy, dnd, cmd, dm, other, part)
        pieces_c = [cn, cm, cnx, cmx, cny, cmy, cnd, cmd]
        dmx, dmy, dmd = swap(dm, 1), swap(dm, 2), swap(dnd, 4)
    w_u, normed_one, inverse_one, hidden_low, act_low, slope = up(
        me, in_low, part, other, vectors_one, b_up, pieces_c
    )
    if fast:
        dmx, dmy, dmd, act_low = tie(dmx, dmy, dmd, act_low)
        pieces_d = [dn, dm, dnx, dmx, dny, dmy, dnd, dmd]
    w_d, *parts = down(me, act_low, pieces_d)
    halves = [
        second_norm(index * part.shape[0], normed_one, part, pair_swap(part), grad_out, vectors_two)
        for index, part in enumerate(parts)
    ]
    results, dz_two, dz_two_low, sums_two = zip(*halves)
    dx, dy, turned = weight_grad(me, [dz_two_low], [act_low], ORDER[:2])
    if fast:
        dx, dy, turned, dz_two_low = tie(dx, dy, turned, dz_two_low)
        dxr, dyr = swap(dx, 1), swap(dy, 2)
    dxl, dyl, do = weight_grad(me, None, [act_low], ORDER[2:], turned=turned)
    d_pre_low, part, sums_up = hidden_back(dz_two_low, slope, w_d, w_u)
    cx, cy, cxl, cyl, co = weight_grad(me, [[hidden_low]], [d_pre_low])
    if fast:
        dxr, dyr, part, cx, cy, dxl, dyl, do = tie(dxr, dyr, part, cx, cy, dxl, dyl, do)
        cxr, cyr = swap(cx, 1), swap(cy, 2)
        dxl, dyl = add_late(dxl, dyl, dxr, dyr)
        dxlr, dylr = swap(dxl, 1), swap(dyl, 2)
    other = pair_swap(part)
    dz_one, dz_one_low, d_qkv, part, sums_one, sums_qkv = attend_back(
        lengths.shape[0], dz_two, part, other, normed_one, inverse_one, gain_one, flag, qkv, prob, w_a
    )
    if fast:
        cxr, cyr, dxlr, dylr, part, d_qkv, dz_one_low = tie(cxr, cyr, dxlr, dylr, part, d_qkv, dz_one_low)
        cxl, cyl = add_late(cxl, cyl, cxr, cyr)
        cxlr, cylr = swap(cxl, 1), swap(cyl, 2)
        d_near, d_mid = add_own(do, dxr, dyr, dxlr, dylr)
        d_midr = swap(d_mid, 4)
    sums_other = pair_swap(sums_one)
    joined = join(width // BLOCKS, sums_one, sums_other, sums_two, sums_up, sums_qkv)
    vector = joined.astype(B16) if fast else None
    ax, ay, axl, ayl, ao = weight_grad(me, [[in_low], [dz_one_low]], [d_qkv, attended], vector=vector)
    if fast:
        cxlr, cylr, d_midr, ax, ay, part = tie(cxlr, cylr, d_midr, ax, ay, part)
        axr, ayr = swap(ax, 1), swap(ay, 2)
        c_near, c_mid = add_own(co, cxr, cyr, cxlr, cylr)
        d_near, d_far = add_mid(d_near, d_midr)
        c_midr, d_farr = swap(c_mid, 4), swap(d_far, 12)
    other = pair_swap(part)
    d_tokens, result = last(dz_one, part, other, flag, results)
    sizes = [width] * 7 + [head_cols] * 2 + [w_up.shape[1]]
    if fast:
        axr, ayr, c_midr, d_farr, d_tokens, result = tie(axr, ayr, c_midr, d_farr, d_tokens, result)
        axl, ayl, vector = late_vector(axl, ayl, axr, ayr, vector)
        axlr, aylr = swap(axl, 1), swap(ayl, 2)
        c_near, c_far = add_mid(c_near, c_midr)
        c_farr = swap(c_far, 12)
        axlr, aylr, c_farr = tie(axlr, aylr, c_farr)
        a_near, a_mid, vector = own_vector(ao, axr, ayr, axlr, aylr, vector)
        a_midr = swap(a_mid, 4)
        d_w_down_t = d_near + d_farr.astype(F32)
        a_midr, d_w_down_t = tie(a_midr, d_w_down_t)
        a_near, a_far, vector = mid_vector(a_near, a_midr, vector)
        a_farr = swap(a_far, 12)
        d_w_up = c_near + c_farr.astype(F32)
        d_wa, summed = far_vector(a_near, a_farr, vector, sizes)
    else:
        full = []
        for parts in ((ax, ay, axl, ayl, ao), (cx, cy, cxl, cyl, co), (dx, dy, dxl, dyl, do)):
            blocks = [None] * BLOCKS
            for member, offsets in zip(parts, ORDER):
                for k, offset in enumerate(offsets):
                    blocks[offset] = member[k]
            full.append(jnp.concatenate(blocks).astype(F32))
        joined = lax.psum(joined, "dp")
        d_wa, d_w_up, d_w_down_t = (
            lax.psum_scatter(member, "dp", scatter_dimension=0, tiled=True) for member in full
        )
        d_wa = [d_wa[:, k * head_cols : (k + 1) * head_cols] for k in range(4)]
        joined = joined.reshape(-1)
        summed = []
        start = 0
        for size in sizes:
            summed.append(joined[start : start + size])
            start += size
    return (
        result,
        d_tokens,
        summed[0],
        d_wa[0],
        summed[7],
        d_wa[1],
        d_wa[2],
        summed[8],
        d_wa[3].T,
        summed[3],
        summed[1],
        summed[2],
        d_w_up,
        summed[9],
        d_w_down_t.T,
        summed[6],
        summed[4],
        summed[5],
    )


def solution(mesh):
    rows, flat, both = P("dp", None), P(), P("dp", "mp")
    return jax.shard_map(
        functools.partial(per_device, mesh.shape["dp"]),
        mesh=mesh,
        in_specs=(rows, P("dp"), P("dp"), flat, both, P("mp"), both, both, P("mp"), P("mp", "dp"),
                  flat, flat, flat, both, P("mp"), P("mp", "dp"), flat, flat, flat, rows),
        out_specs=(rows, rows, flat, both, P("mp"), both, both, P("mp"), P("mp", "dp"), flat, flat,
                   flat, both, P("mp"), P("mp", "dp"), flat, flat, flat),
        check_vma=False,
    )
```

```python
import functools

import jax
import jax.numpy as jnp
from jax import lax
from jax.experimental import pallas as pl
from jax.experimental.pallas import tpu as pltpu
from jax.sharding import PartitionSpec as P

HEAD = 64
NORM_EPS = 1e-05
F32 = jnp.float32
B16 = jnp.bfloat16
MIB = 1 << 20

BLOCKS = 16
NEAR = (0, 12)
MID = (4, 8)


def swap(values, bit):
    return lax.ppermute(values, "dp", [(i, i ^ bit) for i in range(BLOCKS)])


def tie(*values):
    return lax.optimization_barrier(values)


def after(value, *earlier):
    return tie(value, *earlier)[0]


def pair_swap(partial):
    return lax.ppermute(partial, "mp", [(0, 1), (1, 0)])


def as_pieces(full):
    rows = full.shape[0] // BLOCKS
    blocks = full.reshape(BLOCKS, rows, full.shape[1])
    return [
        jnp.stack([blocks[offset + bits[0]], blocks[offset + bits[1]]])
        for offset in range(4)
        for bits in (NEAR, MID)
    ]


SMEM_SPEC = pl.BlockSpec(memory_space=pltpu.SMEM)
VMEM_SPEC = pl.BlockSpec(memory_space=pltpu.VMEM)
CHUNK = 256
UNROLL = 8
LIGHT = pl.CostEstimate(flops=1, bytes_accessed=1, transcendentals=0)


def call(body, name, shapes, operands, scratch=(), limit=16):
    return pl.pallas_call(
        body,
        in_specs=[
            SMEM_SPEC if member.dtype == jnp.int32 and member.ndim == 1 else VMEM_SPEC
            for member in operands
        ],
        out_specs=[VMEM_SPEC] * len(shapes),
        out_shape=[jax.ShapeDtypeStruct(shape, dtype) for shape, dtype in shapes],
        scratch_shapes=[pltpu.VMEM(shape, dtype) for shape, dtype in scratch],
        compiler_params=pltpu.CompilerParams(vmem_limit_bytes=limit * MIB),
        cost_estimate=LIGHT,
        name=name,
    )(*operands)


def chunks(count):
    return [slice(start, start + CHUNK) for start in range(0, count, CHUNK)]


def loop(count, step, size=CHUNK, unroll=1):
    def body(index, carry):
        step(pl.ds(pl.multiple_of(index * size, size), size))
        return carry

    lax.fori_loop(0, count // size, body, 0, unroll=unroll)


PAIRS = [(q + bits[k], 2 * q + m, k) for q in range(4) for m, bits in enumerate((NEAR, MID)) for k in range(2)]


def fill(me, pieces, full_ref):
    rows = pieces[0].shape[1]
    for offset, piece, index in PAIRS:
        block = me ^ offset
        full_ref[pl.ds(pl.multiple_of(block * rows, rows), rows), :] = pieces[piece][index]


def dot(left, right):
    return jnp.dot(left, right, preferred_element_type=F32)


def dot_t(left, right):
    return lax.dot_general(left, right, (((1,), (1,)), ((), ())), preferred_element_type=F32)


def t_dot(left, right):
    return lax.dot_general(left, right, (((0,), (0,)), ((), ())), preferred_element_type=F32)


def row_mean(values):
    return jnp.mean(values, axis=-1, keepdims=True)


def normalize(values):
    centred = values - row_mean(values)
    inverse = lax.rsqrt(row_mean(centred * centred) + NORM_EPS)
    return centred * inverse, inverse


def col_sum(values):
    return jnp.sum(values, axis=0, keepdims=True)


def norm_back(scaled, normed, inverse):
    return inverse * (scaled - row_mean(scaled) - normed * row_mean(scaled * normed))


def two_heads(slots):
    row = lax.broadcasted_iota(jnp.int32, (2 * slots, 2 * HEAD), 0) // slots
    lane = lax.broadcasted_iota(jnp.int32, (2 * slots, 2 * HEAD), 1) // HEAD
    return (row == lane).astype(F32).astype(B16)


def doubled(values, mask):
    return jnp.concatenate([values, values], axis=0) * mask


def attend_body(slots, me_ref, len_ref, in_ref, bias_ref, *rest):
    pieces, (w_ref, qkv_ref, prob_ref, att_ref, part_ref) = rest[:-5], rest[-5:]
    count, width = att_ref.shape
    fill(me_ref[0], pieces, w_ref)

    def project(rows):
        qkv_ref[rows] = (dot(in_ref[rows], w_ref[:, : 3 * width]) + bias_ref[...]).astype(B16)

    loop(count, project, unroll=4)
    mask = two_heads(slots)
    key_slot = lax.broadcasted_iota(jnp.int32, (slots, slots), 1)

    def chain_step(chain, carry):
        valid = key_slot < len_ref[chain]
        rows = pl.ds(pl.multiple_of(chain * slots, slots), slots)
        for pair in range(width // (2 * HEAD)):
            lanes = 2 * HEAD * pair
            query = qkv_ref[rows, lanes : lanes + 2 * HEAD]
            key = qkv_ref[rows, width + lanes : width + lanes + 2 * HEAD]
            value = qkv_ref[rows, 2 * width + lanes : 2 * width + lanes + 2 * HEAD]
            scores = dot_t(query * (HEAD**-0.5), doubled(key, mask))
            probs = []
            for head in range(2):
                part = jnp.where(valid, scores[:, head * slots : (head + 1) * slots], -1e30)
                terms = jnp.exp(part - jnp.max(part, axis=-1, keepdims=True))
                probs.append((terms / jnp.sum(terms, axis=-1, keepdims=True)).astype(B16))
            prob = jnp.concatenate(probs, axis=1)
            prob_ref[rows, 2 * slots * pair : 2 * slots * (pair + 1)] = prob
            att_ref[rows, lanes : lanes + 2 * HEAD] = dot(prob, doubled(value, mask)).astype(B16)
        return carry

    lax.fori_loop(0, count // slots, chain_step, 0, unroll=UNROLL)

    def bring_out(rows):
        part_ref[rows] = dot_t(att_ref[rows], w_ref[:, 3 * width :]).astype(B16)

    loop(count, bring_out, unroll=4)


def attend(me, lengths, in_low, bias, pieces):
    count, width = in_low.shape
    heads = bias.shape[1] // 3
    slots = count // lengths.shape[0]
    shapes = [
        ((width, 4 * heads), B16),
        ((count, 3 * heads), B16),
        ((count, heads // HEAD * slots), B16),
        ((count, heads), B16),
        ((count, width), B16),
    ]
    body = functools.partial(attend_body, slots)
    return call(body, "attend", shapes, [me, lengths, in_low, bias, *pieces])


def up_body(me_ref, in_ref, own_ref, other_ref, vec_ref, bias_ref, *rest):
    pieces, (w_ref, normed_ref, inverse_ref, low_ref, act_ref, slope_ref) = rest[:-6], rest[-6:]
    fill(me_ref[0], pieces, w_ref)
    vectors = vec_ref[...]

    def step(rows):
        attn = own_ref[rows].astype(F32) + other_ref[rows].astype(F32) + vectors[0:1]
        normed, inverse = normalize(in_ref[rows].astype(F32) + attn)
        normed_ref[rows] = normed
        inverse_ref[rows] = jnp.broadcast_to(inverse, (CHUNK, inverse_ref.shape[1]))
        low_ref[rows] = (normed * vectors[1:2] + vectors[2:3]).astype(B16)
        pre = dot(low_ref[rows], w_ref[...]) + bias_ref[...]
        cdf = 0.5 + 0.5 * lax.erf(pre * (2.0**-0.5))
        act_ref[rows] = (pre * cdf).astype(B16)
        density = jnp.exp(pre * pre * -0.5) * 0.3989422804014327
        slope_ref[rows] = (cdf + pre * density).astype(B16)

    loop(in_ref.shape[0], step, unroll=2)


def up(me, in_low, own, other, vectors, bias, pieces):
    count, width = in_low.shape
    units = bias.shape[1]
    shapes = [
        ((width, units), B16),
        ((count, width), F32),
        ((count, 128), F32),
        ((count, width), B16),
        ((count, units), B16),
        ((count, units), B16),
    ]
    return call(up_body, "up", shapes, [me, in_low, own, other, vectors, bias, *pieces])


def down_body(me_ref, act_ref, *rest):
    pieces, (w_ref, part_ref) = rest[:-2], rest[-2:]
    fill(me_ref[0], pieces, w_ref)
    for rows in chunks(part_ref.shape[0]):
        part_ref[rows] = dot_t(act_ref[rows], w_ref[...]).astype(B16)


def down_rest_body(act_ref, w_ref, part_ref):
    half = part_ref.shape[0]
    for rows in chunks(half):
        part_ref[rows] = dot_t(act_ref[half + rows.start : half + rows.stop], w_ref[...]).astype(B16)


def down(me, act, pieces):
    count, units = act.shape
    width = BLOCKS * pieces[0].shape[1]
    half = ((count // 2, width), B16)
    w_down_t, first = call(down_body, "down", [((width, units), B16), half], [me, act, *pieces])
    (second,) = call(down_rest_body, "down_rest", [half], [act, w_down_t])
    return w_down_t, first, second


def second_norm_body(start, normed_ref, own_ref, other_ref, grad_ref, vec_ref, out_ref, dz_ref, low_ref, sum_ref):
    vectors = vec_ref[...]
    sum_ref[...] = jnp.zeros_like(sum_ref)
    for rows in chunks(own_ref.shape[0]):
        there = slice(start + rows.start, start + rows.stop)
        hidden = normed_ref[there] * vectors[0:1] + vectors[1:2]
        ffn = own_ref[rows].astype(F32) + other_ref[rows].astype(F32) + vectors[2:3]
        normed, inverse = normalize(hidden + ffn)
        out_ref[rows] = (normed * vectors[3:4] + vectors[4:5]).astype(B16)
        grad = grad_ref[there].astype(F32)
        dz = norm_back(grad * vectors[3:4], normed, inverse)
        dz_ref[rows] = dz
        low_ref[rows] = dz.astype(B16)
        sum_ref[0:1] += col_sum(grad * normed)
        sum_ref[1:2] += col_sum(grad)
        sum_ref[2:3] += col_sum(dz)


def second_norm(start, normed, own, other, grad, vectors):
    shape = own.shape
    shapes = [(shape, B16), (shape, F32), (shape, B16), ((8, shape[1]), F32)]
    body = functools.partial(second_norm_body, start)
    return call(body, "second_norm", shapes, [normed, own, other, grad, vectors])


def rows_in(halves, rows):
    size = halves[0].shape[0]
    half = halves[rows.start // size]
    return half[rows.start % size : rows.start % size + rows.stop - rows.start]


ORDER = (
    (3, 15, 1, 13),
    (7, 11, 6, 10),
    (5, 9),
    (2, 14),
    (0, 12, 4, 8),
)


def weight_grad(me, lefts, rights, groups=ORDER, vector=None, turned=None):
    count = rights[0].shape[0]
    width = lefts[-1][0].shape[1] if turned is None else turned.shape[0]
    tile = 384 if all(right.shape[1] % 384 == 0 for right in rights) else 128
    total = sum(right.shape[1] for right in rights)
    rows = width // BLOCKS
    n = len(rights)
    flat = [half for left in lefts for half in left] if turned is None else [turned]
    wide = [] if vector is None else [vector]
    keep = turned is None and len(groups) < len(ORDER)
    wanted = [offset for offsets in groups for offset in offsets]

    def body(me_ref, *refs):
        left_refs, right_refs = list(refs[: len(flat)]), refs[len(flat) : len(flat) + n]
        outs = refs[len(flat) + n + len(wide) :]
        placed_ref = outs[-1]
        if wide:
            outs[0][0:2, :, total:] = refs[len(flat) + n][...]
            outs[0][2:4, :, total:] = jnp.zeros((2, rows, 128), B16)
        at = 0
        for index, right_ref in enumerate(right_refs):
            turned_ref = left_refs[0] if turned is not None else outs[-2]
            if turned is None:
                start = 0
                for _ in lefts[index]:
                    half_ref = left_refs.pop(0)
                    turned_ref[:, start : start + half_ref.shape[0]] = half_ref[...].T
                    start += half_ref.shape[0]
            for k, offset in enumerate(wanted):
                place = pl.multiple_of((me_ref[0] ^ offset) * rows, rows)
                placed_ref[k * rows : (k + 1) * rows] = turned_ref[pl.ds(place, rows), :]

            def step(cols, right_ref=right_ref, at=at):
                product = dot(placed_ref[...], right_ref[:, cols]).astype(B16)
                there = pl.ds(pl.multiple_of(at + cols.start, 128), tile)
                first = 0
                for out_ref, offsets in zip(outs, groups):
                    for k in range(len(offsets)):
                        out_ref[k, :, there] = product[first : first + rows]
                        first += rows

            count_tiles = right_ref.shape[1] // tile
            loop(right_ref.shape[1], step, tile, unroll=count_tiles if wide or keep else 1)
            at += right_ref.shape[1]

    shapes = [((len(offsets), rows, total), B16) for offsets in groups]
    shapes[0] = ((len(groups[0]), rows, total + 128 * len(wide)), B16)
    held = ((width, count), B16)
    shapes += [held] * keep
    scratch = [held] * (turned is None and not keep) + [((len(wanted) * rows, count), B16)]
    return call(body, "weight_grad", shapes, [me, *flat, *rights, *wide], scratch)


def hidden_back_body(low_a_ref, low_b_ref, slope_ref, down_ref, up_ref, pre_ref, part_ref, sum_ref):
    sum_ref[...] = jnp.zeros_like(sum_ref)
    half = low_a_ref.shape[0]
    for start, low_ref in ((0, low_a_ref), (half, low_b_ref)):

        def step(here, start=start, low_ref=low_ref):
            rows = pl.ds(pl.multiple_of(start + here.start, CHUNK), CHUNK)
            d_pre = dot(low_ref[here], down_ref[...]) * slope_ref[rows].astype(F32)
            sum_ref[0:1] += col_sum(d_pre)
            pre_ref[rows] = d_pre.astype(B16)
            part_ref[rows] = dot_t(pre_ref[rows], up_ref[...]).astype(B16)

        loop(half, step)


def hidden_back(lows, slope, w_down_t, w_up):
    count, units = slope.shape
    shapes = [((count, units), B16), ((count, w_up.shape[0]), B16), ((8, units), F32)]
    return call(hidden_back_body, "hidden_back", shapes, [*lows, slope, w_down_t, w_up])


def attend_back_body(slots, dz_a_ref, dz_b_ref, own_ref, other_ref, normed_ref, inverse_ref, gain_ref,
                     flag_ref, qkv_ref, prob_ref, w_ref, dz_one_ref, low_ref, d_qkv_ref, part_ref, sum_ref,
                     sum_qkv_ref, d_att_ref):
    count, width = d_att_ref.shape
    sum_ref[...] = jnp.zeros_like(sum_ref)
    sum_qkv_ref[...] = jnp.zeros_like(sum_qkv_ref)
    half = dz_a_ref.shape[0]
    for start, dz_ref in ((0, dz_a_ref), (half, dz_b_ref)):

        def step(here, start=start, dz_ref=dz_ref):
            rows = pl.ds(pl.multiple_of(start + here.start, CHUNK), CHUNK)
            normed = normed_ref[rows]
            d_hidden = dz_ref[here] + (own_ref[rows].astype(F32) + other_ref[rows].astype(F32))
            dz_one = norm_back(d_hidden * gain_ref[...], normed, inverse_ref[rows, 0:1])
            dz_one_ref[rows] = dz_one
            low_ref[rows] = dz_one.astype(B16)
            sum_ref[0:1] += col_sum(d_hidden * normed)
            sum_ref[1:2] += col_sum(d_hidden)
            sum_ref[2:3] += col_sum(dz_one)
            sum_ref[3:4] += col_sum(dz_one * flag_ref[rows, 0:1])
            d_att_ref[rows] = dot(low_ref[rows], w_ref[:, 3 * width :]).astype(B16)

        loop(half, step)
    mask = two_heads(slots)

    def chain_step(chain, carry):
        rows = pl.ds(pl.multiple_of(chain * slots, slots), slots)
        for pair in range(width // (2 * HEAD)):
            lanes = 2 * HEAD * pair
            query = qkv_ref[rows, lanes : lanes + 2 * HEAD]
            key = qkv_ref[rows, width + lanes : width + lanes + 2 * HEAD]
            value = qkv_ref[rows, 2 * width + lanes : 2 * width + lanes + 2 * HEAD]
            d_att = d_att_ref[rows, lanes : lanes + 2 * HEAD]
            prob = prob_ref[rows, 2 * slots * pair : 2 * slots * (pair + 1)]
            d_prob = dot_t(d_att, doubled(value, mask))
            weights = prob.astype(F32)
            products = weights * d_prob
            lows = []
            for head in range(2):
                half = slice(head * slots, (head + 1) * slots)
                total = jnp.sum(products[:, half], axis=-1, keepdims=True)
                lows.append((products[:, half] - weights[:, half] * total).astype(B16))
            low = jnp.concatenate(lows, axis=1)
            d_query = dot(low, doubled(key, mask)) * (HEAD**-0.5)
            tall = jnp.concatenate(lows, axis=0)
            d_key = t_dot(tall, doubled(query, mask)) * (HEAD**-0.5)
            tall = jnp.concatenate([prob[:, :slots], prob[:, slots:]], axis=0)
            d_value = t_dot(tall, doubled(d_att, mask))
            d_qkv_ref[rows, lanes : lanes + 2 * HEAD] = d_query.astype(B16)
            d_qkv_ref[rows, width + lanes : width + lanes + 2 * HEAD] = d_key.astype(B16)
            d_qkv_ref[rows, 2 * width + lanes : 2 * width + lanes + 2 * HEAD] = d_value.astype(B16)
        return carry

    lax.fori_loop(0, count // slots, chain_step, 0)

    def bring_back(rows):
        sum_qkv_ref[0:1] += col_sum(d_qkv_ref[rows].astype(F32))
        part = dot_t(d_qkv_ref[rows], w_ref[:, : 3 * width]).astype(B16)
        part_ref[rows] = part
        sum_ref[4:5] += col_sum(part.astype(F32) * flag_ref[rows, 0:1])

    loop(count, bring_back)


def attend_back(chain_count, dz_two, own, other, normed, inverse, gain, flag, qkv, prob, w_a):
    shape = normed.shape
    heads = qkv.shape[1] // 3
    shapes = [
        (shape, F32),
        (shape, B16),
        (qkv.shape, B16),
        (shape, B16),
        ((8, shape[1]), F32),
        ((8, 3 * heads), F32),
    ]
    operands = [*dz_two, own, other, normed, inverse, gain, flag, qkv, prob, w_a]
    body = functools.partial(attend_back_body, shape[0] // chain_count)
    return call(body, "attend_back", shapes, operands, [((shape[0], heads), B16)])


def join_body(one_ref, other_ref, two_a_ref, two_b_ref, up_ref, qkv_ref, out_ref):
    width = one_ref.shape[1]
    heads = qkv_ref.shape[1] // 3
    rows = out_ref.shape[1]
    out_ref[...] = jnp.zeros_like(out_ref)

    def put(start, values):
        for k in range(values.shape[1] // 128):
            place = (start + 128 * k) // 128
            chunk = values[:, 128 * k : 128 * (k + 1)]
            out_ref[place // rows, place % rows : place % rows + 1] = chunk

    put(0, one_ref[3:4] + (one_ref[4:5] + other_ref[4:5]))
    for k in range(3):
        put((1 + k) * width, one_ref[k : k + 1])
        put((4 + k) * width, two_a_ref[k : k + 1] + two_b_ref[k : k + 1])
    put(7 * width, qkv_ref[0:1, :heads])
    put(7 * width + heads, qkv_ref[0:1, 2 * heads :])
    put(7 * width + 2 * heads, up_ref[0:1])


def join(rows, sums_one, sums_other, sums_two, sums_up, sums_qkv):
    width = sums_one.shape[1]
    length = 7 * width + 2 * sums_qkv.shape[1] // 3 + sums_up.shape[1]
    assert length <= 2 * rows * 128
    operands = [sums_one, sums_other, *sums_two, sums_up, sums_qkv]
    return call(join_body, "join", [((2, rows, 128), F32)], operands, limit=4)[0]


def last_body(dz_ref, own_ref, other_ref, flag_ref, out_a_ref, out_b_ref, tokens_ref, out_ref):
    for rows in chunks(dz_ref.shape[0]):
        total = dz_ref[rows] + (own_ref[rows].astype(F32) + other_ref[rows].astype(F32))
        tokens_ref[rows] = jnp.where(flag_ref[rows, 0:1] > 0.0, 0.0, total)
        out_ref[rows] = rows_in((out_a_ref, out_b_ref), rows)


def last(dz_one, own, other, flag, results):
    shapes = [(dz_one.shape, F32), (dz_one.shape, B16)]
    return call(last_body, "last", shapes, [dz_one, own, other, flag, *results])


def add_late_body(x_ref, y_ref, from_x_ref, from_y_ref, out_x_ref, out_y_ref):
    out_x_ref[...] = (x_ref[...].astype(F32) + from_y_ref[:2].astype(F32)).astype(B16)
    out_y_ref[...] = (y_ref[...].astype(F32) + from_x_ref[:2].astype(F32)).astype(B16)


def add_own_body(own_ref, from_x_ref, from_y_ref, late_x_ref, late_y_ref, near_ref, mid_ref):
    near_ref[...] = (
        own_ref[:2].astype(F32) + from_x_ref[2:].astype(F32) + late_y_ref[...].astype(F32)
    )
    mid_ref[...] = (
        own_ref[2:].astype(F32) + late_x_ref[...].astype(F32) + from_y_ref[2:].astype(F32)
    ).astype(B16)


def add_mid_body(near_ref, mid_ref, own_ref, far_ref):
    own_ref[...] = near_ref[0] + mid_ref[0].astype(F32)
    far_ref[...] = (near_ref[1] + mid_ref[1].astype(F32)).astype(B16)


def late_vector_body(x_ref, y_ref, from_x_ref, from_y_ref, v_ref, out_x_ref, out_y_ref, vector_ref):
    cols = x_ref.shape[2]
    out_x_ref[...] = (x_ref[...].astype(F32) + from_y_ref[:2].astype(F32)).astype(B16)
    out_y_ref[:, :, :cols] = (y_ref[...].astype(F32) + from_x_ref[:2, :, :cols].astype(F32)).astype(B16)
    vector = (v_ref[...].astype(F32) + from_x_ref[:2, :, cols:].astype(F32)).astype(B16)
    out_y_ref[:, :, cols:] = vector
    vector_ref[...] = vector


def own_vector_body(own_ref, from_x_ref, from_y_ref, late_x_ref, late_y_ref, v_ref, near_ref, mid_ref, vector_ref):
    cols = own_ref.shape[2]
    near_ref[...] = (
        own_ref[:2].astype(F32)
        + from_x_ref[2:, :, :cols].astype(F32)
        + late_y_ref[:, :, :cols].astype(F32)
    )
    mid_ref[:, :, :cols] = (
        own_ref[2:].astype(F32) + late_x_ref[...].astype(F32) + from_y_ref[2:].astype(F32)
    ).astype(B16)
    vector = (v_ref[...].astype(F32) + late_y_ref[:, :, cols:].astype(F32)).astype(B16)
    mid_ref[:, :, cols:] = vector
    vector_ref[...] = vector


def mid_vector_body(near_ref, mid_ref, v_ref, own_ref, far_ref, vector_ref):
    cols = own_ref.shape[1]
    own_ref[...] = near_ref[0] + mid_ref[0, :, :cols].astype(F32)
    far_ref[:, :cols] = (near_ref[1] + mid_ref[1, :, :cols].astype(F32)).astype(B16)
    vector = (v_ref[...].astype(F32) + mid_ref[:, :, cols:].astype(F32)).astype(B16)
    for k in range(2):
        far_ref[:, cols + 128 * k : cols + 128 * (k + 1)] = vector[k]
    vector_ref[...] = vector


def far_vector_body(own_ref, far_ref, v_ref, *outs):
    rows, cols = own_ref.shape
    part = cols // 4
    for k in range(4):
        lanes = slice(k * part, (k + 1) * part)
        outs[k][...] = own_ref[:, lanes] + far_ref[:, lanes].astype(F32)
    place = 0
    joined = [
        v_ref[k].astype(F32) + far_ref[:, cols + 128 * k : cols + 128 * (k + 1)].astype(F32) for k in range(2)
    ]
    for out_ref in outs[4:]:
        for k in range(out_ref.shape[0]):
            out_ref[k : k + 1] = joined[place // rows][place % rows : place % rows + 1]
            place += 1


def late_vector(late_x, late_y, from_x, from_y, vector):
    rows, cols = late_x.shape[1:]
    shapes = [(late_x.shape, B16), ((2, rows, cols + 128), B16), (vector.shape, B16)]
    operands = [late_x, late_y, from_x, from_y, vector]
    return call(late_vector_body, "late_vector", shapes, operands, limit=8)


def own_vector(own, from_x, from_y, late_x, late_y, vector):
    rows, cols = own.shape[1:]
    shapes = [((2, rows, cols), F32), ((2, rows, cols + 128), B16), (vector.shape, B16)]
    operands = [own, from_x, from_y, late_x, late_y, vector]
    return call(own_vector_body, "own_vector", shapes, operands, limit=8)


def mid_vector(near, mid, vector):
    rows, cols = near.shape[1:]
    shapes = [((rows, cols), F32), ((rows, cols + 256), B16), (vector.shape, B16)]
    return call(mid_vector_body, "mid_vector", shapes, [near, mid, vector], limit=8)


def far_vector(own, far, vector, sizes):
    rows, cols = own.shape
    shapes = [((rows, cols // 4), F32)] * 4 + [((size // 128, 128), F32) for size in sizes]
    outs = call(far_vector_body, "far_vector", shapes, [own, far, vector], limit=8)
    return outs[:4], [member.reshape(-1) for member in outs[4:]]


def add_late(late_x, late_y, from_x, from_y):
    shape = (late_x.shape, B16)
    return call(add_late_body, "add_late", [shape, shape], [late_x, late_y, from_x, from_y], limit=8)


def add_own(own, from_x, from_y, late_x, late_y):
    shapes = [(late_x.shape, F32), (late_x.shape, B16)]
    return call(add_own_body, "add_own", shapes, [own, from_x, from_y, late_x, late_y], limit=8)


def add_mid(near, mid):
    shapes = [(near.shape[1:], F32), (near.shape[1:], B16)]
    return call(add_mid_body, "add_mid", shapes, [near, mid], limit=8)


def per_device(dp_size, tokens, masked, lengths, mask_vector, w_query, b_query, w_key, w_value,
               b_value, w_out, b_out, gain_one, shift_one, w_up, b_up, w_down, b_down, gain_two,
               shift_two, grad_out):
    head_cols = w_query.shape[1]
    width = tokens.shape[1]
    fast = dp_size == BLOCKS and w_query.shape[0] % 16 == 0
    me = lax.axis_index("dp").astype(jnp.int32).reshape(1)
    if not fast:
        me = jnp.zeros_like(me)

    (b_query, b_value, b_out, gain_one, shift_one, b_up, b_down, gain_two, shift_two) = (
        member.astype(F32)
        for member in (b_query, b_value, b_out, gain_one, shift_one, b_up, b_down, gain_two, shift_two)
    )
    is_masked = (masked == 1)[:, None]
    flag = jnp.broadcast_to(is_masked, (masked.shape[0], 128)).astype(F32)
    in_low = jnp.where(is_masked, mask_vector[None, :], tokens)
    bias_qkv = jnp.concatenate([b_query, jnp.zeros_like(b_query), b_value])[None, :]
    vectors_one = jnp.stack([b_out, gain_one, shift_one])
    vectors_two = jnp.stack([gain_one, shift_one, b_down, gain_two, shift_two])
    b_up, gain_one = b_up[None, :], gain_one[None, :]

    a = jnp.concatenate([w_query, w_key, w_value, w_out.T], axis=1)
    c = w_up
    d = w_down.T
    if fast:
        az = swap(a, 12)
        az, me, flag, in_low, bias_qkv, vectors_one, vectors_two, b_up, gain_one = tie(
            az, me, flag, in_low, bias_qkv, vectors_one, vectors_two, b_up, gain_one
        )
        an = jnp.stack([a, az])
        anx, any_, am = swap(an, 1), swap(an, 2), swap(an, 4)
        anx, any_, am, an, c = tie(anx, any_, am, an, c)
        amx, amy, cz = swap(am, 1), swap(am, 2), swap(c, 12)
        amx, amy, cz, anx, c, d = tie(amx, amy, cz, anx, c, d)
        cn = jnp.stack([c, cz])
        amd, and_, cm = swap(amy, 1), swap(anx, 2), swap(cn, 4)
        cnx, cny, dz = swap(cn, 1), swap(cn, 2), swap(after(d, cm), 12)
        amd, and_, cm, cnx, cny = tie(amd, and_, cm, cnx, cny)
        dn = jnp.stack([d, dz])
        pieces_a = [an, am, anx, amx, any_, amy, and_, amd]
        cmx, cnd, dm = swap(cm, 1), swap(cnx, 2), swap(dn, 4)
        dnx, dny = swap(dn, 1), swap(dn, 2)
    else:
        a, c, d = (lax.all_gather(piece, "dp", axis=0, tiled=True) for piece in (a, c, d))
        pieces_a, pieces_c, pieces_d = as_pieces(a), as_pieces(c), as_pieces(d)
    w_a, qkv, prob, attended, part = attend(me, lengths, in_low, bias_qkv, pieces_a)
    if fast:
        cmx, cnd, dm, dnx, dny, cm, part = tie(cmx, cnd, dm, dnx, dny, cm, part)
        cmy, dnd, cmd = swap(cm, 2), swap(dny, 1), swap(cnd, 4)
    other = pair_swap(part)
    if fast:
        cmy, dnd, cmd, dm, other, part = tie(cmy, dnd, cmd, dm, other, part)
        pieces_c = [cn, cm, cnx, cmx, cny, cmy, cnd, cmd]
        dmx, dmy, dmd = swap(dm, 1), swap(dm, 2), swap(dnd, 4)
    w_u, normed_one, inverse_one, hidden_low, act_low, slope = up(
        me, in_low, part, other, vectors_one, b_up, pieces_c
    )
    if fast:
        dmx, dmy, dmd, act_low = tie(dmx, dmy, dmd, act_low)
        pieces_d = [dn, dm, dnx, dmx, dny, dmy, dnd, dmd]
    w_d, *parts = down(me, act_low, pieces_d)
    halves = [
        second_norm(index * part.shape[0], normed_one, part, pair_swap(part), grad_out, vectors_two)
        for index, part in enumerate(parts)
    ]
    results, dz_two, dz_two_low, sums_two = zip(*halves)
    dx, dy, turned = weight_grad(me, [dz_two_low], [act_low], ORDER[:2])
    if fast:
        dx, dy, turned, dz_two_low = tie(dx, dy, turned, dz_two_low)
        dxr, dyr = swap(dx, 1), swap(dy, 2)
    dxl, dyl, do = weight_grad(me, None, [act_low], ORDER[2:], turned=turned)
    d_pre_low, part, sums_up = hidden_back(dz_two_low, slope, w_d, w_u)
    cx, cy, cxl, cyl, co = weight_grad(me, [[hidden_low]], [d_pre_low])
    if fast:
        dxr, dyr, part, cx, cy, dxl, dyl, do = tie(dxr, dyr, part, cx, cy, dxl, dyl, do)
        cxr, cyr = swap(cx, 1), swap(cy, 2)
        dxl, dyl = add_late(dxl, dyl, dxr, dyr)
        dxlr, dylr = swap(dxl, 1), swap(dyl, 2)
    other = pair_swap(part)
    dz_one, dz_one_low, d_qkv, part, sums_one, sums_qkv = attend_back(
        lengths.shape[0], dz_two, part, other, normed_one, inverse_one, gain_one, flag, qkv, prob, w_a
    )
    if fast:
        cxr, cyr, dxlr, dylr, part, d_qkv, dz_one_low = tie(cxr, cyr, dxlr, dylr, part, d_qkv, dz_one_low)
        cxl, cyl = add_late(cxl, cyl, cxr, cyr)
        cxlr, cylr = swap(cxl, 1), swap(cyl, 2)
        d_near, d_mid = add_own(do, dxr, dyr, dxlr, dylr)
        d_midr = swap(d_mid, 4)
    sums_other = pair_swap(sums_one)
    joined = join(width // BLOCKS, sums_one, sums_other, sums_two, sums_up, sums_qkv)
    vector = joined.astype(B16) if fast else None
    ax, ay, axl, ayl, ao = weight_grad(me, [[in_low], [dz_one_low]], [d_qkv, attended], vector=vector)
    if fast:
        cxlr, cylr, d_midr, ax, ay, part = tie(cxlr, cylr, d_midr, ax, ay, part)
        axr, ayr = swap(ax, 1), swap(ay, 2)
        c_near, c_mid = add_own(co, cxr, cyr, cxlr, cylr)
        d_near, d_far = add_mid(d_near, d_midr)
        c_midr, d_farr = swap(c_mid, 4), swap(d_far, 12)
    other = pair_swap(part)
    d_tokens, result = last(dz_one, part, other, flag, results)
    sizes = [width] * 7 + [head_cols] * 2 + [w_up.shape[1]]
    if fast:
        axr, ayr, c_midr, d_farr, d_tokens, result = tie(axr, ayr, c_midr, d_farr, d_tokens, result)
        axl, ayl, vector = late_vector(axl, ayl, axr, ayr, vector)
        axlr, aylr = swap(axl, 1), swap(ayl, 2)
        c_near, c_far = add_mid(c_near, c_midr)
        c_farr = swap(c_far, 12)
        axlr, aylr, c_farr = tie(axlr, aylr, c_farr)
        a_near, a_mid, vector = own_vector(ao, axr, ayr, axlr, aylr, vector)
        a_midr = swap(a_mid, 4)
        d_w_down_t = d_near + d_farr.astype(F32)
        a_midr, d_w_down_t = tie(a_midr, d_w_down_t)
        a_near, a_far, vector = mid_vector(a_near, a_midr, vector)
        a_farr = swap(a_far, 12)
        d_w_up = c_near + c_farr.astype(F32)
        d_wa, summed = far_vector(a_near, a_farr, vector, sizes)
    else:
        full = []
        for parts in ((ax, ay, axl, ayl, ao), (cx, cy, cxl, cyl, co), (dx, dy, dxl, dyl, do)):
            blocks = [None] * BLOCKS
            for member, offsets in zip(parts, ORDER):
                for k, offset in enumerate(offsets):
                    blocks[offset] = member[k]
            full.append(jnp.concatenate(blocks).astype(F32))
        joined = lax.psum(joined, "dp")
        d_wa, d_w_up, d_w_down_t = (
            lax.psum_scatter(member, "dp", scatter_dimension=0, tiled=True) for member in full
        )
        d_wa = [d_wa[:, k * head_cols : (k + 1) * head_cols] for k in range(4)]
        joined = joined.reshape(-1)
        summed = []
        start = 0
        for size in sizes:
            summed.append(joined[start : start + size])
            start += size
    return (
        result,
        d_tokens,
        summed[0],
        d_wa[0],
        summed[7],
        d_wa[1],
        d_wa[2],
        summed[8],
        d_wa[3].T,
        summed[3],
        summed[1],
        summed[2],
        d_w_up,
        summed[9],
        d_w_down_t.T,
        summed[6],
        summed[4],
        summed[5],
    )


def solution(mesh):
    rows, flat, both = P("dp", None), P(), P("dp", "mp")
    return jax.shard_map(
        functools.partial(per_device, mesh.shape["dp"]),
        mesh=mesh,
        in_specs=(rows, P("dp"), P("dp"), flat, both, P("mp"), both, both, P("mp"), P("mp", "dp"),
                  flat, flat, flat, both, P("mp"), P("mp", "dp"), flat, flat, flat, rows),
        out_specs=(rows, rows, flat, both, P("mp"), both, both, P("mp"), P("mp", "dp"), flat, flat,
                   flat, both, P("mp"), P("mp", "dp"), flat, flat, flat),
        check_vma=False,
    )
```

```python
import functools

import jax
import jax.numpy as jnp
from jax import lax
from jax.experimental import pallas as pl
from jax.experimental.pallas import tpu as pltpu
from jax.sharding import PartitionSpec as P

HEAD = 64
NORM_EPS = 1e-05
F32 = jnp.float32
B16 = jnp.bfloat16
MIB = 1 << 20

BLOCKS = 16
NEAR = (0, 12)
MID = (4, 8)


def swap(values, bit):
    return lax.ppermute(values, "dp", [(i, i ^ bit) for i in range(BLOCKS)])


def tie(*values):
    return lax.optimization_barrier(values)


def after(value, *earlier):
    return tie(value, *earlier)[0]


def pair_swap(partial):
    return lax.ppermute(partial, "mp", [(0, 1), (1, 0)])


def as_pieces(full):
    rows = full.shape[0] // BLOCKS
    blocks = full.reshape(BLOCKS, rows, full.shape[1])
    return [
        jnp.stack([blocks[offset + bits[0]], blocks[offset + bits[1]]])
        for offset in range(4)
        for bits in (NEAR, MID)
    ]


SMEM_SPEC = pl.BlockSpec(memory_space=pltpu.SMEM)
VMEM_SPEC = pl.BlockSpec(memory_space=pltpu.VMEM)
CHUNK = 256
UNROLL = 8
LIGHT = pl.CostEstimate(flops=1, bytes_accessed=1, transcendentals=0)


def call(body, name, shapes, operands, scratch=(), limit=16):
    return pl.pallas_call(
        body,
        in_specs=[
            SMEM_SPEC if member.dtype == jnp.int32 and member.ndim == 1 else VMEM_SPEC
            for member in operands
        ],
        out_specs=[VMEM_SPEC] * len(shapes),
        out_shape=[jax.ShapeDtypeStruct(shape, dtype) for shape, dtype in shapes],
        scratch_shapes=[pltpu.VMEM(shape, dtype) for shape, dtype in scratch],
        compiler_params=pltpu.CompilerParams(vmem_limit_bytes=limit * MIB),
        cost_estimate=LIGHT,
        name=name,
    )(*operands)


def chunks(count):
    return [slice(start, start + CHUNK) for start in range(0, count, CHUNK)]


def loop(count, step, size=CHUNK, unroll=1):
    def body(index, carry):
        step(pl.ds(pl.multiple_of(index * size, size), size))
        return carry

    lax.fori_loop(0, count // size, body, 0, unroll=unroll)


PAIRS = [(q + bits[k], 2 * q + m, k) for q in range(4) for m, bits in enumerate((NEAR, MID)) for k in range(2)]


def fill(me, pieces, full_ref):
    rows = pieces[0].shape[1]
    for offset, piece, index in PAIRS:
        block = me ^ offset
        full_ref[pl.ds(pl.multiple_of(block * rows, rows), rows), :] = pieces[piece][index]


def dot(left, right):
    return jnp.dot(left, right, preferred_element_type=F32)


def dot_t(left, right):
    return lax.dot_general(left, right, (((1,), (1,)), ((), ())), preferred_element_type=F32)


def t_dot(left, right):
    return lax.dot_general(left, right, (((0,), (0,)), ((), ())), preferred_element_type=F32)


def row_mean(values):
    return jnp.mean(values, axis=-1, keepdims=True)


def normalize(values):
    centred = values - row_mean(values)
    inverse = lax.rsqrt(row_mean(centred * centred) + NORM_EPS)
    return centred * inverse, inverse


def col_sum(values):
    return jnp.sum(values, axis=0, keepdims=True)


def norm_back(scaled, normed, inverse):
    return inverse * (scaled - row_mean(scaled) - normed * row_mean(scaled * normed))


def two_heads(slots):
    row = lax.broadcasted_iota(jnp.int32, (2 * slots, 2 * HEAD), 0) // slots
    lane = lax.broadcasted_iota(jnp.int32, (2 * slots, 2 * HEAD), 1) // HEAD
    return (row == lane).astype(F32).astype(B16)


def doubled(values, mask):
    return jnp.concatenate([values, values], axis=0) * mask


def attend_body(slots, me_ref, len_ref, in_ref, bias_ref, *rest):
    pieces, (w_ref, qkv_ref, prob_ref, att_ref, part_ref) = rest[:-5], rest[-5:]
    count, width = att_ref.shape
    fill(me_ref[0], pieces, w_ref)

    def project(rows):
        qkv_ref[rows] = (dot(in_ref[rows], w_ref[:, : 3 * width]) + bias_ref[...]).astype(B16)

    loop(count, project, unroll=4)
    mask = two_heads(slots)
    key_slot = lax.broadcasted_iota(jnp.int32, (slots, slots), 1)

    def chain_step(chain, carry):
        valid = key_slot < len_ref[chain]
        rows = pl.ds(pl.multiple_of(chain * slots, slots), slots)
        for pair in range(width // (2 * HEAD)):
            lanes = 2 * HEAD * pair
            query = qkv_ref[rows, lanes : lanes + 2 * HEAD]
            key = qkv_ref[rows, width + lanes : width + lanes + 2 * HEAD]
            value = qkv_ref[rows, 2 * width + lanes : 2 * width + lanes + 2 * HEAD]
            scores = dot_t(query * (HEAD**-0.5), doubled(key, mask))
            probs = []
            for head in range(2):
                part = jnp.where(valid, scores[:, head * slots : (head + 1) * slots], -1e30)
                terms = jnp.exp(part - jnp.max(part, axis=-1, keepdims=True))
                probs.append((terms / jnp.sum(terms, axis=-1, keepdims=True)).astype(B16))
            prob = jnp.concatenate(probs, axis=1)
            prob_ref[rows, 2 * slots * pair : 2 * slots * (pair + 1)] = prob
            att_ref[rows, lanes : lanes + 2 * HEAD] = dot(prob, doubled(value, mask)).astype(B16)
        return carry

    lax.fori_loop(0, count // slots, chain_step, 0, unroll=UNROLL)

    def bring_out(rows):
        part_ref[rows] = dot_t(att_ref[rows], w_ref[:, 3 * width :]).astype(B16)

    loop(count, bring_out, unroll=4)


def attend(me, lengths, in_low, bias, pieces):
    count, width = in_low.shape
    heads = bias.shape[1] // 3
    slots = count // lengths.shape[0]
    shapes = [
        ((width, 4 * heads), B16),
        ((count, 3 * heads), B16),
        ((count, heads // HEAD * slots), B16),
        ((count, heads), B16),
        ((count, width), B16),
    ]
    body = functools.partial(attend_body, slots)
    return call(body, "attend", shapes, [me, lengths, in_low, bias, *pieces])


def up_body(me_ref, in_ref, own_ref, other_ref, vec_ref, bias_ref, *rest):
    pieces, (w_ref, normed_ref, inverse_ref, low_ref, act_ref, slope_ref) = rest[:-6], rest[-6:]
    fill(me_ref[0], pieces, w_ref)
    vectors = vec_ref[...]

    def step(rows):
        attn = own_ref[rows].astype(F32) + other_ref[rows].astype(F32) + vectors[0:1]
        normed, inverse = normalize(in_ref[rows].astype(F32) + attn)
        normed_ref[rows] = normed
        inverse_ref[rows] = jnp.broadcast_to(inverse, (CHUNK, inverse_ref.shape[1]))
        low_ref[rows] = (normed * vectors[1:2] + vectors[2:3]).astype(B16)
        pre = dot(low_ref[rows], w_ref[...]) + bias_ref[...]
        cdf = 0.5 + 0.5 * lax.erf(pre * (2.0**-0.5))
        act_ref[rows] = (pre * cdf).astype(B16)
        density = jnp.exp(pre * pre * -0.5) * 0.3989422804014327
        slope_ref[rows] = (cdf + pre * density).astype(B16)

    loop(in_ref.shape[0], step, unroll=2)


def up(me, in_low, own, other, vectors, bias, pieces):
    count, width = in_low.shape
    units = bias.shape[1]
    shapes = [
        ((width, units), B16),
        ((count, width), F32),
        ((count, 128), F32),
        ((count, width), B16),
        ((count, units), B16),
        ((count, units), B16),
    ]
    return call(up_body, "up", shapes, [me, in_low, own, other, vectors, bias, *pieces])


def down_body(me_ref, act_ref, *rest):
    pieces, (w_ref, part_ref) = rest[:-2], rest[-2:]
    fill(me_ref[0], pieces, w_ref)
    for rows in chunks(part_ref.shape[0]):
        part_ref[rows] = dot_t(act_ref[rows], w_ref[...]).astype(B16)


def down_rest_body(act_ref, w_ref, part_ref):
    half = part_ref.shape[0]
    for rows in chunks(half):
        part_ref[rows] = dot_t(act_ref[half + rows.start : half + rows.stop], w_ref[...]).astype(B16)


def down(me, act, pieces):
    count, units = act.shape
    width = BLOCKS * pieces[0].shape[1]
    half = ((count // 2, width), B16)
    w_down_t, first = call(down_body, "down", [((width, units), B16), half], [me, act, *pieces])
    (second,) = call(down_rest_body, "down_rest", [half], [act, w_down_t])
    return w_down_t, first, second


def second_norm_body(start, normed_ref, own_ref, other_ref, grad_ref, vec_ref, out_ref, dz_ref, low_ref, sum_ref):
    vectors = vec_ref[...]
    sum_ref[...] = jnp.zeros_like(sum_ref)
    for rows in chunks(own_ref.shape[0]):
        there = slice(start + rows.start, start + rows.stop)
        hidden = normed_ref[there] * vectors[0:1] + vectors[1:2]
        ffn = own_ref[rows].astype(F32) + other_ref[rows].astype(F32) + vectors[2:3]
        normed, inverse = normalize(hidden + ffn)
        out_ref[rows] = (normed * vectors[3:4] + vectors[4:5]).astype(B16)
        grad = grad_ref[there].astype(F32)
        dz = norm_back(grad * vectors[3:4], normed, inverse)
        dz_ref[rows] = dz
        low_ref[rows] = dz.astype(B16)
        sum_ref[0:1] += col_sum(grad * normed)
        sum_ref[1:2] += col_sum(grad)
        sum_ref[2:3] += col_sum(dz)


def second_norm(start, normed, own, other, grad, vectors):
    shape = own.shape
    shapes = [(shape, B16), (shape, F32), (shape, B16), ((8, shape[1]), F32)]
    body = functools.partial(second_norm_body, start)
    return call(body, "second_norm", shapes, [normed, own, other, grad, vectors])


def rows_in(halves, rows):
    size = halves[0].shape[0]
    half = halves[rows.start // size]
    return half[rows.start % size : rows.start % size + rows.stop - rows.start]


ORDER = (
    (3, 15, 1, 13),
    (7, 11, 6, 10),
    (5, 9),
    (2, 14),
    (0, 12, 4, 8),
)


def weight_grad(me, lefts, rights, groups=ORDER, vector=None, turned=None):
    count = rights[0].shape[0]
    width = lefts[-1][0].shape[1] if turned is None else turned.shape[0]
    tile = 384 if all(right.shape[1] % 384 == 0 for right in rights) else 128
    total = sum(right.shape[1] for right in rights)
    rows = width // BLOCKS
    n = len(rights)
    flat = [half for left in lefts for half in left] if turned is None else [turned]
    wide = [] if vector is None else [vector]
    keep = turned is None and len(groups) < len(ORDER)
    wanted = [offset for offsets in groups for offset in offsets]

    def body(me_ref, *refs):
        left_refs, right_refs = list(refs[: len(flat)]), refs[len(flat) : len(flat) + n]
        outs = refs[len(flat) + n + len(wide) :]
        placed_ref = outs[-1]
        if wide:
            outs[0][0:2, :, total:] = refs[len(flat) + n][...]
            outs[0][2:4, :, total:] = jnp.zeros((2, rows, 128), B16)
        at = 0
        for index, right_ref in enumerate(right_refs):
            turned_ref = left_refs[0] if turned is not None else outs[-2]
            if turned is None:
                start = 0
                for _ in lefts[index]:
                    half_ref = left_refs.pop(0)
                    turned_ref[:, start : start + half_ref.shape[0]] = half_ref[...].T
                    start += half_ref.shape[0]
            for k, offset in enumerate(wanted):
                place = pl.multiple_of((me_ref[0] ^ offset) * rows, rows)
                placed_ref[k * rows : (k + 1) * rows] = turned_ref[pl.ds(place, rows), :]

            def step(cols, right_ref=right_ref, at=at):
                product = dot(placed_ref[...], right_ref[:, cols]).astype(B16)
                there = pl.ds(pl.multiple_of(at + cols.start, 128), tile)
                first = 0
                for out_ref, offsets in zip(outs, groups):
                    for k in range(len(offsets)):
                        out_ref[k, :, there] = product[first : first + rows]
                        first += rows

            count_tiles = right_ref.shape[1] // tile
            loop(right_ref.shape[1], step, tile, unroll=count_tiles if wide or keep else 1)
            at += right_ref.shape[1]

    shapes = [((len(offsets), rows, total), B16) for offsets in groups]
    shapes[0] = ((len(groups[0]), rows, total + 128 * len(wide)), B16)
    held = ((width, count), B16)
    shapes += [held] * keep
    scratch = [held] * (turned is None and not keep) + [((len(wanted) * rows, count), B16)]
    return call(body, "weight_grad", shapes, [me, *flat, *rights, *wide], scratch)


def hidden_back_body(low_a_ref, low_b_ref, slope_ref, down_ref, up_ref, pre_ref, part_ref, sum_ref):
    sum_ref[...] = jnp.zeros_like(sum_ref)
    half = low_a_ref.shape[0]
    for start, low_ref in ((0, low_a_ref), (half, low_b_ref)):

        def step(here, start=start, low_ref=low_ref):
            rows = pl.ds(pl.multiple_of(start + here.start, CHUNK), CHUNK)
            d_pre = dot(low_ref[here], down_ref[...]) * slope_ref[rows].astype(F32)
            sum_ref[0:1] += col_sum(d_pre)
            pre_ref[rows] = d_pre.astype(B16)
            part_ref[rows] = dot_t(pre_ref[rows], up_ref[...]).astype(B16)

        loop(half, step)


def hidden_back(lows, slope, w_down_t, w_up):
    count, units = slope.shape
    shapes = [((count, units), B16), ((count, w_up.shape[0]), B16), ((8, units), F32)]
    return call(hidden_back_body, "hidden_back", shapes, [*lows, slope, w_down_t, w_up])


def attend_back_body(slots, dz_a_ref, dz_b_ref, own_ref, other_ref, normed_ref, inverse_ref, gain_ref,
                     flag_ref, qkv_ref, prob_ref, w_ref, dz_one_ref, low_ref, d_qkv_ref, part_ref, sum_ref,
                     sum_qkv_ref, d_att_ref):
    count, width = d_att_ref.shape
    sum_ref[...] = jnp.zeros_like(sum_ref)
    sum_qkv_ref[...] = jnp.zeros_like(sum_qkv_ref)
    half = dz_a_ref.shape[0]
    for start, dz_ref in ((0, dz_a_ref), (half, dz_b_ref)):

        def step(here, start=start, dz_ref=dz_ref):
            rows = pl.ds(pl.multiple_of(start + here.start, CHUNK), CHUNK)
            normed = normed_ref[rows]
            d_hidden = dz_ref[here] + (own_ref[rows].astype(F32) + other_ref[rows].astype(F32))
            dz_one = norm_back(d_hidden * gain_ref[...], normed, inverse_ref[rows, 0:1])
            dz_one_ref[rows] = dz_one
            low_ref[rows] = dz_one.astype(B16)
            sum_ref[0:1] += col_sum(d_hidden * normed)
            sum_ref[1:2] += col_sum(d_hidden)
            sum_ref[2:3] += col_sum(dz_one)
            sum_ref[3:4] += col_sum(dz_one * flag_ref[rows, 0:1])
            d_att_ref[rows] = dot(low_ref[rows], w_ref[:, 3 * width :]).astype(B16)

        loop(half, step)
    mask = two_heads(slots)

    def chain_step(chain, carry):
        rows = pl.ds(pl.multiple_of(chain * slots, slots), slots)
        for pair in range(width // (2 * HEAD)):
            lanes = 2 * HEAD * pair
            query = qkv_ref[rows, lanes : lanes + 2 * HEAD]
            key = qkv_ref[rows, width + lanes : width + lanes + 2 * HEAD]
            value = qkv_ref[rows, 2 * width + lanes : 2 * width + lanes + 2 * HEAD]
            d_att = d_att_ref[rows, lanes : lanes + 2 * HEAD]
            prob = prob_ref[rows, 2 * slots * pair : 2 * slots * (pair + 1)]
            d_prob = dot_t(d_att, doubled(value, mask))
            weights = prob.astype(F32)
            products = weights * d_prob
            lows = []
            for head in range(2):
                half = slice(head * slots, (head + 1) * slots)
                total = jnp.sum(products[:, half], axis=-1, keepdims=True)
                lows.append((products[:, half] - weights[:, half] * total).astype(B16))
            low = jnp.concatenate(lows, axis=1)
            d_query = dot(low, doubled(key, mask)) * (HEAD**-0.5)
            tall = jnp.concatenate(lows, axis=0)
            d_key = t_dot(tall, doubled(query, mask)) * (HEAD**-0.5)
            tall = jnp.concatenate([prob[:, :slots], prob[:, slots:]], axis=0)
            d_value = t_dot(tall, doubled(d_att, mask))
            d_qkv_ref[rows, lanes : lanes + 2 * HEAD] = d_query.astype(B16)
            d_qkv_ref[rows, width + lanes : width + lanes + 2 * HEAD] = d_key.astype(B16)
            d_qkv_ref[rows, 2 * width + lanes : 2 * width + lanes + 2 * HEAD] = d_value.astype(B16)
        return carry

    lax.fori_loop(0, count // slots, chain_step, 0)

    def bring_back(rows):
        sum_qkv_ref[0:1] += col_sum(d_qkv_ref[rows].astype(F32))
        part = dot_t(d_qkv_ref[rows], w_ref[:, : 3 * width]).astype(B16)
        part_ref[rows] = part
        sum_ref[4:5] += col_sum(part.astype(F32) * flag_ref[rows, 0:1])

    loop(count, bring_back)


def attend_back(chain_count, dz_two, own, other, normed, inverse, gain, flag, qkv, prob, w_a):
    shape = normed.shape
    heads = qkv.shape[1] // 3
    shapes = [
        (shape, F32),
        (shape, B16),
        (qkv.shape, B16),
        (shape, B16),
        ((8, shape[1]), F32),
        ((8, 3 * heads), F32),
    ]
    operands = [*dz_two, own, other, normed, inverse, gain, flag, qkv, prob, w_a]
    body = functools.partial(attend_back_body, shape[0] // chain_count)
    return call(body, "attend_back", shapes, operands, [((shape[0], heads), B16)])


def join_body(one_ref, other_ref, two_a_ref, two_b_ref, up_ref, qkv_ref, out_ref):
    width = one_ref.shape[1]
    heads = qkv_ref.shape[1] // 3
    rows = out_ref.shape[1]
    out_ref[...] = jnp.zeros_like(out_ref)

    def put(start, values):
        for k in range(values.shape[1] // 128):
            place = (start + 128 * k) // 128
            chunk = values[:, 128 * k : 128 * (k + 1)]
            out_ref[place // rows, place % rows : place % rows + 1] = chunk

    put(0, one_ref[3:4] + (one_ref[4:5] + other_ref[4:5]))
    for k in range(3):
        put((1 + k) * width, one_ref[k : k + 1])
        put((4 + k) * width, two_a_ref[k : k + 1] + two_b_ref[k : k + 1])
    put(7 * width, qkv_ref[0:1, :heads])
    put(7 * width + heads, qkv_ref[0:1, 2 * heads :])
    put(7 * width + 2 * heads, up_ref[0:1])


def join(rows, sums_one, sums_other, sums_two, sums_up, sums_qkv):
    width = sums_one.shape[1]
    length = 7 * width + 2 * sums_qkv.shape[1] // 3 + sums_up.shape[1]
    assert length <= 2 * rows * 128
    operands = [sums_one, sums_other, *sums_two, sums_up, sums_qkv]
    return call(join_body, "join", [((2, rows, 128), F32)], operands, limit=4)[0]


def last_body(dz_ref, own_ref, other_ref, flag_ref, out_a_ref, out_b_ref, tokens_ref, out_ref):
    for rows in chunks(dz_ref.shape[0]):
        total = dz_ref[rows] + (own_ref[rows].astype(F32) + other_ref[rows].astype(F32))
        tokens_ref[rows] = jnp.where(flag_ref[rows, 0:1] > 0.0, 0.0, total)
        out_ref[rows] = rows_in((out_a_ref, out_b_ref), rows)


def last(dz_one, own, other, flag, results):
    shapes = [(dz_one.shape, F32), (dz_one.shape, B16)]
    return call(last_body, "last", shapes, [dz_one, own, other, flag, *results])


def add_late_body(x_ref, y_ref, from_x_ref, from_y_ref, out_x_ref, out_y_ref):
    out_x_ref[...] = (x_ref[...].astype(F32) + from_y_ref[:2].astype(F32)).astype(B16)
    out_y_ref[...] = (y_ref[...].astype(F32) + from_x_ref[:2].astype(F32)).astype(B16)


def add_own_body(own_ref, from_x_ref, from_y_ref, late_x_ref, late_y_ref, near_ref, mid_ref):
    near_ref[...] = (
        own_ref[:2].astype(F32) + from_x_ref[2:].astype(F32) + late_y_ref[...].astype(F32)
    )
    mid_ref[...] = (
        own_ref[2:].astype(F32) + late_x_ref[...].astype(F32) + from_y_ref[2:].astype(F32)
    ).astype(B16)


def add_mid_body(near_ref, mid_ref, own_ref, far_ref):
    own_ref[...] = near_ref[0] + mid_ref[0].astype(F32)
    far_ref[...] = (near_ref[1] + mid_ref[1].astype(F32)).astype(B16)


def late_vector_body(x_ref, y_ref, from_x_ref, from_y_ref, v_ref, out_x_ref, out_y_ref, vector_ref):
    cols = x_ref.shape[2]
    out_x_ref[...] = (x_ref[...].astype(F32) + from_y_ref[:2].astype(F32)).astype(B16)
    out_y_ref[:, :, :cols] = (y_ref[...].astype(F32) + from_x_ref[:2, :, :cols].astype(F32)).astype(B16)
    vector = (v_ref[...].astype(F32) + from_x_ref[:2, :, cols:].astype(F32)).astype(B16)
    out_y_ref[:, :, cols:] = vector
    vector_ref[...] = vector


def own_vector_body(own_ref, from_x_ref, from_y_ref, late_x_ref, late_y_ref, v_ref, near_ref, mid_ref, vector_ref):
    cols = own_ref.shape[2]
    near_ref[...] = (
        own_ref[:2].astype(F32)
        + from_x_ref[2:, :, :cols].astype(F32)
        + late_y_ref[:, :, :cols].astype(F32)
    )
    mid_ref[...] = (
        own_ref[2:].astype(F32) + late_x_ref[...].astype(F32) + from_y_ref[2:].astype(F32)
    ).astype(B16)
    vector_ref[...] = (v_ref[...].astype(F32) + late_y_ref[:, :, cols:].astype(F32)).astype(B16)


def mid_vector_body(near_ref, mid_ref, v_ref, from_ref, own_ref, far_ref, vector_ref):
    own_ref[...] = near_ref[0] + mid_ref[0].astype(F32)
    far_ref[...] = (near_ref[1] + mid_ref[1].astype(F32)).astype(B16)
    vector_ref[...] = (v_ref[...].astype(F32) + from_ref[...].astype(F32)).astype(B16)


def far_vector_body(own_ref, far_ref, v_ref, from_ref, *outs):
    rows, cols = own_ref.shape
    part = cols // 4
    for k in range(4):
        lanes = slice(k * part, (k + 1) * part)
        outs[k][...] = own_ref[:, lanes] + far_ref[:, lanes].astype(F32)
    place = 0
    joined = [v_ref[k].astype(F32) + from_ref[k].astype(F32) for k in range(2)]
    for out_ref in outs[4:]:
        for k in range(out_ref.shape[0]):
            out_ref[k : k + 1] = joined[place // rows][place % rows : place % rows + 1]
            place += 1


def late_vector(late_x, late_y, from_x, from_y, vector):
    rows, cols = late_x.shape[1:]
    shapes = [(late_x.shape, B16), ((2, rows, cols + 128), B16), (vector.shape, B16)]
    operands = [late_x, late_y, from_x, from_y, vector]
    return call(late_vector_body, "late_vector", shapes, operands, limit=8)


def own_vector(own, from_x, from_y, late_x, late_y, vector):
    shapes = [(late_x.shape, F32), (late_x.shape, B16), (vector.shape, B16)]
    operands = [own, from_x, from_y, late_x, late_y, vector]
    return call(own_vector_body, "own_vector", shapes, operands, limit=8)


def mid_vector(near, mid, vector, other):
    shapes = [(near.shape[1:], F32), (near.shape[1:], B16), (vector.shape, B16)]
    return call(mid_vector_body, "mid_vector", shapes, [near, mid, vector, other], limit=8)


def far_vector(own, far, vector, other, sizes):
    rows, cols = own.shape
    shapes = [((rows, cols // 4), F32)] * 4 + [((size // 128, 128), F32) for size in sizes]
    outs = call(far_vector_body, "far_vector", shapes, [own, far, vector, other], limit=8)
    return outs[:4], [member.reshape(-1) for member in outs[4:]]


def add_late(late_x, late_y, from_x, from_y):
    shape = (late_x.shape, B16)
    return call(add_late_body, "add_late", [shape, shape], [late_x, late_y, from_x, from_y], limit=8)


def add_own(own, from_x, from_y, late_x, late_y):
    shapes = [(late_x.shape, F32), (late_x.shape, B16)]
    return call(add_own_body, "add_own", shapes, [own, from_x, from_y, late_x, late_y], limit=8)


def add_mid(near, mid):
    shapes = [(near.shape[1:], F32), (near.shape[1:], B16)]
    return call(add_mid_body, "add_mid", shapes, [near, mid], limit=8)


def per_device(dp_size, tokens, masked, lengths, mask_vector, w_query, b_query, w_key, w_value,
               b_value, w_out, b_out, gain_one, shift_one, w_up, b_up, w_down, b_down, gain_two,
               shift_two, grad_out):
    head_cols = w_query.shape[1]
    width = tokens.shape[1]
    fast = dp_size == BLOCKS and w_query.shape[0] % 16 == 0
    me = lax.axis_index("dp").astype(jnp.int32).reshape(1)
    if not fast:
        me = jnp.zeros_like(me)

    (b_query, b_value, b_out, gain_one, shift_one, b_up, b_down, gain_two, shift_two) = (
        member.astype(F32)
        for member in (b_query, b_value, b_out, gain_one, shift_one, b_up, b_down, gain_two, shift_two)
    )
    is_masked = (masked == 1)[:, None]
    flag = jnp.broadcast_to(is_masked, (masked.shape[0], 128)).astype(F32)
    in_low = jnp.where(is_masked, mask_vector[None, :], tokens)
    bias_qkv = jnp.concatenate([b_query, jnp.zeros_like(b_query), b_value])[None, :]
    vectors_one = jnp.stack([b_out, gain_one, shift_one])
    vectors_two = jnp.stack([gain_one, shift_one, b_down, gain_two, shift_two])
    b_up, gain_one = b_up[None, :], gain_one[None, :]

    a = jnp.concatenate([w_query, w_key, w_value, w_out.T], axis=1)
    c = w_up
    d = w_down.T
    if fast:
        az = swap(a, 12)
        az, me, flag, in_low, bias_qkv, vectors_one, vectors_two, b_up, gain_one = tie(
            az, me, flag, in_low, bias_qkv, vectors_one, vectors_two, b_up, gain_one
        )
        an = jnp.stack([a, az])
        anx, any_, am = swap(an, 1), swap(an, 2), swap(an, 4)
        anx, any_, am, an, c = tie(anx, any_, am, an, c)
        amx, amy, cz = swap(am, 1), swap(am, 2), swap(c, 12)
        amx, amy, cz, anx, c, d = tie(amx, amy, cz, anx, c, d)
        cn = jnp.stack([c, cz])
        amd, and_, cm = swap(amy, 1), swap(anx, 2), swap(cn, 4)
        cnx, cny, dz = swap(cn, 1), swap(cn, 2), swap(after(d, cm), 12)
        amd, and_, cm, cnx, cny = tie(amd, and_, cm, cnx, cny)
        dn = jnp.stack([d, dz])
        pieces_a = [an, am, anx, amx, any_, amy, and_, amd]
        cmx, cnd, dm = swap(cm, 1), swap(cnx, 2), swap(dn, 4)
        dnx, dny = swap(dn, 1), swap(dn, 2)
    else:
        a, c, d = (lax.all_gather(piece, "dp", axis=0, tiled=True) for piece in (a, c, d))
        pieces_a, pieces_c, pieces_d = as_pieces(a), as_pieces(c), as_pieces(d)
    w_a, qkv, prob, attended, part = attend(me, lengths, in_low, bias_qkv, pieces_a)
    if fast:
        cmx, cnd, dm, dnx, dny, cm, part = tie(cmx, cnd, dm, dnx, dny, cm, part)
        cmy, dnd, cmd = swap(cm, 2), swap(dny, 1), swap(cnd, 4)
    other = pair_swap(part)
    if fast:
        cmy, dnd, cmd, dm, other, part = tie(cmy, dnd, cmd, dm, other, part)
        pieces_c = [cn, cm, cnx, cmx, cny, cmy, cnd, cmd]
        dmx, dmy, dmd = swap(dm, 1), swap(dm, 2), swap(dnd, 4)
    w_u, normed_one, inverse_one, hidden_low, act_low, slope = up(
        me, in_low, part, other, vectors_one, b_up, pieces_c
    )
    if fast:
        dmx, dmy, dmd, act_low = tie(dmx, dmy, dmd, act_low)
        pieces_d = [dn, dm, dnx, dmx, dny, dmy, dnd, dmd]
    w_d, *parts = down(me, act_low, pieces_d)
    halves = [
        second_norm(index * part.shape[0], normed_one, part, pair_swap(part), grad_out, vectors_two)
        for index, part in enumerate(parts)
    ]
    results, dz_two, dz_two_low, sums_two = zip(*halves)
    dx, dy, turned = weight_grad(me, [dz_two_low], [act_low], ORDER[:2])
    if fast:
        dx, dy, turned, dz_two_low = tie(dx, dy, turned, dz_two_low)
        dxr, dyr = swap(dx, 1), swap(dy, 2)
    dxl, dyl, do = weight_grad(me, None, [act_low], ORDER[2:], turned=turned)
    d_pre_low, part, sums_up = hidden_back(dz_two_low, slope, w_d, w_u)
    cx, cy, cxl, cyl, co = weight_grad(me, [[hidden_low]], [d_pre_low])
    if fast:
        dxr, dyr, part, cx, cy, dxl, dyl, do = tie(dxr, dyr, part, cx, cy, dxl, dyl, do)
        cxr, cyr = swap(cx, 1), swap(cy, 2)
        dxl, dyl = add_late(dxl, dyl, dxr, dyr)
        dxlr, dylr = swap(dxl, 1), swap(dyl, 2)
    other = pair_swap(part)
    dz_one, dz_one_low, d_qkv, part, sums_one, sums_qkv = attend_back(
        lengths.shape[0], dz_two, part, other, normed_one, inverse_one, gain_one, flag, qkv, prob, w_a
    )
    if fast:
        cxr, cyr, dxlr, dylr, part, d_qkv, dz_one_low = tie(cxr, cyr, dxlr, dylr, part, d_qkv, dz_one_low)
        cxl, cyl = add_late(cxl, cyl, cxr, cyr)
        cxlr, cylr = swap(cxl, 1), swap(cyl, 2)
        d_near, d_mid = add_own(do, dxr, dyr, dxlr, dylr)
        d_midr = swap(d_mid, 4)
    sums_other = pair_swap(sums_one)
    joined = join(width // BLOCKS, sums_one, sums_other, sums_two, sums_up, sums_qkv)
    vector = joined.astype(B16) if fast else None
    ax, ay, axl, ayl, ao = weight_grad(me, [[in_low], [dz_one_low]], [d_qkv, attended], vector=vector)
    if fast:
        cxlr, cylr, d_midr, ax, ay, part = tie(cxlr, cylr, d_midr, ax, ay, part)
        axr, ayr = swap(ax, 1), swap(ay, 2)
        c_near, c_mid = add_own(co, cxr, cyr, cxlr, cylr)
        d_near, d_far = add_mid(d_near, d_midr)
        c_midr, d_farr = swap(c_mid, 4), swap(d_far, 12)
    other = pair_swap(part)
    d_tokens, result = last(dz_one, part, other, flag, results)
    sizes = [width] * 7 + [head_cols] * 2 + [w_up.shape[1]]
    if fast:
        axr, ayr, c_midr, d_farr, d_tokens, result = tie(axr, ayr, c_midr, d_farr, d_tokens, result)
        axl, ayl, vector = late_vector(axl, ayl, axr, ayr, vector)
        axlr, aylr = swap(axl, 1), swap(ayl, 2)
        c_near, c_far = add_mid(c_near, c_midr)
        c_farr = swap(c_far, 12)
        axlr, aylr, c_farr = tie(axlr, aylr, c_farr)
        a_near, a_mid, vector = own_vector(ao, axr, ayr, axlr, aylr, vector)
        a_midr, other = swap(a_mid, 4), swap(vector, 4)
        d_w_down_t = d_near + d_farr.astype(F32)
        a_midr, other, d_w_down_t = tie(a_midr, other, d_w_down_t)
        a_near, a_far, vector = mid_vector(a_near, a_midr, vector, other)
        a_farr, other = swap(a_far, 12), swap(vector, 12)
        d_w_up = c_near + c_farr.astype(F32)
        d_wa, summed = far_vector(a_near, a_farr, vector, other, sizes)
    else:
        full = []
        for parts in ((ax, ay, axl, ayl, ao), (cx, cy, cxl, cyl, co), (dx, dy, dxl, dyl, do)):
            blocks = [None] * BLOCKS
            for member, offsets in zip(parts, ORDER):
                for k, offset in enumerate(offsets):
                    blocks[offset] = member[k]
            full.append(jnp.concatenate(blocks).astype(F32))
        joined = lax.psum(joined, "dp")
        d_wa, d_w_up, d_w_down_t = (
            lax.psum_scatter(member, "dp", scatter_dimension=0, tiled=True) for member in full
        )
        d_wa = [d_wa[:, k * head_cols : (k + 1) * head_cols] for k in range(4)]
        joined = joined.reshape(-1)
        summed = []
        start = 0
        for size in sizes:
            summed.append(joined[start : start + size])
            start += size
    return (
        result,
        d_tokens,
        summed[0],
        d_wa[0],
        summed[7],
        d_wa[1],
        d_wa[2],
        summed[8],
        d_wa[3].T,
        summed[3],
        summed[1],
        summed[2],
        d_w_up,
        summed[9],
        d_w_down_t.T,
        summed[6],
        summed[4],
        summed[5],
    )


def solution(mesh):
    rows, flat, both = P("dp", None), P(), P("dp", "mp")
    return jax.shard_map(
        functools.partial(per_device, mesh.shape["dp"]),
        mesh=mesh,
        in_specs=(rows, P("dp"), P("dp"), flat, both, P("mp"), both, both, P("mp"), P("mp", "dp"),
                  flat, flat, flat, both, P("mp"), P("mp", "dp"), flat, flat, flat, rows),
        out_specs=(rows, rows, flat, both, P("mp"), both, both, P("mp"), P("mp", "dp"), flat, flat,
                   flat, both, P("mp"), P("mp", "dp"), flat, flat, flat),
        check_vma=False,
    )
```

```python
import functools

import jax
import jax.numpy as jnp
from jax import lax
from jax.experimental import pallas as pl
from jax.experimental.pallas import tpu as pltpu
from jax.sharding import PartitionSpec as P

HEAD = 64
NORM_EPS = 1e-05
F32 = jnp.float32
B16 = jnp.bfloat16
MIB = 1 << 20

BLOCKS = 16
NEAR = (0, 12)
MID = (4, 8)


def swap(values, bit):
    return lax.ppermute(values, "dp", [(i, i ^ bit) for i in range(BLOCKS)])


def tie(*values):
    return lax.optimization_barrier(values)


def after(value, *earlier):
    return tie(value, *earlier)[0]


def pair_swap(partial):
    return lax.ppermute(partial, "mp", [(0, 1), (1, 0)])


def as_pieces(full):
    rows = full.shape[0] // BLOCKS
    blocks = full.reshape(BLOCKS, rows, full.shape[1])
    return [
        jnp.stack([blocks[offset + bits[0]], blocks[offset + bits[1]]])
        for offset in range(4)
        for bits in (NEAR, MID)
    ]


SMEM_SPEC = pl.BlockSpec(memory_space=pltpu.SMEM)
VMEM_SPEC = pl.BlockSpec(memory_space=pltpu.VMEM)
CHUNK = 256
UNROLL = 8
LIGHT = pl.CostEstimate(flops=1, bytes_accessed=1, transcendentals=0)


def call(body, name, shapes, operands, scratch=(), limit=16):
    return pl.pallas_call(
        body,
        in_specs=[
            SMEM_SPEC if member.dtype == jnp.int32 and member.ndim == 1 else VMEM_SPEC
            for member in operands
        ],
        out_specs=[VMEM_SPEC] * len(shapes),
        out_shape=[jax.ShapeDtypeStruct(shape, dtype) for shape, dtype in shapes],
        scratch_shapes=[pltpu.VMEM(shape, dtype) for shape, dtype in scratch],
        compiler_params=pltpu.CompilerParams(vmem_limit_bytes=limit * MIB),
        cost_estimate=LIGHT,
        name=name,
    )(*operands)


def chunks(count):
    return [slice(start, start + CHUNK) for start in range(0, count, CHUNK)]


def loop(count, step, size=CHUNK, unroll=1):
    def body(index, carry):
        step(pl.ds(pl.multiple_of(index * size, size), size))
        return carry

    lax.fori_loop(0, count // size, body, 0, unroll=unroll)


PAIRS = [(q + bits[k], 2 * q + m, k) for q in range(4) for m, bits in enumerate((NEAR, MID)) for k in range(2)]


def fill(me, pieces, full_ref):
    rows = pieces[0].shape[1]
    for offset, piece, index in PAIRS:
        block = me ^ offset
        full_ref[pl.ds(pl.multiple_of(block * rows, rows), rows), :] = pieces[piece][index]


def dot(left, right):
    return jnp.dot(left, right, preferred_element_type=F32)


def dot_t(left, right):
    return lax.dot_general(left, right, (((1,), (1,)), ((), ())), preferred_element_type=F32)


def t_dot(left, right):
    return lax.dot_general(left, right, (((0,), (0,)), ((), ())), preferred_element_type=F32)


def row_mean(values):
    return jnp.mean(values, axis=-1, keepdims=True)


def normalize(values):
    centred = values - row_mean(values)
    inverse = lax.rsqrt(row_mean(centred * centred) + NORM_EPS)
    return centred * inverse, inverse


def col_sum(values):
    return jnp.sum(values, axis=0, keepdims=True)


def norm_back(scaled, normed, inverse):
    return inverse * (scaled - row_mean(scaled) - normed * row_mean(scaled * normed))


def two_heads(slots):
    row = lax.broadcasted_iota(jnp.int32, (2 * slots, 2 * HEAD), 0) // slots
    lane = lax.broadcasted_iota(jnp.int32, (2 * slots, 2 * HEAD), 1) // HEAD
    return (row == lane).astype(F32).astype(B16)


def doubled(values, mask):
    return jnp.concatenate([values, values], axis=0) * mask


def attend_body(slots, me_ref, len_ref, in_ref, bias_ref, *rest):
    pieces, (w_ref, qkv_ref, prob_ref, att_ref, part_ref) = rest[:-5], rest[-5:]
    count, width = att_ref.shape
    fill(me_ref[0], pieces, w_ref)

    def project(rows):
        qkv_ref[rows] = (dot(in_ref[rows], w_ref[:, : 3 * width]) + bias_ref[...]).astype(B16)

    loop(count, project, unroll=4)
    mask = two_heads(slots)
    key_slot = lax.broadcasted_iota(jnp.int32, (slots, slots), 1)

    def chain_step(chain, carry):
        valid = key_slot < len_ref[chain]
        rows = pl.ds(pl.multiple_of(chain * slots, slots), slots)
        for pair in range(width // (2 * HEAD)):
            lanes = 2 * HEAD * pair
            query = qkv_ref[rows, lanes : lanes + 2 * HEAD]
            key = qkv_ref[rows, width + lanes : width + lanes + 2 * HEAD]
            value = qkv_ref[rows, 2 * width + lanes : 2 * width + lanes + 2 * HEAD]
            scores = dot_t(query * (HEAD**-0.5), doubled(key, mask))
            probs = []
            for head in range(2):
                part = jnp.where(valid, scores[:, head * slots : (head + 1) * slots], -1e30)
                terms = jnp.exp(part - jnp.max(part, axis=-1, keepdims=True))
                probs.append((terms / jnp.sum(terms, axis=-1, keepdims=True)).astype(B16))
            prob = jnp.concatenate(probs, axis=1)
            prob_ref[rows, 2 * slots * pair : 2 * slots * (pair + 1)] = prob
            att_ref[rows, lanes : lanes + 2 * HEAD] = dot(prob, doubled(value, mask)).astype(B16)
        return carry

    lax.fori_loop(0, count // slots, chain_step, 0, unroll=UNROLL)

    def bring_out(rows):
        part_ref[rows] = dot_t(att_ref[rows], w_ref[:, 3 * width :]).astype(B16)

    loop(count, bring_out, unroll=4)


def attend(me, lengths, in_low, bias, pieces):
    count, width = in_low.shape
    heads = bias.shape[1] // 3
    slots = count // lengths.shape[0]
    shapes = [
        ((width, 4 * heads), B16),
        ((count, 3 * heads), B16),
        ((count, heads // HEAD * slots), B16),
        ((count, heads), B16),
        ((count, width), B16),
    ]
    body = functools.partial(attend_body, slots)
    return call(body, "attend", shapes, [me, lengths, in_low, bias, *pieces])


def up_body(me_ref, in_ref, own_ref, other_ref, vec_ref, bias_ref, *rest):
    pieces, (w_ref, normed_ref, inverse_ref, low_ref, act_ref, slope_ref) = rest[:-6], rest[-6:]
    fill(me_ref[0], pieces, w_ref)
    vectors = vec_ref[...]

    def step(rows):
        attn = own_ref[rows].astype(F32) + other_ref[rows].astype(F32) + vectors[0:1]
        normed, inverse = normalize(in_ref[rows].astype(F32) + attn)
        normed_ref[rows] = normed
        inverse_ref[rows] = jnp.broadcast_to(inverse, (CHUNK, inverse_ref.shape[1]))
        low_ref[rows] = (normed * vectors[1:2] + vectors[2:3]).astype(B16)
        pre = dot(low_ref[rows], w_ref[...]) + bias_ref[...]
        cdf = 0.5 + 0.5 * lax.erf(pre * (2.0**-0.5))
        act_ref[rows] = (pre * cdf).astype(B16)
        density = jnp.exp(pre * pre * -0.5) * 0.3989422804014327
        slope_ref[rows] = (cdf + pre * density).astype(B16)

    loop(in_ref.shape[0], step, unroll=2)


def up(me, in_low, own, other, vectors, bias, pieces):
    count, width = in_low.shape
    units = bias.shape[1]
    shapes = [
        ((width, units), B16),
        ((count, width), F32),
        ((count, 128), F32),
        ((count, width), B16),
        ((count, units), B16),
        ((count, units), B16),
    ]
    return call(up_body, "up", shapes, [me, in_low, own, other, vectors, bias, *pieces])


def down_body(me_ref, act_ref, *rest):
    pieces, (w_ref, part_ref) = rest[:-2], rest[-2:]
    fill(me_ref[0], pieces, w_ref)
    for rows in chunks(part_ref.shape[0]):
        part_ref[rows] = dot_t(act_ref[rows], w_ref[...]).astype(B16)


def down_rest_body(act_ref, w_ref, part_ref):
    half = part_ref.shape[0]
    for rows in chunks(half):
        part_ref[rows] = dot_t(act_ref[half + rows.start : half + rows.stop], w_ref[...]).astype(B16)


def down(me, act, pieces):
    count, units = act.shape
    width = BLOCKS * pieces[0].shape[1]
    half = ((count // 2, width), B16)
    w_down_t, first = call(down_body, "down", [((width, units), B16), half], [me, act, *pieces])
    (second,) = call(down_rest_body, "down_rest", [half], [act, w_down_t])
    return w_down_t, first, second


def second_norm_body(start, normed_ref, own_ref, other_ref, grad_ref, vec_ref, out_ref, dz_ref, low_ref, sum_ref):
    vectors = vec_ref[...]
    sum_ref[...] = jnp.zeros_like(sum_ref)
    for rows in chunks(own_ref.shape[0]):
        there = slice(start + rows.start, start + rows.stop)
        hidden = normed_ref[there] * vectors[0:1] + vectors[1:2]
        ffn = own_ref[rows].astype(F32) + other_ref[rows].astype(F32) + vectors[2:3]
        normed, inverse = normalize(hidden + ffn)
        out_ref[rows] = (normed * vectors[3:4] + vectors[4:5]).astype(B16)
        grad = grad_ref[there].astype(F32)
        dz = norm_back(grad * vectors[3:4], normed, inverse)
        dz_ref[rows] = dz
        low_ref[rows] = dz.astype(B16)
        sum_ref[0:1] += col_sum(grad * normed)
        sum_ref[1:2] += col_sum(grad)
        sum_ref[2:3] += col_sum(dz)


def second_norm(start, normed, own, other, grad, vectors):
    shape = own.shape
    shapes = [(shape, B16), (shape, F32), (shape, B16), ((8, shape[1]), F32)]
    body = functools.partial(second_norm_body, start)
    return call(body, "second_norm", shapes, [normed, own, other, grad, vectors])


def rows_in(halves, rows):
    size = halves[0].shape[0]
    half = halves[rows.start // size]
    return half[rows.start % size : rows.start % size + rows.stop - rows.start]


ORDER = (
    (3, 15, 1, 13),
    (7, 11, 6, 10),
    (5, 9),
    (2, 14),
    (0, 12, 4, 8),
)


def weight_grad(me, lefts, rights, groups=ORDER, vector=None, turned=None):
    count = rights[0].shape[0]
    width = lefts[-1][0].shape[1] if turned is None else turned.shape[0]
    tile = 384 if all(right.shape[1] % 384 == 0 for right in rights) else 128
    total = sum(right.shape[1] for right in rights)
    rows = width // BLOCKS
    n = len(rights)
    flat = [half for left in lefts for half in left] if turned is None else [turned]
    wide = [] if vector is None else [vector]
    keep = turned is None and len(groups) < len(ORDER)
    wanted = [offset for offsets in groups for offset in offsets]

    def body(me_ref, *refs):
        left_refs, right_refs = list(refs[: len(flat)]), refs[len(flat) : len(flat) + n]
        outs = refs[len(flat) + n + len(wide) :]
        placed_ref = outs[-1]
        if wide:
            outs[0][0:2, :, total:] = refs[len(flat) + n][...]
            outs[0][2:4, :, total:] = jnp.zeros((2, rows, 128), B16)
        at = 0
        for index, right_ref in enumerate(right_refs):
            turned_ref = left_refs[0] if turned is not None else outs[-2]
            if turned is None:
                start = 0
                for _ in lefts[index]:
                    half_ref = left_refs.pop(0)
                    turned_ref[:, start : start + half_ref.shape[0]] = half_ref[...].T
                    start += half_ref.shape[0]
            for k, offset in enumerate(wanted):
                place = pl.multiple_of((me_ref[0] ^ offset) * rows, rows)
                placed_ref[k * rows : (k + 1) * rows] = turned_ref[pl.ds(place, rows), :]

            def step(cols, right_ref=right_ref, at=at):
                product = dot(placed_ref[...], right_ref[:, cols]).astype(B16)
                there = pl.ds(pl.multiple_of(at + cols.start, 128), tile)
                first = 0
                for out_ref, offsets in zip(outs, groups):
                    for k in range(len(offsets)):
                        out_ref[k, :, there] = product[first : first + rows]
                        first += rows

            count_tiles = right_ref.shape[1] // tile
            loop(right_ref.shape[1], step, tile, unroll=count_tiles if wide or keep else 1)
            at += right_ref.shape[1]

    shapes = [((len(offsets), rows, total), B16) for offsets in groups]
    shapes[0] = ((len(groups[0]), rows, total + 128 * len(wide)), B16)
    held = ((width, count), B16)
    shapes += [held] * keep
    scratch = [held] * (turned is None and not keep) + [((len(wanted) * rows, count), B16)]
    return call(body, "weight_grad", shapes, [me, *flat, *rights, *wide], scratch)


def hidden_back_body(low_a_ref, low_b_ref, slope_ref, down_ref, up_ref, pre_ref, part_ref, sum_ref):
    sum_ref[...] = jnp.zeros_like(sum_ref)
    half = low_a_ref.shape[0]
    for start, low_ref in ((0, low_a_ref), (half, low_b_ref)):

        def step(here, start=start, low_ref=low_ref):
            rows = pl.ds(pl.multiple_of(start + here.start, CHUNK), CHUNK)
            d_pre = dot(low_ref[here], down_ref[...]) * slope_ref[rows].astype(F32)
            sum_ref[0:1] += col_sum(d_pre)
            pre_ref[rows] = d_pre.astype(B16)
            part_ref[rows] = dot_t(pre_ref[rows], up_ref[...]).astype(B16)

        loop(half, step)


def hidden_back(lows, slope, w_down_t, w_up):
    count, units = slope.shape
    shapes = [((count, units), B16), ((count, w_up.shape[0]), B16), ((8, units), F32)]
    return call(hidden_back_body, "hidden_back", shapes, [*lows, slope, w_down_t, w_up])


def attend_back_body(slots, dz_a_ref, dz_b_ref, own_ref, other_ref, normed_ref, inverse_ref, gain_ref,
                     flag_ref, qkv_ref, prob_ref, w_ref, dz_one_ref, low_ref, d_qkv_ref, part_ref, sum_ref,
                     sum_qkv_ref, d_att_ref):
    count, width = d_att_ref.shape
    sum_ref[...] = jnp.zeros_like(sum_ref)
    sum_qkv_ref[...] = jnp.zeros_like(sum_qkv_ref)
    half = dz_a_ref.shape[0]
    for start, dz_ref in ((0, dz_a_ref), (half, dz_b_ref)):

        def step(here, start=start, dz_ref=dz_ref):
            rows = pl.ds(pl.multiple_of(start + here.start, CHUNK), CHUNK)
            normed = normed_ref[rows]
            d_hidden = dz_ref[here] + (own_ref[rows].astype(F32) + other_ref[rows].astype(F32))
            dz_one = norm_back(d_hidden * gain_ref[...], normed, inverse_ref[rows, 0:1])
            dz_one_ref[rows] = dz_one
            low_ref[rows] = dz_one.astype(B16)
            sum_ref[0:1] += col_sum(d_hidden * normed)
            sum_ref[1:2] += col_sum(d_hidden)
            sum_ref[2:3] += col_sum(dz_one)
            sum_ref[3:4] += col_sum(dz_one * flag_ref[rows, 0:1])
            d_att_ref[rows] = dot(low_ref[rows], w_ref[:, 3 * width :]).astype(B16)

        loop(half, step)
    mask = two_heads(slots)

    def chain_step(chain, carry):
        rows = pl.ds(pl.multiple_of(chain * slots, slots), slots)
        for pair in range(width // (2 * HEAD)):
            lanes = 2 * HEAD * pair
            query = qkv_ref[rows, lanes : lanes + 2 * HEAD]
            key = qkv_ref[rows, width + lanes : width + lanes + 2 * HEAD]
            value = qkv_ref[rows, 2 * width + lanes : 2 * width + lanes + 2 * HEAD]
            d_att = d_att_ref[rows, lanes : lanes + 2 * HEAD]
            prob = prob_ref[rows, 2 * slots * pair : 2 * slots * (pair + 1)]
            d_prob = dot_t(d_att, doubled(value, mask))
            weights = prob.astype(F32)
            products = weights * d_prob
            lows = []
            for head in range(2):
                half = slice(head * slots, (head + 1) * slots)
                total = jnp.sum(products[:, half], axis=-1, keepdims=True)
                lows.append((products[:, half] - weights[:, half] * total).astype(B16))
            low = jnp.concatenate(lows, axis=1)
            d_query = dot(low, doubled(key, mask)) * (HEAD**-0.5)
            tall = jnp.concatenate(lows, axis=0)
            d_key = t_dot(tall, doubled(query, mask)) * (HEAD**-0.5)
            tall = jnp.concatenate([prob[:, :slots], prob[:, slots:]], axis=0)
            d_value = t_dot(tall, doubled(d_att, mask))
            d_qkv_ref[rows, lanes : lanes + 2 * HEAD] = d_query.astype(B16)
            d_qkv_ref[rows, width + lanes : width + lanes + 2 * HEAD] = d_key.astype(B16)
            d_qkv_ref[rows, 2 * width + lanes : 2 * width + lanes + 2 * HEAD] = d_value.astype(B16)
        return carry

    lax.fori_loop(0, count // slots, chain_step, 0)

    def bring_back(rows):
        sum_qkv_ref[0:1] += col_sum(d_qkv_ref[rows].astype(F32))
        part = dot_t(d_qkv_ref[rows], w_ref[:, : 3 * width]).astype(B16)
        part_ref[rows] = part
        sum_ref[4:5] += col_sum(part.astype(F32) * flag_ref[rows, 0:1])

    loop(count, bring_back)


def attend_back(chain_count, dz_two, own, other, normed, inverse, gain, flag, qkv, prob, w_a):
    shape = normed.shape
    heads = qkv.shape[1] // 3
    shapes = [
        (shape, F32),
        (shape, B16),
        (qkv.shape, B16),
        (shape, B16),
        ((8, shape[1]), F32),
        ((8, 3 * heads), F32),
    ]
    operands = [*dz_two, own, other, normed, inverse, gain, flag, qkv, prob, w_a]
    body = functools.partial(attend_back_body, shape[0] // chain_count)
    return call(body, "attend_back", shapes, operands, [((shape[0], heads), B16)])


def join_body(one_ref, other_ref, two_a_ref, two_b_ref, up_ref, qkv_ref, out_ref):
    width = one_ref.shape[1]
    heads = qkv_ref.shape[1] // 3
    rows = out_ref.shape[1]
    out_ref[...] = jnp.zeros_like(out_ref)

    def put(start, values):
        for k in range(values.shape[1] // 128):
            place = (start + 128 * k) // 128
            chunk = values[:, 128 * k : 128 * (k + 1)]
            out_ref[place // rows, place % rows : place % rows + 1] = chunk

    put(0, one_ref[3:4] + (one_ref[4:5] + other_ref[4:5]))
    for k in range(3):
        put((1 + k) * width, one_ref[k : k + 1])
        put((4 + k) * width, two_a_ref[k : k + 1] + two_b_ref[k : k + 1])
    put(7 * width, qkv_ref[0:1, :heads])
    put(7 * width + heads, qkv_ref[0:1, 2 * heads :])
    put(7 * width + 2 * heads, up_ref[0:1])


def join(rows, sums_one, sums_other, sums_two, sums_up, sums_qkv):
    width = sums_one.shape[1]
    length = 7 * width + 2 * sums_qkv.shape[1] // 3 + sums_up.shape[1]
    assert length <= 2 * rows * 128
    operands = [sums_one, sums_other, *sums_two, sums_up, sums_qkv]
    return call(join_body, "join", [((2, rows, 128), F32)], operands, limit=4)[0]


def last_body(dz_ref, own_ref, other_ref, flag_ref, out_a_ref, out_b_ref, tokens_ref, out_ref):
    for rows in chunks(dz_ref.shape[0]):
        total = dz_ref[rows] + (own_ref[rows].astype(F32) + other_ref[rows].astype(F32))
        tokens_ref[rows] = jnp.where(flag_ref[rows, 0:1] > 0.0, 0.0, total)
        out_ref[rows] = rows_in((out_a_ref, out_b_ref), rows)


def last(dz_one, own, other, flag, results):
    shapes = [(dz_one.shape, F32), (dz_one.shape, B16)]
    return call(last_body, "last", shapes, [dz_one, own, other, flag, *results])


def add_late_body(x_ref, y_ref, from_x_ref, from_y_ref, out_x_ref, out_y_ref):
    out_x_ref[...] = (x_ref[...].astype(F32) + from_y_ref[:2].astype(F32)).astype(B16)
    out_y_ref[...] = (y_ref[...].astype(F32) + from_x_ref[:2].astype(F32)).astype(B16)


def add_own_body(own_ref, from_x_ref, from_y_ref, late_x_ref, late_y_ref, near_ref, mid_ref):
    near_ref[...] = (
        own_ref[:2].astype(F32) + from_x_ref[2:].astype(F32) + late_y_ref[...].astype(F32)
    )
    mid_ref[...] = (
        own_ref[2:].astype(F32) + late_x_ref[...].astype(F32) + from_y_ref[2:].astype(F32)
    ).astype(B16)


def add_mid_body(near_ref, mid_ref, own_ref, far_ref):
    own_ref[...] = near_ref[0] + mid_ref[0].astype(F32)
    far_ref[...] = (near_ref[1] + mid_ref[1].astype(F32)).astype(B16)


def late_vector_body(x_ref, y_ref, from_x_ref, from_y_ref, v_ref, out_x_ref, out_y_ref, vector_ref):
    cols = x_ref.shape[2]
    out_x_ref[...] = (x_ref[...].astype(F32) + from_y_ref[:2].astype(F32)).astype(B16)
    out_y_ref[:, :, :cols] = (y_ref[...].astype(F32) + from_x_ref[:2, :, :cols].astype(F32)).astype(B16)
    vector = (v_ref[...].astype(F32) + from_x_ref[:2, :, cols:].astype(F32)).astype(B16)
    out_y_ref[:, :, cols:] = vector
    vector_ref[...] = vector


def own_vector_body(own_ref, from_x_ref, from_y_ref, late_x_ref, late_y_ref, v_ref, near_ref, mid_ref, vector_ref):
    cols = own_ref.shape[2]
    near_ref[...] = (
        own_ref[:2].astype(F32)
        + from_x_ref[2:, :, :cols].astype(F32)
        + late_y_ref[:, :, :cols].astype(F32)
    )
    mid_ref[:, :, :cols] = (
        own_ref[2:].astype(F32) + late_x_ref[...].astype(F32) + from_y_ref[2:].astype(F32)
    ).astype(B16)
    vector = (v_ref[...].astype(F32) + late_y_ref[:, :, cols:].astype(F32)).astype(B16)
    mid_ref[:, :, cols:] = vector
    vector_ref[...] = vector


def mid_vector_body(near_ref, mid_ref, v_ref, own_ref, far_ref, vector_ref):
    cols = own_ref.shape[1]
    own_ref[...] = near_ref[0] + mid_ref[0, :, :cols].astype(F32)
    far_ref[:, :cols] = (near_ref[1] + mid_ref[1, :, :cols].astype(F32)).astype(B16)
    vector = (v_ref[...].astype(F32) + mid_ref[:, :, cols:].astype(F32)).astype(B16)
    for k in range(2):
        far_ref[:, cols + 128 * k : cols + 128 * (k + 1)] = vector[k]
    vector_ref[...] = vector


def far_vector_body(own_ref, far_ref, v_ref, *outs):
    rows, cols = own_ref.shape
    part = cols // 4
    for k in range(4):
        lanes = slice(k * part, (k + 1) * part)
        outs[k][...] = own_ref[:, lanes] + far_ref[:, lanes].astype(F32)
    place = 0
    joined = [
        v_ref[k].astype(F32) + far_ref[:, cols + 128 * k : cols + 128 * (k + 1)].astype(F32) for k in range(2)
    ]
    for out_ref in outs[4:]:
        for k in range(out_ref.shape[0]):
            out_ref[k : k + 1] = joined[place // rows][place % rows : place % rows + 1]
            place += 1


def late_vector(late_x, late_y, from_x, from_y, vector):
    rows, cols = late_x.shape[1:]
    shapes = [(late_x.shape, B16), ((2, rows, cols + 128), B16), (vector.shape, B16)]
    operands = [late_x, late_y, from_x, from_y, vector]
    return call(late_vector_body, "late_vector", shapes, operands, limit=8)


def own_vector(own, from_x, from_y, late_x, late_y, vector):
    rows, cols = own.shape[1:]
    shapes = [((2, rows, cols), F32), ((2, rows, cols + 128), B16), (vector.shape, B16)]
    operands = [own, from_x, from_y, late_x, late_y, vector]
    return call(own_vector_body, "own_vector", shapes, operands, limit=8)


def mid_vector(near, mid, vector):
    rows, cols = near.shape[1:]
    shapes = [((rows, cols), F32), ((rows, cols + 256), B16), (vector.shape, B16)]
    return call(mid_vector_body, "mid_vector", shapes, [near, mid, vector], limit=8)


def far_vector(own, far, vector, sizes):
    rows, cols = own.shape
    shapes = [((rows, cols // 4), F32)] * 4 + [((size // 128, 128), F32) for size in sizes]
    outs = call(far_vector_body, "far_vector", shapes, [own, far, vector], limit=8)
    return outs[:4], [member.reshape(-1) for member in outs[4:]]


def add_late(late_x, late_y, from_x, from_y):
    shape = (late_x.shape, B16)
    return call(add_late_body, "add_late", [shape, shape], [late_x, late_y, from_x, from_y], limit=8)


def add_own(own, from_x, from_y, late_x, late_y):
    shapes = [(late_x.shape, F32), (late_x.shape, B16)]
    return call(add_own_body, "add_own", shapes, [own, from_x, from_y, late_x, late_y], limit=8)


def add_mid(near, mid):
    shapes = [(near.shape[1:], F32), (near.shape[1:], B16)]
    return call(add_mid_body, "add_mid", shapes, [near, mid], limit=8)


def per_device(dp_size, tokens, masked, lengths, mask_vector, w_query, b_query, w_key, w_value,
               b_value, w_out, b_out, gain_one, shift_one, w_up, b_up, w_down, b_down, gain_two,
               shift_two, grad_out):
    head_cols = w_query.shape[1]
    width = tokens.shape[1]
    fast = dp_size == BLOCKS and w_query.shape[0] % 16 == 0
    me = lax.axis_index("dp").astype(jnp.int32).reshape(1)
    if not fast:
        me = jnp.zeros_like(me)

    (b_query, b_value, b_out, gain_one, shift_one, b_up, b_down, gain_two, shift_two) = (
        member.astype(F32)
        for member in (b_query, b_value, b_out, gain_one, shift_one, b_up, b_down, gain_two, shift_two)
    )
    is_masked = (masked == 1)[:, None]
    flag = jnp.broadcast_to(is_masked, (masked.shape[0], 128)).astype(F32)
    in_low = jnp.where(is_masked, mask_vector[None, :], tokens)
    bias_qkv = jnp.concatenate([b_query, jnp.zeros_like(b_query), b_value])[None, :]
    vectors_one = jnp.stack([b_out, gain_one, shift_one])
    vectors_two = jnp.stack([gain_one, shift_one, b_down, gain_two, shift_two])
    b_up, gain_one = b_up[None, :], gain_one[None, :]

    a = jnp.concatenate([w_query, w_key, w_value, w_out.T], axis=1)
    c = w_up
    d = w_down.T
    if fast:
        az = swap(a, 12)
        az, me, flag, in_low, bias_qkv, vectors_one, vectors_two, b_up, gain_one = tie(
            az, me, flag, in_low, bias_qkv, vectors_one, vectors_two, b_up, gain_one
        )
        an = jnp.stack([a, az])
        anx, any_, am = swap(an, 1), swap(an, 2), swap(an, 4)
        anx, any_, am, an, c = tie(anx, any_, am, an, c)
        amx, amy, cz = swap(am, 1), swap(am, 2), swap(c, 12)
        amx, amy, cz, anx, c, d = tie(amx, amy, cz, anx, c, d)
        cn = jnp.stack([c, cz])
        amd, and_, cm = swap(amy, 1), swap(anx, 2), swap(cn, 4)
        cnx, cny, dz = swap(cn, 1), swap(cn, 2), swap(after(d, cm), 12)
        amd, and_, cm, cnx, cny = tie(amd, and_, cm, cnx, cny)
        dn = jnp.stack([d, dz])
        pieces_a = [an, am, anx, amx, any_, amy, and_, amd]
        cmx, cnd, dm = swap(cm, 1), swap(cnx, 2), swap(dn, 4)
        dnx, dny = swap(dn, 1), swap(dn, 2)
    else:
        a, c, d = (lax.all_gather(piece, "dp", axis=0, tiled=True) for piece in (a, c, d))
        pieces_a, pieces_c, pieces_d = as_pieces(a), as_pieces(c), as_pieces(d)
    w_a, qkv, prob, attended, part = attend(me, lengths, in_low, bias_qkv, pieces_a)
    if fast:
        cmx, cnd, dm, dnx, dny, cm, part = tie(cmx, cnd, dm, dnx, dny, cm, part)
        cmy, dnd, cmd = swap(cm, 2), swap(dny, 1), swap(cnd, 4)
    other = pair_swap(part)
    if fast:
        cmy, dnd, cmd, dm, other, part = tie(cmy, dnd, cmd, dm, other, part)
        pieces_c = [cn, cm, cnx, cmx, cny, cmy, cnd, cmd]
        dmx, dmy, dmd = swap(dm, 1), swap(dm, 2), swap(dnd, 4)
    w_u, normed_one, inverse_one, hidden_low, act_low, slope = up(
        me, in_low, part, other, vectors_one, b_up, pieces_c
    )
    if fast:
        dmx, dmy, dmd, act_low = tie(dmx, dmy, dmd, act_low)
        pieces_d = [dn, dm, dnx, dmx, dny, dmy, dnd, dmd]
    w_d, *parts = down(me, act_low, pieces_d)
    halves = [
        second_norm(index * part.shape[0], normed_one, part, pair_swap(part), grad_out, vectors_two)
        for index, part in enumerate(parts)
    ]
    results, dz_two, dz_two_low, sums_two = zip(*halves)
    dx, dy, turned = weight_grad(me, [dz_two_low], [act_low], ORDER[:2])
    if fast:
        dx, dy, turned, dz_two_low = tie(dx, dy, turned, dz_two_low)
        dxr, dyr = swap(dx, 1), swap(dy, 2)
    dxl, dyl, do = weight_grad(me, None, [act_low], ORDER[2:], turned=turned)
    d_pre_low, part, sums_up = hidden_back(dz_two_low, slope, w_d, w_u)
    cx, cy, cxl, cyl, co = weight_grad(me, [[hidden_low]], [d_pre_low])
    if fast:
        dxr, dyr, part, cx, cy, dxl, dyl, do = tie(dxr, dyr, part, cx, cy, dxl, dyl, do)
        cxr, cyr = swap(cx, 1), swap(cy, 2)
        dxl, dyl = add_late(dxl, dyl, dxr, dyr)
        dxlr, dylr = swap(dxl, 1), swap(dyl, 2)
    other = pair_swap(part)
    dz_one, dz_one_low, d_qkv, part, sums_one, sums_qkv = attend_back(
        lengths.shape[0], dz_two, part, other, normed_one, inverse_one, gain_one, flag, qkv, prob, w_a
    )
    if fast:
        cxr, cyr, dxlr, dylr, part, d_qkv, dz_one_low = tie(cxr, cyr, dxlr, dylr, part, d_qkv, dz_one_low)
        cxl, cyl = add_late(cxl, cyl, cxr, cyr)
        cxlr, cylr = swap(cxl, 1), swap(cyl, 2)
        d_near, d_mid = add_own(do, dxr, dyr, dxlr, dylr)
        d_midr = swap(d_mid, 4)
    sums_other = pair_swap(sums_one)
    joined = join(width // BLOCKS, sums_one, sums_other, sums_two, sums_up, sums_qkv)
    vector = joined.astype(B16) if fast else None
    ax, ay, axl, ayl, ao = weight_grad(me, [[in_low], [dz_one_low]], [d_qkv, attended], vector=vector)
    if fast:
        c_near, c_mid = add_own(co, cxr, cyr, cxlr, cylr)
        c_near, c_mid, d_midr, ax, ay, part = tie(c_near, c_mid, d_midr, ax, ay, part)
        axr, ayr = swap(ax, 1), swap(ay, 2)
        d_near, d_far = add_mid(d_near, d_midr)
        c_midr, d_farr = swap(c_mid, 4), swap(d_far, 12)
    other = pair_swap(part)
    d_tokens, result = last(dz_one, part, other, flag, results)
    sizes = [width] * 7 + [head_cols] * 2 + [w_up.shape[1]]
    if fast:
        axr, ayr, c_midr, d_farr, d_tokens, result = tie(axr, ayr, c_midr, d_farr, d_tokens, result)
        axl, ayl, vector = late_vector(axl, ayl, axr, ayr, vector)
        axlr, aylr = swap(axl, 1), swap(ayl, 2)
        c_near, c_far = add_mid(c_near, c_midr)
        c_farr = swap(c_far, 12)
        axlr, aylr, c_farr = tie(axlr, aylr, c_farr)
        a_near, a_mid, vector = own_vector(ao, axr, ayr, axlr, aylr, vector)
        a_midr = swap(a_mid, 4)
        d_w_down_t = d_near + d_farr.astype(F32)
        a_midr, d_w_down_t = tie(a_midr, d_w_down_t)
        a_near, a_far, vector = mid_vector(a_near, a_midr, vector)
        a_farr = swap(a_far, 12)
        d_w_up = c_near + c_farr.astype(F32)
        d_wa, summed = far_vector(a_near, a_farr, vector, sizes)
    else:
        full = []
        for parts in ((ax, ay, axl, ayl, ao), (cx, cy, cxl, cyl, co), (dx, dy, dxl, dyl, do)):
            blocks = [None] * BLOCKS
            for member, offsets in zip(parts, ORDER):
                for k, offset in enumerate(offsets):
                    blocks[offset] = member[k]
            full.append(jnp.concatenate(blocks).astype(F32))
        joined = lax.psum(joined, "dp")
        d_wa, d_w_up, d_w_down_t = (
            lax.psum_scatter(member, "dp", scatter_dimension=0, tiled=True) for member in full
        )
        d_wa = [d_wa[:, k * head_cols : (k + 1) * head_cols] for k in range(4)]
        joined = joined.reshape(-1)
        summed = []
        start = 0
        for size in sizes:
            summed.append(joined[start : start + size])
            start += size
    return (
        result,
        d_tokens,
        summed[0],
        d_wa[0],
        summed[7],
        d_wa[1],
        d_wa[2],
        summed[8],
        d_wa[3].T,
        summed[3],
        summed[1],
        summed[2],
        d_w_up,
        summed[9],
        d_w_down_t.T,
        summed[6],
        summed[4],
        summed[5],
    )


def solution(mesh):
    rows, flat, both = P("dp", None), P(), P("dp", "mp")
    return jax.shard_map(
        functools.partial(per_device, mesh.shape["dp"]),
        mesh=mesh,
        in_specs=(rows, P("dp"), P("dp"), flat, both, P("mp"), both, both, P("mp"), P("mp", "dp"),
                  flat, flat, flat, both, P("mp"), P("mp", "dp"), flat, flat, flat, rows),
        out_specs=(rows, rows, flat, both, P("mp"), both, both, P("mp"), P("mp", "dp"), flat, flat,
                   flat, both, P("mp"), P("mp", "dp"), flat, flat, flat),
        check_vma=False,
    )
```

```python
import functools

import jax
import jax.numpy as jnp
from jax import lax
from jax.experimental import pallas as pl
from jax.experimental.pallas import tpu as pltpu
from jax.sharding import PartitionSpec as P

HEAD = 64
NORM_EPS = 1e-05
F32 = jnp.float32
B16 = jnp.bfloat16
MIB = 1 << 20

BLOCKS = 16
NEAR = (0, 12)
MID = (4, 8)


def swap(values, bit):
    return lax.ppermute(values, "dp", [(i, i ^ bit) for i in range(BLOCKS)])


def tie(*values):
    return lax.optimization_barrier(values)


def after(value, *earlier):
    return tie(value, *earlier)[0]


def pair_swap(partial):
    return lax.ppermute(partial, "mp", [(0, 1), (1, 0)])


def as_pieces(full):
    rows = full.shape[0] // BLOCKS
    blocks = full.reshape(BLOCKS, rows, full.shape[1])
    return [
        jnp.stack([blocks[offset + bits[0]], blocks[offset + bits[1]]])
        for offset in range(4)
        for bits in (NEAR, MID)
    ]


SMEM_SPEC = pl.BlockSpec(memory_space=pltpu.SMEM)
VMEM_SPEC = pl.BlockSpec(memory_space=pltpu.VMEM)
CHUNK = 256
UNROLL = 8
LIGHT = pl.CostEstimate(flops=1, bytes_accessed=1, transcendentals=0)


def call(body, name, shapes, operands, scratch=(), limit=16):
    return pl.pallas_call(
        body,
        in_specs=[
            SMEM_SPEC if member.dtype == jnp.int32 and member.ndim == 1 else VMEM_SPEC
            for member in operands
        ],
        out_specs=[VMEM_SPEC] * len(shapes),
        out_shape=[jax.ShapeDtypeStruct(shape, dtype) for shape, dtype in shapes],
        scratch_shapes=[pltpu.VMEM(shape, dtype) for shape, dtype in scratch],
        compiler_params=pltpu.CompilerParams(vmem_limit_bytes=limit * MIB),
        cost_estimate=LIGHT,
        name=name,
    )(*operands)


def chunks(count):
    return [slice(start, start + CHUNK) for start in range(0, count, CHUNK)]


def loop(count, step, size=CHUNK, unroll=1):
    def body(index, carry):
        step(pl.ds(pl.multiple_of(index * size, size), size))
        return carry

    lax.fori_loop(0, count // size, body, 0, unroll=unroll)


PAIRS = [(q + bits[k], 2 * q + m, k) for q in range(4) for m, bits in enumerate((NEAR, MID)) for k in range(2)]


def fill(me, pieces, full_ref):
    rows = pieces[0].shape[1]
    for offset, piece, index in PAIRS:
        block = me ^ offset
        full_ref[pl.ds(pl.multiple_of(block * rows, rows), rows), :] = pieces[piece][index]


def dot(left, right):
    return jnp.dot(left, right, preferred_element_type=F32)


def dot_t(left, right):
    return lax.dot_general(left, right, (((1,), (1,)), ((), ())), preferred_element_type=F32)


def t_dot(left, right):
    return lax.dot_general(left, right, (((0,), (0,)), ((), ())), preferred_element_type=F32)


def row_mean(values):
    return jnp.mean(values, axis=-1, keepdims=True)


def normalize(values):
    centred = values - row_mean(values)
    inverse = lax.rsqrt(row_mean(centred * centred) + NORM_EPS)
    return centred * inverse, inverse


def col_sum(values):
    return jnp.sum(values, axis=0, keepdims=True)


def norm_back(scaled, normed, inverse):
    return inverse * (scaled - row_mean(scaled) - normed * row_mean(scaled * normed))


def two_heads(slots):
    row = lax.broadcasted_iota(jnp.int32, (2 * slots, 2 * HEAD), 0) // slots
    lane = lax.broadcasted_iota(jnp.int32, (2 * slots, 2 * HEAD), 1) // HEAD
    return (row == lane).astype(F32).astype(B16)


def doubled(values, mask):
    return jnp.concatenate([values, values], axis=0) * mask


def attend_body(slots, me_ref, len_ref, in_ref, bias_ref, *rest):
    pieces, (w_ref, qkv_ref, prob_ref, att_ref, part_ref) = rest[:-5], rest[-5:]
    count, width = att_ref.shape
    fill(me_ref[0], pieces, w_ref)

    def project(rows):
        qkv_ref[rows] = (dot(in_ref[rows], w_ref[:, : 3 * width]) + bias_ref[...]).astype(B16)

    loop(count, project, unroll=4)
    mask = two_heads(slots)
    key_slot = lax.broadcasted_iota(jnp.int32, (slots, slots), 1)

    def chain_step(chain, carry):
        valid = key_slot < len_ref[chain]
        rows = pl.ds(pl.multiple_of(chain * slots, slots), slots)
        for pair in range(width // (2 * HEAD)):
            lanes = 2 * HEAD * pair
            query = qkv_ref[rows, lanes : lanes + 2 * HEAD]
            key = qkv_ref[rows, width + lanes : width + lanes + 2 * HEAD]
            value = qkv_ref[rows, 2 * width + lanes : 2 * width + lanes + 2 * HEAD]
            scores = dot_t(query * (HEAD**-0.5), doubled(key, mask))
            probs = []
            for head in range(2):
                part = jnp.where(valid, scores[:, head * slots : (head + 1) * slots], -1e30)
                terms = jnp.exp(part - jnp.max(part, axis=-1, keepdims=True))
                probs.append((terms / jnp.sum(terms, axis=-1, keepdims=True)).astype(B16))
            prob = jnp.concatenate(probs, axis=1)
            prob_ref[rows, 2 * slots * pair : 2 * slots * (pair + 1)] = prob
            att_ref[rows, lanes : lanes + 2 * HEAD] = dot(prob, doubled(value, mask)).astype(B16)
        return carry

    lax.fori_loop(0, count // slots, chain_step, 0, unroll=UNROLL)

    def bring_out(rows):
        part_ref[rows] = dot_t(att_ref[rows], w_ref[:, 3 * width :]).astype(B16)

    loop(count, bring_out, unroll=4)


def attend(me, lengths, in_low, bias, pieces):
    count, width = in_low.shape
    heads = bias.shape[1] // 3
    slots = count // lengths.shape[0]
    shapes = [
        ((width, 4 * heads), B16),
        ((count, 3 * heads), B16),
        ((count, heads // HEAD * slots), B16),
        ((count, heads), B16),
        ((count, width), B16),
    ]
    body = functools.partial(attend_body, slots)
    return call(body, "attend", shapes, [me, lengths, in_low, bias, *pieces])


def up_body(me_ref, in_ref, own_ref, other_ref, vec_ref, bias_ref, *rest):
    pieces, (w_ref, normed_ref, inverse_ref, low_ref, act_ref, slope_ref) = rest[:-6], rest[-6:]
    fill(me_ref[0], pieces, w_ref)
    vectors = vec_ref[...]

    def step(rows):
        attn = own_ref[rows].astype(F32) + other_ref[rows].astype(F32) + vectors[0:1]
        normed, inverse = normalize(in_ref[rows].astype(F32) + attn)
        normed_ref[rows] = normed
        inverse_ref[rows] = jnp.broadcast_to(inverse, (CHUNK, inverse_ref.shape[1]))
        low_ref[rows] = (normed * vectors[1:2] + vectors[2:3]).astype(B16)
        pre = dot(low_ref[rows], w_ref[...]) + bias_ref[...]
        cdf = 0.5 + 0.5 * lax.erf(pre * (2.0**-0.5))
        act_ref[rows] = (pre * cdf).astype(B16)
        density = jnp.exp(pre * pre * -0.5) * 0.3989422804014327
        slope_ref[rows] = (cdf + pre * density).astype(B16)

    loop(in_ref.shape[0], step, unroll=2)


def up(me, in_low, own, other, vectors, bias, pieces):
    count, width = in_low.shape
    units = bias.shape[1]
    shapes = [
        ((width, units), B16),
        ((count, width), F32),
        ((count, 128), F32),
        ((count, width), B16),
        ((count, units), B16),
        ((count, units), B16),
    ]
    return call(up_body, "up", shapes, [me, in_low, own, other, vectors, bias, *pieces])


def down_body(me_ref, act_ref, *rest):
    pieces, (w_ref, part_ref) = rest[:-2], rest[-2:]
    fill(me_ref[0], pieces, w_ref)
    part_ref[...] = dot_t(act_ref[: part_ref.shape[0]], w_ref[...]).astype(B16)


def down_rest_body(act_ref, w_ref, part_ref):
    half = part_ref.shape[0]
    part_ref[...] = dot_t(act_ref[half:], w_ref[...]).astype(B16)


def down(me, act, pieces):
    count, units = act.shape
    width = BLOCKS * pieces[0].shape[1]
    half = ((count // 2, width), B16)
    w_down_t, first = call(down_body, "down", [((width, units), B16), half], [me, act, *pieces])
    (second,) = call(down_rest_body, "down_rest", [half], [act, w_down_t])
    return w_down_t, first, second


def second_norm_body(start, normed_ref, own_ref, other_ref, grad_ref, vec_ref, out_ref, dz_ref, low_ref, sum_ref):
    vectors = vec_ref[...]
    sum_ref[...] = jnp.zeros_like(sum_ref)
    for rows in chunks(own_ref.shape[0]):
        there = slice(start + rows.start, start + rows.stop)
        hidden = normed_ref[there] * vectors[0:1] + vectors[1:2]
        ffn = own_ref[rows].astype(F32) + other_ref[rows].astype(F32) + vectors[2:3]
        normed, inverse = normalize(hidden + ffn)
        out_ref[rows] = (normed * vectors[3:4] + vectors[4:5]).astype(B16)
        grad = grad_ref[there].astype(F32)
        dz = norm_back(grad * vectors[3:4], normed, inverse)
        dz_ref[rows] = dz
        low_ref[rows] = dz.astype(B16)
        sum_ref[0:1] += col_sum(grad * normed)
        sum_ref[1:2] += col_sum(grad)
        sum_ref[2:3] += col_sum(dz)


def second_norm(start, normed, own, other, grad, vectors):
    shape = own.shape
    shapes = [(shape, B16), (shape, F32), (shape, B16), ((8, shape[1]), F32)]
    body = functools.partial(second_norm_body, start)
    return call(body, "second_norm", shapes, [normed, own, other, grad, vectors])


def rows_in(halves, rows):
    size = halves[0].shape[0]
    half = halves[rows.start // size]
    return half[rows.start % size : rows.start % size + rows.stop - rows.start]


ORDER = (
    (3, 15, 1, 13),
    (7, 11, 6, 10),
    (5, 9),
    (2, 14),
    (0, 12, 4, 8),
)


def weight_grad(me, lefts, rights, groups=ORDER, vector=None, turned=None):
    count = rights[0].shape[0]
    width = lefts[-1][0].shape[1] if turned is None else turned.shape[0]
    tile = 384 if all(right.shape[1] % 384 == 0 for right in rights) else 128
    total = sum(right.shape[1] for right in rights)
    rows = width // BLOCKS
    n = len(rights)
    flat = [half for left in lefts for half in left] if turned is None else [turned]
    wide = [] if vector is None else [vector]
    keep = turned is None and len(groups) < len(ORDER)
    wanted = [offset for offsets in groups for offset in offsets]
    if keep and total % (2 * tile) == 0:
        tile *= 2

    def body(me_ref, *refs):
        left_refs, right_refs = list(refs[: len(flat)]), refs[len(flat) : len(flat) + n]
        outs = refs[len(flat) + n + len(wide) :]
        placed_ref = outs[-1]
        if wide:
            outs[0][0:2, :, total:] = refs[len(flat) + n][...]
            outs[0][2:4, :, total:] = jnp.zeros((2, rows, 128), B16)
        at = 0
        for index, right_ref in enumerate(right_refs):
            turned_ref = left_refs[0] if turned is not None else outs[-2]
            if turned is None:
                start = 0
                for _ in lefts[index]:
                    half_ref = left_refs.pop(0)
                    turned_ref[:, start : start + half_ref.shape[0]] = half_ref[...].T
                    start += half_ref.shape[0]
            for k, offset in enumerate(wanted):
                place = pl.multiple_of((me_ref[0] ^ offset) * rows, rows)
                placed_ref[k * rows : (k + 1) * rows] = turned_ref[pl.ds(place, rows), :]

            def step(cols, right_ref=right_ref, at=at):
                product = dot(placed_ref[...], right_ref[:, cols]).astype(B16)
                there = pl.ds(pl.multiple_of(at + cols.start, 128), tile)
                first = 0
                for out_ref, offsets in zip(outs, groups):
                    for k in range(len(offsets)):
                        out_ref[k, :, there] = product[first : first + rows]
                        first += rows

            count_tiles = right_ref.shape[1] // tile
            loop(right_ref.shape[1], step, tile, unroll=count_tiles if wide or keep else 1)
            at += right_ref.shape[1]

    shapes = [((len(offsets), rows, total), B16) for offsets in groups]
    shapes[0] = ((len(groups[0]), rows, total + 128 * len(wide)), B16)
    held = ((width, count), B16)
    shapes += [held] * keep
    scratch = [held] * (turned is None and not keep) + [((len(wanted) * rows, count), B16)]
    return call(body, "weight_grad", shapes, [me, *flat, *rights, *wide], scratch)


def hidden_back_body(low_a_ref, low_b_ref, slope_ref, down_ref, up_ref, pre_ref, part_ref, sum_ref):
    sum_ref[...] = jnp.zeros_like(sum_ref)
    half = low_a_ref.shape[0]
    for start, low_ref in ((0, low_a_ref), (half, low_b_ref)):

        def step(here, start=start, low_ref=low_ref):
            rows = pl.ds(pl.multiple_of(start + here.start, CHUNK), CHUNK)
            d_pre = dot(low_ref[here], down_ref[...]) * slope_ref[rows].astype(F32)
            sum_ref[0:1] += col_sum(d_pre)
            pre_ref[rows] = d_pre.astype(B16)
            part_ref[rows] = dot_t(pre_ref[rows], up_ref[...]).astype(B16)

        loop(half, step)


def hidden_back(lows, slope, w_down_t, w_up):
    count, units = slope.shape
    shapes = [((count, units), B16), ((count, w_up.shape[0]), B16), ((8, units), F32)]
    return call(hidden_back_body, "hidden_back", shapes, [*lows, slope, w_down_t, w_up])


def attend_back_body(slots, dz_a_ref, dz_b_ref, own_ref, other_ref, normed_ref, inverse_ref, gain_ref,
                     flag_ref, qkv_ref, prob_ref, w_ref, dz_one_ref, low_ref, d_qkv_ref, part_ref, sum_ref,
                     sum_qkv_ref, d_att_ref):
    count, width = d_att_ref.shape
    sum_ref[...] = jnp.zeros_like(sum_ref)
    sum_qkv_ref[...] = jnp.zeros_like(sum_qkv_ref)
    half = dz_a_ref.shape[0]
    for start, dz_ref in ((0, dz_a_ref), (half, dz_b_ref)):

        def step(here, start=start, dz_ref=dz_ref):
            rows = pl.ds(pl.multiple_of(start + here.start, CHUNK), CHUNK)
            normed = normed_ref[rows]
            d_hidden = dz_ref[here] + (own_ref[rows].astype(F32) + other_ref[rows].astype(F32))
            dz_one = norm_back(d_hidden * gain_ref[...], normed, inverse_ref[rows, 0:1])
            dz_one_ref[rows] = dz_one
            low_ref[rows] = dz_one.astype(B16)
            sum_ref[0:1] += col_sum(d_hidden * normed)
            sum_ref[1:2] += col_sum(d_hidden)
            sum_ref[2:3] += col_sum(dz_one)
            sum_ref[3:4] += col_sum(dz_one * flag_ref[rows, 0:1])
            d_att_ref[rows] = dot(low_ref[rows], w_ref[:, 3 * width :]).astype(B16)

        loop(half, step)
    mask = two_heads(slots)

    def chain_step(chain, carry):
        rows = pl.ds(pl.multiple_of(chain * slots, slots), slots)
        for pair in range(width // (2 * HEAD)):
            lanes = 2 * HEAD * pair
            query = qkv_ref[rows, lanes : lanes + 2 * HEAD]
            key = qkv_ref[rows, width + lanes : width + lanes + 2 * HEAD]
            value = qkv_ref[rows, 2 * width + lanes : 2 * width + lanes + 2 * HEAD]
            d_att = d_att_ref[rows, lanes : lanes + 2 * HEAD]
            prob = prob_ref[rows, 2 * slots * pair : 2 * slots * (pair + 1)]
            d_prob = dot_t(d_att, doubled(value, mask))
            weights = prob.astype(F32)
            products = weights * d_prob
            lows = []
            for head in range(2):
                half = slice(head * slots, (head + 1) * slots)
                total = jnp.sum(products[:, half], axis=-1, keepdims=True)
                lows.append((products[:, half] - weights[:, half] * total).astype(B16))
            low = jnp.concatenate(lows, axis=1)
            d_query = dot(low, doubled(key, mask)) * (HEAD**-0.5)
            tall = jnp.concatenate(lows, axis=0)
            d_key = t_dot(tall, doubled(query, mask)) * (HEAD**-0.5)
            tall = jnp.concatenate([prob[:, :slots], prob[:, slots:]], axis=0)
            d_value = t_dot(tall, doubled(d_att, mask))
            d_qkv_ref[rows, lanes : lanes + 2 * HEAD] = d_query.astype(B16)
            d_qkv_ref[rows, width + lanes : width + lanes + 2 * HEAD] = d_key.astype(B16)
            d_qkv_ref[rows, 2 * width + lanes : 2 * width + lanes + 2 * HEAD] = d_value.astype(B16)
        return carry

    lax.fori_loop(0, count // slots, chain_step, 0)

    def bring_back(rows):
        sum_qkv_ref[0:1] += col_sum(d_qkv_ref[rows].astype(F32))
        part = dot_t(d_qkv_ref[rows], w_ref[:, : 3 * width]).astype(B16)
        part_ref[rows] = part
        sum_ref[4:5] += col_sum(part.astype(F32) * flag_ref[rows, 0:1])

    loop(count, bring_back)


def attend_back(chain_count, dz_two, own, other, normed, inverse, gain, flag, qkv, prob, w_a):
    shape = normed.shape
    heads = qkv.shape[1] // 3
    shapes = [
        (shape, F32),
        (shape, B16),
        (qkv.shape, B16),
        (shape, B16),
        ((8, shape[1]), F32),
        ((8, 3 * heads), F32),
    ]
    operands = [*dz_two, own, other, normed, inverse, gain, flag, qkv, prob, w_a]
    body = functools.partial(attend_back_body, shape[0] // chain_count)
    return call(body, "attend_back", shapes, operands, [((shape[0], heads), B16)])


def join_body(one_ref, other_ref, two_a_ref, two_b_ref, up_ref, qkv_ref, out_ref):
    width = one_ref.shape[1]
    heads = qkv_ref.shape[1] // 3
    rows = out_ref.shape[1]
    out_ref[...] = jnp.zeros_like(out_ref)

    def put(start, values):
        for k in range(values.shape[1] // 128):
            place = (start + 128 * k) // 128
            chunk = values[:, 128 * k : 128 * (k + 1)]
            out_ref[place // rows, place % rows : place % rows + 1] = chunk

    put(0, one_ref[3:4] + (one_ref[4:5] + other_ref[4:5]))
    for k in range(3):
        put((1 + k) * width, one_ref[k : k + 1])
        put((4 + k) * width, two_a_ref[k : k + 1] + two_b_ref[k : k + 1])
    put(7 * width, qkv_ref[0:1, :heads])
    put(7 * width + heads, qkv_ref[0:1, 2 * heads :])
    put(7 * width + 2 * heads, up_ref[0:1])


def join(rows, sums_one, sums_other, sums_two, sums_up, sums_qkv):
    width = sums_one.shape[1]
    length = 7 * width + 2 * sums_qkv.shape[1] // 3 + sums_up.shape[1]
    assert length <= 2 * rows * 128
    operands = [sums_one, sums_other, *sums_two, sums_up, sums_qkv]
    return call(join_body, "join", [((2, rows, 128), F32)], operands, limit=4)[0]


def last_body(dz_ref, own_ref, other_ref, flag_ref, out_a_ref, out_b_ref, tokens_ref, out_ref):
    for rows in chunks(dz_ref.shape[0]):
        total = dz_ref[rows] + (own_ref[rows].astype(F32) + other_ref[rows].astype(F32))
        tokens_ref[rows] = jnp.where(flag_ref[rows, 0:1] > 0.0, 0.0, total)
        out_ref[rows] = rows_in((out_a_ref, out_b_ref), rows)


def last(dz_one, own, other, flag, results):
    shapes = [(dz_one.shape, F32), (dz_one.shape, B16)]
    return call(last_body, "last", shapes, [dz_one, own, other, flag, *results])


def add_late_body(x_ref, y_ref, from_x_ref, from_y_ref, out_x_ref, out_y_ref):
    out_x_ref[...] = (x_ref[...].astype(F32) + from_y_ref[:2].astype(F32)).astype(B16)
    out_y_ref[...] = (y_ref[...].astype(F32) + from_x_ref[:2].astype(F32)).astype(B16)


def add_own_body(own_ref, from_x_ref, from_y_ref, late_x_ref, late_y_ref, near_ref, mid_ref):
    near_ref[...] = (
        own_ref[:2].astype(F32) + from_x_ref[2:].astype(F32) + late_y_ref[...].astype(F32)
    )
    mid_ref[...] = (
        own_ref[2:].astype(F32) + late_x_ref[...].astype(F32) + from_y_ref[2:].astype(F32)
    ).astype(B16)


def add_mid_body(near_ref, mid_ref, own_ref, far_ref):
    own_ref[...] = near_ref[0] + mid_ref[0].astype(F32)
    far_ref[...] = (near_ref[1] + mid_ref[1].astype(F32)).astype(B16)


def late_vector_body(x_ref, y_ref, from_x_ref, from_y_ref, v_ref, out_x_ref, out_y_ref, vector_ref):
    cols = x_ref.shape[2]
    out_x_ref[...] = (x_ref[...].astype(F32) + from_y_ref[:2].astype(F32)).astype(B16)
    out_y_ref[:, :, :cols] = (y_ref[...].astype(F32) + from_x_ref[:2, :, :cols].astype(F32)).astype(B16)
    vector = (v_ref[...].astype(F32) + from_x_ref[:2, :, cols:].astype(F32)).astype(B16)
    out_y_ref[:, :, cols:] = vector
    vector_ref[...] = vector


def own_vector_body(own_ref, from_x_ref, from_y_ref, late_x_ref, late_y_ref, v_ref, near_ref, mid_ref, vector_ref):
    cols = own_ref.shape[2]
    near_ref[...] = (
        own_ref[:2].astype(F32)
        + from_x_ref[2:, :, :cols].astype(F32)
        + late_y_ref[:, :, :cols].astype(F32)
    )
    mid_ref[:, :, :cols] = (
        own_ref[2:].astype(F32) + late_x_ref[...].astype(F32) + from_y_ref[2:].astype(F32)
    ).astype(B16)
    vector = (v_ref[...].astype(F32) + late_y_ref[:, :, cols:].astype(F32)).astype(B16)
    mid_ref[:, :, cols:] = vector
    vector_ref[...] = vector


def mid_vector_body(near_ref, mid_ref, v_ref, own_ref, far_ref, vector_ref):
    cols = own_ref.shape[1]
    own_ref[...] = near_ref[0] + mid_ref[0, :, :cols].astype(F32)
    far_ref[:, :cols] = (near_ref[1] + mid_ref[1, :, :cols].astype(F32)).astype(B16)
    vector = (v_ref[...].astype(F32) + mid_ref[:, :, cols:].astype(F32)).astype(B16)
    for k in range(2):
        far_ref[:, cols + 128 * k : cols + 128 * (k + 1)] = vector[k]
    vector_ref[...] = vector


def far_vector_body(own_ref, far_ref, v_ref, *outs):
    rows, cols = own_ref.shape
    part = cols // 4
    for k in range(4):
        lanes = slice(k * part, (k + 1) * part)
        outs[k][...] = own_ref[:, lanes] + far_ref[:, lanes].astype(F32)
    place = 0
    joined = [
        v_ref[k].astype(F32) + far_ref[:, cols + 128 * k : cols + 128 * (k + 1)].astype(F32) for k in range(2)
    ]
    for out_ref in outs[4:]:
        for k in range(out_ref.shape[0]):
            out_ref[k : k + 1] = joined[place // rows][place % rows : place % rows + 1]
            place += 1


def late_vector(late_x, late_y, from_x, from_y, vector):
    rows, cols = late_x.shape[1:]
    shapes = [(late_x.shape, B16), ((2, rows, cols + 128), B16), (vector.shape, B16)]
    operands = [late_x, late_y, from_x, from_y, vector]
    return call(late_vector_body, "late_vector", shapes, operands, limit=8)


def own_vector(own, from_x, from_y, late_x, late_y, vector):
    rows, cols = own.shape[1:]
    shapes = [((2, rows, cols), F32), ((2, rows, cols + 128), B16), (vector.shape, B16)]
    operands = [own, from_x, from_y, late_x, late_y, vector]
    return call(own_vector_body, "own_vector", shapes, operands, limit=8)


def mid_vector(near, mid, vector):
    rows, cols = near.shape[1:]
    shapes = [((rows, cols), F32), ((rows, cols + 256), B16), (vector.shape, B16)]
    return call(mid_vector_body, "mid_vector", shapes, [near, mid, vector], limit=8)


def far_vector(own, far, vector, sizes):
    rows, cols = own.shape
    shapes = [((rows, cols // 4), F32)] * 4 + [((size // 128, 128), F32) for size in sizes]
    outs = call(far_vector_body, "far_vector", shapes, [own, far, vector], limit=8)
    return outs[:4], [member.reshape(-1) for member in outs[4:]]


def add_late(late_x, late_y, from_x, from_y):
    shape = (late_x.shape, B16)
    return call(add_late_body, "add_late", [shape, shape], [late_x, late_y, from_x, from_y], limit=8)


def add_own(own, from_x, from_y, late_x, late_y):
    shapes = [(late_x.shape, F32), (late_x.shape, B16)]
    return call(add_own_body, "add_own", shapes, [own, from_x, from_y, late_x, late_y], limit=8)


def add_mid(near, mid):
    shapes = [(near.shape[1:], F32), (near.shape[1:], B16)]
    return call(add_mid_body, "add_mid", shapes, [near, mid], limit=8)


def per_device(dp_size, tokens, masked, lengths, mask_vector, w_query, b_query, w_key, w_value,
               b_value, w_out, b_out, gain_one, shift_one, w_up, b_up, w_down, b_down, gain_two,
               shift_two, grad_out):
    head_cols = w_query.shape[1]
    width = tokens.shape[1]
    fast = dp_size == BLOCKS and w_query.shape[0] % 16 == 0
    me = lax.axis_index("dp").astype(jnp.int32).reshape(1)
    if not fast:
        me = jnp.zeros_like(me)

    (b_query, b_value, b_out, gain_one, shift_one, b_up, b_down, gain_two, shift_two) = (
        member.astype(F32)
        for member in (b_query, b_value, b_out, gain_one, shift_one, b_up, b_down, gain_two, shift_two)
    )
    is_masked = (masked == 1)[:, None]
    flag = jnp.broadcast_to(is_masked, (masked.shape[0], 128)).astype(F32)
    in_low = jnp.where(is_masked, mask_vector[None, :], tokens)
    bias_qkv = jnp.concatenate([b_query, jnp.zeros_like(b_query), b_value])[None, :]
    vectors_one = jnp.stack([b_out, gain_one, shift_one])
    vectors_two = jnp.stack([gain_one, shift_one, b_down, gain_two, shift_two])
    b_up, gain_one = b_up[None, :], gain_one[None, :]

    a = jnp.concatenate([w_query, w_key, w_value, w_out.T], axis=1)
    c = w_up
    d = w_down.T
    if fast:
        az = swap(a, 12)
        az, me, flag, in_low, bias_qkv, vectors_one, vectors_two, b_up, gain_one = tie(
            az, me, flag, in_low, bias_qkv, vectors_one, vectors_two, b_up, gain_one
        )
        an = jnp.stack([a, az])
        anx, any_, am = swap(an, 1), swap(an, 2), swap(an, 4)
        anx, any_, am, an, c = tie(anx, any_, am, an, c)
        amx, amy, cz = swap(am, 1), swap(am, 2), swap(c, 12)
        amx, amy, cz, anx, c, d = tie(amx, amy, cz, anx, c, d)
        cn = jnp.stack([c, cz])
        amd, and_, cm = swap(amy, 1), swap(anx, 2), swap(cn, 4)
        cnx, cny, dz = swap(cn, 1), swap(cn, 2), swap(after(d, cm), 12)
        amd, and_, cm, cnx, cny = tie(amd, and_, cm, cnx, cny)
        dn = jnp.stack([d, dz])
        pieces_a = [an, am, anx, amx, any_, amy, and_, amd]
        cmx, cnd, dm = swap(cm, 1), swap(cnx, 2), swap(dn, 4)
        dnx, dny = swap(dn, 1), swap(dn, 2)
    else:
        a, c, d = (lax.all_gather(piece, "dp", axis=0, tiled=True) for piece in (a, c, d))
        pieces_a, pieces_c, pieces_d = as_pieces(a), as_pieces(c), as_pieces(d)
    w_a, qkv, prob, attended, part = attend(me, lengths, in_low, bias_qkv, pieces_a)
    if fast:
        cmx, cnd, dm, dnx, dny, cm, part = tie(cmx, cnd, dm, dnx, dny, cm, part)
        cmy, dnd, cmd = swap(cm, 2), swap(dny, 1), swap(cnd, 4)
    other = pair_swap(part)
    if fast:
        cmy, dnd, cmd, dm, other, part = tie(cmy, dnd, cmd, dm, other, part)
        pieces_c = [cn, cm, cnx, cmx, cny, cmy, cnd, cmd]
        dmx, dmy, dmd = swap(dm, 1), swap(dm, 2), swap(dnd, 4)
    w_u, normed_one, inverse_one, hidden_low, act_low, slope = up(
        me, in_low, part, other, vectors_one, b_up, pieces_c
    )
    if fast:
        dmx, dmy, dmd, act_low = tie(dmx, dmy, dmd, act_low)
        pieces_d = [dn, dm, dnx, dmx, dny, dmy, dnd, dmd]
    w_d, *parts = down(me, act_low, pieces_d)
    halves = [
        second_norm(index * part.shape[0], normed_one, part, pair_swap(part), grad_out, vectors_two)
        for index, part in enumerate(parts)
    ]
    results, dz_two, dz_two_low, sums_two = zip(*halves)
    dx, dy, turned = weight_grad(me, [dz_two_low], [act_low], ORDER[:2])
    if fast:
        dx, dy, turned, dz_two_low = tie(dx, dy, turned, dz_two_low)
        dxr, dyr = swap(dx, 1), swap(dy, 2)
    dxl, dyl, do = weight_grad(me, None, [act_low], ORDER[2:], turned=turned)
    d_pre_low, part, sums_up = hidden_back(dz_two_low, slope, w_d, w_u)
    cx, cy, cxl, cyl, co = weight_grad(me, [[hidden_low]], [d_pre_low])
    if fast:
        dxr, dyr, part, cx, cy, dxl, dyl, do = tie(dxr, dyr, part, cx, cy, dxl, dyl, do)
        cxr, cyr = swap(cx, 1), swap(cy, 2)
        dxl, dyl = add_late(dxl, dyl, dxr, dyr)
        dxlr, dylr = swap(dxl, 1), swap(dyl, 2)
    other = pair_swap(part)
    dz_one, dz_one_low, d_qkv, part, sums_one, sums_qkv = attend_back(
        lengths.shape[0], dz_two, part, other, normed_one, inverse_one, gain_one, flag, qkv, prob, w_a
    )
    if fast:
        cxr, cyr, dxlr, dylr, part, d_qkv, dz_one_low = tie(cxr, cyr, dxlr, dylr, part, d_qkv, dz_one_low)
        cxl, cyl = add_late(cxl, cyl, cxr, cyr)
        cxlr, cylr = swap(cxl, 1), swap(cyl, 2)
        d_near, d_mid = add_own(do, dxr, dyr, dxlr, dylr)
        d_midr = swap(d_mid, 4)
    sums_other = pair_swap(sums_one)
    joined = join(width // BLOCKS, sums_one, sums_other, sums_two, sums_up, sums_qkv)
    vector = joined.astype(B16) if fast else None
    ax, ay, axl, ayl, ao = weight_grad(me, [[in_low], [dz_one_low]], [d_qkv, attended], vector=vector)
    if fast:
        c_near, c_mid = add_own(co, cxr, cyr, cxlr, cylr)
        c_near, c_mid, d_midr, ax, ay, part = tie(c_near, c_mid, d_midr, ax, ay, part)
        axr, ayr = swap(ax, 1), swap(ay, 2)
        d_near, d_far = add_mid(d_near, d_midr)
        c_midr, d_farr = swap(c_mid, 4), swap(d_far, 12)
    other = pair_swap(part)
    d_tokens, result = last(dz_one, part, other, flag, results)
    sizes = [width] * 7 + [head_cols] * 2 + [w_up.shape[1]]
    if fast:
        axr, ayr, c_midr, d_farr, d_tokens, result = tie(axr, ayr, c_midr, d_farr, d_tokens, result)
        axl, ayl, vector = late_vector(axl, ayl, axr, ayr, vector)
        axlr, aylr = swap(axl, 1), swap(ayl, 2)
        c_near, c_far = add_mid(c_near, c_midr)
        c_farr = swap(c_far, 12)
        axlr, aylr, c_farr = tie(axlr, aylr, c_farr)
        a_near, a_mid, vector = own_vector(ao, axr, ayr, axlr, aylr, vector)
        a_midr = swap(a_mid, 4)
        d_w_down_t = d_near + d_farr.astype(F32)
        a_midr, d_w_down_t = tie(a_midr, d_w_down_t)
        a_near, a_far, vector = mid_vector(a_near, a_midr, vector)
        a_farr = swap(a_far, 12)
        d_w_up = c_near + c_farr.astype(F32)
        d_wa, summed = far_vector(a_near, a_farr, vector, sizes)
    else:
        full = []
        for parts in ((ax, ay, axl, ayl, ao), (cx, cy, cxl, cyl, co), (dx, dy, dxl, dyl, do)):
            blocks = [None] * BLOCKS
            for member, offsets in zip(parts, ORDER):
                for k, offset in enumerate(offsets):
                    blocks[offset] = member[k]
            full.append(jnp.concatenate(blocks).astype(F32))
        joined = lax.psum(joined, "dp")
        d_wa, d_w_up, d_w_down_t = (
            lax.psum_scatter(member, "dp", scatter_dimension=0, tiled=True) for member in full
        )
        d_wa = [d_wa[:, k * head_cols : (k + 1) * head_cols] for k in range(4)]
        joined = joined.reshape(-1)
        summed = []
        start = 0
        for size in sizes:
            summed.append(joined[start : start + size])
            start += size
    return (
        result,
        d_tokens,
        summed[0],
        d_wa[0],
        summed[7],
        d_wa[1],
        d_wa[2],
        summed[8],
        d_wa[3].T,
        summed[3],
        summed[1],
        summed[2],
        d_w_up,
        summed[9],
        d_w_down_t.T,
        summed[6],
        summed[4],
        summed[5],
    )


def solution(mesh):
    rows, flat, both = P("dp", None), P(), P("dp", "mp")
    return jax.shard_map(
        functools.partial(per_device, mesh.shape["dp"]),
        mesh=mesh,
        in_specs=(rows, P("dp"), P("dp"), flat, both, P("mp"), both, both, P("mp"), P("mp", "dp"),
                  flat, flat, flat, both, P("mp"), P("mp", "dp"), flat, flat, flat, rows),
        out_specs=(rows, rows, flat, both, P("mp"), both, both, P("mp"), P("mp", "dp"), flat, flat,
                   flat, both, P("mp"), P("mp", "dp"), flat, flat, flat),
        check_vma=False,
    )
```
